32 devices in a mesh: seq: 8 (over z, x), head: 4 (over y, core).
Axes of the slice: x: 2, y: 2, z: 4, core: 2. Of those that a mesh axis runs over, the one named last changes fastest.
Arguments:
- tokens: bfloat16 [2048, 3072], P('seq', 'head'), may hold values from -6 to 6
- norm_gain: float32 [3072], replicated, may hold values from 0.1 to 1.9
- w_query: bfloat16 [3072, 3072], P(None, 'head'), may hold values from -0.109375 to 0.109375
- w_key: bfloat16 [3072, 1024], P(None, 'head'), may hold values from -0.3125 to 0.3125
- w_value: bfloat16 [3072, 1024], P(None, 'head'), may hold values from -0.109375 to 0.109375
- w_out: bfloat16 [3072, 3072], P('head'), may hold values from -0.109375 to 0.109375
- keys_cache: bfloat16 [16384, 1024], P('seq', 'head'), may hold values from -120 to 120
- values_cache: bfloat16 [16384, 1024], P('seq', 'head'), may hold values from -6 to 6
- cached_lengths: int32 [4], replicated, may hold values from 0 to 3584, as said below
- rope_offsets: int32 [4], replicated, may hold values from 0 to 8191
Outputs:
- attn_proj: bfloat16 [2048, 3072], P('seq', 'head')
- keys_updated: bfloat16 [16384, 1024], P('seq', 'head')
- values_updated: bfloat16 [16384, 1024], P('seq', 'head')
The draws below stay inside these ranges and needn't reach their ends.
Inputs may be any that keep to these rules, and one draw needn't show every extreme that they name: `cached_lengths`: in every draw one request has exactly 3584 cached tokens.
All inputs are finite; a program needn't handle non-finite values.
Results may differ from the reference program's by a relative error of at most 0.02.
Values may be sent and summed in bfloat16 or wider, within the bound.
No kernel may reach another device: no remote copies, remote signals or barrier semaphores. Data moves between devices by JAX's collectives and lax.ppermute only.
A program may use at most 128 MiB of HBM per device.

```python
import math
import jax
import jax.numpy as jnp
from jax import lax

D = 3072
HQ = 24
KV = 8
HD = 128
TOK_DEV = 256
REQS = 4
GROUP = 2
NEW_LEN = 512
CACHE_MAX = 3584
CAP_DEV = 2048
TOKENS = 2048
SLOTS = 16384


def draw_keys_cache(key, part):
    first_key = jax.random.fold_in(key, 0)
    entries = jnp.clip(jax.random.normal(first_key, (SLOTS, KV * HD), jnp.float32), -3.3, 3.3) * 3.0
    return entries.astype(jnp.bfloat16)


def draw_values_cache(key, part):
    first_key, second_key = jax.random.split(key)
    noise = jnp.clip(jax.random.normal(first_key, (SLOTS // CAP_DEV, CAP_DEV, KV * HD), jnp.float32), -4.0, 4.0)
    offsets = jax.random.uniform(second_key, (SLOTS // CAP_DEV, 1, KV * HD), jnp.float32, -2.0, 2.0)
    shifted = noise + offsets
    return shifted.reshape(SLOTS, KV * HD).astype(jnp.bfloat16)


def draw_cached_lengths(key, part):
    first_key, second_key = jax.random.split(key)
    lengths = jax.random.randint(first_key, (REQS,), 0, CACHE_MAX + 1)
    longest = jax.random.randint(second_key, (), 0, REQS)
    return jnp.where(jnp.arange(REQS) == longest, CACHE_MAX, lengths).astype(jnp.int32)


def plant(values, stream_key, smallest, top_value):
    extent = values.shape
    place = [jax.random.randint(jax.random.fold_in(stream_key, axis), (), 0, extent[axis]) for axis in range(len(extent))]
    values = values.at[tuple(place)].set(smallest)
    longest = extent.index(max(extent))
    place[longest] = (place[longest] + 1) % extent[longest]
    return values.at[tuple(place)].set(top_value)


def shard_levels(own_key, shape, cuts, low, high):
    def one(axis_at, parts):
        draws = jax.random.uniform(jax.random.fold_in(jax.random.fold_in(own_key, 6), axis_at), (parts,), jnp.float32, low / len(cuts), high / len(cuts))
        return jnp.repeat(jnp.exp(draws), shape[axis_at] // parts).reshape((-1,) + (1,) * (len(shape) - axis_at - 1))

    gain = one(*cuts[0])
    for cut in cuts[1:]:
        gain = gain * one(*cut)
    return gain


def scatter_about(rng, dims, spread, most, cuts=(), held_as=jnp.bfloat16):
    level = shard_levels(rng, dims, cuts, -0.22, 0.18) if cuts else 1.0
    values = jax.random.normal(rng, dims, jnp.float32) * spread * level
    return jnp.minimum(jnp.maximum(values, -most), most).astype(held_as)


def setup_inputs(seed: int = 0) -> dict:
    key_list = jax.random.split(jax.random.key(seed), 11)
    tokens = scatter_about(key_list[0], (TOKENS, D), 1.0, 6.0, ((0, 8), (1, 4)))
    norm_gain = jnp.clip(1.0 + 0.18 * jax.random.normal(key_list[1], (D,), jnp.float32), 0.1, 1.9)
    w_query = scatter_about(key_list[2], (D, HQ * HD), D ** -0.5, 0.109375, ((1, 4),))
    w_key = scatter_about(key_list[3], (D, KV * HD), (D // 9) ** -0.5, 0.3125, ((1, 4),))
    w_value = scatter_about(key_list[4], (D, KV * HD), D ** -0.5, 0.109375, ((1, 4),))
    w_out = scatter_about(key_list[5], (HQ * HD, D), (HQ * HD) ** -0.5, 0.109375, ((0, 4),))
    keys_cache = draw_keys_cache(jax.random.fold_in(key_list[10], 71), 0)
    values_cache = draw_values_cache(jax.random.fold_in(key_list[10], 71), 0)
    cached_lengths = draw_cached_lengths(jax.random.fold_in(key_list[10], 71), 0)
    rope_offsets = plant(jax.random.randint(key_list[9], (REQS,), 0, 8192), jax.random.fold_in(key_list[9], 1), 0, 8191).astype(jnp.int32)
    return {"tokens": tokens, "norm_gain": norm_gain, "w_query": w_query, "w_key": w_key, "w_value": w_value, "w_out": w_out, "keys_cache": keys_cache, "values_cache": values_cache, "cached_lengths": cached_lengths, "rope_offsets": rope_offsets}


rope_base = 500000.0

def rotate(vectors, positions):
    half_width = vectors.shape[-1] // 2
    frequency = rope_base ** (-jnp.arange(half_width, dtype=jnp.float32) * 2.0 / vectors.shape[-1])
    angles = positions.astype(jnp.float32)[:, None] * frequency[None, :]
    cosine = jnp.cos(angles)[:, None, :]
    sine_part = jnp.sin(angles)[:, None, :]
    first_half = vectors[..., :half_width]
    second_half = vectors[..., half_width:]
    return jnp.concatenate([first_half * cosine - second_half * sine_part, second_half * cosine + first_half * sine_part], -1)

def to_requests(array, rows):
    width = array.shape[-1]
    return array.reshape(GROUP, REQS, rows, width).transpose(1, 0, 2, 3).reshape(REQS * GROUP * rows, width)

def from_requests(array, rows):
    width = array.shape[-1]
    return array.reshape(REQS, GROUP, rows, width).transpose(1, 0, 2, 3).reshape(REQS * GROUP * rows, width)

def reference(tokens, norm_gain, w_query, w_key, w_value, w_out, keys_cache, values_cache, cached_lengths, rope_offsets):
    ordered = to_requests(tokens, TOK_DEV)
    widened = ordered.astype(jnp.float32)
    normed = (widened * lax.rsqrt(lax.optimization_barrier(jnp.mean(widened * widened, -1, keepdims=True)) + 1e-05) * norm_gain).astype(jnp.bfloat16)
    token_index = jnp.arange(TOKENS, dtype=jnp.int32)
    owner = token_index // NEW_LEN
    within = token_index % NEW_LEN
    positions = rope_offsets[owner] + cached_lengths[owner] + within
    repeat = HQ // KV
    queries = rotate(jnp.dot(normed, w_query, preferred_element_type=jnp.float32).reshape(TOKENS, HQ, HD), positions).astype(jnp.bfloat16)
    new_keys = rotate(jnp.dot(normed, w_key, preferred_element_type=jnp.float32).reshape(TOKENS, KV, HD), positions).astype(jnp.bfloat16)
    new_values = jnp.dot(normed, w_value, preferred_element_type=jnp.float32).astype(jnp.bfloat16)
    capacity = SLOTS // REQS
    slots = jnp.arange(capacity, dtype=jnp.int32)
    source = slots[None, :] - cached_lengths[:, None]
    inside = (source >= 0) & (source < NEW_LEN)
    picked = jnp.clip(source, 0, NEW_LEN - 1).astype(jnp.int32)

    def update(old_cache, fresh):
        old_cache = to_requests(old_cache, CAP_DEV).reshape(REQS, capacity, KV * HD)
        fresh = fresh.reshape(REQS, NEW_LEN, KV * HD)
        chosen = jnp.take_along_axis(fresh, picked[:, :, None], axis=1)
        return jnp.where(inside[:, :, None], chosen, old_cache).reshape(SLOTS, KV * HD)
    keys_ordered = update(keys_cache, new_keys)
    values_ordered = update(values_cache, new_values)
    query_rows = math.gcd(NEW_LEN, 128)
    per_request = NEW_LEN // query_rows
    request_ids = (jnp.arange(REQS * per_request, dtype=jnp.int32) // per_request).astype(jnp.int32)
    starts = (jnp.arange(REQS * per_request, dtype=jnp.int32) % per_request * query_rows).astype(jnp.int32)
    key_table = keys_ordered.reshape(REQS, capacity, KV, HD)
    value_table = values_ordered.reshape(REQS, capacity, KV, HD)

    def one_block(block_item):
        request, start = block_item
        query_block = lax.dynamic_slice_in_dim(queries, request * NEW_LEN + start, query_rows, 0)
        query_block = query_block.reshape(query_rows, KV, repeat, HD).astype(jnp.float32)
        key_block = lax.dynamic_index_in_dim(key_table, request, 0, False).astype(jnp.float32)
        value_block = lax.dynamic_index_in_dim(value_table, request, 0, False).astype(jnp.float32)
        scores = jnp.einsum('qgrd,kgd->grqk', query_block, key_block) / math.sqrt(HD)
        limit = lax.dynamic_index_in_dim(cached_lengths, request, 0, False) + start + jnp.arange(query_rows, dtype=jnp.int32)
        visible = slots[None, :] <= limit[:, None]
        masked = jnp.where(visible, scores, -jnp.inf)
        running_max = lax.optimization_barrier(jnp.max(masked, -1, keepdims=True))
        weights = jnp.where(visible, jnp.exp(masked - running_max), 0.0)
        denominator = lax.optimization_barrier(jnp.sum(weights, -1))
        rounded = lax.optimization_barrier(weights.astype(jnp.bfloat16))
        summed = jnp.einsum('grqk,kgd->qgrd', rounded.astype(jnp.float32), value_block)
        return (summed / denominator.transpose(2, 0, 1)[..., None]).astype(jnp.bfloat16)
    attended = lax.map(one_block, (request_ids, starts)).reshape(TOKENS, HQ * HD)
    projected = jnp.dot(attended, w_out, preferred_element_type=jnp.float32).astype(jnp.bfloat16)
    attn_proj = from_requests(projected, TOK_DEV)
    keys_updated = from_requests(keys_ordered, CAP_DEV)
    values_updated = from_requests(values_ordered, CAP_DEV)
    return (attn_proj, keys_updated, values_updated)
```

```python
import functools
import math

import jax
import jax.numpy as jnp
from jax import lax
from jax.experimental import pallas as pl
from jax.experimental.pallas import tpu as pltpu
from jax.sharding import PartitionSpec as P

HD = 128
LANES = 128
STAT_ROWS = 8
ROW_TILE = 16
CORES = 2
MIB = 1 << 20

rope_base = 500000.0
neg_large = -1e30
log2_scale = math.log2(math.e) / math.sqrt(HD)

VMEM = pl.BlockSpec(memory_space=pltpu.VMEM)
SMEM = pl.BlockSpec(memory_space=pltpu.SMEM)


def shifted(shard, axis, by):
    devices = lax.axis_size(axis)
    return lax.ppermute(shard, axis, [(i, (i + by) % devices) for i in range(devices)])


def other_core(shard):
    devices = lax.axis_size("head")
    return lax.ppermute(shard, "head", [(i, i ^ 1) for i in range(devices)])


def rope_tables(positions):
    half_width = HD // 2
    frequency = rope_base ** (-jnp.arange(half_width, dtype=jnp.float32) * 2.0 / HD)
    angles = positions.astype(jnp.float32)[:, None] * frequency[None, :]
    cosine = jnp.cos(angles)
    sine = jnp.sin(angles)
    return jnp.concatenate([cosine, cosine], -1), jnp.concatenate([-sine, sine], -1)


def rotate(vectors, cosine, sine):
    return vectors * cosine + pltpu.roll(vectors, HD // 2, 1) * sine


def normed_slices(owner, x_refs, gain):
    rows, width = x_refs[0].shape
    total = jnp.zeros((rows, 1), jnp.float32)
    for x_ref in x_refs:
        wide = x_ref[...].astype(jnp.float32)
        total = total + jnp.sum(wide * wide, -1, keepdims=True)
    factor = lax.rsqrt(total / (width * len(x_refs)) + 1e-05)
    for index, x_ref in enumerate(x_refs):
        wide = x_ref[...].astype(jnp.float32)
        yield (wide * factor * gain[owner[index]]).astype(jnp.bfloat16)


def weight_rows(owner, index, width):
    return pl.ds(pl.multiple_of(owner[index] * width, LANES), width)


def dot(left, right):
    return jnp.dot(left, right, preferred_element_type=jnp.float32)


def dot_transposed(left, right):
    return lax.dot_general(
        left, right, (((1,), (1,)), ((), ())), preferred_element_type=jnp.float32
    )


def stat_rows(columns, rows):
    lane = lax.broadcasted_iota(jnp.int32, (rows, LANES), 1)
    table = jnp.zeros((rows, LANES), jnp.float32)
    for index, column in enumerate(columns):
        table = jnp.where(lane == index, column, table)
    return table.T[:STAT_ROWS]


def attend_kernel(slices, kv_heads, keep_queries, owner, visible_slots, *refs):
    x_refs = refs[:slices]
    gain, w_query, cosine, sine, keys, values = refs[slices : slices + 6]
    partial, stats = refs[slices + 6 : slices + 8]
    rows, width = x_refs[0].shape
    q_heads = w_query.shape[1] // HD
    repeat = q_heads // kv_heads
    product = jnp.zeros((rows, q_heads * HD), jnp.float32)
    for index, normed in enumerate(normed_slices(owner, x_refs, gain)):
        product = product + dot(normed, w_query[weight_rows(owner, index, width), :])
    slot = lax.broadcasted_iota(jnp.int32, (1, keys.shape[0]), 1)
    visible = slot < visible_slots[0]
    columns = []
    for head in range(q_heads):
        own = slice(head * HD, (head + 1) * HD)
        shared = slice(head // repeat * HD, (head // repeat + 1) * HD)
        query = rotate(product[:, own], cosine[...], sine[...]).astype(jnp.bfloat16)
        if keep_queries:
            refs[slices + 8][:, own] = query
        scores = jnp.where(visible, dot_transposed(query, keys[:, shared]), neg_large)
        largest = jnp.max(scores, -1, keepdims=True)
        weights = jnp.exp2((scores - largest) * log2_scale)
        denominator = jnp.sum(weights, -1, keepdims=True)
        summed = dot(weights.astype(jnp.bfloat16), values[:, shared])
        partial[:, own] = (summed / denominator).astype(partial.dtype)
        columns.append(largest * log2_scale + jnp.log2(denominator))
    stats[...] = stat_rows(columns, rows)


def attend(owner, visible_slots, pieces, gain, w_query, tables, keys, values, kv_heads, own):
    rows, width = pieces[0].shape
    out_width = w_query.shape[1]
    out_shape = [
        jax.ShapeDtypeStruct((rows, out_width), jnp.float32 if own else jnp.bfloat16),
        jax.ShapeDtypeStruct((STAT_ROWS, rows), jnp.float32),
    ]
    if own:
        out_shape.append(jax.ShapeDtypeStruct((rows, out_width), jnp.bfloat16))
    slots = keys.shape[0]
    flops = 2 * rows * out_width * (w_query.shape[0] + 2 * slots)
    return pl.pallas_call(
        functools.partial(attend_kernel, len(pieces), kv_heads, own),
        out_shape=out_shape,
        in_specs=[SMEM, SMEM] + [VMEM] * (len(pieces) + 6),
        out_specs=[VMEM] * len(out_shape),
        compiler_params=pltpu.CompilerParams(vmem_limit_bytes=48 * MIB),
        cost_estimate=pl.CostEstimate(
            flops=flops,
            bytes_accessed=2 * (w_query.size + 2 * keys.size + 2 * rows * out_width),
            transcendentals=rows * out_width // HD * slots,
        ),
        name="attend_own" if own else "attend_partner",
    )(owner, visible_slots, *pieces, gain, w_query, *tables, keys, values)


def fresh_kernel(slices, kv_heads, owner, *refs):
    x_refs = refs[:slices]
    gain, w_key, w_value, cosine, sine, new_keys, new_values = refs[slices:]
    rows, width = x_refs[0].shape
    key_sum = jnp.zeros(new_keys.shape, jnp.float32)
    value_sum = jnp.zeros(new_values.shape, jnp.float32)
    for index, normed in enumerate(normed_slices(owner, x_refs, gain)):
        along = weight_rows(owner, index, width)
        key_sum = key_sum + dot(normed, w_key[along, :])
        value_sum = value_sum + dot(normed, w_value[along, :])
    for head in range(kv_heads):
        own = slice(head * HD, (head + 1) * HD)
        new_keys[:, own] = rotate(key_sum[:, own], cosine[...], sine[...]).astype(jnp.bfloat16)
    new_values[...] = value_sum.astype(jnp.bfloat16)


def fresh(owner, pieces, gain, w_key, w_value, tables, kv_heads):
    rows = pieces[0].shape[0]
    shape = jax.ShapeDtypeStruct((rows, w_key.shape[1]), jnp.bfloat16)
    return pl.pallas_call(
        functools.partial(fresh_kernel, len(pieces), kv_heads),
        out_shape=[shape, shape],
        in_specs=[SMEM] + [VMEM] * (len(pieces) + 5),
        out_specs=[VMEM, VMEM],
        compiler_params=pltpu.CompilerParams(vmem_limit_bytes=32 * MIB),
        cost_estimate=pl.CostEstimate(
            flops=4 * rows * w_key.size, bytes_accessed=4 * w_key.size, transcendentals=0
        ),
        name="fresh_kv",
    )(owner, *pieces, gain, w_key, w_value, *tables)


def write_rows(target, fresh_rows, first):
    rows = fresh_rows.shape[0]
    slab_rows = target.shape[0]
    span = rows + ROW_TILE
    start = jnp.clip(first // ROW_TILE * ROW_TILE, 0, slab_rows - span)
    window = pl.ds(pl.multiple_of(start, ROW_TILE), span)
    shift = start - first
    place = lax.broadcasted_iota(jnp.int32, (span, rows), 0) + shift
    chosen = place == lax.broadcasted_iota(jnp.int32, (span, rows), 1)
    moved = dot(chosen.astype(jnp.bfloat16), fresh_rows)
    row = lax.broadcasted_iota(jnp.int32, (span, target.shape[1]), 0) + shift
    inside = (row >= 0) & (row < rows)
    old = target[window, :].astype(jnp.float32)
    target[window, :] = jnp.where(inside, moved, old).astype(jnp.bfloat16)


def update_kernel(sources, kv_heads, first_token, first_slot, queries, *refs):
    key_refs = refs[:sources]
    value_refs = refs[sources : 2 * sources]
    keys, values, partial, stats, keys_updated, values_updated = refs[2 * sources :]
    rows = queries.shape[0]
    q_heads = queries.shape[1] // HD
    repeat = q_heads // kv_heads
    fresh_keys = jnp.concatenate([ref[...] for ref in key_refs], 0)
    fresh_values = jnp.concatenate([ref[...] for ref in value_refs], 0)
    token = lax.broadcasted_iota(jnp.int32, (rows, rows), 0)
    within = lax.broadcasted_iota(jnp.int32, (rows, rows), 1)
    visible = jnp.concatenate(
        [
            within + first_token[source] <= token + first_token[0]
            for source in range(sources)
        ],
        1,
    )
    columns = []
    for head in range(q_heads):
        own = slice(head * HD, (head + 1) * HD)
        shared = slice(head // repeat * HD, (head // repeat + 1) * HD)
        scores = jnp.where(
            visible, dot_transposed(queries[:, own], fresh_keys[:, shared]), neg_large
        )
        largest = jnp.max(scores, -1, keepdims=True)
        weights = jnp.exp2((scores - largest) * log2_scale)
        denominator = jnp.sum(weights, -1, keepdims=True)
        summed = dot(weights.astype(jnp.bfloat16), fresh_values[:, shared])
        partial[:, own] = summed / denominator
        columns.append(largest * log2_scale + jnp.log2(denominator))
    stats[...] = stat_rows(columns, rows)
    keys_updated[...] = keys[...]
    values_updated[...] = values[...]
    for source in range(sources):
        write_rows(keys_updated, key_refs[source][...], first_slot[source])
        write_rows(values_updated, value_refs[source][...], first_slot[source])


def update(first_token, first_slot, queries, new_keys, new_values, keys, values, kv_heads):
    rows, width = queries.shape
    sources = len(new_keys)
    slab = jax.ShapeDtypeStruct(keys.shape, keys.dtype)
    return pl.pallas_call(
        functools.partial(update_kernel, sources, kv_heads),
        out_shape=[
            jax.ShapeDtypeStruct((rows, width), jnp.float32),
            jax.ShapeDtypeStruct((STAT_ROWS, rows), jnp.float32),
            slab,
            slab,
        ],
        in_specs=[SMEM, SMEM] + [VMEM] * (2 * sources + 3),
        out_specs=[VMEM] * 4,
        compiler_params=pltpu.CompilerParams(vmem_limit_bytes=48 * MIB),
        cost_estimate=pl.CostEstimate(
            flops=4 * rows * width * rows * sources,
            bytes_accessed=8 * keys.size,
            transcendentals=rows * width // HD * rows * sources,
        ),
        name="fresh_attend_update",
    )(first_token, first_slot, queries, *new_keys, *new_values, keys, values)


def project_kernel(count, block_of, *refs):
    partials = refs[:count]
    stats = refs[count : 2 * count]
    w_out, projected = refs[2 * count :]
    rows = partials[0].shape[0]
    blocks, _, width = projected.shape
    padding = jnp.zeros((LANES - STAT_ROWS, rows), jnp.float32)
    logs = [jnp.concatenate([stat[...], padding], 0).T for stat in stats]
    largest = functools.reduce(jnp.maximum, logs)
    shares = [jnp.exp2(log - largest) for log in logs]
    total = functools.reduce(jnp.add, shares)
    heads = []
    for head in range(partials[0].shape[1] // HD):
        own = slice(head * HD, (head + 1) * HD)
        column = slice(head, head + 1)
        merged = functools.reduce(
            jnp.add,
            [
                part[:, own].astype(jnp.float32) * share[:, column]
                for part, share in zip(partials, shares)
            ],
        )
        heads.append((merged / total[:, column]).astype(jnp.bfloat16))
    attended = jnp.concatenate(heads, 1)
    for block in range(blocks):
        along = pl.ds(pl.multiple_of(block_of[block] * width, LANES), width)
        projected[block] = dot(attended, w_out[:, along]).astype(projected.dtype)


def project(block_of, partials, stats, w_out):
    rows, width = partials[0].shape
    blocks = block_of.shape[0]
    return pl.pallas_call(
        functools.partial(project_kernel, len(partials)),
        out_shape=jax.ShapeDtypeStruct((blocks, rows, w_out.shape[1] // blocks), jnp.bfloat16),
        in_specs=[SMEM] + [VMEM] * (2 * len(partials) + 1),
        out_specs=VMEM,
        compiler_params=pltpu.CompilerParams(vmem_limit_bytes=40 * MIB),
        cost_estimate=pl.CostEstimate(
            flops=2 * rows * w_out.size, bytes_accessed=2 * w_out.size, transcendentals=0
        ),
        name="combine_project",
    )(block_of, *partials, *stats, w_out)


def shards(
    tokens,
    norm_gain,
    w_query,
    w_key,
    w_value,
    w_out,
    keys_cache,
    values_cache,
    cached_lengths,
    rope_offsets,
):
    rows, width = tokens.shape
    slab_rows = keys_cache.shape[0]
    requests = cached_lengths.shape[0]
    groups = lax.axis_size("seq") // requests
    heads = lax.axis_size("head")
    chips = heads // CORES
    kv_heads = w_key.shape[1] // HD
    member = lax.axis_index("seq")
    head_member = lax.axis_index("head")
    request = member % requests
    position_in = member // requests
    length = lax.dynamic_index_in_dim(cached_lengths, request, 0, False)
    offset = lax.dynamic_index_in_dim(rope_offsets, request, 0, False)
    gain = norm_gain.reshape(heads, 1, width)

    chip_shifts = [(head_member - CORES * k) % heads for k in range(chips)]
    owner = jnp.stack(chip_shifts + [one ^ 1 for one in chip_shifts]).astype(jnp.int32)

    def all_features(own):
        along = [own] + [shifted(own, "head", CORES * k) for k in range(1, chips)]
        return along + [other_core(piece) for piece in along]

    arrived = [tokens] + [shifted(tokens, "seq", k * requests) for k in range(1, groups)]
    sources = [(position_in - k) % groups for k in range(groups)]
    index_new = jnp.arange(rows, dtype=jnp.int32)
    tables = [rope_tables(offset + length + s * rows + index_new) for s in sources]
    visible_slots = jnp.clip(length - position_in * slab_rows, 0, slab_rows).reshape(1)

    pieces = [all_features(piece) for piece in arrived]
    partials = []
    stats = []
    for k in range(1, groups):
        partial, stat = attend(
            owner, visible_slots, pieces[k], gain, w_query, tables[k], keys_cache, values_cache,
            kv_heads, False,
        )
        partials.append(shifted(partial, "seq", -k * requests))
        stats.append(shifted(stat, "seq", -k * requests))
    partial, stat, queries = attend(
        owner, visible_slots, pieces[0], gain, w_query, tables[0], keys_cache, values_cache,
        kv_heads, True,
    )
    partials.append(partial)
    stats.append(stat)
    new_rows = [
        fresh(owner, pieces[k], gain, w_key, w_value, tables[k], kv_heads) for k in range(groups)
    ]
    first_token = jnp.stack([s * rows for s in sources]).astype(jnp.int32)
    first_slot = length - position_in * slab_rows + first_token
    partial, stat, keys_updated, values_updated = update(
        first_token, first_slot, queries, [k for k, _ in new_rows], [v for _, v in new_rows],
        keys_cache, values_cache, kv_heads,
    )
    partials.append(partial)
    stats.append(stat)

    ahead = [(head_member + CORES * k) % heads for k in range(chips)]
    block_of = jnp.stack(ahead + [one ^ 1 for one in ahead]).astype(jnp.int32)
    projected = project(block_of, partials, stats, w_out)
    received = other_core(projected[chips:])
    summed = projected[:chips].astype(jnp.float32) + received.astype(jnp.float32)
    total = summed[0]
    for k in range(1, chips):
        arrived_sum = shifted(summed[k].astype(jnp.bfloat16), "head", CORES * k)
        total = total + arrived_sum.astype(jnp.float32)
    return (total.astype(jnp.bfloat16), keys_updated, values_updated)


def solution(mesh):
    return jax.shard_map(
        shards,
        mesh=mesh,
        in_specs=(
            P("seq", "head"),
            P(),
            P(None, "head"),
            P(None, "head"),
            P(None, "head"),
            P("head", None),
            P("seq", "head"),
            P("seq", "head"),
            P(),
            P(),
        ),
        out_specs=(P("seq", "head"), P("seq", "head"), P("seq", "head")),
        check_vma=False,
    )
```

```python
import functools
import math

import jax
import jax.numpy as jnp
from jax import lax
from jax.experimental import pallas as pl
from jax.experimental.pallas import tpu as pltpu
from jax.sharding import PartitionSpec as P

HD = 128
LANES = 128
STAT_ROWS = 8
ROW_TILE = 16
CORES = 2
CHUNKS = 2
MIB = 1 << 20

rope_base = 500000.0
neg_large = -1e30
log2_scale = math.log2(math.e) / math.sqrt(HD)

VMEM = pl.BlockSpec(memory_space=pltpu.VMEM)
SMEM = pl.BlockSpec(memory_space=pltpu.SMEM)


def shifted(shard, axis, by):
    devices = lax.axis_size(axis)
    return lax.ppermute(shard, axis, [(i, (i + by) % devices) for i in range(devices)])


def other_core(shard):
    devices = lax.axis_size("head")
    return lax.ppermute(shard, "head", [(i, i ^ 1) for i in range(devices)])


def all_features(own):
    chips = lax.axis_size("head") // CORES
    along = [own] + [shifted(own, "head", CORES * k) for k in range(1, chips)]
    return along + [other_core(piece) for piece in along]


def place_of(requests):
    member = lax.axis_index("seq")
    return lax.rem(member, requests), lax.div(member, requests)


def source_of(position_in, turn, groups):
    return lax.rem(position_in + (groups - turn), groups)


def dot(left, right):
    return jnp.dot(left, right, preferred_element_type=jnp.float32)


def dot_transposed(left, right):
    return lax.dot_general(
        left, right, (((1,), (1,)), ((), ())), preferred_element_type=jnp.float32
    )


def call(kernel, out_shape, scalars, arrays, limit, flops, transcendentals, name):
    moved = sum(a.size * a.dtype.itemsize for a in arrays)
    moved += sum(math.prod(s.shape) * s.dtype.itemsize for s in out_shape)
    return pl.pallas_call(
        kernel,
        out_shape=out_shape,
        in_specs=[SMEM] * len(scalars) + [VMEM] * len(arrays),
        out_specs=[VMEM] * len(out_shape),
        compiler_params=pltpu.CompilerParams(vmem_limit_bytes=limit * MIB),
        cost_estimate=pl.CostEstimate(
            flops=flops, bytes_accessed=moved, transcendentals=transcendentals
        ),
        name=name,
    )(*scalars, *arrays)


def prepare_kernel(groups, rows, lengths, offsets, keys, values, cosine, sine, wide_keys, wide_values):
    request, position_in = place_of(lengths.shape[0])
    length = lengths[request]
    slots = keys.shape[0]
    lane = lax.broadcasted_iota(jnp.int32, (rows, LANES), 1)
    row = lax.broadcasted_iota(jnp.int32, (rows, LANES), 0)
    half = lax.rem(lane, HD // 2).astype(jnp.float32)
    frequency = jnp.exp2(half * (-2.0 / HD * math.log2(rope_base)))
    sign = jnp.where(lane < HD // 2, -1.0, 1.0)
    for turn in range(groups):
        first = offsets[request] + length + source_of(position_in, turn, groups) * rows
        angles = (row + first).astype(jnp.float32) * frequency
        part = slice(turn * rows, (turn + 1) * rows)
        cosine[part] = jnp.cos(angles)
        sine[part] = jnp.sin(angles) * sign
    slot = lax.broadcasted_iota(jnp.int32, (slots, LANES), 0) + position_in * slots
    lane = lax.broadcasted_iota(jnp.int32, (slots, LANES), 1)
    bias = jnp.where((lane == 0) & (slot >= length), neg_large, 0.0).astype(jnp.bfloat16)
    ones = jnp.where(lane == 0, 1.0, 0.0).astype(jnp.bfloat16)
    for head in range(keys.shape[1] // HD):
        own = slice(head * HD, (head + 1) * HD)
        wide_keys[head, :, :HD] = keys[:, own]
        wide_keys[head, :, HD:] = bias
        wide_values[head, :, :HD] = values[:, own]
        wide_values[head, :, HD:] = ones


def prepare(lengths, offsets, keys, values, groups, rows):
    table = jax.ShapeDtypeStruct((groups * rows, LANES), jnp.float32)
    slots, width = keys.shape
    wide = jax.ShapeDtypeStruct((width // HD, slots, HD + LANES), jnp.bfloat16)
    return call(
        functools.partial(prepare_kernel, groups, rows),
        [table, table, wide, wide],
        [lengths, offsets],
        [keys, values],
        24,
        40 * groups * rows * LANES,
        0,
        "rope_tables_wide_caches",
    )


def rotate(vectors, cosine, sine):
    return vectors * cosine + pltpu.roll(vectors, HD // 2, 1) * sine


def project_normed(pieces, gain, weights):
    heads = gain.shape[0]
    width = gain.shape[2]
    me = lax.axis_index("head")
    squares = 0.0
    sums = [0.0] * len(weights)
    for index, piece in enumerate(pieces):
        owner = lax.rem(me + (heads - CORES * (index % (heads // CORES))), heads)
        if index >= heads // CORES:
            owner = owner ^ 1
        wide = piece.astype(jnp.float32)
        scaled = (wide * gain[owner]).astype(jnp.bfloat16)
        along = pl.ds(pl.multiple_of(owner * width, LANES), width)
        for place, weight in enumerate(weights):
            sums[place] = sums[place] + dot(scaled, weight[along, :])
        squares = squares + jnp.sum(wide * wide, -1, keepdims=True)
    factor = lax.rsqrt(squares / (heads * width) + 1e-05)
    return [total * factor for total in sums]


def stat_rows(columns, rows):
    lane = lax.broadcasted_iota(jnp.int32, (rows, LANES), 1)
    table = jnp.zeros((rows, LANES), jnp.float32)
    for index, column in enumerate(columns):
        table = jnp.where(lane == index, column, table)
    return table.T[:STAT_ROWS]


def attend_kernel(count, own, row_at, table_at, *refs):
    x_refs = refs[:count]
    gain, w_query, cosine, sine, wide_keys, wide_values = refs[count : count + 6]
    outputs = refs[count + 6 :]
    rows = outputs[0].shape[0] - (0 if own else ROW_TILE)
    pieces = [ref[row_at : row_at + rows] for ref in x_refs]
    (product,) = project_normed(pieces, gain, [w_query])
    cosine = cosine[table_at : table_at + rows]
    sine = sine[table_at : table_at + rows]
    kv_heads = wide_keys.shape[0]
    repeat = product.shape[1] // HD // kv_heads
    lane = lax.broadcasted_iota(jnp.int32, (repeat * rows, LANES), 1)
    mark = jnp.where(lane == 0, 1.0, 0.0).astype(jnp.bfloat16)
    queries = [
        (rotate(product[:, head * HD : (head + 1) * HD], cosine, sine) * log2_scale).astype(
            jnp.bfloat16
        )
        for head in range(kv_heads * repeat)
    ]
    scores = []
    for head in range(kv_heads):
        stacked = jnp.concatenate(queries[head * repeat : (head + 1) * repeat], 0)
        scores.append(dot_transposed(jnp.concatenate([stacked, mark], 1), wide_keys[head]))
    columns = []
    for head in range(kv_heads):
        largest = jnp.max(scores[head], -1, keepdims=True)
        weights = jnp.exp2(scores[head] - largest).astype(jnp.bfloat16)
        summed = dot(weights, wide_values[head])
        denominator = summed[:, HD : HD + 1]
        result = summed[:, :HD] / denominator
        logs = largest + jnp.log2(denominator)
        for turn in range(repeat):
            part = slice(turn * rows, (turn + 1) * rows)
            at = (head * repeat + turn) * HD
            outputs[0][:rows, at : at + HD] = result[part].astype(outputs[0].dtype)
            columns.append(logs[part])
    stats = stat_rows(columns, rows)
    if own:
        outputs[1][...] = stats
        outputs[2][...] = jnp.concatenate(queries, 1)
        return
    tail = jnp.zeros((ROW_TILE, outputs[0].shape[1]), jnp.bfloat16)
    outputs[0][rows:] = tail
    rest = jnp.concatenate([stats, jnp.zeros((ROW_TILE - STAT_ROWS, rows), jnp.float32)], 0)
    for part in range(3):
        rounded = rest.astype(jnp.bfloat16)
        outputs[0][rows:, part * rows : (part + 1) * rows] = rounded
        rest = rest - rounded.astype(jnp.float32)


def attend(pieces, gain, w_query, tables, wide_keys, wide_values, own, rows, row_at, table_at):
    out_width = w_query.shape[1]
    slots = wide_keys.shape[1]
    if own:
        out_shape = [
            jax.ShapeDtypeStruct((rows, out_width), jnp.float32),
            jax.ShapeDtypeStruct((STAT_ROWS, rows), jnp.float32),
            jax.ShapeDtypeStruct((rows, out_width), jnp.bfloat16),
        ]
    else:
        out_shape = [jax.ShapeDtypeStruct((rows + ROW_TILE, out_width), jnp.bfloat16)]
    return call(
        functools.partial(attend_kernel, len(pieces), own, row_at, table_at),
        out_shape,
        [],
        [*pieces, gain, w_query, *tables, wide_keys, wide_values],
        28,
        2 * rows * out_width * (w_query.shape[0] + 4 * slots),
        rows * out_width // HD * slots,
        "attend_own" if own else "attend_partner",
    )


def fresh_kernel(chunks, table_at, *refs):
    x_refs = refs[:-7]
    gain, w_key, w_value, cosine, sine, new_keys, new_values = refs[-7:]
    count = len(x_refs) // chunks
    rows = new_keys.shape[0]
    pieces = [
        jnp.concatenate([x_refs[chunk * count + index][...] for chunk in range(chunks)], 0)
        for index in range(count)
    ]
    keys, values = project_normed(pieces, gain, [w_key, w_value])
    cosine = cosine[table_at : table_at + rows]
    sine = sine[table_at : table_at + rows]
    for head in range(keys.shape[1] // HD):
        own = slice(head * HD, (head + 1) * HD)
        new_keys[:, own] = rotate(keys[:, own], cosine, sine).astype(jnp.bfloat16)
    new_values[...] = values.astype(jnp.bfloat16)


def fresh(chunks, gain, w_key, w_value, tables, table_at):
    rows = sum(pieces[0].shape[0] for pieces in chunks)
    shape = jax.ShapeDtypeStruct((rows, w_key.shape[1]), jnp.bfloat16)
    return call(
        functools.partial(fresh_kernel, len(chunks), table_at),
        [shape, shape],
        [],
        [*(piece for pieces in chunks for piece in pieces), gain, w_key, w_value, *tables],
        20,
        4 * rows * w_key.size,
        0,
        "fresh_kv",
    )


def write_rows(target, fresh_rows, first):
    rows = fresh_rows.shape[0]
    slab_rows = target.shape[0]
    span = rows + ROW_TILE
    start = jnp.clip(first, 0, slab_rows - span)
    start = start - lax.rem(start, ROW_TILE)
    window = pl.ds(pl.multiple_of(start, ROW_TILE), span)
    shift = start - first
    place = lax.broadcasted_iota(jnp.int32, (span, rows), 0) + shift
    chosen = place == lax.broadcasted_iota(jnp.int32, (span, rows), 1)
    moved = dot(chosen.astype(jnp.bfloat16), fresh_rows)
    row = lax.broadcasted_iota(jnp.int32, (span, target.shape[1]), 0) + shift
    inside = (row >= 0) & (row < rows)
    old = target[window, :].astype(jnp.float32)
    target[window, :] = jnp.where(inside, moved, old).astype(jnp.bfloat16)


def update_kernel(groups, chunks, kv_heads, lengths, *refs):
    query_refs = refs[:chunks]
    key_refs = refs[chunks : chunks + groups]
    value_refs = refs[chunks + groups : chunks + 2 * groups]
    keys, values, partial, stats, keys_updated, values_updated = refs[chunks + 2 * groups :]
    request, position_in = place_of(lengths.shape[0])
    sources = [source_of(position_in, turn, groups) for turn in range(groups)]
    rows, width = partial.shape
    repeat = width // HD // kv_heads
    queries = jnp.concatenate([ref[...] for ref in query_refs], 0)
    fresh_keys = jnp.concatenate([ref[...] for ref in key_refs], 0)
    fresh_values = jnp.concatenate([ref[...] for ref in value_refs], 0)
    token = lax.broadcasted_iota(jnp.int32, (rows, rows), 0)
    within = lax.broadcasted_iota(jnp.int32, (rows, rows), 1)
    visible = jnp.concatenate(
        [within + source * rows <= token + position_in * rows for source in sources], 1
    )
    columns = []
    for head in range(kv_heads * repeat):
        own = slice(head * HD, (head + 1) * HD)
        shared = slice(head // repeat * HD, (head // repeat + 1) * HD)
        scores = jnp.where(
            visible, dot_transposed(queries[:, own], fresh_keys[:, shared]), neg_large
        )
        largest = jnp.max(scores, -1, keepdims=True)
        weights = jnp.exp2(scores - largest)
        denominator = jnp.sum(weights, -1, keepdims=True)
        summed = dot(weights.astype(jnp.bfloat16), fresh_values[:, shared])
        partial[:, own] = summed / denominator
        columns.append(largest + jnp.log2(denominator))
    stats[...] = stat_rows(columns, rows)
    keys_updated[...] = keys[...]
    values_updated[...] = values[...]
    for turn in range(groups):
        first = lengths[request] + sources[turn] * rows - position_in * keys.shape[0]
        write_rows(keys_updated, key_refs[turn][...], first)
        write_rows(values_updated, value_refs[turn][...], first)


def update(lengths, queries, new_keys, new_values, keys, values):
    rows = sum(query.shape[0] for query in queries)
    width = queries[0].shape[1]
    groups = len(new_keys)
    slab = jax.ShapeDtypeStruct(keys.shape, keys.dtype)
    return call(
        functools.partial(update_kernel, groups, len(queries), keys.shape[1] // HD),
        [
            jax.ShapeDtypeStruct((rows, width), jnp.float32),
            jax.ShapeDtypeStruct((STAT_ROWS, rows), jnp.float32),
            slab,
            slab,
        ],
        [lengths],
        [*queries, *new_keys, *new_values, keys, values],
        28,
        4 * rows * width * rows * groups,
        rows * width // HD * rows * groups,
        "fresh_attend_update",
    )


def project_kernel(row_at, own_partial, own_stats, fresh_partial, fresh_stats, *refs):
    received = refs[:-3]
    w_out, near, far = refs[-3:]
    rows, width = own_partial.shape
    chips, _, block_width = near.shape
    heads = 2 * chips
    part = slice(row_at, row_at + rows)
    padding = jnp.zeros((LANES - STAT_ROWS, rows), jnp.float32)
    stats = [own_stats[...], fresh_stats[:, part]]
    for ref in received:
        stats.append(
            sum(
                ref[rows:, turn * rows : (turn + 1) * rows].astype(jnp.float32)
                for turn in range(3)
            )[:STAT_ROWS]
        )
    logs = [jnp.concatenate([stat, padding], 0).T for stat in stats]
    largest = functools.reduce(jnp.maximum, logs)
    shares = [jnp.exp2(log - largest) for log in logs]
    total = functools.reduce(jnp.add, shares)
    shares = [share / total for share in shares]
    attended = []
    for head in range(width // HD):
        own = slice(head * HD, (head + 1) * HD)
        column = slice(head, head + 1)
        merged = own_partial[:, own] * shares[0][:, column]
        merged = merged + fresh_partial[part, own] * shares[1][:, column]
        for ref, share in zip(received, shares[2:]):
            merged = merged + ref[:rows, own].astype(jnp.float32) * share[:, column]
        attended.append(merged.astype(jnp.bfloat16))
    attended = jnp.concatenate(attended, 1)
    me = lax.axis_index("head")
    for target, flip in ((far, 1), (near, 0)):
        for ahead in range(chips):
            block = lax.rem(me + CORES * ahead, heads) ^ flip
            along = pl.ds(pl.multiple_of(block * block_width, LANES), block_width)
            target[ahead] = dot(attended, w_out[:, along]).astype(target.dtype)


def project(row_at, own, fresh_part, received, w_out, chips):
    rows = own[0].shape[0]
    shape = jax.ShapeDtypeStruct((chips, rows, w_out.shape[1] // (2 * chips)), jnp.bfloat16)
    return call(
        functools.partial(project_kernel, row_at),
        [shape, shape],
        [],
        [*own, *fresh_part, *received, w_out],
        20,
        2 * rows * w_out.size,
        0,
        "combine_project",
    )


def shards(
    tokens,
    norm_gain,
    w_query,
    w_key,
    w_value,
    w_out,
    keys_cache,
    values_cache,
    cached_lengths,
    rope_offsets,
):
    rows, width = tokens.shape
    requests = cached_lengths.shape[0]
    groups = lax.axis_size("seq") // requests
    heads = lax.axis_size("head")
    chips = heads // CORES
    chunk_rows = rows // CHUNKS
    gain = norm_gain.reshape(heads, 1, width)

    arrived = [
        [
            shifted(tokens[at : at + chunk_rows], "seq", turn * requests)
            for at in range(0, rows, chunk_rows)
        ]
        for turn in range(1, groups)
    ]
    *tables, wide_keys, wide_values = prepare(
        cached_lengths, rope_offsets, keys_cache, values_cache, groups, rows
    )

    def attend_chunk(pieces, own, chunk, turn):
        return attend(
            pieces, gain, w_query, tables, wide_keys, wide_values, own, chunk_rows,
            chunk * chunk_rows if own else 0, turn * rows + chunk * chunk_rows,
        )

    own_pieces = all_features(tokens)
    own_parts = [attend_chunk(own_pieces, True, chunk, 0) for chunk in range(CHUNKS)]
    new_rows = [fresh([own_pieces], gain, w_key, w_value, tables, 0)]
    received = [[] for _ in range(CHUNKS)]
    for turn in range(1, groups):
        chunks = [all_features(piece) for piece in arrived[turn - 1]]
        for chunk in range(CHUNKS):
            (packed,) = attend_chunk(chunks[chunk], False, chunk, turn)
            received[chunk].append(shifted(packed, "seq", -turn * requests))
        new_rows.append(fresh(chunks, gain, w_key, w_value, tables, turn * rows))
    *fresh_part, keys_updated, values_updated = update(
        cached_lengths, [part[2] for part in own_parts], [k for k, _ in new_rows],
        [v for _, v in new_rows], keys_cache, values_cache,
    )
    outputs = []
    for chunk in range(CHUNKS):
        near, far = project(
            chunk * chunk_rows, own_parts[chunk][:2], fresh_part, received[chunk], w_out, chips
        )
        summed = near.astype(jnp.float32) + other_core(far).astype(jnp.float32)
        total = summed[0]
        for ahead in range(1, chips):
            piece = shifted(summed[ahead].astype(jnp.bfloat16), "head", CORES * ahead)
            total = total + piece.astype(jnp.float32)
        outputs.append(total.astype(jnp.bfloat16))
    return (jnp.concatenate(outputs, 0), keys_updated, values_updated)


def solution(mesh):
    return jax.shard_map(
        shards,
        mesh=mesh,
        in_specs=(
            P("seq", "head"),
            P(),
            P(None, "head"),
            P(None, "head"),
            P(None, "head"),
            P("head", None),
            P("seq", "head"),
            P("seq", "head"),
            P(),
            P(),
        ),
        out_specs=(P("seq", "head"), P("seq", "head"), P("seq", "head")),
        check_vma=False,
    )
```

```python
import functools
import math

import jax
import jax.numpy as jnp
from jax import lax
from jax.experimental import pallas as pl
from jax.experimental.pallas import tpu as pltpu
from jax.sharding import PartitionSpec as P

HD = 128
LANES = 128
STAT_ROWS = 8
ROW_TILE = 16
CORES = 2
CHUNKS = 2
COST_WEIGHT = 0.02
MIB = 1 << 20

rope_base = 500000.0
neg_large = -1e30
log2_scale = math.log2(math.e) / math.sqrt(HD)

VMEM = pl.BlockSpec(memory_space=pltpu.VMEM)
SMEM = pl.BlockSpec(memory_space=pltpu.SMEM)
ANY = pl.BlockSpec(memory_space=pl.ANY)


def shifted(shard, axis, by):
    devices = lax.axis_size(axis)
    return lax.ppermute(shard, axis, [(i, (i + by) % devices) for i in range(devices)])


def other_core(shard):
    devices = lax.axis_size("head")
    return lax.ppermute(shard, "head", [(i, i ^ 1) for i in range(devices)])


def other_chips(own):
    chips = lax.axis_size("head") // CORES
    return [shifted(own, "head", CORES * k) for k in range(1, chips)]


def place_of(requests):
    member = lax.axis_index("seq")
    return lax.rem(member, requests), lax.div(member, requests)


def source_of(position_in, turn, groups):
    return lax.rem(position_in + (groups - turn), groups)


def dot(left, right):
    return jnp.dot(left, right, preferred_element_type=jnp.float32)


def dot_transposed(left, right):
    return lax.dot_general(
        left, right, (((1,), (1,)), ((), ())), preferred_element_type=jnp.float32
    )


def call(kernel, out_shape, scalars, arrays, limit, flops, transcendentals, name, earlier=()):
    moved = sum(a.size * a.dtype.itemsize for a in arrays)
    moved += sum(math.prod(s.shape) * s.dtype.itemsize for s in out_shape)
    read = len(scalars) + len(arrays)
    skipped = len(earlier)

    def body(*refs):
        kernel(*refs[:read], *refs[read + skipped :])

    return pl.pallas_call(
        body,
        out_shape=out_shape,
        in_specs=[SMEM] * len(scalars) + [VMEM] * len(arrays) + [ANY] * skipped,
        out_specs=[VMEM] * len(out_shape),
        compiler_params=pltpu.CompilerParams(vmem_limit_bytes=limit * MIB),
        cost_estimate=pl.CostEstimate(
            flops=int(COST_WEIGHT * flops),
            bytes_accessed=int(COST_WEIGHT * moved),
            transcendentals=int(COST_WEIGHT * transcendentals),
        ),
        name=name,
    )(*scalars, *arrays, *earlier)


def whole_of(blocks):
    parts = [block[...] for block in blocks]
    return jnp.concatenate(parts, 0) if len(parts) > 1 else parts[0]


def relay_kernel(count, *refs):
    whole = whole_of(refs[:count])
    at = 0
    for ref in refs[count:]:
        ref[...] = whole[at : at + ref.shape[0]]
        at = (at + ref.shape[0]) % whole.shape[0]


def relay(blocks, sizes, earlier):
    shapes = [jax.ShapeDtypeStruct((size, *blocks[0].shape[1:]), blocks[0].dtype) for size in sizes]
    kernel = functools.partial(relay_kernel, len(blocks))
    return call(kernel, shapes, [], [*blocks], 4, 0, 0, "relay", earlier)


def prepare_kernel(groups, lengths, offsets, tokens, keys, values, *outputs):
    late, cosine, sine, wide_keys, wide_values = outputs
    rows = tokens.shape[0]
    late[...] = tokens[rows - late.shape[0] :]
    request, position_in = place_of(lengths.shape[0])
    length = lengths[request]
    slots = keys.shape[0]
    lane = lax.broadcasted_iota(jnp.int32, (rows, LANES), 1)
    row = lax.broadcasted_iota(jnp.int32, (rows, LANES), 0)
    half = lax.rem(lane, HD // 2).astype(jnp.float32)
    frequency = jnp.exp2(half * (-2.0 / HD * math.log2(rope_base)))
    sign = jnp.where(lane < HD // 2, -1.0, 1.0)
    for turn in range(groups):
        first = offsets[request] + length + source_of(position_in, turn, groups) * rows
        angles = (row + first).astype(jnp.float32) * frequency
        part = slice(turn * rows, (turn + 1) * rows)
        cosine[part] = jnp.cos(angles)
        sine[part] = jnp.sin(angles) * sign
    slot = lax.broadcasted_iota(jnp.int32, (slots, LANES), 0) + position_in * slots
    lane = lax.broadcasted_iota(jnp.int32, (slots, LANES), 1)
    bias = jnp.where((lane == 0) & (slot >= length), neg_large, 0.0).astype(jnp.bfloat16)
    ones = jnp.where(lane == 0, 1.0, 0.0).astype(jnp.bfloat16)
    for head in range(keys.shape[1] // HD):
        own = slice(head * HD, (head + 1) * HD)
        wide_keys[head, :, :HD] = keys[:, own]
        wide_keys[head, :, HD:] = bias
        wide_values[head, :, :HD] = values[:, own]
        wide_values[head, :, HD:] = ones


def prepare(lengths, offsets, tokens, keys, values, groups, late_rows):
    rows, token_width = tokens.shape
    late = jax.ShapeDtypeStruct((late_rows, token_width), tokens.dtype)
    table = jax.ShapeDtypeStruct((groups * rows, LANES), jnp.float32)
    slots, width = keys.shape
    wide = jax.ShapeDtypeStruct((width // HD, slots, HD + LANES), jnp.bfloat16)
    return call(
        functools.partial(prepare_kernel, groups),
        [late, table, table, wide, wide],
        [lengths, offsets],
        [tokens, keys, values],
        24,
        40 * groups * rows * LANES,
        0,
        "rope_tables_wide_caches",
    )


def rotate(vectors, cosine, sine):
    return vectors * cosine + pltpu.roll(vectors, HD // 2, 1) * sine


def project_normed(pieces, gain, weights):
    heads = gain.shape[0]
    width = gain.shape[2]
    me = lax.axis_index("head")
    squares = 0.0
    sums = [0.0] * len(weights)
    for index, piece in enumerate(pieces):
        owner = lax.rem(me + (heads - CORES * (index % (heads // CORES))), heads)
        if index >= heads // CORES:
            owner = owner ^ 1
        wide = piece.astype(jnp.float32)
        scaled = (wide * gain[owner]).astype(jnp.bfloat16)
        along = pl.ds(pl.multiple_of(owner * width, LANES), width)
        for place, weight in enumerate(weights):
            sums[place] = sums[place] + dot(scaled, weight[along, :])
        squares = squares + jnp.sum(wide * wide, -1, keepdims=True)
    factor = lax.rsqrt(squares / (heads * width) + 1e-05)
    return [total * factor for total in sums]


def stat_rows(columns, rows):
    lane = lax.broadcasted_iota(jnp.int32, (rows, LANES), 1)
    table = jnp.zeros((rows, LANES), jnp.float32)
    for index, column in enumerate(columns):
        table = jnp.where(lane == index, column, table)
    return table.T[:STAT_ROWS]


def split_refs(counts, refs):
    parts = []
    for count in counts:
        parts.append(refs[:count])
        refs = refs[count:]
    return parts, refs


def rows_of(blocks, row_at, rows):
    parts = []
    at = 0
    for block in blocks:
        size = block.shape[0]
        low, high = max(row_at - at, 0), min(row_at + rows - at, size)
        if low < high:
            parts.append(block[low:high])
        at += size
    return jnp.concatenate(parts, 0) if len(parts) > 1 else parts[0]


def attend_kernel(counts, own, row_at, rows, table_at, *refs):
    blocks, refs = split_refs(counts, refs)
    gain, w_query, cosine, sine, wide_keys, wide_values, *outputs = refs
    pieces = [rows_of(one, row_at, rows) for one in blocks]
    (product,) = project_normed(pieces, gain, [w_query])
    cosine = cosine[table_at : table_at + rows]
    sine = sine[table_at : table_at + rows]
    kv_heads = wide_keys.shape[0]
    repeat = product.shape[1] // HD // kv_heads
    queries = [
        (rotate(product[:, head * HD : (head + 1) * HD], cosine, sine) * log2_scale).astype(
            jnp.bfloat16
        )
        for head in range(kv_heads * repeat)
    ]
    step = min(rows, LANES)
    lane = lax.broadcasted_iota(jnp.int32, (repeat * step, LANES), 1)
    mark = jnp.where(lane == 0, 1.0, 0.0).astype(jnp.bfloat16)
    tiles = [(head, at) for head in range(kv_heads) for at in range(0, rows, step)]

    def scores_of(head, at):
        stacked = jnp.concatenate(
            [query[at : at + step] for query in queries[head * repeat : (head + 1) * repeat]], 0
        )
        return dot_transposed(jnp.concatenate([stacked, mark], 1), wide_keys[head])

    columns = {}
    following = scores_of(*tiles[0])
    for index, (head, at) in enumerate(tiles):
        scores = following
        if index + 1 < len(tiles):
            following = scores_of(*tiles[index + 1])
        largest = jnp.max(scores, -1, keepdims=True)
        weights = jnp.exp2(scores - largest).astype(jnp.bfloat16)
        summed = dot(weights, wide_values[head])
        denominator = summed[:, HD : HD + 1]
        result = summed[:, :HD] / denominator
        logs = largest + jnp.log2(denominator)
        for turn in range(repeat):
            part = slice(turn * step, (turn + 1) * step)
            to = slice((head * repeat + turn) * HD, (head * repeat + turn + 1) * HD)
            outputs[0][at : at + step, to] = result[part].astype(outputs[0].dtype)
            columns.setdefault(head * repeat + turn, []).append(logs[part])
    stats = stat_rows([jnp.concatenate(parts, 0) for parts in columns.values()], rows)
    if own:
        outputs[1][...] = stats
        outputs[2][...] = jnp.concatenate(queries, 1)
        return
    outputs[0][rows:] = jnp.zeros((ROW_TILE, outputs[0].shape[1]), jnp.bfloat16)
    rest = jnp.concatenate([stats, jnp.zeros((ROW_TILE - STAT_ROWS, rows), jnp.float32)], 0)
    for part in range(3):
        rounded = rest.astype(jnp.bfloat16)
        outputs[0][rows:, part * rows : (part + 1) * rows] = rounded
        rest = rest - rounded.astype(jnp.float32)


def attend(
    pieces, gain, w_query, tables, wide_keys, wide_values, own, row_at, rows, table_at, earlier
):
    counts = [len(blocks) for blocks in pieces]
    flat = [block for blocks in pieces for block in blocks]
    out_width = w_query.shape[1]
    slots = wide_keys.shape[1]
    if own:
        out_shape = [
            jax.ShapeDtypeStruct((rows, out_width), jnp.float32),
            jax.ShapeDtypeStruct((STAT_ROWS, rows), jnp.float32),
            jax.ShapeDtypeStruct((rows, out_width), jnp.bfloat16),
        ]
    else:
        out_shape = [jax.ShapeDtypeStruct((rows + ROW_TILE, out_width), jnp.bfloat16)]
    return call(
        functools.partial(attend_kernel, counts, own, row_at, rows, table_at),
        out_shape,
        [],
        [*flat, gain, w_query, *tables, wide_keys, wide_values],
        28,
        2 * rows * out_width * (w_query.shape[0] + 4 * slots),
        rows * out_width // HD * slots,
        "attend_own" if own else "attend_partner",
        earlier,
    )


def fresh_kernel(counts, table_at, *refs):
    blocks, refs = split_refs(counts, refs)
    gain, w_key, w_value, cosine, sine, new_keys, new_values = refs
    rows = new_keys.shape[0]
    pieces = [whole_of(one) for one in blocks]
    keys, values = project_normed(pieces, gain, [w_key, w_value])
    cosine = cosine[table_at : table_at + rows]
    sine = sine[table_at : table_at + rows]
    for head in range(keys.shape[1] // HD):
        own = slice(head * HD, (head + 1) * HD)
        new_keys[:, own] = rotate(keys[:, own], cosine, sine).astype(jnp.bfloat16)
    new_values[...] = values.astype(jnp.bfloat16)


def fresh(pieces, gain, w_key, w_value, tables, table_at, earlier):
    flat = [block for blocks in pieces for block in blocks]
    rows = sum(block.shape[0] for block in pieces[0])
    shape = jax.ShapeDtypeStruct((rows, w_key.shape[1]), jnp.bfloat16)
    return call(
        functools.partial(fresh_kernel, [len(blocks) for blocks in pieces], table_at),
        [shape, shape],
        [],
        [*flat, gain, w_key, w_value, *tables],
        20,
        4 * rows * w_key.size,
        0,
        "fresh_kv",
        earlier,
    )


def write_rows(target, fresh_rows, first):
    rows = fresh_rows.shape[0]
    slab_rows = target.shape[0]
    span = rows + ROW_TILE
    start = jnp.clip(first, 0, slab_rows - span)
    start = start - lax.rem(start, ROW_TILE)
    window = pl.ds(pl.multiple_of(start, ROW_TILE), span)
    shift = start - first
    place = lax.broadcasted_iota(jnp.int32, (span, rows), 0) + shift
    chosen = place == lax.broadcasted_iota(jnp.int32, (span, rows), 1)
    moved = dot(chosen.astype(jnp.bfloat16), fresh_rows)
    row = lax.broadcasted_iota(jnp.int32, (span, target.shape[1]), 0) + shift
    inside = (row >= 0) & (row < rows)
    old = target[window, :].astype(jnp.float32)
    target[window, :] = jnp.where(inside, moved, old).astype(jnp.bfloat16)


def attend_fresh_kernel(groups, requests, *refs):
    query_refs, refs = refs[:CHUNKS], refs[CHUNKS:]
    old_refs, refs = refs[: 2 * CHUNKS], refs[2 * CHUNKS :]
    key_refs, value_refs, refs = refs[:groups], refs[groups : 2 * groups], refs[2 * groups :]
    partial, stats = refs
    position_in = place_of(requests)[1]
    sources = [source_of(position_in, turn, groups) for turn in range(groups)]
    rows, width = partial.shape
    kv_heads = key_refs[0].shape[1] // HD
    repeat = width // HD // kv_heads
    queries = whole_of(query_refs)
    old_partial = whole_of(old_refs[0::2])
    old_stats = jnp.concatenate([ref[...] for ref in old_refs[1::2]], 1)
    fresh_keys = whole_of(key_refs)
    fresh_values = whole_of(value_refs)
    token = lax.rem(lax.broadcasted_iota(jnp.int32, (repeat * rows, rows), 0), rows)
    within = lax.broadcasted_iota(jnp.int32, (repeat * rows, rows), 1)
    visible = jnp.concatenate(
        [within + source * rows <= token + position_in * rows for source in sources], 1
    )
    padding = jnp.zeros((LANES - STAT_ROWS, rows), jnp.float32)
    old_logs = jnp.concatenate([old_stats, padding], 0).T
    columns = []
    for head in range(kv_heads):
        own = [
            slice((head * repeat + turn) * HD, (head * repeat + turn + 1) * HD)
            for turn in range(repeat)
        ]
        shared = slice(head * HD, (head + 1) * HD)
        stacked = jnp.concatenate([queries[:, one] for one in own], 0)
        scores = jnp.where(visible, dot_transposed(stacked, fresh_keys[:, shared]), neg_large)
        largest = jnp.max(scores, -1, keepdims=True)
        weights = jnp.exp2(scores - largest)
        denominator = jnp.sum(weights, -1, keepdims=True)
        summed = dot(weights.astype(jnp.bfloat16), fresh_values[:, shared])
        for turn, one in enumerate(own):
            part = slice(turn * rows, (turn + 1) * rows)
            old_log = old_logs[:, head * repeat + turn : head * repeat + turn + 1]
            top = jnp.maximum(old_log, largest[part])
            old_share = jnp.exp2(old_log - top)
            share = jnp.exp2(largest[part] - top)
            total = old_share + share * denominator[part]
            partial[:, one] = (old_partial[:, one] * old_share + summed[part] * share) / total
            columns.append(top + jnp.log2(total))
    stats[...] = stat_rows(columns, rows)


def attend_fresh(requests, queries, old, new_keys, new_values):
    groups = len(new_keys)
    rows = new_keys[0].shape[0]
    width = queries[0].shape[1]
    return call(
        functools.partial(attend_fresh_kernel, groups, requests),
        [
            jax.ShapeDtypeStruct((rows, width), jnp.float32),
            jax.ShapeDtypeStruct((STAT_ROWS, rows), jnp.float32),
        ],
        [],
        [*queries, *old, *new_keys, *new_values],
        24,
        4 * rows * width * rows * groups,
        rows * width // HD * rows * groups,
        "attend_fresh",
    )


def update_kernel(groups, lengths, *refs):
    key_refs, value_refs, refs = refs[:groups], refs[groups : 2 * groups], refs[2 * groups :]
    keys, values, keys_updated, values_updated = refs
    request, position_in = place_of(lengths.shape[0])
    rows = key_refs[0].shape[0]
    keys_updated[...] = keys[...]
    values_updated[...] = values[...]
    for turn in range(groups):
        source = source_of(position_in, turn, groups)
        first = lengths[request] + source * rows - position_in * keys.shape[0]
        write_rows(keys_updated, key_refs[turn][...], first)
        write_rows(values_updated, value_refs[turn][...], first)


def update(lengths, new_keys, new_values, keys, values, earlier):
    groups = len(new_keys)
    slab = jax.ShapeDtypeStruct(keys.shape, keys.dtype)
    return call(
        functools.partial(update_kernel, groups),
        [slab, slab],
        [lengths],
        [*new_keys, *new_values, keys, values],
        20,
        4 * new_keys[0].size * new_keys[0].shape[0] * groups,
        0,
        "update_caches",
        earlier,
    )


def project_kernel(row_at, own_partial, own_stats, *refs):
    heads = lax.axis_size("head")
    chips = heads // CORES
    outputs = 3 * chips - 1
    received = refs[: -1 - outputs]
    w_out = refs[-1 - outputs]
    near, far = refs[-outputs:][:chips], refs[-outputs:][chips:]
    width = own_partial.shape[1]
    rows, block_width = near[0].shape
    part = slice(row_at, row_at + rows)
    padding = jnp.zeros((LANES - STAT_ROWS, rows), jnp.float32)
    stats = [own_stats[:, part]]
    for ref in received:
        stats.append(
            sum(
                ref[rows:, turn * rows : (turn + 1) * rows].astype(jnp.float32)
                for turn in range(3)
            )[:STAT_ROWS]
        )
    logs = [jnp.concatenate([stat, padding], 0).T for stat in stats]
    largest = functools.reduce(jnp.maximum, logs)
    shares = [jnp.exp2(log - largest) for log in logs]
    total = functools.reduce(jnp.add, shares)
    shares = [share / total for share in shares]
    attended = []
    for head in range(width // HD):
        own = slice(head * HD, (head + 1) * HD)
        column = slice(head, head + 1)
        merged = own_partial[part, own] * shares[0][:, column]
        for ref, share in zip(received, shares[1:]):
            merged = merged + ref[:rows, own].astype(jnp.float32) * share[:, column]
        attended.append(merged.astype(jnp.bfloat16))
    attended = jnp.concatenate(attended, 1)
    me = lax.axis_index("head")
    def product(ahead, flip):
        block = lax.rem(me + CORES * ahead, heads) ^ flip
        along = pl.ds(pl.multiple_of(block * block_width, LANES), block_width)
        return dot(attended, w_out[:, along]).astype(jnp.bfloat16)

    middle = block_width // 2
    for ahead in range(1, chips):
        result = product(ahead, 1)
        far[2 * ahead - 1][...] = result[:, :middle]
        far[2 * ahead][...] = result[:, middle:]
    far[0][...] = product(0, 1)
    for ahead in range(chips):
        near[ahead][...] = product(ahead, 0)


def project(row_at, rows, own, received, w_out, heads, earlier):
    chips = heads // CORES
    width = w_out.shape[1] // heads
    shape = jax.ShapeDtypeStruct((rows, width), jnp.bfloat16)
    half = jax.ShapeDtypeStruct((rows, width // 2), jnp.bfloat16)
    blocks = call(
        functools.partial(project_kernel, row_at),
        [shape] * chips + [shape] + [half] * (2 * chips - 2),
        [],
        [*own, *received, w_out],
        20,
        2 * rows * w_out.size,
        0,
        "combine_project",
        earlier,
    )
    near, far = blocks[:chips], blocks[chips:]
    return near, [far[:1]] + [far[2 * k - 1 : 2 * k + 1] for k in range(1, chips)]


def sum_kernel(count, *refs):
    total = refs[0][...].astype(jnp.float32)
    total = total + jnp.concatenate([ref[...] for ref in refs[1:count]], 1).astype(jnp.float32)
    refs[count][...] = total.astype(jnp.bfloat16)


def sum_cores(near, far, earlier):
    return call(
        functools.partial(sum_kernel, 1 + len(far)),
        [jax.ShapeDtypeStruct(near.shape, near.dtype)],
        [],
        [near, *far],
        8,
        near.size,
        0,
        "sum_cores",
        earlier,
    )[0]


def finish_kernel(*refs):
    *parts, result = refs
    count = len(parts) // CHUNKS
    rows = parts[0].shape[0]
    for chunk in range(CHUNKS):
        total = 0.0
        for ref in parts[chunk * count : (chunk + 1) * count]:
            total = total + ref[...].astype(jnp.float32)
        result[chunk * rows : (chunk + 1) * rows] = total.astype(jnp.bfloat16)


def finish(parts):
    rows, width = parts[0].shape
    shape = jax.ShapeDtypeStruct((CHUNKS * rows, width), jnp.bfloat16)
    return call(finish_kernel, [shape], [], parts, 8, CHUNKS * rows * width, 0, "finish")[0]


def shards(
    tokens,
    norm_gain,
    w_query,
    w_key,
    w_value,
    w_out,
    keys_cache,
    values_cache,
    cached_lengths,
    rope_offsets,
):
    rows, width = tokens.shape
    requests = cached_lengths.shape[0]
    groups = lax.axis_size("seq") // requests
    heads = lax.axis_size("head")
    chips = heads // CORES
    chunk_rows = rows // CHUNKS
    gain = norm_gain.reshape(heads, 1, width)

    early = tokens[:chunk_rows]
    late, *tables, wide_keys, wide_values = prepare(
        cached_lengths, rope_offsets, tokens, keys_cache, values_cache, groups, rows - chunk_rows
    )
    sent = [early, late]
    arrived = [
        [shifted(piece, "seq", turn * requests) for piece in sent] for turn in range(1, groups)
    ]

    def attend_rows(pieces, own, chunk, turn, earlier):
        at = chunk * chunk_rows
        return attend(
            pieces, gain, w_query, tables, wide_keys, wide_values, own, at if own else 0,
            chunk_rows, turn * rows + at, earlier,
        )

    half = chunk_rows // 2
    first = [relay([pieces[0]], [chunk_rows, half, half], [late]) for pieces in arrived]
    earlier = [cut[0] for cut in first]
    own_cuts = [
        relay([piece], [rows, half, half, rows - chunk_rows], earlier)
        for piece in other_chips(tokens)
    ]
    own_pieces = [[tokens]] + [[cut[0]] for cut in own_cuts] + [[other_core(tokens)]]
    own_pieces += [[other_core(block) for block in cut[1:]] for cut in own_cuts]
    own_early = [
        blocks if len(blocks) == 1 else blocks[: len(blocks) - 1] for blocks in own_pieces
    ]
    *own_part, queries = attend_rows(own_early, True, 0, 0, earlier)
    own_queries = [queries]
    earlier = [queries]
    gathered = []
    for cut in first:
        blocks = zip(*[other_chips(piece) for piece in cut[1:]])
        from_chips = [relay(one, [chunk_rows], earlier)[0] for one in blocks]
        along = [cut[0]] + from_chips
        gathered.append([along + [other_core(one) for one in along]])
        earlier = earlier + from_chips
    second = [relay([pieces[1]], [rows - chunk_rows], earlier)[0] for pieces in arrived]
    new_rows = [fresh(own_pieces, gain, w_key, w_value, tables, 0, second)]
    earlier = [new_rows[0][0]]
    received = [[] for _ in range(CHUNKS)]
    for turn in range(1, groups):
        pieces = [[block] for block in gathered[turn - 1][0]]
        (packed,) = attend_rows(pieces, False, 0, turn, earlier)
        received[0].append(shifted(packed, "seq", -turn * requests))
        earlier = [packed]
    for pieces, piece in zip(gathered, second):
        from_chips = [
            relay([one], [rows - chunk_rows], earlier)[0] for one in other_chips(piece)
        ]
        along = [piece] + from_chips
        pieces.append(along + [other_core(one) for one in along])
        earlier = earlier + from_chips
    *late_part, queries = attend_rows(own_pieces, True, 1, 0, earlier)
    own_part += late_part
    own_queries.append(queries)
    earlier = [queries]
    for turn in range(1, groups):
        pieces = [[block] for block in gathered[turn - 1][1]]
        (packed,) = attend_rows(pieces, False, 1, turn, earlier)
        received[1].append(shifted(packed, "seq", -turn * requests))
        earlier = [packed]
    for turn in range(1, groups):
        pieces = [list(blocks) for blocks in zip(*gathered[turn - 1])]
        new_rows.append(fresh(pieces, gain, w_key, w_value, tables, turn * rows, earlier))
    new_keys, new_values = zip(*new_rows)
    own_part = attend_fresh(requests, own_queries, own_part, new_keys, new_values)

    parts = []
    earlier = before_sums = []
    for chunk in range(CHUNKS):
        nears, fars = project(
            chunk * chunk_rows, chunk_rows, own_part, received[chunk], w_out, heads, earlier
        )
        fars = [[other_core(part) for part in far] for far in fars]
        earlier = [nears[0]] + before_sums
        if chunk == 0:
            keys_updated, values_updated = update(
                cached_lengths, new_keys, new_values, keys_cache, values_cache, earlier
            )
            earlier = [keys_updated]
        sums = [sum_cores(near, far, earlier) for near, far in zip(nears[1:], fars[1:])]
        from_chips = [shifted(one, "head", CORES * k) for k, one in enumerate(sums, 1)]
        parts += [nears[0], *fars[0], *from_chips]
        earlier, before_sums = sums, from_chips
    return (finish(parts), keys_updated, values_updated)


def solution(mesh):
    return jax.shard_map(
        shards,
        mesh=mesh,
        in_specs=(
            P("seq", "head"),
            P(),
            P(None, "head"),
            P(None, "head"),
            P(None, "head"),
            P("head", None),
            P("seq", "head"),
            P("seq", "head"),
            P(),
            P(),
        ),
        out_specs=(P("seq", "head"), P("seq", "head"), P("seq", "head")),
        check_vma=False,
    )
```

```python
import functools
import math

import jax
import jax.numpy as jnp
from jax import lax
from jax.experimental import pallas as pl
from jax.experimental.pallas import tpu as pltpu
from jax.sharding import PartitionSpec as P

HD = 128
LANES = 128
STAT_ROWS = 8
ROW_TILE = 16
CORES = 2
CHUNKS = 2
COST_WEIGHT = 0.02
FIRST_MICROS = 1
FLOPS_PER_MICRO = 1_000_000_000
MIB = 1 << 20

rope_base = 500000.0
neg_large = -1e30
log2_scale = math.log2(math.e) / math.sqrt(HD)

VMEM = pl.BlockSpec(memory_space=pltpu.VMEM)
ANY = pl.BlockSpec(memory_space=pl.ANY)


def shifted(shard, axis, by):
    devices = lax.axis_size(axis)
    return lax.ppermute(shard, axis, [(i, (i + by) % devices) for i in range(devices)])


def other_core(shard):
    devices = lax.axis_size("head")
    return lax.ppermute(shard, "head", [(i, i ^ 1) for i in range(devices)])


def other_chips(own):
    chips = lax.axis_size("head") // CORES
    return [shifted(own, "head", CORES * k) for k in range(1, chips)]


def place_of(requests):
    member = lax.axis_index("seq")
    return lax.rem(member, requests), lax.div(member, requests)


def source_of(position_in, turn, groups):
    return lax.rem(position_in + (groups - turn), groups)


def dot(left, right):
    return jnp.dot(left, right, preferred_element_type=jnp.float32)


def dot_transposed(left, right):
    return lax.dot_general(
        left, right, (((1,), (1,)), ((), ())), preferred_element_type=jnp.float32
    )


def call(
    kernel, out_shape, arrays, limit, flops, transcendentals, name, earlier=(),
    scratch=(), micros=0,
):
    moved = sum(a.size * a.dtype.itemsize for a in arrays)
    moved += sum(math.prod(s.shape) * s.dtype.itemsize for s in out_shape)
    read = len(arrays)
    skipped = len(earlier)

    def body(*refs):
        kernel(*refs[:read], *refs[read + skipped :])

    return pl.pallas_call(
        body,
        out_shape=out_shape,
        in_specs=[VMEM] * len(arrays) + [ANY] * skipped,
        out_specs=[VMEM] * len(out_shape),
        scratch_shapes=scratch,
        compiler_params=pltpu.CompilerParams(vmem_limit_bytes=limit * MIB),
        cost_estimate=pl.CostEstimate(
            flops=max(int(COST_WEIGHT * flops), micros * FLOPS_PER_MICRO),
            bytes_accessed=int(COST_WEIGHT * moved),
            transcendentals=int(COST_WEIGHT * transcendentals),
        ),
        name=name,
    )(*arrays, *earlier)


def whole_of(blocks):
    parts = [block[...] for block in blocks]
    return jnp.concatenate(parts, 0) if len(parts) > 1 else parts[0]


def relay_kernel(count, *refs):
    whole = whole_of(refs[:count])
    at = 0
    for ref in refs[count:]:
        ref[...] = whole[at : at + ref.shape[0]]
        at = (at + ref.shape[0]) % whole.shape[0]


def relay(blocks, sizes, earlier):
    shapes = [jax.ShapeDtypeStruct((size, *blocks[0].shape[1:]), blocks[0].dtype) for size in sizes]
    kernel = functools.partial(relay_kernel, len(blocks))
    return call(kernel, shapes, [*blocks], 4, 0, 0, "relay", earlier)


def mark_kernel(mark):
    lane = lax.broadcasted_iota(jnp.int32, mark.shape, 1)
    mark[...] = jnp.where(lane == 0, 1.0, 0.0).astype(mark.dtype)


def marks(rows):
    shape = jax.ShapeDtypeStruct((rows, LANES), jnp.bfloat16)
    return call(mark_kernel, [shape], [], 4, 0, 0, "marks", micros=FIRST_MICROS)[0]


def tables_kernel(groups, tokens, lengths_in, offsets_in, late, cosine, sine, *scratch):
    lengths, offsets, semaphores = scratch
    numbers = [
        pltpu.make_async_copy(lengths_in, lengths, semaphores.at[0]),
        pltpu.make_async_copy(offsets_in, offsets, semaphores.at[1]),
    ]
    for copy in numbers:
        copy.start()
    rows = tokens.shape[0]
    late[...] = tokens[rows - late.shape[0] :]
    for copy in numbers:
        copy.wait()
    request, position_in = place_of(lengths.shape[0])
    lane = lax.broadcasted_iota(jnp.int32, (rows, LANES), 1)
    row = lax.broadcasted_iota(jnp.int32, (rows, LANES), 0)
    half = lax.rem(lane, HD // 2).astype(jnp.float32)
    frequency = jnp.exp2(half * (-2.0 / HD * math.log2(rope_base)))
    sign = jnp.where(lane < HD // 2, -1.0, 1.0)
    for turn in range(groups):
        first = source_of(position_in, turn, groups) * rows
        first = first + offsets[request] + lengths[request]
        angles = (row + first).astype(jnp.float32) * frequency
        part = slice(turn * rows, (turn + 1) * rows)
        cosine[part] = jnp.cos(angles)
        sine[part] = jnp.sin(angles) * sign


def rope_tables(tokens, lengths, offsets, groups, late_rows, earlier):
    rows, token_width = tokens.shape
    late = jax.ShapeDtypeStruct((late_rows, token_width), tokens.dtype)
    table = jax.ShapeDtypeStruct((groups * rows, LANES), jnp.float32)
    return call(
        functools.partial(tables_kernel, groups),
        [late, table, table],
        [tokens, lengths, offsets],
        12,
        0,
        0,
        "rope_tables",
        earlier,
        [
            pltpu.SMEM(lengths.shape, lengths.dtype),
            pltpu.SMEM(offsets.shape, offsets.dtype),
            pltpu.SemaphoreType.DMA((2,)),
        ],
        FIRST_MICROS,
    )


def widen_kernel(keys, values, mark, lengths_in, wide_keys, wide_values, lengths, semaphore):
    number = pltpu.make_async_copy(lengths_in, lengths, semaphore)
    number.start()
    slots = keys.shape[0]
    heads = keys.shape[1] // HD
    for head in range(heads):
        own = slice(head * HD, (head + 1) * HD)
        wide_keys[head, :, :HD] = keys[:, own]
        wide_values[head, :, :HD] = values[:, own]
        wide_values[head, :, HD:] = mark[:slots]
    number.wait()
    request, position_in = place_of(lengths.shape[0])
    slot = lax.broadcasted_iota(jnp.int32, (slots, LANES), 0) + position_in * slots
    lane = lax.broadcasted_iota(jnp.int32, (slots, LANES), 1)
    bias = jnp.where((lane == 0) & (slot >= lengths[request]), neg_large, 0.0).astype(jnp.bfloat16)
    for head in range(heads):
        wide_keys[head, :, HD:] = bias


def widen(keys, values, mark, lengths, earlier):
    slots, width = keys.shape
    wide = jax.ShapeDtypeStruct((width // HD, slots, HD + LANES), jnp.bfloat16)
    return call(
        widen_kernel,
        [wide, wide],
        [keys, values, mark, lengths],
        12,
        0,
        0,
        "widen_caches",
        earlier,
        [pltpu.SMEM(lengths.shape, lengths.dtype), pltpu.SemaphoreType.DMA],
        FIRST_MICROS,
    )


def rotate(vectors, cosine, sine):
    return vectors * cosine + pltpu.roll(vectors, HD // 2, 1) * sine


def project_normed(pieces, gain, weights):
    heads = gain.shape[0]
    width = gain.shape[2]
    me = lax.axis_index("head")
    squares = 0.0
    sums = [0.0] * len(weights)
    for index, piece in enumerate(pieces):
        owner = lax.rem(me + (heads - CORES * (index % (heads // CORES))), heads)
        if index >= heads // CORES:
            owner = owner ^ 1
        wide = piece.astype(jnp.float32)
        scaled = (wide * gain[owner]).astype(jnp.bfloat16)
        along = pl.ds(pl.multiple_of(owner * width, LANES), width)
        for place, weight in enumerate(weights):
            sums[place] = sums[place] + dot(scaled, weight[along, :])
        squares = squares + jnp.sum(wide * wide, -1, keepdims=True)
    factor = lax.rsqrt(squares / (heads * width) + 1e-05)
    return [total * factor for total in sums]


def stat_rows(columns, rows):
    lane = lax.broadcasted_iota(jnp.int32, (rows, LANES), 1)
    table = jnp.zeros((rows, LANES), jnp.float32)
    for index, column in enumerate(columns):
        table = jnp.where(lane == index, column, table)
    return table.T[:STAT_ROWS]


def split_refs(counts, refs):
    parts = []
    for count in counts:
        parts.append(refs[:count])
        refs = refs[count:]
    return parts, refs


def rows_of(blocks, row_at, rows):
    parts = []
    at = 0
    for block in blocks:
        size = block.shape[0]
        low, high = max(row_at - at, 0), min(row_at + rows - at, size)
        if low < high:
            parts.append(block[low:high])
        at += size
    return jnp.concatenate(parts, 0) if len(parts) > 1 else parts[0]


def attend_kernel(counts, own, row_at, rows, table_at, *refs):
    blocks, refs = split_refs(counts, refs)
    gain, w_query, cosine, sine, wide_keys, wide_values, mark, *outputs = refs
    pieces = [rows_of(one, row_at, rows) for one in blocks]
    (product,) = project_normed(pieces, gain, [w_query])
    cosine = cosine[table_at : table_at + rows]
    sine = sine[table_at : table_at + rows]
    kv_heads = wide_keys.shape[0]
    repeat = product.shape[1] // HD // kv_heads
    queries = [
        (rotate(product[:, head * HD : (head + 1) * HD], cosine, sine) * log2_scale).astype(
            jnp.bfloat16
        )
        for head in range(kv_heads * repeat)
    ]
    step = min(rows, LANES)
    mark = mark[: repeat * step]
    tiles = [(head, at) for head in range(kv_heads) for at in range(0, rows, step)]

    def scores_of(head, at):
        stacked = jnp.concatenate(
            [query[at : at + step] for query in queries[head * repeat : (head + 1) * repeat]], 0
        )
        return dot_transposed(jnp.concatenate([stacked, mark], 1), wide_keys[head])

    columns = {}
    following = scores_of(*tiles[0])
    for index, (head, at) in enumerate(tiles):
        scores = following
        if index + 1 < len(tiles):
            following = scores_of(*tiles[index + 1])
        largest = jnp.max(scores, -1, keepdims=True)
        weights = jnp.exp2(scores - largest).astype(jnp.bfloat16)
        summed = dot(weights, wide_values[head])
        denominator = summed[:, HD : HD + 1]
        result = summed[:, :HD] / denominator
        logs = largest + jnp.log2(denominator)
        for turn in range(repeat):
            part = slice(turn * step, (turn + 1) * step)
            to = slice((head * repeat + turn) * HD, (head * repeat + turn + 1) * HD)
            outputs[0][at : at + step, to] = result[part].astype(outputs[0].dtype)
            columns.setdefault(head * repeat + turn, []).append(logs[part])
    stats = stat_rows([jnp.concatenate(parts, 0) for parts in columns.values()], rows)
    if own:
        outputs[1][...] = stats
        outputs[2][...] = jnp.concatenate(queries, 1)
        return
    outputs[0][rows:] = jnp.zeros((ROW_TILE, outputs[0].shape[1]), jnp.bfloat16)
    rest = jnp.concatenate([stats, jnp.zeros((ROW_TILE - STAT_ROWS, rows), jnp.float32)], 0)
    for part in range(3):
        rounded = rest.astype(jnp.bfloat16)
        outputs[0][rows:, part * rows : (part + 1) * rows] = rounded
        rest = rest - rounded.astype(jnp.float32)


def attend(
    pieces, gain, w_query, tables, wide_keys, wide_values, mark, own, row_at, rows, table_at,
    earlier,
):
    counts = [len(blocks) for blocks in pieces]
    flat = [block for blocks in pieces for block in blocks]
    out_width = w_query.shape[1]
    slots = wide_keys.shape[1]
    if own:
        out_shape = [
            jax.ShapeDtypeStruct((rows, out_width), jnp.float32),
            jax.ShapeDtypeStruct((STAT_ROWS, rows), jnp.float32),
            jax.ShapeDtypeStruct((rows, out_width), jnp.bfloat16),
        ]
    else:
        out_shape = [jax.ShapeDtypeStruct((rows + ROW_TILE, out_width), jnp.bfloat16)]
    return call(
        functools.partial(attend_kernel, counts, own, row_at, rows, table_at),
        out_shape,
        [*flat, gain, w_query, *tables, wide_keys, wide_values, mark],
        28,
        2 * rows * out_width * (w_query.shape[0] + 4 * slots),
        rows * out_width // HD * slots,
        "attend_own" if own else "attend_partner",
        earlier,
    )


def fresh_kernel(counts, table_at, *refs):
    blocks, refs = split_refs(counts, refs)
    gain, w_key, w_value, cosine, sine, new_keys, new_values = refs
    rows = new_keys.shape[0]
    pieces = [whole_of(one) for one in blocks]
    keys, values = project_normed(pieces, gain, [w_key, w_value])
    cosine = cosine[table_at : table_at + rows]
    sine = sine[table_at : table_at + rows]
    for head in range(keys.shape[1] // HD):
        own = slice(head * HD, (head + 1) * HD)
        new_keys[:, own] = rotate(keys[:, own], cosine, sine).astype(jnp.bfloat16)
    new_values[...] = values.astype(jnp.bfloat16)


def fresh(pieces, gain, w_key, w_value, tables, table_at, earlier):
    flat = [block for blocks in pieces for block in blocks]
    rows = sum(block.shape[0] for block in pieces[0])
    shape = jax.ShapeDtypeStruct((rows, w_key.shape[1]), jnp.bfloat16)
    return call(
        functools.partial(fresh_kernel, [len(blocks) for blocks in pieces], table_at),
        [shape, shape],
        [*flat, gain, w_key, w_value, *tables],
        20,
        4 * rows * w_key.size,
        0,
        "fresh_kv",
        earlier,
    )


def write_rows(target, fresh_rows, first):
    rows = fresh_rows.shape[0]
    slab_rows = target.shape[0]
    span = rows + ROW_TILE
    start = jnp.clip(first, 0, slab_rows - span)
    start = start - lax.rem(start, ROW_TILE)
    window = pl.ds(pl.multiple_of(start, ROW_TILE), span)
    shift = start - first
    place = lax.broadcasted_iota(jnp.int32, (span, rows), 0) + shift
    chosen = place == lax.broadcasted_iota(jnp.int32, (span, rows), 1)
    moved = dot(chosen.astype(jnp.bfloat16), fresh_rows)
    row = lax.broadcasted_iota(jnp.int32, (span, target.shape[1]), 0) + shift
    inside = (row >= 0) & (row < rows)
    old = target[window, :].astype(jnp.float32)
    target[window, :] = jnp.where(inside, moved, old).astype(jnp.bfloat16)


def attend_fresh_kernel(groups, requests, *refs):
    query_refs, refs = refs[:CHUNKS], refs[CHUNKS:]
    key_refs, value_refs, refs = refs[:groups], refs[groups : 2 * groups], refs[2 * groups :]
    partial, stats = refs
    position_in = place_of(requests)[1]
    rows, width = partial.shape
    kv_heads = key_refs[0].shape[1] // HD
    repeat = width // HD // kv_heads
    queries = whole_of(query_refs)
    token = lax.broadcasted_iota(jnp.int32, (rows, rows), 0)
    within = lax.broadcasted_iota(jnp.int32, (rows, rows), 1)
    causal = jnp.where(within <= token, 0.0, neg_large)
    causal = jnp.concatenate([causal] * repeat, 0)
    lane = lax.broadcasted_iota(jnp.int32, (rows, LANES), 1)
    ones = jnp.where(lane == 0, 1.0, 0.0).astype(jnp.bfloat16)
    hidden = [jnp.zeros((rows, LANES), jnp.bfloat16)]
    for turn in range(1, groups):
        later = source_of(position_in, turn, groups) > position_in
        hidden.append(jnp.where((lane == 0) & later, neg_large, 0.0).astype(jnp.bfloat16))
    columns = []
    for head in range(kv_heads):
        own = [
            slice((head * repeat + turn) * HD, (head * repeat + turn + 1) * HD)
            for turn in range(repeat)
        ]
        shared = slice(head * HD, (head + 1) * HD)
        stacked = jnp.concatenate([queries[:, one] for one in own], 0)
        stacked = jnp.concatenate([stacked, jnp.concatenate([ones] * repeat, 0)], 1)
        scores = [
            dot_transposed(stacked, jnp.concatenate([ref[:, shared], bias], 1))
            for ref, bias in zip(key_refs, hidden)
        ]
        scores = jnp.concatenate([scores[0] + causal] + scores[1:], 1)
        largest = jnp.max(scores, -1, keepdims=True)
        weights = jnp.exp2(scores - largest).astype(jnp.bfloat16)
        wide_values = [jnp.concatenate([ref[:, shared], ones], 1) for ref in value_refs]
        summed = dot(weights, jnp.concatenate(wide_values, 0))
        denominator = summed[:, HD : HD + 1]
        result = summed[:, :HD] / denominator
        logs = largest + jnp.log2(denominator)
        for turn, one in enumerate(own):
            part = slice(turn * rows, (turn + 1) * rows)
            partial[:, one] = result[part]
            columns.append(logs[part])
    stats[...] = stat_rows(columns, rows)


def attend_fresh(requests, queries, new_keys, new_values):
    groups = len(new_keys)
    rows = new_keys[0].shape[0]
    width = queries[0].shape[1]
    return call(
        functools.partial(attend_fresh_kernel, groups, requests),
        [
            jax.ShapeDtypeStruct((rows, width), jnp.float32),
            jax.ShapeDtypeStruct((STAT_ROWS, rows), jnp.float32),
        ],
        [*queries, *new_keys, *new_values],
        24,
        4 * rows * width * rows * groups,
        rows * width // HD * rows * groups,
        "attend_fresh",
    )


def update_kernel(groups, *refs):
    key_refs, value_refs, refs = refs[:groups], refs[groups : 2 * groups], refs[2 * groups :]
    keys, values, lengths_in, keys_updated, values_updated, done, lengths, semaphore = refs
    number = pltpu.make_async_copy(lengths_in, lengths, semaphore)
    number.start()
    keys_updated[...] = keys[...]
    values_updated[...] = values[...]
    done[...] = jnp.zeros(done.shape, done.dtype)
    number.wait()
    request, position_in = place_of(lengths.shape[0])
    rows = key_refs[0].shape[0]
    for turn in range(groups):
        source = source_of(position_in, turn, groups)
        first = lengths[request] + source * rows - position_in * keys.shape[0]
        write_rows(keys_updated, key_refs[turn][...], first)
        write_rows(values_updated, value_refs[turn][...], first)


def update(lengths, new_keys, new_values, keys, values, earlier):
    groups = len(new_keys)
    slab = jax.ShapeDtypeStruct(keys.shape, keys.dtype)
    return call(
        functools.partial(update_kernel, groups),
        [slab, slab, jax.ShapeDtypeStruct((STAT_ROWS, LANES), jnp.float32)],
        [*new_keys, *new_values, keys, values, lengths],
        20,
        4 * new_keys[0].size * new_keys[0].shape[0] * groups,
        0,
        "update_caches",
        earlier,
        [pltpu.SMEM(lengths.shape, lengths.dtype), pltpu.SemaphoreType.DMA],
    )


def project_kernel(row_at, own_partial, own_stats, fresh_partial, fresh_stats, *refs):
    heads = lax.axis_size("head")
    chips = heads // CORES
    outputs = 3 * chips - 1
    received = refs[: -1 - outputs]
    w_out = refs[-1 - outputs]
    near, far = refs[-outputs:][:chips], refs[-outputs:][chips:]
    width = own_partial.shape[1]
    rows, block_width = near[0].shape
    part = slice(row_at, row_at + rows)
    padding = jnp.zeros((LANES - STAT_ROWS, rows), jnp.float32)
    stats = [own_stats[...], fresh_stats[:, part]]
    for ref in received:
        stats.append(
            sum(
                ref[rows:, turn * rows : (turn + 1) * rows].astype(jnp.float32)
                for turn in range(3)
            )[:STAT_ROWS]
        )
    logs = [jnp.concatenate([stat, padding], 0).T for stat in stats]
    largest = functools.reduce(jnp.maximum, logs)
    shares = [jnp.exp2(log - largest) for log in logs]
    total = functools.reduce(jnp.add, shares)
    shares = [share / total for share in shares]
    attended = []
    for head in range(width // HD):
        own = slice(head * HD, (head + 1) * HD)
        column = slice(head, head + 1)
        merged = own_partial[:, own] * shares[0][:, column]
        merged = merged + fresh_partial[part, own] * shares[1][:, column]
        for ref, share in zip(received, shares[2:]):
            merged = merged + ref[:rows, own].astype(jnp.float32) * share[:, column]
        attended.append(merged.astype(jnp.bfloat16))
    attended = jnp.concatenate(attended, 1)
    me = lax.axis_index("head")
    def product(ahead, flip):
        block = lax.rem(me + CORES * ahead, heads) ^ flip
        along = pl.ds(pl.multiple_of(block * block_width, LANES), block_width)
        return dot(attended, w_out[:, along]).astype(jnp.bfloat16)

    middle = block_width // 2
    for ahead in range(1, chips):
        result = product(ahead, 1)
        far[2 * ahead - 1][...] = result[:, :middle]
        far[2 * ahead][...] = result[:, middle:]
    far[0][...] = product(0, 1)
    for ahead in range(chips):
        near[ahead][...] = product(ahead, 0)


def project(row_at, rows, own, fresh_part, received, w_out, heads, earlier):
    chips = heads // CORES
    width = w_out.shape[1] // heads
    shape = jax.ShapeDtypeStruct((rows, width), jnp.bfloat16)
    half = jax.ShapeDtypeStruct((rows, width // 2), jnp.bfloat16)
    blocks = call(
        functools.partial(project_kernel, row_at),
        [shape] * chips + [shape] + [half] * (2 * chips - 2),
        [*own, *fresh_part, *received, w_out],
        20,
        2 * rows * w_out.size,
        0,
        "combine_project",
        earlier,
    )
    near, far = blocks[:chips], blocks[chips:]
    return near, [far[:1]] + [far[2 * k - 1 : 2 * k + 1] for k in range(1, chips)]


def sum_kernel(count, *refs):
    total = refs[0][...].astype(jnp.float32)
    total = total + jnp.concatenate([ref[...] for ref in refs[1:count]], 1).astype(jnp.float32)
    refs[count][...] = total.astype(jnp.bfloat16)


def sum_cores(near, far, earlier):
    return call(
        functools.partial(sum_kernel, 1 + len(far)),
        [jax.ShapeDtypeStruct(near.shape, near.dtype)],
        [near, *far],
        8,
        near.size,
        0,
        "sum_cores",
        earlier,
    )[0]


def finish_kernel(*refs):
    *parts, result = refs
    count = len(parts) // CHUNKS
    rows = parts[0].shape[0]
    for chunk in range(CHUNKS):
        total = 0.0
        for ref in parts[chunk * count : (chunk + 1) * count]:
            total = total + ref[...].astype(jnp.float32)
        result[chunk * rows : (chunk + 1) * rows] = total.astype(jnp.bfloat16)


def finish(parts, earlier):
    rows, width = parts[0].shape
    shape = jax.ShapeDtypeStruct((CHUNKS * rows, width), jnp.bfloat16)
    flops = CHUNKS * rows * width
    return call(finish_kernel, [shape], parts, 8, flops, 0, "finish", earlier)[0]


def shards(
    tokens,
    norm_gain,
    w_query,
    w_key,
    w_value,
    w_out,
    keys_cache,
    values_cache,
    cached_lengths,
    rope_offsets,
):
    rows, width = tokens.shape
    requests = cached_lengths.shape[0]
    groups = lax.axis_size("seq") // requests
    heads = lax.axis_size("head")
    chips = heads // CORES
    chunk_rows = rows // CHUNKS
    gain = norm_gain.reshape(heads, 1, width)

    early = tokens[:chunk_rows]
    mark = marks(keys_cache.shape[0])
    late, *tables = rope_tables(
        tokens, cached_lengths, rope_offsets, groups, rows - chunk_rows, [mark]
    )
    wide_keys, wide_values = widen(keys_cache, values_cache, mark, cached_lengths, [late])
    sent = [early, late]
    arrived = [
        [shifted(piece, "seq", turn * requests) for piece in sent] for turn in range(1, groups)
    ]

    def attend_rows(pieces, own, chunk, turn, earlier):
        at = chunk * chunk_rows
        return attend(
            pieces, gain, w_query, tables, wide_keys, wide_values, mark, own, at if own else 0,
            chunk_rows, turn * rows + at, earlier,
        )

    half = chunk_rows // 2
    first = [relay([pieces[0]], [chunk_rows, half, half], [wide_keys]) for pieces in arrived]
    earlier = [cut[0] for cut in first]
    own_cuts = [
        relay([piece], [rows, half, half, rows - chunk_rows], earlier)
        for piece in other_chips(tokens)
    ]
    own_pieces = [[tokens]] + [[cut[0]] for cut in own_cuts] + [[other_core(tokens)]]
    own_pieces += [[other_core(block) for block in cut[1:]] for cut in own_cuts]
    own_early = [
        blocks if len(blocks) == 1 else blocks[: len(blocks) - 1] for blocks in own_pieces
    ]
    *own_part, queries = attend_rows(own_early, True, 0, 0, earlier)
    own_queries = [queries]
    earlier = [queries]
    gathered = []
    for cut in first:
        blocks = zip(*[other_chips(piece) for piece in cut[1:]])
        from_chips = [relay(one, [chunk_rows], earlier)[0] for one in blocks]
        along = [cut[0]] + from_chips
        gathered.append([along + [other_core(one) for one in along]])
        earlier = earlier + from_chips
    second = [relay([pieces[1]], [rows - chunk_rows], earlier)[0] for pieces in arrived]
    new_rows = [fresh(own_pieces, gain, w_key, w_value, tables, 0, second)]
    earlier = [new_rows[0][0]]
    received = [[] for _ in range(CHUNKS)]
    for turn in range(1, groups):
        pieces = [[block] for block in gathered[turn - 1][0]]
        (packed,) = attend_rows(pieces, False, 0, turn, earlier)
        received[0].append(shifted(packed, "seq", -turn * requests))
        earlier = [packed]
    for pieces, piece in zip(gathered, second):
        from_chips = [
            relay([one], [rows - chunk_rows], earlier)[0] for one in other_chips(piece)
        ]
        along = [piece] + from_chips
        pieces.append(along + [other_core(one) for one in along])
        earlier = earlier + from_chips
    *late_part, queries = attend_rows(own_pieces, True, 1, 0, earlier)
    own_part += late_part
    own_queries.append(queries)
    earlier = [queries]
    for turn in range(1, groups):
        pieces = [[block] for block in gathered[turn - 1][1]]
        (packed,) = attend_rows(pieces, False, 1, turn, earlier)
        received[1].append(shifted(packed, "seq", -turn * requests))
        earlier = [packed]
    for turn in range(1, groups):
        pieces = [list(blocks) for blocks in zip(*gathered[turn - 1])]
        new_rows.append(fresh(pieces, gain, w_key, w_value, tables, turn * rows, earlier))
    new_keys, new_values = zip(*new_rows)
    fresh_part = attend_fresh(requests, own_queries, new_keys, new_values)

    parts = []
    earlier = before_sums = []
    for chunk in range(CHUNKS):
        nears, fars = project(
            chunk * chunk_rows, chunk_rows, own_part[2 * chunk : 2 * chunk + 2], fresh_part,
            received[chunk], w_out, heads, earlier,
        )
        fars = [[other_core(part) for part in far] for far in fars]
        earlier = [nears[0]] + before_sums
        sums = [sum_cores(near, far, earlier) for near, far in zip(nears[1:], fars[1:])]
        from_chips = [shifted(one, "head", CORES * k) for k, one in enumerate(sums, 1)]
        parts += [nears[0], *fars[0], *from_chips]
        earlier, before_sums = sums, from_chips
    keys_updated, values_updated, done = update(
        cached_lengths, new_keys, new_values, keys_cache, values_cache, earlier
    )
    return (finish(parts, [done]), keys_updated, values_updated)


def solution(mesh):
    return jax.shard_map(
        shards,
        mesh=mesh,
        in_specs=(
            P("seq", "head"),
            P(),
            P(None, "head"),
            P(None, "head"),
            P(None, "head"),
            P("head", None),
            P("seq", "head"),
            P("seq", "head"),
            P(),
            P(),
        ),
        out_specs=(P("seq", "head"), P("seq", "head"), P("seq", "head")),
        check_vma=False,
    )
```

```python
import functools
import math

import jax
import jax.numpy as jnp
from jax import lax
from jax.experimental import pallas as pl
from jax.experimental.pallas import tpu as pltpu
from jax.sharding import PartitionSpec as P

HD = 128
LANES = 128
STAT_ROWS = 8
ROW_TILE = 16
CORES = 2
CHUNKS = 2
COST_WEIGHT = 0.0005
FIRST_MICROS = 1
FLOPS_PER_MICRO = 1_000_000_000
MIB = 1 << 20

rope_base = 500000.0
neg_large = -1e30
log2_scale = math.log2(math.e) / math.sqrt(HD)

VMEM = pl.BlockSpec(memory_space=pltpu.VMEM)
ANY = pl.BlockSpec(memory_space=pl.ANY)


def shifted(shard, axis, by):
    devices = lax.axis_size(axis)
    return lax.ppermute(shard, axis, [(i, (i + by) % devices) for i in range(devices)])


def other_core(shard):
    devices = lax.axis_size("head")
    return lax.ppermute(shard, "head", [(i, i ^ 1) for i in range(devices)])


def other_chips(own):
    chips = lax.axis_size("head") // CORES
    return [shifted(own, "head", CORES * k) for k in range(1, chips)]


def place_of(requests):
    member = lax.axis_index("seq")
    return lax.rem(member, requests), lax.div(member, requests)


def source_of(position_in, turn, groups):
    return lax.rem(position_in + (groups - turn), groups)


def dot(left, right):
    return jnp.dot(left, right, preferred_element_type=jnp.float32)


def dot_transposed(left, right):
    return lax.dot_general(
        left, right, (((1,), (1,)), ((), ())), preferred_element_type=jnp.float32
    )


def call(
    kernel, out_shape, arrays, limit, flops, transcendentals, name, earlier=(),
    scratch=(), micros=0,
):
    moved = sum(a.size * a.dtype.itemsize for a in arrays)
    moved += sum(math.prod(s.shape) * s.dtype.itemsize for s in out_shape)
    read = len(arrays)
    skipped = len(earlier)

    def body(*refs):
        kernel(*refs[:read], *refs[read + skipped :])

    return pl.pallas_call(
        body,
        out_shape=out_shape,
        in_specs=[VMEM] * len(arrays) + [ANY] * skipped,
        out_specs=[VMEM] * len(out_shape),
        scratch_shapes=scratch,
        compiler_params=pltpu.CompilerParams(vmem_limit_bytes=limit * MIB),
        cost_estimate=pl.CostEstimate(
            flops=max(int(COST_WEIGHT * flops), micros * FLOPS_PER_MICRO),
            bytes_accessed=int(COST_WEIGHT * moved),
            transcendentals=int(COST_WEIGHT * transcendentals),
        ),
        name=name,
    )(*arrays, *earlier)


def whole_of(blocks):
    parts = [block[...] for block in blocks]
    return jnp.concatenate(parts, 0) if len(parts) > 1 else parts[0]


def relay_kernel(count, *refs):
    whole = whole_of(refs[:count])
    at = 0
    for ref in refs[count:]:
        ref[...] = whole[at : at + ref.shape[0]]
        at = (at + ref.shape[0]) % whole.shape[0]


def relay(blocks, sizes, earlier):
    shapes = [jax.ShapeDtypeStruct((size, *blocks[0].shape[1:]), blocks[0].dtype) for size in sizes]
    kernel = functools.partial(relay_kernel, len(blocks))
    return call(kernel, shapes, [*blocks], 4, 0, 0, "relay", earlier)


def mark_kernel(mark):
    lane = lax.broadcasted_iota(jnp.int32, mark.shape, 1)
    mark[...] = jnp.where(lane == 0, 1.0, 0.0).astype(mark.dtype)


def marks(rows):
    shape = jax.ShapeDtypeStruct((rows, LANES), jnp.bfloat16)
    return call(mark_kernel, [shape], [], 4, 0, 0, "marks", micros=FIRST_MICROS)[0]


def tables_kernel(groups, lengths_in, offsets_in, cosine, sine, *scratch):
    lengths, offsets, semaphores = scratch
    numbers = [
        pltpu.make_async_copy(lengths_in, lengths, semaphores.at[0]),
        pltpu.make_async_copy(offsets_in, offsets, semaphores.at[1]),
    ]
    for copy in numbers:
        copy.start()
    rows = cosine.shape[0] // groups
    for copy in numbers:
        copy.wait()
    request, position_in = place_of(lengths.shape[0])
    lane = lax.broadcasted_iota(jnp.int32, (rows, LANES), 1)
    row = lax.broadcasted_iota(jnp.int32, (rows, LANES), 0)
    half = lax.rem(lane, HD // 2).astype(jnp.float32)
    frequency = jnp.exp2(half * (-2.0 / HD * math.log2(rope_base)))
    sign = jnp.where(lane < HD // 2, -1.0, 1.0)
    for turn in range(groups):
        first = source_of(position_in, turn, groups) * rows
        first = first + offsets[request] + lengths[request]
        angles = (row + first).astype(jnp.float32) * frequency
        part = slice(turn * rows, (turn + 1) * rows)
        cosine[part] = jnp.cos(angles)
        sine[part] = jnp.sin(angles) * sign


def rope_tables(lengths, offsets, groups, rows, earlier):
    table = jax.ShapeDtypeStruct((groups * rows, LANES), jnp.float32)
    return call(
        functools.partial(tables_kernel, groups),
        [table, table],
        [lengths, offsets],
        12,
        0,
        0,
        "rope_tables",
        earlier,
        [
            pltpu.SMEM(lengths.shape, lengths.dtype),
            pltpu.SMEM(offsets.shape, offsets.dtype),
            pltpu.SemaphoreType.DMA((2,)),
        ],
        FIRST_MICROS,
    )


def widen_kernel(keys, values, mark, lengths_in, wide_keys, wide_values, lengths, semaphore):
    number = pltpu.make_async_copy(lengths_in, lengths, semaphore)
    number.start()
    slots = keys.shape[0]
    heads = keys.shape[1] // HD
    for head in range(heads):
        own = slice(head * HD, (head + 1) * HD)
        wide_keys[head, :, :HD] = keys[:, own]
        wide_values[head, :, :HD] = values[:, own]
        wide_values[head, :, HD:] = mark[:slots]
    number.wait()
    request, position_in = place_of(lengths.shape[0])
    slot = lax.broadcasted_iota(jnp.int32, (slots, LANES), 0) + position_in * slots
    lane = lax.broadcasted_iota(jnp.int32, (slots, LANES), 1)
    bias = jnp.where((lane == 0) & (slot >= lengths[request]), neg_large, 0.0).astype(jnp.bfloat16)
    for head in range(heads):
        wide_keys[head, :, HD:] = bias


def widen(keys, values, mark, lengths, earlier):
    slots, width = keys.shape
    wide = jax.ShapeDtypeStruct((width // HD, slots, HD + LANES), jnp.bfloat16)
    return call(
        widen_kernel,
        [wide, wide],
        [keys, values, mark, lengths],
        12,
        0,
        0,
        "widen_caches",
        earlier,
        [pltpu.SMEM(lengths.shape, lengths.dtype), pltpu.SemaphoreType.DMA],
        FIRST_MICROS,
    )


def rotate(vectors, cosine, sine):
    return vectors * cosine + pltpu.roll(vectors, HD // 2, 1) * sine


def project_normed(pieces, gain, weights):
    heads = gain.shape[0]
    width = gain.shape[2]
    me = lax.axis_index("head")
    squares = 0.0
    sums = [0.0] * len(weights)
    for index, piece in enumerate(pieces):
        owner = lax.rem(me + (heads - CORES * (index % (heads // CORES))), heads)
        if index >= heads // CORES:
            owner = owner ^ 1
        wide = piece.astype(jnp.float32)
        scaled = (wide * gain[owner]).astype(jnp.bfloat16)
        along = pl.ds(pl.multiple_of(owner * width, LANES), width)
        for place, weight in enumerate(weights):
            sums[place] = sums[place] + dot(scaled, weight[along, :])
        squares = squares + jnp.sum(wide * wide, -1, keepdims=True)
    factor = lax.rsqrt(squares / (heads * width) + 1e-05)
    return [total * factor for total in sums]


def stat_rows(columns, rows):
    lane = lax.broadcasted_iota(jnp.int32, (rows, LANES), 1)
    table = jnp.zeros((rows, LANES), jnp.float32)
    for index, column in enumerate(columns):
        table = jnp.where(lane == index, column, table)
    return table.T[:STAT_ROWS]


def split_refs(counts, refs):
    parts = []
    for count in counts:
        parts.append(refs[:count])
        refs = refs[count:]
    return parts, refs


def rows_of(blocks, row_at, rows):
    parts = []
    at = 0
    for block in blocks:
        size = block.shape[0]
        low, high = max(row_at - at, 0), min(row_at + rows - at, size)
        if low < high:
            parts.append(block[low:high])
        at += size
    return jnp.concatenate(parts, 0) if len(parts) > 1 else parts[0]


def attend_kernel(counts, own, row_at, rows, table_at, *refs):
    blocks, refs = split_refs(counts, refs)
    gain, w_query, cosine, sine, wide_keys, wide_values, mark, *outputs = refs
    pieces = [rows_of(one, row_at, rows) for one in blocks]
    (product,) = project_normed(pieces, gain, [w_query])
    cosine = cosine[table_at : table_at + rows]
    sine = sine[table_at : table_at + rows]
    kv_heads = wide_keys.shape[0]
    repeat = product.shape[1] // HD // kv_heads
    queries = [
        (rotate(product[:, head * HD : (head + 1) * HD], cosine, sine) * log2_scale).astype(
            jnp.bfloat16
        )
        for head in range(kv_heads * repeat)
    ]
    step = min(rows, LANES)
    mark = mark[: repeat * step]
    tiles = [(head, at) for head in range(kv_heads) for at in range(0, rows, step)]

    def scores_of(head, at):
        stacked = jnp.concatenate(
            [query[at : at + step] for query in queries[head * repeat : (head + 1) * repeat]], 0
        )
        return dot_transposed(jnp.concatenate([stacked, mark], 1), wide_keys[head])

    columns = {}
    following = scores_of(*tiles[0])
    for index, (head, at) in enumerate(tiles):
        scores = following
        if index + 1 < len(tiles):
            following = scores_of(*tiles[index + 1])
        largest = jnp.max(scores, -1, keepdims=True)
        weights = jnp.exp2(scores - largest).astype(jnp.bfloat16)
        summed = dot(weights, wide_values[head])
        denominator = summed[:, HD : HD + 1]
        result = summed[:, :HD] / denominator
        logs = largest + jnp.log2(denominator)
        for turn in range(repeat):
            part = slice(turn * step, (turn + 1) * step)
            to = slice((head * repeat + turn) * HD, (head * repeat + turn + 1) * HD)
            outputs[0][at : at + step, to] = result[part].astype(outputs[0].dtype)
            columns.setdefault(head * repeat + turn, []).append(logs[part])
    stats = stat_rows([jnp.concatenate(parts, 0) for parts in columns.values()], rows)
    if own:
        outputs[1][...] = stats
        outputs[2][...] = jnp.concatenate(queries, 1)
        return
    outputs[0][rows:] = jnp.zeros((ROW_TILE, outputs[0].shape[1]), jnp.bfloat16)
    rest = jnp.concatenate([stats, jnp.zeros((ROW_TILE - STAT_ROWS, rows), jnp.float32)], 0)
    for part in range(3):
        rounded = rest.astype(jnp.bfloat16)
        outputs[0][rows:, part * rows : (part + 1) * rows] = rounded
        rest = rest - rounded.astype(jnp.float32)


def attend(
    pieces, gain, w_query, tables, wide_keys, wide_values, mark, own, row_at, rows, table_at,
    earlier,
):
    counts = [len(blocks) for blocks in pieces]
    flat = [block for blocks in pieces for block in blocks]
    out_width = w_query.shape[1]
    slots = wide_keys.shape[1]
    if own:
        out_shape = [
            jax.ShapeDtypeStruct((rows, out_width), jnp.float32),
            jax.ShapeDtypeStruct((STAT_ROWS, rows), jnp.float32),
            jax.ShapeDtypeStruct((rows, out_width), jnp.bfloat16),
        ]
    else:
        out_shape = [jax.ShapeDtypeStruct((rows + ROW_TILE, out_width), jnp.bfloat16)]
    return call(
        functools.partial(attend_kernel, counts, own, row_at, rows, table_at),
        out_shape,
        [*flat, gain, w_query, *tables, wide_keys, wide_values, mark],
        28,
        2 * rows * out_width * (w_query.shape[0] + 4 * slots),
        rows * out_width // HD * slots,
        "attend_own" if own else "attend_partner",
        earlier,
    )


def fresh_kernel(counts, table_at, *refs):
    blocks, refs = split_refs(counts, refs)
    gain, w_key, w_value, cosine, sine, new_keys, new_values = refs
    rows = new_keys.shape[0]
    pieces = [whole_of(one) for one in blocks]
    keys, values = project_normed(pieces, gain, [w_key, w_value])
    cosine = cosine[table_at : table_at + rows]
    sine = sine[table_at : table_at + rows]
    for head in range(keys.shape[1] // HD):
        own = slice(head * HD, (head + 1) * HD)
        new_keys[:, own] = rotate(keys[:, own], cosine, sine).astype(jnp.bfloat16)
    new_values[...] = values.astype(jnp.bfloat16)


def fresh(pieces, gain, w_key, w_value, tables, table_at, earlier):
    flat = [block for blocks in pieces for block in blocks]
    rows = sum(block.shape[0] for block in pieces[0])
    shape = jax.ShapeDtypeStruct((rows, w_key.shape[1]), jnp.bfloat16)
    return call(
        functools.partial(fresh_kernel, [len(blocks) for blocks in pieces], table_at),
        [shape, shape],
        [*flat, gain, w_key, w_value, *tables],
        20,
        4 * rows * w_key.size,
        0,
        "fresh_kv",
        earlier,
    )


def write_rows(target, fresh_rows, first):
    rows = fresh_rows.shape[0]
    slab_rows = target.shape[0]
    span = rows + ROW_TILE
    start = jnp.clip(first, 0, slab_rows - span)
    start = start - lax.rem(start, ROW_TILE)
    window = pl.ds(pl.multiple_of(start, ROW_TILE), span)
    shift = start - first
    place = lax.broadcasted_iota(jnp.int32, (span, rows), 0) + shift
    chosen = place == lax.broadcasted_iota(jnp.int32, (span, rows), 1)
    moved = dot(chosen.astype(jnp.bfloat16), fresh_rows)
    row = lax.broadcasted_iota(jnp.int32, (span, target.shape[1]), 0) + shift
    inside = (row >= 0) & (row < rows)
    old = target[window, :].astype(jnp.float32)
    target[window, :] = jnp.where(inside, moved, old).astype(jnp.bfloat16)


def attend_fresh_kernel(groups, requests, *refs):
    query_refs, refs = refs[:CHUNKS], refs[CHUNKS:]
    key_refs, value_refs, refs = refs[:groups], refs[groups : 2 * groups], refs[2 * groups :]
    partial, stats = refs
    position_in = place_of(requests)[1]
    rows, width = partial.shape
    kv_heads = key_refs[0].shape[1] // HD
    repeat = width // HD // kv_heads
    queries = whole_of(query_refs)
    token = lax.broadcasted_iota(jnp.int32, (rows, rows), 0)
    within = lax.broadcasted_iota(jnp.int32, (rows, rows), 1)
    causal = jnp.where(within <= token, 0.0, neg_large)
    causal = jnp.concatenate([causal] * repeat, 0)
    lane = lax.broadcasted_iota(jnp.int32, (rows, LANES), 1)
    ones = jnp.where(lane == 0, 1.0, 0.0).astype(jnp.bfloat16)
    hidden = [jnp.zeros((rows, LANES), jnp.bfloat16)]
    for turn in range(1, groups):
        later = source_of(position_in, turn, groups) > position_in
        hidden.append(jnp.where((lane == 0) & later, neg_large, 0.0).astype(jnp.bfloat16))
    columns = []
    for head in range(kv_heads):
        own = [
            slice((head * repeat + turn) * HD, (head * repeat + turn + 1) * HD)
            for turn in range(repeat)
        ]
        shared = slice(head * HD, (head + 1) * HD)
        stacked = jnp.concatenate([queries[:, one] for one in own], 0)
        stacked = jnp.concatenate([stacked, jnp.concatenate([ones] * repeat, 0)], 1)
        scores = [
            dot_transposed(stacked, jnp.concatenate([ref[:, shared], bias], 1))
            for ref, bias in zip(key_refs, hidden)
        ]
        scores = jnp.concatenate([scores[0] + causal] + scores[1:], 1)
        largest = jnp.max(scores, -1, keepdims=True)
        weights = jnp.exp2(scores - largest).astype(jnp.bfloat16)
        wide_values = [jnp.concatenate([ref[:, shared], ones], 1) for ref in value_refs]
        summed = dot(weights, jnp.concatenate(wide_values, 0))
        denominator = summed[:, HD : HD + 1]
        result = summed[:, :HD] / denominator
        logs = largest + jnp.log2(denominator)
        for turn, one in enumerate(own):
            part = slice(turn * rows, (turn + 1) * rows)
            partial[:, one] = result[part]
            columns.append(logs[part])
    stats[...] = stat_rows(columns, rows)


def attend_fresh(requests, queries, new_keys, new_values):
    groups = len(new_keys)
    rows = new_keys[0].shape[0]
    width = queries[0].shape[1]
    return call(
        functools.partial(attend_fresh_kernel, groups, requests),
        [
            jax.ShapeDtypeStruct((rows, width), jnp.float32),
            jax.ShapeDtypeStruct((STAT_ROWS, rows), jnp.float32),
        ],
        [*queries, *new_keys, *new_values],
        24,
        4 * rows * width * rows * groups,
        rows * width // HD * rows * groups,
        "attend_fresh",
    )


def update_kernel(groups, *refs):
    key_refs, value_refs, refs = refs[:groups], refs[groups : 2 * groups], refs[2 * groups :]
    keys, values, lengths_in, keys_updated, values_updated, done, lengths, semaphore = refs
    number = pltpu.make_async_copy(lengths_in, lengths, semaphore)
    number.start()
    keys_updated[...] = keys[...]
    values_updated[...] = values[...]
    done[...] = jnp.zeros(done.shape, done.dtype)
    number.wait()
    request, position_in = place_of(lengths.shape[0])
    rows = key_refs[0].shape[0]
    for turn in range(groups):
        source = source_of(position_in, turn, groups)
        first = lengths[request] + source * rows - position_in * keys.shape[0]
        write_rows(keys_updated, key_refs[turn][...], first)
        write_rows(values_updated, value_refs[turn][...], first)


def update(lengths, new_keys, new_values, keys, values, earlier):
    groups = len(new_keys)
    slab = jax.ShapeDtypeStruct(keys.shape, keys.dtype)
    return call(
        functools.partial(update_kernel, groups),
        [slab, slab, jax.ShapeDtypeStruct((STAT_ROWS, LANES), jnp.float32)],
        [*new_keys, *new_values, keys, values, lengths],
        20,
        4 * new_keys[0].size * new_keys[0].shape[0] * groups,
        0,
        "update_caches",
        earlier,
        [pltpu.SMEM(lengths.shape, lengths.dtype), pltpu.SemaphoreType.DMA],
    )


def project_kernel(row_at, own_partial, own_stats, fresh_partial, fresh_stats, *refs):
    heads = lax.axis_size("head")
    chips = heads // CORES
    outputs = 3 * chips - 1
    received = refs[: -1 - outputs]
    w_out = refs[-1 - outputs]
    near, far = refs[-outputs:][:chips], refs[-outputs:][chips:]
    width = own_partial.shape[1]
    rows, block_width = near[0].shape
    part = slice(row_at, row_at + rows)
    padding = jnp.zeros((LANES - STAT_ROWS, rows), jnp.float32)
    stats = [own_stats[...], fresh_stats[:, part]]
    for ref in received:
        stats.append(
            sum(
                ref[rows:, turn * rows : (turn + 1) * rows].astype(jnp.float32)
                for turn in range(3)
            )[:STAT_ROWS]
        )
    logs = [jnp.concatenate([stat, padding], 0).T for stat in stats]
    largest = functools.reduce(jnp.maximum, logs)
    shares = [jnp.exp2(log - largest) for log in logs]
    total = functools.reduce(jnp.add, shares)
    shares = [share / total for share in shares]
    attended = []
    for head in range(width // HD):
        own = slice(head * HD, (head + 1) * HD)
        column = slice(head, head + 1)
        merged = own_partial[:, own] * shares[0][:, column]
        merged = merged + fresh_partial[part, own] * shares[1][:, column]
        for ref, share in zip(received, shares[2:]):
            merged = merged + ref[:rows, own].astype(jnp.float32) * share[:, column]
        attended.append(merged.astype(jnp.bfloat16))
    attended = jnp.concatenate(attended, 1)
    me = lax.axis_index("head")
    def product(ahead, flip):
        block = lax.rem(me + CORES * ahead, heads) ^ flip
        along = pl.ds(pl.multiple_of(block * block_width, LANES), block_width)
        return dot(attended, w_out[:, along]).astype(jnp.bfloat16)

    middle = block_width // 2
    for ahead in range(1, chips):
        result = product(ahead, 1)
        far[2 * ahead - 1][...] = result[:, :middle]
        far[2 * ahead][...] = result[:, middle:]
    far[0][...] = product(0, 1)
    for ahead in range(chips):
        near[ahead][...] = product(ahead, 0)


def project(row_at, rows, own, fresh_part, received, w_out, heads, earlier):
    chips = heads // CORES
    width = w_out.shape[1] // heads
    shape = jax.ShapeDtypeStruct((rows, width), jnp.bfloat16)
    half = jax.ShapeDtypeStruct((rows, width // 2), jnp.bfloat16)
    blocks = call(
        functools.partial(project_kernel, row_at),
        [shape] * chips + [shape] + [half] * (2 * chips - 2),
        [*own, *fresh_part, *received, w_out],
        20,
        2 * rows * w_out.size,
        0,
        "combine_project",
        earlier,
    )
    near, far = blocks[:chips], blocks[chips:]
    return near, [far[:1]] + [far[2 * k - 1 : 2 * k + 1] for k in range(1, chips)]


def sum_kernel(count, *refs):
    total = refs[0][...].astype(jnp.float32)
    total = total + jnp.concatenate([ref[...] for ref in refs[1:count]], 1).astype(jnp.float32)
    refs[count][...] = total.astype(jnp.bfloat16)


def sum_cores(near, far, earlier):
    return call(
        functools.partial(sum_kernel, 1 + len(far)),
        [jax.ShapeDtypeStruct(near.shape, near.dtype)],
        [near, *far],
        8,
        near.size,
        0,
        "sum_cores",
        earlier,
    )[0]


def finish_kernel(*refs):
    *parts, result = refs
    count = len(parts) // CHUNKS
    rows = parts[0].shape[0]
    for chunk in range(CHUNKS):
        total = 0.0
        for ref in parts[chunk * count : (chunk + 1) * count]:
            total = total + ref[...].astype(jnp.float32)
        result[chunk * rows : (chunk + 1) * rows] = total.astype(jnp.bfloat16)


def finish(parts, earlier):
    rows, width = parts[0].shape
    shape = jax.ShapeDtypeStruct((CHUNKS * rows, width), jnp.bfloat16)
    flops = CHUNKS * rows * width
    return call(finish_kernel, [shape], parts, 8, flops, 0, "finish", earlier)[0]


def shards(
    tokens,
    norm_gain,
    w_query,
    w_key,
    w_value,
    w_out,
    keys_cache,
    values_cache,
    cached_lengths,
    rope_offsets,
):
    rows, width = tokens.shape
    requests = cached_lengths.shape[0]
    groups = lax.axis_size("seq") // requests
    heads = lax.axis_size("head")
    chips = heads // CORES
    chunk_rows = rows // CHUNKS
    gain = norm_gain.reshape(heads, 1, width)

    early = tokens[:chunk_rows]
    mark = marks(keys_cache.shape[0])
    tables = rope_tables(cached_lengths, rope_offsets, groups, rows, [mark])
    wide_keys, wide_values = widen(keys_cache, values_cache, mark, cached_lengths, tables[:1])

    def attend_rows(pieces, own, chunk, turn, earlier):
        at = chunk * chunk_rows
        return attend(
            pieces, gain, w_query, tables, wide_keys, wide_values, mark, own, at if own else 0,
            chunk_rows, turn * rows + at, earlier,
        )

    half = chunk_rows // 2
    first = [shifted(early, "seq", turn * requests) for turn in range(1, groups)]
    from_chips = other_chips(tokens)
    (late,) = relay([tokens[chunk_rows:]], [rows - chunk_rows], from_chips + [wide_keys])
    second = [shifted(late, "seq", turn * requests) for turn in range(1, groups)]
    own_cuts = [relay([piece], [rows, half, half, rows - chunk_rows], [late]) for piece in from_chips]
    earlier = [cut[0] for cut in own_cuts]
    first = [relay([piece], [chunk_rows, half, half], earlier) for piece in first]
    earlier = [cut[0] for cut in first]
    own_pieces = [[tokens]] + [[cut[0]] for cut in own_cuts] + [[other_core(tokens)]]
    own_pieces += [[other_core(block) for block in cut[1:]] for cut in own_cuts]
    own_early = [
        blocks if len(blocks) == 1 else blocks[: len(blocks) - 1] for blocks in own_pieces
    ]
    *own_part, queries = attend_rows(own_early, True, 0, 0, earlier)
    own_queries = [queries]
    earlier = [queries]
    gathered = []
    for cut in first:
        blocks = zip(*[other_chips(piece) for piece in cut[1:]])
        from_chips = [relay(one, [chunk_rows], earlier)[0] for one in blocks]
        along = [cut[0]] + from_chips
        gathered.append([along + [other_core(one) for one in along]])
        earlier = earlier + from_chips
    second = [relay([piece], [rows - chunk_rows], earlier)[0] for piece in second]
    new_rows = [fresh(own_pieces, gain, w_key, w_value, tables, 0, second)]
    earlier = [new_rows[0][0]]
    received = [[] for _ in range(CHUNKS)]
    for turn in range(1, groups):
        pieces = [[block] for block in gathered[turn - 1][0]]
        (packed,) = attend_rows(pieces, False, 0, turn, earlier)
        received[0].append(shifted(packed, "seq", -turn * requests))
        earlier = [packed]
    for pieces, piece in zip(gathered, second):
        from_chips = [
            relay([one], [rows - chunk_rows], earlier)[0] for one in other_chips(piece)
        ]
        along = [piece] + from_chips
        pieces.append(along + [other_core(one) for one in along])
        earlier = earlier + from_chips
    *late_part, queries = attend_rows(own_pieces, True, 1, 0, earlier)
    own_part += late_part
    own_queries.append(queries)
    earlier = [queries]
    for turn in range(1, groups):
        pieces = [[block] for block in gathered[turn - 1][1]]
        (packed,) = attend_rows(pieces, False, 1, turn, earlier)
        received[1].append(shifted(packed, "seq", -turn * requests))
        earlier = [packed]
    for turn in range(1, groups):
        pieces = [list(blocks) for blocks in zip(*gathered[turn - 1])]
        new_rows.append(fresh(pieces, gain, w_key, w_value, tables, turn * rows, earlier))
    new_keys, new_values = zip(*new_rows)
    fresh_part = attend_fresh(requests, own_queries, new_keys, new_values)

    parts = []
    earlier = before_sums = []
    for chunk in range(CHUNKS):
        nears, fars = project(
            chunk * chunk_rows, chunk_rows, own_part[2 * chunk : 2 * chunk + 2], fresh_part,
            received[chunk], w_out, heads, earlier,
        )
        fars = [[other_core(part) for part in far] for far in fars]
        earlier = [nears[0]] + before_sums
        sums = [sum_cores(near, far, earlier) for near, far in zip(nears[1:], fars[1:])]
        from_chips = [shifted(one, "head", CORES * k) for k, one in enumerate(sums, 1)]
        parts += [nears[0], *fars[0], *from_chips]
        earlier, before_sums = sums, from_chips
    keys_updated, values_updated, done = update(
        cached_lengths, new_keys, new_values, keys_cache, values_cache, earlier
    )
    return (finish(parts, [done]), keys_updated, values_updated)


def solution(mesh):
    return jax.shard_map(
        shards,
        mesh=mesh,
        in_specs=(
            P("seq", "head"),
            P(),
            P(None, "head"),
            P(None, "head"),
            P(None, "head"),
            P("head", None),
            P("seq", "head"),
            P("seq", "head"),
            P(),
            P(),
        ),
        out_specs=(P("seq", "head"), P("seq", "head"), P("seq", "head")),
        check_vma=False,
    )
```

```python
import functools
import math

import jax
import jax.numpy as jnp
from jax import lax
from jax.experimental import pallas as pl
from jax.experimental.pallas import tpu as pltpu
from jax.sharding import PartitionSpec as P

HD = 128
LANES = 128
STAT_ROWS = 8
ROW_TILE = 16
CORES = 2
CHUNKS = 2
COST_WEIGHT = 0.0005
FIRST_MICROS = 1
FLOPS_PER_MICRO = 1_000_000_000
MIB = 1 << 20

rope_base = 500000.0
neg_large = -1e30
log2_scale = math.log2(math.e) / math.sqrt(HD)

VMEM = pl.BlockSpec(memory_space=pltpu.VMEM)
ANY = pl.BlockSpec(memory_space=pl.ANY)


def shifted(shard, axis, by):
    devices = lax.axis_size(axis)
    return lax.ppermute(shard, axis, [(i, (i + by) % devices) for i in range(devices)])


def other_core(shard):
    devices = lax.axis_size("head")
    return lax.ppermute(shard, "head", [(i, i ^ 1) for i in range(devices)])


def other_chips(own):
    chips = lax.axis_size("head") // CORES
    return [shifted(own, "head", CORES * k) for k in range(1, chips)]


def place_of(requests):
    member = lax.axis_index("seq")
    return lax.rem(member, requests), lax.div(member, requests)


def source_of(position_in, turn, groups):
    return lax.rem(position_in + (groups - turn), groups)


def dot(left, right):
    return jnp.dot(left, right, preferred_element_type=jnp.float32)


def dot_transposed(left, right):
    return lax.dot_general(
        left, right, (((1,), (1,)), ((), ())), preferred_element_type=jnp.float32
    )


def call(
    kernel, out_shape, arrays, limit, flops, transcendentals, name, earlier=(),
    scratch=(), micros=0,
):
    moved = sum(a.size * a.dtype.itemsize for a in arrays)
    moved += sum(math.prod(s.shape) * s.dtype.itemsize for s in out_shape)
    read = len(arrays)
    skipped = len(earlier)

    def body(*refs):
        kernel(*refs[:read], *refs[read + skipped :])

    return pl.pallas_call(
        body,
        out_shape=out_shape,
        in_specs=[VMEM] * len(arrays) + [ANY] * skipped,
        out_specs=[VMEM] * len(out_shape),
        scratch_shapes=scratch,
        compiler_params=pltpu.CompilerParams(vmem_limit_bytes=limit * MIB),
        cost_estimate=pl.CostEstimate(
            flops=max(int(COST_WEIGHT * flops), micros * FLOPS_PER_MICRO),
            bytes_accessed=int(COST_WEIGHT * moved),
            transcendentals=int(COST_WEIGHT * transcendentals),
        ),
        name=name,
    )(*arrays, *earlier)


def whole_of(blocks):
    parts = [block[...] for block in blocks]
    return jnp.concatenate(parts, 0) if len(parts) > 1 else parts[0]


def relay_kernel(count, *refs):
    whole = whole_of(refs[:count])
    at = 0
    for ref in refs[count:]:
        ref[...] = whole[at : at + ref.shape[0]]
        at = (at + ref.shape[0]) % whole.shape[0]


def relay(blocks, sizes, earlier):
    shapes = [jax.ShapeDtypeStruct((size, *blocks[0].shape[1:]), blocks[0].dtype) for size in sizes]
    kernel = functools.partial(relay_kernel, len(blocks))
    return call(kernel, shapes, [*blocks], 4, 0, 0, "relay", earlier)


def mark_kernel(mark):
    lane = lax.broadcasted_iota(jnp.int32, mark.shape, 1)
    mark[...] = jnp.where(lane == 0, 1.0, 0.0).astype(mark.dtype)


def marks(rows):
    shape = jax.ShapeDtypeStruct((rows, LANES), jnp.bfloat16)
    return call(mark_kernel, [shape], [], 4, 0, 0, "marks", micros=FIRST_MICROS)[0]


def tables_kernel(groups, lengths_in, offsets_in, cosine, sine, *scratch):
    lengths, offsets, semaphores = scratch
    numbers = [
        pltpu.make_async_copy(lengths_in, lengths, semaphores.at[0]),
        pltpu.make_async_copy(offsets_in, offsets, semaphores.at[1]),
    ]
    for copy in numbers:
        copy.start()
    rows = cosine.shape[0] // groups
    for copy in numbers:
        copy.wait()
    request, position_in = place_of(lengths.shape[0])
    lane = lax.broadcasted_iota(jnp.int32, (rows, LANES), 1)
    row = lax.broadcasted_iota(jnp.int32, (rows, LANES), 0)
    half = lax.rem(lane, HD // 2).astype(jnp.float32)
    frequency = jnp.exp2(half * (-2.0 / HD * math.log2(rope_base)))
    sign = jnp.where(lane < HD // 2, -1.0, 1.0)
    for turn in range(groups):
        first = source_of(position_in, turn, groups) * rows
        first = first + offsets[request] + lengths[request]
        angles = (row + first).astype(jnp.float32) * frequency
        part = slice(turn * rows, (turn + 1) * rows)
        cosine[part] = jnp.cos(angles)
        sine[part] = jnp.sin(angles) * sign


def rope_tables(lengths, offsets, groups, rows, earlier):
    table = jax.ShapeDtypeStruct((groups * rows, LANES), jnp.float32)
    return call(
        functools.partial(tables_kernel, groups),
        [table, table],
        [lengths, offsets],
        12,
        0,
        0,
        "rope_tables",
        earlier,
        [
            pltpu.SMEM(lengths.shape, lengths.dtype),
            pltpu.SMEM(offsets.shape, offsets.dtype),
            pltpu.SemaphoreType.DMA((2,)),
        ],
        FIRST_MICROS,
    )


def widen_kernel(keys, values, mark, lengths_in, wide_keys, wide_values, lengths, semaphore):
    number = pltpu.make_async_copy(lengths_in, lengths, semaphore)
    number.start()
    slots = keys.shape[0]
    heads = keys.shape[1] // HD
    for head in range(heads):
        own = slice(head * HD, (head + 1) * HD)
        wide_keys[head, :, :HD] = keys[:, own]
        wide_values[head, :, :HD] = values[:, own]
        wide_values[head, :, HD:] = mark[:slots]
    number.wait()
    request, position_in = place_of(lengths.shape[0])
    slot = lax.broadcasted_iota(jnp.int32, (slots, LANES), 0) + position_in * slots
    lane = lax.broadcasted_iota(jnp.int32, (slots, LANES), 1)
    bias = jnp.where((lane == 0) & (slot >= lengths[request]), neg_large, 0.0).astype(jnp.bfloat16)
    for head in range(heads):
        wide_keys[head, :, HD:] = bias


def widen(keys, values, mark, lengths, earlier):
    slots, width = keys.shape
    wide = jax.ShapeDtypeStruct((width // HD, slots, HD + LANES), jnp.bfloat16)
    return call(
        widen_kernel,
        [wide, wide],
        [keys, values, mark, lengths],
        12,
        0,
        0,
        "widen_caches",
        earlier,
        [pltpu.SMEM(lengths.shape, lengths.dtype), pltpu.SemaphoreType.DMA],
        FIRST_MICROS,
    )


def rotate(vectors, cosine, sine):
    return vectors * cosine + pltpu.roll(vectors, HD // 2, 1) * sine


def project_normed(pieces, gain, weights):
    heads = gain.shape[0]
    width = gain.shape[2]
    me = lax.axis_index("head")
    squares = 0.0
    sums = [0.0] * len(weights)
    for index, piece in enumerate(pieces):
        owner = lax.rem(me + (heads - CORES * (index % (heads // CORES))), heads)
        if index >= heads // CORES:
            owner = owner ^ 1
        wide = piece.astype(jnp.float32)
        scaled = (wide * gain[owner]).astype(jnp.bfloat16)
        along = pl.ds(pl.multiple_of(owner * width, LANES), width)
        for place, weight in enumerate(weights):
            sums[place] = sums[place] + dot(scaled, weight[along, :])
        squares = squares + jnp.sum(wide * wide, -1, keepdims=True)
    factor = lax.rsqrt(squares / (heads * width) + 1e-05)
    return [total * factor for total in sums]


def stat_rows(columns, rows):
    lane = lax.broadcasted_iota(jnp.int32, (rows, LANES), 1)
    table = jnp.zeros((rows, LANES), jnp.float32)
    for index, column in enumerate(columns):
        table = jnp.where(lane == index, column, table)
    return table.T[:STAT_ROWS]


def split_refs(counts, refs):
    parts = []
    for count in counts:
        parts.append(refs[:count])
        refs = refs[count:]
    return parts, refs


def rows_of(blocks, row_at, rows):
    parts = []
    at = 0
    for block in blocks:
        size = block.shape[0]
        low, high = max(row_at - at, 0), min(row_at + rows - at, size)
        if low < high:
            parts.append(block[low:high])
        at += size
    return jnp.concatenate(parts, 0) if len(parts) > 1 else parts[0]


def attend_kernel(counts, own, row_at, rows, table_at, *refs):
    blocks, refs = split_refs(counts, refs)
    gain, w_query, cosine, sine, wide_keys, wide_values, mark, *outputs = refs
    pieces = [rows_of(one, row_at, rows) for one in blocks]
    (product,) = project_normed(pieces, gain, [w_query])
    cosine = cosine[table_at : table_at + rows]
    sine = sine[table_at : table_at + rows]
    kv_heads = wide_keys.shape[0]
    repeat = product.shape[1] // HD // kv_heads
    queries = [
        (rotate(product[:, head * HD : (head + 1) * HD], cosine, sine) * log2_scale).astype(
            jnp.bfloat16
        )
        for head in range(kv_heads * repeat)
    ]
    step = min(rows, LANES)
    mark = mark[: repeat * step]
    tiles = [(head, at) for head in range(kv_heads) for at in range(0, rows, step)]

    def scores_of(head, at):
        stacked = jnp.concatenate(
            [query[at : at + step] for query in queries[head * repeat : (head + 1) * repeat]], 0
        )
        return dot_transposed(jnp.concatenate([stacked, mark], 1), wide_keys[head])

    columns = {}
    following = scores_of(*tiles[0])
    for index, (head, at) in enumerate(tiles):
        scores = following
        if index + 1 < len(tiles):
            following = scores_of(*tiles[index + 1])
        largest = jnp.max(scores, -1, keepdims=True)
        weights = jnp.exp2(scores - largest).astype(jnp.bfloat16)
        summed = dot(weights, wide_values[head])
        denominator = summed[:, HD : HD + 1]
        result = summed[:, :HD] / denominator
        logs = largest + jnp.log2(denominator)
        for turn in range(repeat):
            part = slice(turn * step, (turn + 1) * step)
            to = slice((head * repeat + turn) * HD, (head * repeat + turn + 1) * HD)
            outputs[0][at : at + step, to] = result[part].astype(outputs[0].dtype)
            columns.setdefault(head * repeat + turn, []).append(logs[part])
    stats = stat_rows([jnp.concatenate(parts, 0) for parts in columns.values()], rows)
    if own:
        outputs[1][...] = stats
        outputs[2][...] = jnp.concatenate(queries, 1)
        return
    outputs[0][rows:] = jnp.zeros((ROW_TILE, outputs[0].shape[1]), jnp.bfloat16)
    rest = jnp.concatenate([stats, jnp.zeros((ROW_TILE - STAT_ROWS, rows), jnp.float32)], 0)
    for part in range(3):
        rounded = rest.astype(jnp.bfloat16)
        outputs[0][rows:, part * rows : (part + 1) * rows] = rounded
        rest = rest - rounded.astype(jnp.float32)


def attend(
    pieces, gain, w_query, tables, wide_keys, wide_values, mark, own, row_at, rows, table_at,
    earlier,
):
    counts = [len(blocks) for blocks in pieces]
    flat = [block for blocks in pieces for block in blocks]
    out_width = w_query.shape[1]
    slots = wide_keys.shape[1]
    if own:
        out_shape = [
            jax.ShapeDtypeStruct((rows, out_width), jnp.float32),
            jax.ShapeDtypeStruct((STAT_ROWS, rows), jnp.float32),
            jax.ShapeDtypeStruct((rows, out_width), jnp.bfloat16),
        ]
    else:
        out_shape = [jax.ShapeDtypeStruct((rows + ROW_TILE, out_width), jnp.bfloat16)]
    return call(
        functools.partial(attend_kernel, counts, own, row_at, rows, table_at),
        out_shape,
        [*flat, gain, w_query, *tables, wide_keys, wide_values, mark],
        28,
        2 * rows * out_width * (w_query.shape[0] + 4 * slots),
        rows * out_width // HD * slots,
        "attend_own" if own else "attend_partner",
        earlier,
    )


def fresh_kernel(counts, table_at, *refs):
    blocks, refs = split_refs(counts, refs)
    gain, w_key, w_value, cosine, sine, new_keys, new_values = refs
    rows = new_keys.shape[0]
    pieces = [whole_of(one) for one in blocks]
    keys, values = project_normed(pieces, gain, [w_key, w_value])
    cosine = cosine[table_at : table_at + rows]
    sine = sine[table_at : table_at + rows]
    for head in range(keys.shape[1] // HD):
        own = slice(head * HD, (head + 1) * HD)
        new_keys[:, own] = rotate(keys[:, own], cosine, sine).astype(jnp.bfloat16)
    new_values[...] = values.astype(jnp.bfloat16)


def fresh(pieces, gain, w_key, w_value, tables, table_at, earlier):
    flat = [block for blocks in pieces for block in blocks]
    rows = sum(block.shape[0] for block in pieces[0])
    shape = jax.ShapeDtypeStruct((rows, w_key.shape[1]), jnp.bfloat16)
    return call(
        functools.partial(fresh_kernel, [len(blocks) for blocks in pieces], table_at),
        [shape, shape],
        [*flat, gain, w_key, w_value, *tables],
        20,
        4 * rows * w_key.size,
        0,
        "fresh_kv",
        earlier,
    )


def write_rows(target, fresh_rows, first):
    rows = fresh_rows.shape[0]
    slab_rows = target.shape[0]
    span = rows + ROW_TILE
    start = jnp.clip(first, 0, slab_rows - span)
    start = start - lax.rem(start, ROW_TILE)
    window = pl.ds(pl.multiple_of(start, ROW_TILE), span)
    shift = start - first
    place = lax.broadcasted_iota(jnp.int32, (span, rows), 0) + shift
    chosen = place == lax.broadcasted_iota(jnp.int32, (span, rows), 1)
    moved = dot(chosen.astype(jnp.bfloat16), fresh_rows)
    row = lax.broadcasted_iota(jnp.int32, (span, target.shape[1]), 0) + shift
    inside = (row >= 0) & (row < rows)
    old = target[window, :].astype(jnp.float32)
    target[window, :] = jnp.where(inside, moved, old).astype(jnp.bfloat16)


def attend_fresh_kernel(groups, requests, *refs):
    query_refs, refs = refs[:CHUNKS], refs[CHUNKS:]
    key_refs, value_refs, refs = refs[:groups], refs[groups : 2 * groups], refs[2 * groups :]
    partial, stats = refs
    position_in = place_of(requests)[1]
    rows, width = partial.shape
    kv_heads = key_refs[0].shape[1] // HD
    repeat = width // HD // kv_heads
    queries = whole_of(query_refs)
    token = lax.broadcasted_iota(jnp.int32, (rows, rows), 0)
    within = lax.broadcasted_iota(jnp.int32, (rows, rows), 1)
    causal = jnp.where(within <= token, 0.0, neg_large)
    causal = jnp.concatenate([causal] * repeat, 0)
    lane = lax.broadcasted_iota(jnp.int32, (rows, LANES), 1)
    ones = jnp.where(lane == 0, 1.0, 0.0).astype(jnp.bfloat16)
    hidden = [jnp.zeros((rows, LANES), jnp.bfloat16)]
    for turn in range(1, groups):
        later = source_of(position_in, turn, groups) > position_in
        hidden.append(jnp.where((lane == 0) & later, neg_large, 0.0).astype(jnp.bfloat16))
    columns = []
    for head in range(kv_heads):
        own = [
            slice((head * repeat + turn) * HD, (head * repeat + turn + 1) * HD)
            for turn in range(repeat)
        ]
        shared = slice(head * HD, (head + 1) * HD)
        stacked = jnp.concatenate([queries[:, one] for one in own], 0)
        stacked = jnp.concatenate([stacked, jnp.concatenate([ones] * repeat, 0)], 1)
        scores = [
            dot_transposed(stacked, jnp.concatenate([ref[:, shared], bias], 1))
            for ref, bias in zip(key_refs, hidden)
        ]
        scores = jnp.concatenate([scores[0] + causal] + scores[1:], 1)
        largest = jnp.max(scores, -1, keepdims=True)
        weights = jnp.exp2(scores - largest).astype(jnp.bfloat16)
        wide_values = [jnp.concatenate([ref[:, shared], ones], 1) for ref in value_refs]
        summed = dot(weights, jnp.concatenate(wide_values, 0))
        denominator = summed[:, HD : HD + 1]
        result = summed[:, :HD] / denominator
        logs = largest + jnp.log2(denominator)
        for turn, one in enumerate(own):
            part = slice(turn * rows, (turn + 1) * rows)
            partial[:, one] = result[part]
            columns.append(logs[part])
    stats[...] = stat_rows(columns, rows)


def attend_fresh(requests, queries, new_keys, new_values):
    groups = len(new_keys)
    rows = new_keys[0].shape[0]
    width = queries[0].shape[1]
    return call(
        functools.partial(attend_fresh_kernel, groups, requests),
        [
            jax.ShapeDtypeStruct((rows, width), jnp.float32),
            jax.ShapeDtypeStruct((STAT_ROWS, rows), jnp.float32),
        ],
        [*queries, *new_keys, *new_values],
        24,
        4 * rows * width * rows * groups,
        rows * width // HD * rows * groups,
        "attend_fresh",
    )


def update_kernel(groups, *refs):
    key_refs, value_refs, refs = refs[:groups], refs[groups : 2 * groups], refs[2 * groups :]
    keys, values, lengths_in, keys_updated, values_updated, done, lengths, semaphore = refs
    number = pltpu.make_async_copy(lengths_in, lengths, semaphore)
    number.start()
    keys_updated[...] = keys[...]
    values_updated[...] = values[...]
    done[...] = jnp.zeros(done.shape, done.dtype)
    number.wait()
    request, position_in = place_of(lengths.shape[0])
    rows = key_refs[0].shape[0]
    for turn in range(groups):
        source = source_of(position_in, turn, groups)
        first = lengths[request] + source * rows - position_in * keys.shape[0]
        write_rows(keys_updated, key_refs[turn][...], first)
        write_rows(values_updated, value_refs[turn][...], first)


def update(lengths, new_keys, new_values, keys, values, earlier):
    groups = len(new_keys)
    slab = jax.ShapeDtypeStruct(keys.shape, keys.dtype)
    return call(
        functools.partial(update_kernel, groups),
        [slab, slab, jax.ShapeDtypeStruct((STAT_ROWS, LANES), jnp.float32)],
        [*new_keys, *new_values, keys, values, lengths],
        20,
        4 * new_keys[0].size * new_keys[0].shape[0] * groups,
        0,
        "update_caches",
        earlier,
        [pltpu.SMEM(lengths.shape, lengths.dtype), pltpu.SemaphoreType.DMA],
    )


def combine_kernel(row_at, own_partial, own_stats, fresh_partial, fresh_stats, *refs):
    heads = lax.axis_size("head")
    chips = heads // CORES
    outputs = 2 * chips - 1
    received = refs[: -1 - outputs]
    w_out, merged_rows = refs[-1 - outputs], refs[-outputs]
    far = refs[1 - outputs :]
    width = own_partial.shape[1]
    rows = merged_rows.shape[0]
    part = slice(row_at, row_at + rows)
    padding = jnp.zeros((LANES - STAT_ROWS, rows), jnp.float32)
    stats = [own_stats[...], fresh_stats[:, part]]
    for ref in received:
        stats.append(
            sum(
                ref[rows:, turn * rows : (turn + 1) * rows].astype(jnp.float32)
                for turn in range(3)
            )[:STAT_ROWS]
        )
    logs = [jnp.concatenate([stat, padding], 0).T for stat in stats]
    largest = functools.reduce(jnp.maximum, logs)
    shares = [jnp.exp2(log - largest) for log in logs]
    total = functools.reduce(jnp.add, shares)
    shares = [share / total for share in shares]
    attended = []
    for head in range(width // HD):
        own = slice(head * HD, (head + 1) * HD)
        column = slice(head, head + 1)
        merged = own_partial[:, own] * shares[0][:, column]
        merged = merged + fresh_partial[part, own] * shares[1][:, column]
        for ref, share in zip(received, shares[2:]):
            merged = merged + ref[:rows, own].astype(jnp.float32) * share[:, column]
        attended.append(merged.astype(jnp.bfloat16))
    attended = jnp.concatenate(attended, 1)
    merged_rows[...] = attended
    for ahead in range(1, chips):
        result = block_product(attended, w_out, ahead, 1)
        middle = result.shape[1] // 2
        far[2 * ahead - 2][...] = result[:, :middle]
        far[2 * ahead - 1][...] = result[:, middle:]


def block_product(attended, w_out, ahead, flip):
    heads = lax.axis_size("head")
    block_width = w_out.shape[1] // heads
    block = lax.rem(lax.axis_index("head") + CORES * ahead, heads) ^ flip
    along = pl.ds(pl.multiple_of(block * block_width, LANES), block_width)
    return dot(attended, w_out[:, along]).astype(jnp.bfloat16)


def project_kernel(merged_rows, w_out, far, *near):
    attended = merged_rows[...]
    far[...] = block_product(attended, w_out, 0, 1)
    for ahead, target in enumerate(near):
        target[...] = block_product(attended, w_out, ahead, 0)


def combine(row_at, rows, own, fresh_part, received, w_out, heads, earlier):
    chips = heads // CORES
    width = w_out.shape[1] // heads
    merged = jax.ShapeDtypeStruct((rows, own[0].shape[1]), jnp.bfloat16)
    half = jax.ShapeDtypeStruct((rows, width // 2), jnp.bfloat16)
    merged, *far = call(
        functools.partial(combine_kernel, row_at),
        [merged] + [half] * (2 * chips - 2),
        [*own, *fresh_part, *received, w_out],
        20,
        rows * w_out.size,
        0,
        "combine",
        earlier,
    )
    return merged, [far[2 * k : 2 * k + 2] for k in range(chips - 1)]


def project(merged, w_out, heads):
    block = jax.ShapeDtypeStruct((merged.shape[0], w_out.shape[1] // heads), jnp.bfloat16)
    far, *near = call(
        project_kernel,
        [block] * (1 + heads // CORES),
        [merged, w_out],
        20,
        2 * merged.shape[0] * w_out.size,
        0,
        "project",
    )
    return far, near


def sum_kernel(count, *refs):
    total = refs[0][...].astype(jnp.float32)
    total = total + jnp.concatenate([ref[...] for ref in refs[1:count]], 1).astype(jnp.float32)
    refs[count][...] = total.astype(jnp.bfloat16)


def sum_cores(near, far, earlier):
    return call(
        functools.partial(sum_kernel, 1 + len(far)),
        [jax.ShapeDtypeStruct(near.shape, near.dtype)],
        [near, *far],
        8,
        near.size,
        0,
        "sum_cores",
        earlier,
    )[0]


def finish_kernel(*refs):
    *parts, result = refs
    count = len(parts) // CHUNKS
    rows = parts[0].shape[0]
    for chunk in range(CHUNKS):
        total = 0.0
        for ref in parts[chunk * count : (chunk + 1) * count]:
            total = total + ref[...].astype(jnp.float32)
        result[chunk * rows : (chunk + 1) * rows] = total.astype(jnp.bfloat16)


def finish(parts, earlier):
    rows, width = parts[0].shape
    shape = jax.ShapeDtypeStruct((CHUNKS * rows, width), jnp.bfloat16)
    flops = CHUNKS * rows * width
    return call(finish_kernel, [shape], parts, 8, flops, 0, "finish", earlier)[0]


def shards(
    tokens,
    norm_gain,
    w_query,
    w_key,
    w_value,
    w_out,
    keys_cache,
    values_cache,
    cached_lengths,
    rope_offsets,
):
    rows, width = tokens.shape
    requests = cached_lengths.shape[0]
    groups = lax.axis_size("seq") // requests
    heads = lax.axis_size("head")
    chips = heads // CORES
    chunk_rows = rows // CHUNKS
    gain = norm_gain.reshape(heads, 1, width)

    early = tokens[:chunk_rows]
    mark = marks(keys_cache.shape[0])
    tables = rope_tables(cached_lengths, rope_offsets, groups, rows, [mark])
    wide_keys, wide_values = widen(keys_cache, values_cache, mark, cached_lengths, tables[:1])

    def attend_rows(pieces, own, chunk, turn, earlier):
        at = chunk * chunk_rows
        return attend(
            pieces, gain, w_query, tables, wide_keys, wide_values, mark, own, at if own else 0,
            chunk_rows, turn * rows + at, earlier,
        )

    half = chunk_rows // 2
    first = [shifted(early, "seq", turn * requests) for turn in range(1, groups)]
    from_chips = other_chips(tokens)
    (late,) = relay([tokens[chunk_rows:]], [rows - chunk_rows], from_chips + [wide_keys])
    second = [shifted(late, "seq", turn * requests) for turn in range(1, groups)]
    own_cuts = [relay([piece], [rows, half, half, rows - chunk_rows], [late]) for piece in from_chips]
    own_pieces = [[tokens]] + [[cut[0]] for cut in own_cuts] + [[other_core(tokens)]]
    own_pieces += [[other_core(block) for block in cut[1:]] for cut in own_cuts]
    own_early = [
        blocks if len(blocks) == 1 else blocks[: len(blocks) - 1] for blocks in own_pieces
    ]
    *own_part, queries = attend_rows(own_early, True, 0, 0, [cut[0] for cut in own_cuts])
    own_queries = [queries]

    earlier = [queries]
    first = [relay([piece], [chunk_rows], earlier)[0] for piece in first]
    first_from_chips = [other_chips(piece) for piece in first]
    *late_part, queries = attend_rows(own_pieces, True, 1, 0, first)
    own_part += late_part
    own_queries.append(queries)
    earlier = [queries]
    second = [relay([piece], [rows - chunk_rows], earlier)[0] for piece in second]
    second_from_chips = [other_chips(piece) for piece in second]
    earlier = second

    def gather_cores(piece, from_chips, earlier):
        passed = [relay([one], [one.shape[0]], earlier)[0] for one in from_chips]
        along = [piece] + passed
        return along + [other_core(one) for one in along], passed

    gathered = []
    for piece, from_chips in zip(first, first_from_chips):
        along, passed = gather_cores(piece, from_chips, earlier)
        gathered.append([along])
        earlier = earlier + passed
    new_rows = [fresh(own_pieces, gain, w_key, w_value, tables, 0, earlier)]
    earlier = [new_rows[0][0]]
    received = [[] for _ in range(CHUNKS)]
    for turn in range(1, groups):
        pieces = [[block] for block in gathered[turn - 1][0]]
        (packed,) = attend_rows(pieces, False, 0, turn, earlier)
        received[0].append(shifted(packed, "seq", -turn * requests))
        earlier = [packed]
    for blocks, piece, from_chips in zip(gathered, second, second_from_chips):
        along, passed = gather_cores(piece, from_chips, earlier)
        blocks.append(along)
        earlier = earlier + passed
    for turn in range(1, groups):
        pieces = [[block] for block in gathered[turn - 1][1]]
        (packed,) = attend_rows(pieces, False, 1, turn, earlier)
        received[1].append(shifted(packed, "seq", -turn * requests))
        earlier = [packed]
    for turn in range(1, groups):
        pieces = [list(blocks) for blocks in zip(*gathered[turn - 1])]
        new_rows.append(fresh(pieces, gain, w_key, w_value, tables, turn * rows, earlier))
    new_keys, new_values = zip(*new_rows)
    fresh_part = attend_fresh(requests, own_queries, new_keys, new_values)

    parts = []
    earlier = before_sums = []
    for chunk in range(CHUNKS):
        merged, fars = combine(
            chunk * chunk_rows, chunk_rows, own_part[2 * chunk : 2 * chunk + 2], fresh_part,
            received[chunk], w_out, heads, earlier,
        )
        fars = [[other_core(part) for part in far] for far in fars]
        far, near = project(merged, w_out, heads)
        earlier = [far] + before_sums
        sums = [sum_cores(one, parts_far, earlier) for one, parts_far in zip(near[1:], fars)]
        from_chips = [shifted(one, "head", CORES * k) for k, one in enumerate(sums, 1)]
        parts += [near[0], other_core(far), *from_chips]
        earlier, before_sums = sums, from_chips
    keys_updated, values_updated, done = update(
        cached_lengths, new_keys, new_values, keys_cache, values_cache, earlier
    )
    return (finish(parts, [done]), keys_updated, values_updated)


def solution(mesh):
    return jax.shard_map(
        shards,
        mesh=mesh,
        in_specs=(
            P("seq", "head"),
            P(),
            P(None, "head"),
            P(None, "head"),
            P(None, "head"),
            P("head", None),
            P("seq", "head"),
            P("seq", "head"),
            P(),
            P(),
        ),
        out_specs=(P("seq", "head"), P("seq", "head"), P("seq", "head")),
        check_vma=False,
    )
```

```python
import functools
import math

import jax
import jax.numpy as jnp
from jax import lax
from jax.experimental import pallas as pl
from jax.experimental.pallas import tpu as pltpu
from jax.sharding import PartitionSpec as P

HD = 128
LANES = 128
STAT_ROWS = 8
ROW_TILE = 16
CORES = 2
CHUNK_UNITS = (5, 5, 6)
FAR_PIECES = 3
COST_WEIGHT = 0.0005
FIRST_MICROS = 2
FLOPS_PER_MICRO = 1_000_000_000
MIB = 1 << 20

rope_base = 500000.0
neg_large = -1e30
log2_scale = math.log2(math.e) / math.sqrt(HD)

VMEM = pl.BlockSpec(memory_space=pltpu.VMEM)
ANY = pl.BlockSpec(memory_space=pl.ANY)


def shifted(shard, axis, by):
    devices = lax.axis_size(axis)
    return lax.ppermute(shard, axis, [(i, (i + by) % devices) for i in range(devices)])


def other_core(shard):
    devices = lax.axis_size("head")
    return lax.ppermute(shard, "head", [(i, i ^ 1) for i in range(devices)])


def other_chips(own):
    chips = lax.axis_size("head") // CORES
    return [shifted(own, "head", CORES * k) for k in range(1, chips)]


def place_of(requests):
    member = lax.axis_index("seq")
    return lax.rem(member, requests), lax.div(member, requests)


def source_of(position_in, turn, groups):
    return lax.rem(position_in + (groups - turn), groups)


def dot(left, right):
    return jnp.dot(left, right, preferred_element_type=jnp.float32)


def dot_transposed(left, right):
    return lax.dot_general(
        left, right, (((1,), (1,)), ((), ())), preferred_element_type=jnp.float32
    )


def call(
    kernel, out_shape, arrays, limit, flops, transcendentals, name, earlier=(),
    scratch=(), micros=0,
):
    moved = sum(a.size * a.dtype.itemsize for a in arrays)
    moved += sum(math.prod(s.shape) * s.dtype.itemsize for s in out_shape)
    read = len(arrays)
    skipped = len(earlier)

    def body(*refs):
        kernel(*refs[:read], *refs[read + skipped :])

    return pl.pallas_call(
        body,
        out_shape=out_shape,
        in_specs=[VMEM] * len(arrays) + [ANY] * skipped,
        out_specs=[VMEM] * len(out_shape),
        scratch_shapes=scratch,
        compiler_params=pltpu.CompilerParams(vmem_limit_bytes=limit * MIB),
        cost_estimate=pl.CostEstimate(
            flops=max(int(COST_WEIGHT * flops), int(micros * FLOPS_PER_MICRO)),
            bytes_accessed=int(COST_WEIGHT * moved),
            transcendentals=int(COST_WEIGHT * transcendentals),
        ),
        name=name,
    )(*arrays, *earlier)


def whole_of(blocks):
    parts = [block[...] for block in blocks]
    return jnp.concatenate(parts, 0) if len(parts) > 1 else parts[0]


def relay_kernel(count, *refs):
    whole = whole_of(refs[:count])
    at = 0
    for ref in refs[count:]:
        ref[...] = whole[at : at + ref.shape[0]]
        at = (at + ref.shape[0]) % whole.shape[0]


def relay(blocks, sizes, earlier):
    shapes = [jax.ShapeDtypeStruct((size, *blocks[0].shape[1:]), blocks[0].dtype) for size in sizes]
    kernel = functools.partial(relay_kernel, len(blocks))
    return call(kernel, shapes, [*blocks], 4, 0, 0, "relay", earlier)


def mark_kernel(mark):
    lane = lax.broadcasted_iota(jnp.int32, mark.shape, 1)
    mark[...] = jnp.where(lane == 0, 1.0, 0.0).astype(mark.dtype)


def marks(rows):
    shape = jax.ShapeDtypeStruct((rows, LANES), jnp.bfloat16)
    return call(mark_kernel, [shape], [], 4, 0, 0, "marks", micros=FIRST_MICROS)[0]


def tables_kernel(groups, lengths_in, offsets_in, cosine, sine, *scratch):
    lengths, offsets, semaphores = scratch
    numbers = [
        pltpu.make_async_copy(lengths_in, lengths, semaphores.at[0]),
        pltpu.make_async_copy(offsets_in, offsets, semaphores.at[1]),
    ]
    for copy in numbers:
        copy.start()
    rows = cosine.shape[0] // groups
    for copy in numbers:
        copy.wait()
    request, position_in = place_of(lengths.shape[0])
    lane = lax.broadcasted_iota(jnp.int32, (rows, LANES), 1)
    row = lax.broadcasted_iota(jnp.int32, (rows, LANES), 0)
    half = lax.rem(lane, HD // 2).astype(jnp.float32)
    frequency = jnp.exp2(half * (-2.0 / HD * math.log2(rope_base)))
    sign = jnp.where(lane < HD // 2, -1.0, 1.0)
    for turn in range(groups):
        first = source_of(position_in, turn, groups) * rows
        first = first + offsets[request] + lengths[request]
        angles = (row + first).astype(jnp.float32) * frequency
        part = slice(turn * rows, (turn + 1) * rows)
        cosine[part] = jnp.cos(angles)
        sine[part] = jnp.sin(angles) * sign


def rope_tables(lengths, offsets, groups, rows, earlier):
    table = jax.ShapeDtypeStruct((groups * rows, LANES), jnp.float32)
    return call(
        functools.partial(tables_kernel, groups),
        [table, table],
        [lengths, offsets],
        12,
        0,
        0,
        "rope_tables",
        earlier,
        [
            pltpu.SMEM(lengths.shape, lengths.dtype),
            pltpu.SMEM(offsets.shape, offsets.dtype),
            pltpu.SemaphoreType.DMA((2,)),
        ],
    )


def widen_kernel(keys, values, mark, lengths_in, wide_keys, wide_values, lengths, semaphore):
    number = pltpu.make_async_copy(lengths_in, lengths, semaphore)
    number.start()
    slots = keys.shape[0]
    heads = keys.shape[1] // HD
    for head in range(heads):
        own = slice(head * HD, (head + 1) * HD)
        wide_keys[head, :, :HD] = keys[:, own]
        wide_values[head, :, :HD] = values[:, own]
        wide_values[head, :, HD:] = mark[:slots]
    number.wait()
    request, position_in = place_of(lengths.shape[0])
    slot = lax.broadcasted_iota(jnp.int32, (slots, LANES), 0) + position_in * slots
    lane = lax.broadcasted_iota(jnp.int32, (slots, LANES), 1)
    bias = jnp.where((lane == 0) & (slot >= lengths[request]), neg_large, 0.0).astype(jnp.bfloat16)
    for head in range(heads):
        wide_keys[head, :, HD:] = bias


def widen(keys, values, mark, lengths, earlier):
    slots, width = keys.shape
    wide = jax.ShapeDtypeStruct((width // HD, slots, HD + LANES), jnp.bfloat16)
    return call(
        widen_kernel,
        [wide, wide],
        [keys, values, mark, lengths],
        12,
        0,
        0,
        "widen_caches",
        earlier,
        [pltpu.SMEM(lengths.shape, lengths.dtype), pltpu.SemaphoreType.DMA],
    )


def rotate(vectors, cosine, sine):
    return vectors * cosine + pltpu.roll(vectors, HD // 2, 1) * sine


def project_normed(pieces, gain, weights):
    heads = gain.shape[0]
    width = gain.shape[2]
    me = lax.axis_index("head")
    squares = 0.0
    sums = [0.0] * len(weights)
    for index, piece in enumerate(pieces):
        owner = lax.rem(me + (heads - CORES * (index % (heads // CORES))), heads)
        if index >= heads // CORES:
            owner = owner ^ 1
        wide = piece.astype(jnp.float32)
        scaled = (wide * gain[owner]).astype(jnp.bfloat16)
        along = pl.ds(pl.multiple_of(owner * width, LANES), width)
        for place, weight in enumerate(weights):
            sums[place] = sums[place] + dot(scaled, weight[along, :])
        squares = squares + jnp.sum(wide * wide, -1, keepdims=True)
    factor = lax.rsqrt(squares / (heads * width) + 1e-05)
    return [total * factor for total in sums]


def stat_rows(columns, rows):
    padded = -(-rows // LANES) * LANES
    lane = lax.broadcasted_iota(jnp.int32, (padded, LANES), 1)
    table = jnp.zeros((padded, LANES), jnp.float32)
    for index, column in enumerate(columns):
        if padded > rows:
            filler = jnp.zeros((padded - rows, 1), jnp.float32)
            column = jnp.concatenate([column, filler], 0)
        table = jnp.where(lane == index, column, table)
    return table.T[:STAT_ROWS]


def stat_columns(stats):
    padding = jnp.zeros((LANES - STAT_ROWS, stats.shape[1]), jnp.float32)
    return jnp.concatenate([stats, padding], 0).T


def stat_places(count, width):
    places = []
    for index in range(3 * count):
        row, lane = divmod(index * LANES, width)
        places.append((row * ROW_TILE, lane))
    return [places[3 * chunk : 3 * chunk + 3] for chunk in range(count)]


def tail_rows(count, width):
    return -(-3 * count * LANES // width) * ROW_TILE if count else 0


def split_refs(counts, refs):
    parts = []
    for count in counts:
        parts.append(refs[:count])
        refs = refs[count:]
    return parts, refs


def head_queries(product, cosine, sine):
    return [
        (rotate(product[:, at : at + HD], cosine, sine) * log2_scale).astype(jnp.bfloat16)
        for at in range(0, product.shape[1], HD)
    ]


def stack_heads(queries, head, repeat, at, rows):
    own = queries[head * repeat : (head + 1) * repeat]
    return jnp.concatenate([query[at : at + rows] for query in own], 0)


def weigh(scores, values):
    largest = functools.reduce(
        jnp.maximum, [jnp.max(score, -1, keepdims=True) for score in scores]
    )
    summed = 0.0
    for score, value in zip(scores, values):
        weights = jnp.exp2(score - largest).astype(jnp.bfloat16)
        summed = summed + dot(weights, value)
    denominator = summed[:, HD : HD + 1]
    return summed[:, :HD] / denominator, largest + jnp.log2(denominator)


def attend_kernel(counts, sent, table_at, *refs):
    *blocks, weights, old_stats = split_refs([*counts, 7, max(sent - 1, 0)], refs)[0]
    outputs = refs[sum(counts) + 7 + max(sent - 1, 0) :]
    gain, w_query, cosine, sine, wide_keys, wide_values, mark = weights
    pieces = [whole_of(one) for one in blocks]
    rows = pieces[0].shape[0]
    (product,) = project_normed(pieces, gain, [w_query])
    part = slice(table_at, table_at + rows)
    queries = head_queries(product, cosine[part], sine[part])
    kv_heads = wide_keys.shape[0]
    repeat = len(queries) // kv_heads
    ones = mark[: repeat * rows]
    scores = []
    for head in range(kv_heads):
        stacked = jnp.concatenate([stack_heads(queries, head, repeat, 0, rows), ones], 1)
        scores.append(dot_transposed(stacked, wide_keys[head]))
    columns = []
    for head in range(kv_heads):
        result, logs = weigh([scores[head]], [wide_values[head]])
        for turn in range(repeat):
            at = (head * repeat + turn) * HD
            outputs[0][:rows, at : at + HD] = result[turn * rows : (turn + 1) * rows].astype(
                jnp.bfloat16
            )
            columns.append(logs[turn * rows : (turn + 1) * rows])
    stats = stat_rows(columns, rows)
    if not sent:
        outputs[1][...] = stats
        return
    packed = outputs[0]
    packed[rows:] = jnp.zeros((packed.shape[0] - rows, packed.shape[1]), jnp.bfloat16)
    padding = jnp.zeros((ROW_TILE - STAT_ROWS, LANES), jnp.float32)
    places = stat_places(sent, packed.shape[1])
    for rest, parts in zip([ref[...] for ref in old_stats] + [stats], places):
        rest = jnp.concatenate([rest, padding], 0)
        for row, lane in parts:
            rounded = rest.astype(jnp.bfloat16)
            packed[rows + row : rows + row + ROW_TILE, lane : lane + LANES] = rounded
            rest = rest - rounded.astype(jnp.float32)


def attend(
    pieces, gain, w_query, tables, wide_keys, wide_values, mark, table_at, sent, old_stats, earlier
):
    counts = [len(blocks) for blocks in pieces]
    flat = [block for blocks in pieces for block in blocks]
    rows = sum(block.shape[0] for block in pieces[0])
    out_width = w_query.shape[1]
    slots = wide_keys.shape[1]
    total = rows + tail_rows(sent, out_width)
    out_shape = [jax.ShapeDtypeStruct((total, out_width), jnp.bfloat16)]
    if not sent:
        out_shape.append(jax.ShapeDtypeStruct((STAT_ROWS, LANES), jnp.float32))
    return call(
        functools.partial(attend_kernel, counts, sent, table_at),
        out_shape,
        [*flat, gain, w_query, *tables, wide_keys, wide_values, mark, *old_stats],
        28,
        2 * rows * out_width * (w_query.shape[0] + 4 * slots),
        rows * out_width // HD * slots,
        "attend_partner",
        earlier,
    )


def attend_own_kernel(requests, counts, others, *refs):
    parts, outputs = split_refs([*counts, 9, others, others], refs)
    *blocks, weights, other_keys, other_values = parts
    pieces = [whole_of(one) for one in blocks]
    gain, w_query, w_key, w_value, cosine, sine, wide_keys, wide_values, mark = weights
    partial, stats, new_keys, new_values = outputs
    rows = pieces[0].shape[0]
    groups = others + 1
    query_sum, key_sum, value_sum = project_normed(pieces, gain, [w_query, w_key, w_value])
    cosine, sine = cosine[:rows], sine[:rows]
    queries = head_queries(query_sum, cosine, sine)
    kv_heads = wide_keys.shape[0]
    repeat = len(queries) // kv_heads
    own_keys = []
    for head in range(kv_heads):
        shared = slice(head * HD, (head + 1) * HD)
        own_keys.append(rotate(key_sum[:, shared], cosine, sine).astype(jnp.bfloat16))
        new_keys[:, shared] = own_keys[head]
    own_values = value_sum.astype(jnp.bfloat16)
    new_values[...] = own_values
    ones = mark[:rows]
    position_in = place_of(requests)[1]
    hidden = []
    for turn in range(1, groups):
        later = source_of(position_in, turn, groups) > position_in
        hidden.append(jnp.where(later, ones.astype(jnp.float32) * neg_large, 0.0).astype(jnp.bfloat16))
    fresh_keys = []
    fresh_values = []
    for head in range(kv_heads):
        shared = slice(head * HD, (head + 1) * HD)
        wide = [jnp.concatenate([own_values[:, shared], ones], 1)]
        wide += [jnp.concatenate([ref[:, shared], ones], 1) for ref in other_values]
        fresh_values.append(wide)
        fresh_keys.append(
            [jnp.concatenate([ref[:, shared], bias], 1) for ref, bias in zip(other_keys, hidden)]
        )
    step = min(rows, LANES)
    tiles = [(head, at) for head in range(kv_heads) for at in range(0, rows, step)]
    marked = mark[: repeat * step]

    def scores_of(head, at):
        stacked = stack_heads(queries, head, repeat, at, step)
        token = lax.broadcasted_iota(jnp.int32, (step, rows), 0) + at
        within = lax.broadcasted_iota(jnp.int32, (step, rows), 1)
        causal = jnp.concatenate([jnp.where(within <= token, 0.0, neg_large)] * repeat, 0)
        fresh = dot_transposed(stacked, own_keys[head]) + causal
        stacked = jnp.concatenate([stacked, marked], 1)
        return [dot_transposed(stacked, wide_keys[head]), fresh] + [
            dot_transposed(stacked, keys) for keys in fresh_keys[head]
        ]

    columns = {}
    following = scores_of(*tiles[0])
    for index, (head, at) in enumerate(tiles):
        scores = following
        if index + 1 < len(tiles):
            following = scores_of(*tiles[index + 1])
        result, logs = weigh(scores, [wide_values[head]] + fresh_values[head])
        for turn in range(repeat):
            part = slice(turn * step, (turn + 1) * step)
            to = slice((head * repeat + turn) * HD, (head * repeat + turn + 1) * HD)
            partial[at : at + step, to] = result[part]
            columns.setdefault(head * repeat + turn, []).append(logs[part])
    stats[...] = stat_rows([jnp.concatenate(parts, 0) for parts in columns.values()], rows)


def attend_own(
    requests, pieces, gain, weights, tables, wide_keys, wide_values, mark, other_rows, earlier
):
    counts = [len(blocks) for blocks in pieces]
    flat = [block for blocks in pieces for block in blocks]
    rows = sum(block.shape[0] for block in pieces[0])
    out_width = weights[0].shape[1]
    slots = wide_keys.shape[1]
    new = jax.ShapeDtypeStruct((rows, weights[1].shape[1]), jnp.bfloat16)
    other_keys, other_values = zip(*other_rows)
    return call(
        functools.partial(attend_own_kernel, requests, counts, len(other_rows)),
        [
            jax.ShapeDtypeStruct((rows, out_width), jnp.float32),
            jax.ShapeDtypeStruct((STAT_ROWS, rows), jnp.float32),
            new,
            new,
        ],
        [
            *flat, gain, *weights, *tables, wide_keys, wide_values, mark, *other_keys,
            *other_values,
        ],
        28,
        2 * rows * out_width * (weights[0].shape[0] + 4 * slots),
        rows * out_width // HD * slots,
        "attend_own",
        earlier,
    )


def fresh_kernel(counts, table_at, *refs):
    blocks, refs = split_refs(counts, refs)
    gain, w_key, w_value, cosine, sine, new_keys, new_values = refs
    rows = new_keys.shape[0]
    pieces = [whole_of(one) for one in blocks]
    keys, values = project_normed(pieces, gain, [w_key, w_value])
    cosine = cosine[table_at : table_at + rows]
    sine = sine[table_at : table_at + rows]
    for head in range(keys.shape[1] // HD):
        own = slice(head * HD, (head + 1) * HD)
        new_keys[:, own] = rotate(keys[:, own], cosine, sine).astype(jnp.bfloat16)
    new_values[...] = values.astype(jnp.bfloat16)


def fresh(pieces, gain, w_key, w_value, tables, table_at, earlier):
    flat = [block for blocks in pieces for block in blocks]
    rows = sum(block.shape[0] for block in pieces[0])
    shape = jax.ShapeDtypeStruct((rows, w_key.shape[1]), jnp.bfloat16)
    return call(
        functools.partial(fresh_kernel, [len(blocks) for blocks in pieces], table_at),
        [shape, shape],
        [*flat, gain, w_key, w_value, *tables],
        20,
        4 * rows * w_key.size,
        0,
        "fresh_kv",
        earlier,
    )


def write_rows(target, fresh_rows, first):
    rows = fresh_rows.shape[0]
    slab_rows = target.shape[0]
    span = rows + ROW_TILE
    start = jnp.clip(first, 0, slab_rows - span)
    start = start - lax.rem(start, ROW_TILE)
    window = pl.ds(pl.multiple_of(start, ROW_TILE), span)
    shift = start - first
    place = lax.broadcasted_iota(jnp.int32, (span, rows), 0) + shift
    chosen = place == lax.broadcasted_iota(jnp.int32, (span, rows), 1)
    moved = dot(chosen.astype(jnp.bfloat16), fresh_rows)
    row = lax.broadcasted_iota(jnp.int32, (span, target.shape[1]), 0) + shift
    inside = (row >= 0) & (row < rows)
    old = target[window, :].astype(jnp.float32)
    target[window, :] = jnp.where(inside, moved, old).astype(jnp.bfloat16)


def update_kernel(groups, *refs):
    key_refs, value_refs, refs = refs[:groups], refs[groups : 2 * groups], refs[2 * groups :]
    keys, values, lengths_in, keys_updated, values_updated, done, lengths, semaphore = refs
    number = pltpu.make_async_copy(lengths_in, lengths, semaphore)
    number.start()
    keys_updated[...] = keys[...]
    values_updated[...] = values[...]
    done[...] = jnp.zeros(done.shape, done.dtype)
    number.wait()
    request, position_in = place_of(lengths.shape[0])
    rows = key_refs[0].shape[0]
    for turn in range(groups):
        source = source_of(position_in, turn, groups)
        first = lengths[request] + source * rows - position_in * keys.shape[0]
        write_rows(keys_updated, key_refs[turn][...], first)
        write_rows(values_updated, value_refs[turn][...], first)


def update(lengths, new_keys, new_values, keys, values, earlier):
    groups = len(new_keys)
    slab = jax.ShapeDtypeStruct(keys.shape, keys.dtype)
    return call(
        functools.partial(update_kernel, groups),
        [slab, slab, jax.ShapeDtypeStruct((STAT_ROWS, LANES), jnp.float32)],
        [*new_keys, *new_values, keys, values, lengths],
        20,
        4 * new_keys[0].size * new_keys[0].shape[0] * groups,
        0,
        "update_caches",
        earlier,
        [pltpu.SMEM(lengths.shape, lengths.dtype), pltpu.SemaphoreType.DMA],
    )


def combine_kernel(row_at, sizes, *refs):
    heads = lax.axis_size("head")
    chips = heads // CORES
    outputs = FAR_PIECES * (chips - 1)
    (own_partial, own_stats), refs = refs[:2], refs[2:]
    received = refs[: -2 - outputs]
    w_out, merged_rows, *far = refs[-2 - outputs :]
    width = own_partial.shape[1]
    rows = merged_rows.shape[0]
    part = slice(row_at, row_at + rows)
    logs = [stat_columns(own_stats[...])[part]]
    partials = [own_partial[part]]
    for turn in range(0, len(received), len(sizes)):
        chunks = received[turn : turn + len(sizes)]
        last = chunks[-1]
        columns = []
        for size, places in zip(sizes, stat_places(len(sizes), width)):
            stats = sum(
                last[sizes[-1] + row : sizes[-1] + row + ROW_TILE, lane : lane + LANES].astype(
                    jnp.float32
                )
                for row, lane in places
            )
            columns.append(stat_columns(stats[:STAT_ROWS])[:size])
        logs.append(jnp.concatenate(columns, 0))
        partials.append(jnp.concatenate([ref[:size] for ref, size in zip(chunks, sizes)], 0))
    largest = functools.reduce(jnp.maximum, logs)
    shares = [jnp.exp2(log - largest) for log in logs]
    total = functools.reduce(jnp.add, shares)
    shares = [share / total for share in shares]
    attended = []
    for head in range(width // HD):
        at = slice(head * HD, (head + 1) * HD)
        column = slice(head, head + 1)
        merged = 0.0
        for partial, share in zip(partials, shares):
            merged = merged + partial[:, at].astype(jnp.float32) * share[:, column]
        attended.append(merged.astype(jnp.bfloat16))
    attended = jnp.concatenate(attended, 1)
    merged_rows[...] = attended
    for ahead in range(1, chips):
        result = block_product(attended, w_out, ahead, 1)
        piece = result.shape[1] // FAR_PIECES
        for index in range(FAR_PIECES):
            target = far[FAR_PIECES * (ahead - 1) + index]
            target[...] = result[:, index * piece : (index + 1) * piece]


def block_product(attended, w_out, ahead, flip):
    heads = lax.axis_size("head")
    block_width = w_out.shape[1] // heads
    block = lax.rem(lax.axis_index("head") + CORES * ahead, heads) ^ flip
    along = pl.ds(pl.multiple_of(block * block_width, LANES), block_width)
    return dot(attended, w_out[:, along]).astype(jnp.bfloat16)


def project_kernel(merged_rows, w_out, far, *near):
    attended = merged_rows[...]
    far[...] = block_product(attended, w_out, 0, 1)
    for ahead, target in enumerate(near):
        target[...] = block_product(attended, w_out, ahead, 0)


def combine(row_at, sizes, own, received, w_out, heads, earlier):
    rows = sum(sizes)
    chips = heads // CORES
    width = w_out.shape[1] // heads
    merged = jax.ShapeDtypeStruct((rows, own[0].shape[1]), jnp.bfloat16)
    piece = jax.ShapeDtypeStruct((rows, width // FAR_PIECES), jnp.bfloat16)
    merged, *far = call(
        functools.partial(combine_kernel, row_at, sizes),
        [merged] + [piece] * (FAR_PIECES * (chips - 1)),
        [*own, *received, w_out],
        20,
        rows * w_out.size,
        0,
        "combine",
        earlier,
    )
    return merged, [far[k * FAR_PIECES : (k + 1) * FAR_PIECES] for k in range(chips - 1)]


def project(merged, w_out, heads):
    block = jax.ShapeDtypeStruct((merged.shape[0], w_out.shape[1] // heads), jnp.bfloat16)
    far, *near = call(
        project_kernel,
        [block] * (1 + heads // CORES),
        [merged, w_out],
        20,
        2 * merged.shape[0] * w_out.size,
        0,
        "project",
    )
    return far, near


def sum_kernel(near, *refs):
    *far, result = refs
    total = jnp.concatenate([ref[...] for ref in far], 1).astype(jnp.float32)
    result[...] = (near[...].astype(jnp.float32) + total).astype(result.dtype)


def sum_cores(near, far, earlier):
    shape = jax.ShapeDtypeStruct(near.shape, near.dtype)
    return call(sum_kernel, [shape], [near, *far], 8, near.size, 0, "sum_cores", earlier)[0]


def finish_kernel(counts, *refs):
    groups, (result,) = split_refs(counts, refs)
    at = 0
    for group in groups:
        rows = group[0].shape[0]
        total = sum(ref[...].astype(jnp.float32) for ref in group)
        result[at : at + rows] = total.astype(result.dtype)
        at += rows


def finish(groups, earlier):
    parts = [part for group in groups for part in group]
    rows = sum(group[0].shape[0] for group in groups)
    shape = jax.ShapeDtypeStruct((rows, parts[0].shape[1]), jnp.bfloat16)
    kernel = functools.partial(finish_kernel, [len(group) for group in groups])
    return call(kernel, [shape], parts, 8, 0, 0, "finish", earlier)[0]


def shards(
    tokens,
    norm_gain,
    w_query,
    w_key,
    w_value,
    w_out,
    keys_cache,
    values_cache,
    cached_lengths,
    rope_offsets,
):
    rows, width = tokens.shape
    requests = cached_lengths.shape[0]
    groups = lax.axis_size("seq") // requests
    heads = lax.axis_size("head")
    chips = heads // CORES
    gain = norm_gain.reshape(heads, 1, width)
    sizes = [rows * units // sum(CHUNK_UNITS) for units in CHUNK_UNITS]
    starts = [sum(sizes[:chunk]) for chunk in range(len(sizes))]
    cuts = [tokens[at : at + size] for at, size in zip(starts, sizes)]

    mark = marks(keys_cache.shape[0])
    tables = rope_tables(cached_lengths, rope_offsets, groups, rows, [mark])
    wide_keys, wide_values = widen(keys_cache, values_cache, mark, cached_lengths, tables[:1])

    def send_tokens(piece):
        return [shifted(piece, "seq", turn * requests) for turn in range(1, groups)]

    from_chips = other_chips(tokens)
    arrived = [send_tokens(cuts[0])]
    earlier = [wide_keys]
    (late,) = relay([cuts[1]], sizes[1:2], earlier)
    arrived.append(send_tokens(late))
    own_crossed = other_core(tokens)
    earlier = [late, own_crossed]

    def to_chips(chunk, earlier):
        passed = [relay([piece], sizes[chunk : chunk + 1], earlier)[0] for piece in arrived[chunk]]
        sent = [(piece, other_chips(piece), other_core(piece)) for piece in passed]
        return sent, passed

    def to_cores(chunk, sent, earlier):
        gathered = []
        size = sizes[chunk]
        for own, others, crossed in sent:
            passed = [relay([one], [size, size // 2, size // 2], earlier + [crossed]) for one in others]
            gathered.append(
                [[own]] + [[one[0]] for one in passed] + [[crossed]]
                + [[other_core(part) for part in one[1:]] for one in passed]
            )
            earlier = [one[0] for one in passed]
        return gathered, earlier

    sent_1, earlier = to_chips(0, earlier)
    (late,) = relay([cuts[2]], sizes[2:], from_chips + earlier)
    arrived.append(send_tokens(late))
    sent_2, earlier = to_chips(1, [late])
    gathered_1, earlier = to_cores(0, sent_1, earlier)

    statistics = [0, 2, 1]
    received = [[] for _ in sizes]
    kept = [[] for _ in range(groups)]

    def attend_chunk(chunk, gathered, earlier):
        partials = []
        for turn in range(1, groups):
            packed, *stats = attend(
                gathered[turn - 1], gain, w_query, tables, wide_keys, wide_values, mark,
                turn * rows + starts[chunk], statistics[chunk],
                kept[turn] if statistics[chunk] > 1 else [], earlier,
            )
            kept[turn] += stats
            earlier = [packed]
            partials.append(packed)
        return partials, earlier

    def send_back(chunk, partials):
        received[chunk] = [
            shifted(packed, "seq", -turn * requests) for turn, packed in enumerate(partials, 1)
        ]

    partials, earlier = attend_chunk(0, gathered_1, earlier)
    send_back(0, partials)
    sent_3, earlier = to_chips(2, earlier)
    gathered_2, earlier = to_cores(1, sent_2, earlier)
    partials, earlier = attend_chunk(1, gathered_2, earlier)
    own_along = [
        relay([piece], [rows, rows // 2, rows // 2], earlier) for piece in from_chips
    ]
    own_pieces = [[tokens]] + [[one[0]] for one in own_along] + [[own_crossed]]
    own_pieces += [[other_core(part) for part in one[1:]] for one in own_along]
    earlier = earlier + [one[0] for one in own_along]
    received[0] = [relay([piece], sizes[:1], earlier)[0] for piece in received[0]]
    partials = [relay([piece], piece.shape[:1], received[0])[0] for piece in partials]
    send_back(1, partials)
    gathered_3, earlier = to_cores(2, sent_3, partials)
    partials, earlier = attend_chunk(2, gathered_3, earlier)
    send_back(2, partials)
    gathered = [gathered_1, gathered_2, gathered_3]
    other_rows = []
    for turn in range(1, groups):
        pieces = [sum(blocks, []) for blocks in zip(*[chunk[turn - 1] for chunk in gathered])]
        other_rows.append(fresh(pieces, gain, w_key, w_value, tables, turn * rows, earlier))
        earlier = [other_rows[-1][0]]
    *own_part, own_keys, own_values = attend_own(
        requests, own_pieces, gain, [w_query, w_key, w_value], tables, wide_keys, wide_values,
        mark, other_rows, earlier,
    )
    new_keys, new_values = zip((own_keys, own_values), *other_rows)

    parts = []
    earlier = []
    for chunks in ((0, 1), (2,)):
        merged, fars = combine(
            starts[chunks[0]], [sizes[chunk] for chunk in chunks], own_part,
            [piece for turn in zip(*[received[chunk] for chunk in chunks]) for piece in turn],
            w_out, heads, earlier,
        )
        fars = [[other_core(part) for part in far] for far in fars]
        far, near = project(merged, w_out, heads)
        sums = [sum_cores(one, parts_far, [far]) for one, parts_far in zip(near[1:], fars)]
        from_chips = [shifted(one, "head", CORES * k) for k, one in enumerate(sums, 1)]
        parts.append([near[0], other_core(far), *from_chips])
        earlier = sums
    keys_updated, values_updated, done = update(
        cached_lengths, new_keys, new_values, keys_cache, values_cache, earlier
    )
    return (finish(parts, [done]), keys_updated, values_updated)


def solution(mesh):
    return jax.shard_map(
        shards,
        mesh=mesh,
        in_specs=(
            P("seq", "head"),
            P(),
            P(None, "head"),
            P(None, "head"),
            P(None, "head"),
            P("head", None),
            P("seq", "head"),
            P("seq", "head"),
            P(),
            P(),
        ),
        out_specs=(P("seq", "head"), P("seq", "head"), P("seq", "head")),
        check_vma=False,
    )
```

```python
import functools
import math

import jax
import jax.numpy as jnp
from jax import lax
from jax.experimental import pallas as pl
from jax.experimental.pallas import tpu as pltpu
from jax.sharding import PartitionSpec as P

HD = 128
LANES = 128
STAT_ROWS = 8
ROW_TILE = 16
CORES = 2
CHUNK_UNITS = (7, 9)
PIECES = 2
COST_WEIGHT = 0.0005
FIRST_MICROS = 2
FLOPS_PER_MICRO = 1_000_000_000
MIB = 1 << 20

rope_base = 500000.0
neg_large = -1e30
log2_scale = math.log2(math.e) / math.sqrt(HD)

VMEM = pl.BlockSpec(memory_space=pltpu.VMEM)
ANY = pl.BlockSpec(memory_space=pl.ANY)


def shifted(shard, axis, by):
    devices = lax.axis_size(axis)
    return lax.ppermute(shard, axis, [(i, (i + by) % devices) for i in range(devices)])


def other_core(shard):
    devices = lax.axis_size("head")
    return lax.ppermute(shard, "head", [(i, i ^ 1) for i in range(devices)])


def other_chips(own):
    chips = lax.axis_size("head") // CORES
    return [shifted(own, "head", CORES * k) for k in range(1, chips)]


def place_of(requests):
    member = lax.axis_index("seq")
    return lax.rem(member, requests), lax.div(member, requests)


def source_of(position_in, turn, groups):
    return lax.rem(position_in + (groups - turn), groups)


def dot(left, right):
    return jnp.dot(left, right, preferred_element_type=jnp.float32)


def dot_transposed(left, right):
    return lax.dot_general(
        left, right, (((1,), (1,)), ((), ())), preferred_element_type=jnp.float32
    )


def call(
    kernel, out_shape, arrays, limit, flops, transcendentals, name, earlier=(),
    scratch=(), micros=0,
):
    moved = sum(a.size * a.dtype.itemsize for a in arrays)
    moved += sum(math.prod(s.shape) * s.dtype.itemsize for s in out_shape)
    read = len(arrays)
    skipped = len(earlier)

    def body(*refs):
        kernel(*refs[:read], *refs[read + skipped :])

    return pl.pallas_call(
        body,
        out_shape=out_shape,
        in_specs=[VMEM] * len(arrays) + [ANY] * skipped,
        out_specs=[VMEM] * len(out_shape),
        scratch_shapes=scratch,
        compiler_params=pltpu.CompilerParams(vmem_limit_bytes=limit * MIB),
        cost_estimate=pl.CostEstimate(
            flops=max(int(COST_WEIGHT * flops), int(micros * FLOPS_PER_MICRO)),
            bytes_accessed=int(COST_WEIGHT * moved),
            transcendentals=int(COST_WEIGHT * transcendentals),
        ),
        name=name,
    )(*arrays, *earlier)


def whole_of(blocks):
    parts = [block[...] for block in blocks]
    return jnp.concatenate(parts, 0) if len(parts) > 1 else parts[0]


def relay_kernel(count, *refs):
    whole = whole_of(refs[:count])
    at = 0
    for ref in refs[count:]:
        ref[...] = whole[at : at + ref.shape[0]]
        at = (at + ref.shape[0]) % whole.shape[0]


def relay(blocks, sizes, earlier):
    shapes = [jax.ShapeDtypeStruct((size, *blocks[0].shape[1:]), blocks[0].dtype) for size in sizes]
    kernel = functools.partial(relay_kernel, len(blocks))
    return call(kernel, shapes, [*blocks], 4, 0, 0, "relay", earlier)


def mark_kernel(mark):
    lane = lax.broadcasted_iota(jnp.int32, mark.shape, 1)
    mark[...] = jnp.where(lane == 0, 1.0, 0.0).astype(mark.dtype)


def marks(rows):
    shape = jax.ShapeDtypeStruct((rows, LANES), jnp.bfloat16)
    return call(mark_kernel, [shape], [], 4, 0, 0, "marks", micros=FIRST_MICROS)[0]


def tables_kernel(groups, lengths_in, offsets_in, cosine, sine, *scratch):
    lengths, offsets, semaphores = scratch
    numbers = [
        pltpu.make_async_copy(lengths_in, lengths, semaphores.at[0]),
        pltpu.make_async_copy(offsets_in, offsets, semaphores.at[1]),
    ]
    for copy in numbers:
        copy.start()
    rows = cosine.shape[0] // groups
    for copy in numbers:
        copy.wait()
    request, position_in = place_of(lengths.shape[0])
    lane = lax.broadcasted_iota(jnp.int32, (rows, LANES), 1)
    row = lax.broadcasted_iota(jnp.int32, (rows, LANES), 0)
    half = lax.rem(lane, HD // 2).astype(jnp.float32)
    frequency = jnp.exp2(half * (-2.0 / HD * math.log2(rope_base)))
    sign = jnp.where(lane < HD // 2, -1.0, 1.0)
    for turn in range(groups):
        first = source_of(position_in, turn, groups) * rows
        first = first + offsets[request] + lengths[request]
        angles = (row + first).astype(jnp.float32) * frequency
        part = slice(turn * rows, (turn + 1) * rows)
        cosine[part] = jnp.cos(angles)
        sine[part] = jnp.sin(angles) * sign


def rope_tables(lengths, offsets, groups, rows, earlier):
    table = jax.ShapeDtypeStruct((groups * rows, LANES), jnp.float32)
    return call(
        functools.partial(tables_kernel, groups),
        [table, table],
        [lengths, offsets],
        12,
        0,
        0,
        "rope_tables",
        earlier,
        [
            pltpu.SMEM(lengths.shape, lengths.dtype),
            pltpu.SMEM(offsets.shape, offsets.dtype),
            pltpu.SemaphoreType.DMA((2,)),
        ],
    )


def widen_kernel(keys, values, mark, lengths_in, wide_keys, wide_values, lengths, semaphore):
    number = pltpu.make_async_copy(lengths_in, lengths, semaphore)
    number.start()
    slots = keys.shape[0]
    heads = keys.shape[1] // HD
    for head in range(heads):
        own = slice(head * HD, (head + 1) * HD)
        wide_keys[head, :, :HD] = keys[:, own]
        wide_values[head, :, :HD] = values[:, own]
        wide_values[head, :, HD:] = mark[:slots]
    number.wait()
    request, position_in = place_of(lengths.shape[0])
    slot = lax.broadcasted_iota(jnp.int32, (slots, LANES), 0) + position_in * slots
    lane = lax.broadcasted_iota(jnp.int32, (slots, LANES), 1)
    bias = jnp.where((lane == 0) & (slot >= lengths[request]), neg_large, 0.0).astype(jnp.bfloat16)
    for head in range(heads):
        wide_keys[head, :, HD:] = bias


def widen(keys, values, mark, lengths, earlier):
    slots, width = keys.shape
    wide = jax.ShapeDtypeStruct((width // HD, slots, HD + LANES), jnp.bfloat16)
    return call(
        widen_kernel,
        [wide, wide],
        [keys, values, mark, lengths],
        12,
        0,
        0,
        "widen_caches",
        earlier,
        [pltpu.SMEM(lengths.shape, lengths.dtype), pltpu.SemaphoreType.DMA],
    )


def rotate(vectors, cosine, sine):
    return vectors * cosine + pltpu.roll(vectors, HD // 2, 1) * sine


def project_normed(pieces, gain, weights):
    heads = gain.shape[0]
    width = gain.shape[2]
    me = lax.axis_index("head")
    squares = 0.0
    sums = [0.0] * len(weights)
    for index, piece in enumerate(pieces):
        owner = lax.rem(me + (heads - CORES * (index % (heads // CORES))), heads)
        if index >= heads // CORES:
            owner = owner ^ 1
        wide = piece.astype(jnp.float32)
        scaled = (wide * gain[owner]).astype(jnp.bfloat16)
        along = pl.ds(pl.multiple_of(owner * width, LANES), width)
        for place, weight in enumerate(weights):
            sums[place] = sums[place] + dot(scaled, weight[along, :])
        squares = squares + jnp.sum(wide * wide, -1, keepdims=True)
    factor = lax.rsqrt(squares / (heads * width) + 1e-05)
    return [total * factor for total in sums]


def stat_rows(columns, rows):
    padded = -(-rows // LANES) * LANES
    lane = lax.broadcasted_iota(jnp.int32, (padded, LANES), 1)
    table = jnp.zeros((padded, LANES), jnp.float32)
    for index, column in enumerate(columns):
        if padded > rows:
            filler = jnp.zeros((padded - rows, 1), jnp.float32)
            column = jnp.concatenate([column, filler], 0)
        table = jnp.where(lane == index, column, table)
    return table.T[:STAT_ROWS]


def stat_columns(stats):
    padding = jnp.zeros((LANES - STAT_ROWS, stats.shape[1]), jnp.float32)
    return jnp.concatenate([stats, padding], 0).T


def stat_places(rows, width):
    lanes = -(-rows // LANES) * LANES
    in_row = width // lanes
    return [(part // in_row * ROW_TILE, part % in_row * lanes) for part in range(3)], lanes


def tail_rows(rows, width):
    return stat_places(rows, width)[0][-1][0] + ROW_TILE


def split_refs(counts, refs):
    parts = []
    for count in counts:
        parts.append(refs[:count])
        refs = refs[count:]
    return parts, refs


def head_queries(product, cosine, sine):
    return [
        (rotate(product[:, at : at + HD], cosine, sine) * log2_scale).astype(jnp.bfloat16)
        for at in range(0, product.shape[1], HD)
    ]


def stack_heads(queries, head, repeat, at, rows):
    own = queries[head * repeat : (head + 1) * repeat]
    return jnp.concatenate([query[at : at + rows] for query in own], 0)


def weigh(scores, values):
    largest = functools.reduce(
        jnp.maximum, [jnp.max(score, -1, keepdims=True) for score in scores]
    )
    summed = 0.0
    for score, value in zip(scores, values):
        weights = jnp.exp2(score - largest).astype(jnp.bfloat16)
        summed = summed + dot(weights, value)
    denominator = summed[:, HD : HD + 1]
    return summed[:, :HD] / denominator, largest + jnp.log2(denominator)


def project_kernel(counts, table_at, *refs):
    *blocks, weights = split_refs([*counts, 6], refs)[0]
    queries, keys, values = refs[sum(counts) + 6 :]
    gain, w_query, w_key, w_value, cosine, sine = weights
    part = slice(table_at, table_at + queries.shape[0])
    pieces = [
        one[0][part] if one[0].shape[0] > queries.shape[0] else whole_of(one) for one in blocks
    ]
    query_sum, key_sum, value_sum = project_normed(pieces, gain, [w_query, w_key, w_value])
    cosine, sine = cosine[part], sine[part]
    queries[...] = jnp.concatenate(head_queries(query_sum, cosine, sine), 1)
    for at in range(0, keys.shape[1], HD):
        own = slice(at, at + HD)
        keys[:, own] = rotate(key_sum[:, own], cosine, sine).astype(jnp.bfloat16)
    values[...] = value_sum.astype(jnp.bfloat16)


def project_rows(pieces, gain, weights, tables, table_at, rows, earlier):
    flat = [block for blocks in pieces for block in blocks]
    return call(
        functools.partial(project_kernel, [len(blocks) for blocks in pieces], table_at),
        [jax.ShapeDtypeStruct((rows, weight.shape[1]), jnp.bfloat16) for weight in weights],
        [*flat, gain, *weights, *tables],
        24,
        2 * rows * sum(weight.size for weight in weights),
        0,
        "project_qkv",
        earlier,
    )


def attend_heads(queries, wide_keys, wide_values, mark, fresh, store):
    rows = queries.shape[0]
    kv_heads = wide_keys.shape[0]
    repeat = queries.shape[1] // HD // kv_heads
    marked = mark[: repeat * rows]
    scores = []
    values = []
    for head in range(kv_heads):
        shared = slice(head * HD, (head + 1) * HD)
        stacked = jnp.concatenate(
            [
                queries[:, (head * repeat + turn) * HD : (head * repeat + turn + 1) * HD]
                for turn in range(repeat)
            ],
            0,
        )
        wide = jnp.concatenate([stacked, marked], 1)
        found = [dot_transposed(wide, wide_keys[head])]
        held = [wide_values[head]]
        for keys, new_values, column, bias in fresh:
            if bias is None:
                added = jnp.concatenate([keys[:, shared], column], 1)
                found.append(dot_transposed(wide, added))
            else:
                bias = jnp.concatenate([bias] * repeat, 0)
                found.append(dot_transposed(stacked, keys[:, shared]) + bias)
            held.append(jnp.concatenate([new_values[:, shared], mark[: keys.shape[0]]], 1))
        scores.append(found)
        values.append(held)
    columns = []
    for head in range(kv_heads):
        result, logs = weigh(scores[head], values[head])
        for turn in range(repeat):
            part = slice(turn * rows, (turn + 1) * rows)
            store((head * repeat + turn) * HD, result[part])
            columns.append(logs[part])
    return stat_rows(columns, rows)


def attend_kernel(requests, groups, turn, blocks, queries, wide_keys, wide_values, mark, *refs):
    (new_keys, new_values), (packed,) = split_refs([blocks, blocks], refs)
    rows = queries.shape[0]
    position_in = place_of(requests)[1]
    hidden = position_in > source_of(position_in, turn, groups)
    fresh = []
    for keys, values in zip(new_keys, new_values):
        bias = mark[: keys.shape[0]].astype(jnp.float32) * neg_large
        fresh.append((keys, values, jnp.where(hidden, bias, 0.0).astype(jnp.bfloat16), None))

    def store(at, result):
        packed[:rows, at : at + HD] = result.astype(packed.dtype)

    rest = attend_heads(queries[...], wide_keys, wide_values, mark, fresh, store)
    width = packed.shape[1]
    packed[rows:] = jnp.zeros((packed.shape[0] - rows, width), packed.dtype)
    rest = jnp.concatenate([rest, jnp.zeros((ROW_TILE - STAT_ROWS, rest.shape[1]), jnp.float32)], 0)
    places, lanes = stat_places(rows, width)
    for row, lane in places:
        rounded = rest.astype(packed.dtype)
        packed[rows + row : rows + row + ROW_TILE, lane : lane + lanes] = rounded
        rest = rest - rounded.astype(jnp.float32)


def attend(requests, groups, turn, queries, wides, mark, new_rows, earlier):
    rows, width = queries.shape
    slots = wides[0].shape[1]
    new_keys, new_values = zip(*new_rows)
    shape = jax.ShapeDtypeStruct((rows + tail_rows(rows, width), width), jnp.bfloat16)
    return call(
        functools.partial(attend_kernel, requests, groups, turn, len(new_rows)),
        [shape],
        [queries, *wides, mark, *new_keys, *new_values],
        28,
        8 * rows * width * slots,
        rows * width // HD * slots,
        "attend_partner",
        earlier,
    )[0]


def attend_own_kernel(blocks, queries, wide_keys, wide_values, mark, *refs):
    (new_keys, new_values), (partial, stats) = split_refs([blocks, blocks], refs)
    rows = queries.shape[0]
    fresh = [
        (keys, values, jnp.zeros((keys.shape[0], LANES), jnp.bfloat16), None)
        for keys, values in zip(new_keys[:-1], new_values[:-1])
    ]
    token = lax.broadcasted_iota(jnp.int32, (rows, rows), 0)
    within = lax.broadcasted_iota(jnp.int32, (rows, rows), 1)
    causal = jnp.where(within <= token, 0.0, neg_large)
    fresh.append((new_keys[-1], new_values[-1], None, causal))

    def store(at, result):
        partial[:, at : at + HD] = result

    stats[...] = attend_heads(queries[...], wide_keys, wide_values, mark, fresh, store)


def attend_own(queries, wides, mark, new_rows, earlier):
    rows, width = queries.shape
    slots = wides[0].shape[1]
    new_keys, new_values = zip(*new_rows)
    return call(
        functools.partial(attend_own_kernel, len(new_rows)),
        [
            jax.ShapeDtypeStruct((rows, width), jnp.float32),
            jax.ShapeDtypeStruct((STAT_ROWS, -(-rows // LANES) * LANES), jnp.float32),
        ],
        [queries, *wides, mark, *new_keys, *new_values],
        28,
        8 * rows * width * slots,
        rows * width // HD * slots,
        "attend_own",
        earlier,
    )


def write_rows(target, fresh_rows, first):
    rows = fresh_rows.shape[0]
    slab_rows = target.shape[0]
    span = rows + ROW_TILE
    start = jnp.clip(first, 0, slab_rows - span)
    start = start - lax.rem(start, ROW_TILE)
    window = pl.ds(pl.multiple_of(start, ROW_TILE), span)
    shift = start - first
    place = lax.broadcasted_iota(jnp.int32, (span, rows), 0) + shift
    chosen = place == lax.broadcasted_iota(jnp.int32, (span, rows), 1)
    moved = dot(chosen.astype(jnp.bfloat16), fresh_rows)
    row = lax.broadcasted_iota(jnp.int32, (span, target.shape[1]), 0) + shift
    inside = (row >= 0) & (row < rows)
    old = target[window, :].astype(jnp.float32)
    target[window, :] = jnp.where(inside, moved, old).astype(jnp.bfloat16)


def update_kernel(groups, chunks, *refs):
    (new_keys, new_values, pairs), refs = split_refs([chunks, chunks, groups - 1], refs)
    keys, values, lengths_in, keys_updated, values_updated, done, lengths, semaphore = refs
    number = pltpu.make_async_copy(lengths_in, lengths, semaphore)
    number.start()
    keys_updated[...] = keys[...]
    values_updated[...] = values[...]
    done[...] = jnp.zeros(done.shape, done.dtype)
    number.wait()
    request, position_in = place_of(lengths.shape[0])
    rows = sum(ref.shape[0] for ref in new_keys)
    width = keys.shape[1]
    for turn in range(groups):
        source = source_of(position_in, turn, groups)
        first = lengths[request] + source * rows - position_in * keys.shape[0]
        if turn:
            write_rows(keys_updated, pairs[turn - 1][:, :width], first)
            write_rows(values_updated, pairs[turn - 1][:, width:], first)
        else:
            write_rows(keys_updated, whole_of(new_keys), first)
            write_rows(values_updated, whole_of(new_values), first)


def update(lengths, new_rows, pairs, keys, values, earlier):
    new_keys, new_values = zip(*new_rows)
    slab = jax.ShapeDtypeStruct(keys.shape, keys.dtype)
    return call(
        functools.partial(update_kernel, len(pairs) + 1, len(new_rows)),
        [slab, slab, jax.ShapeDtypeStruct((STAT_ROWS, LANES), jnp.float32)],
        [*new_keys, *new_values, *pairs, keys, values, lengths],
        20,
        0,
        0,
        "update_caches",
        earlier,
        [pltpu.SMEM(lengths.shape, lengths.dtype), pltpu.SemaphoreType.DMA],
    )


def pair_kernel(chunks, *refs):
    (new_keys, new_values), (pair,) = split_refs([chunks, chunks], refs)
    pair[...] = jnp.concatenate([whole_of(new_keys), whole_of(new_values)], 1)


def pair_rows(new_rows, earlier):
    new_keys, new_values = zip(*new_rows)
    rows = sum(keys.shape[0] for keys in new_keys)
    shape = jax.ShapeDtypeStruct((rows, 2 * new_keys[0].shape[1]), new_keys[0].dtype)
    kernel = functools.partial(pair_kernel, len(new_rows))
    return call(kernel, [shape], [*new_keys, *new_values], 8, 0, 0, "pair_rows", earlier)[0]


def combine_kernel(own_partial, own_stats, *refs):
    heads = lax.axis_size("head")
    chips = heads // CORES
    outputs = PIECES * (chips - 1)
    received = refs[: -2 - outputs]
    w_out, merged_rows, *far = refs[-2 - outputs :]
    rows, width = own_partial.shape
    logs = [stat_columns(own_stats[...])[:rows]]
    partials = [own_partial[...]]
    for packed in received:
        places, lanes = stat_places(rows, width)
        stats = sum(
            packed[rows + row : rows + row + ROW_TILE, lane : lane + lanes].astype(jnp.float32)
            for row, lane in places
        )
        logs.append(stat_columns(stats[:STAT_ROWS])[:rows])
        partials.append(packed[:rows])
    largest = functools.reduce(jnp.maximum, logs)
    shares = [jnp.exp2(log - largest) for log in logs]
    total = functools.reduce(jnp.add, shares)
    shares = [share / total for share in shares]
    attended = []
    for head in range(width // HD):
        at = slice(head * HD, (head + 1) * HD)
        column = slice(head, head + 1)
        merged = 0.0
        for partial, share in zip(partials, shares):
            merged = merged + partial[:, at].astype(jnp.float32) * share[:, column]
        attended.append(merged.astype(jnp.bfloat16))
    attended = jnp.concatenate(attended, 1)
    merged_rows[...] = attended
    for ahead in range(1, chips):
        store_pieces(block_product(attended, w_out, ahead, 1), far[PIECES * (ahead - 1) :][:PIECES])


def store_pieces(block, targets):
    width = targets[0].shape[1]
    for index, target in enumerate(targets):
        target[...] = block[:, index * width : (index + 1) * width]


def block_product(attended, w_out, ahead, flip):
    heads = lax.axis_size("head")
    block_width = w_out.shape[1] // heads
    block = lax.rem(lax.axis_index("head") + CORES * ahead, heads) ^ flip
    along = pl.ds(pl.multiple_of(block * block_width, LANES), block_width)
    return dot(attended, w_out[:, along]).astype(jnp.bfloat16)


def near_kernel(merged_rows, w_out, *refs):
    far, near = refs[:PIECES], refs[PIECES:]
    attended = merged_rows[...]
    store_pieces(block_product(attended, w_out, 0, 1), far)
    for ahead, target in enumerate(near):
        target[...] = block_product(attended, w_out, ahead, 0)


def combine(own, received, w_out, heads, earlier):
    chips = heads // CORES
    rows = own[0].shape[0]
    width = w_out.shape[1] // heads
    merged = jax.ShapeDtypeStruct(own[0].shape, jnp.bfloat16)
    piece = jax.ShapeDtypeStruct((rows, width // PIECES), jnp.bfloat16)
    merged, *far = call(
        combine_kernel,
        [merged] + [piece] * (PIECES * (chips - 1)),
        [*own, *received, w_out],
        20,
        rows * w_out.size,
        0,
        "combine",
        earlier,
    )
    return merged, [far[k * PIECES : (k + 1) * PIECES] for k in range(chips - 1)]


def project_near(merged, w_out, heads):
    rows = merged.shape[0]
    width = w_out.shape[1] // heads
    block = jax.ShapeDtypeStruct((rows, width), jnp.bfloat16)
    piece = jax.ShapeDtypeStruct((rows, width // PIECES), jnp.bfloat16)
    outputs = call(
        near_kernel,
        [piece] * PIECES + [block] * (heads // CORES),
        [merged, w_out],
        20,
        2 * rows * w_out.size,
        0,
        "project_near",
    )
    return outputs[:PIECES], outputs[PIECES:]


def sum_kernel(count, near, *refs):
    far, pieces = refs[:count], refs[count:]
    total = jnp.concatenate([ref[...] for ref in far], 1).astype(jnp.float32)
    store_pieces((near[...].astype(jnp.float32) + total).astype(jnp.bfloat16), pieces)


def sum_cores(near, far, pieces, earlier):
    rows, width = near.shape
    shape = jax.ShapeDtypeStruct((rows, width // pieces), near.dtype)
    kernel = functools.partial(sum_kernel, len(far))
    return call(kernel, [shape] * pieces, [near, *far], 8, near.size, 0, "sum_cores", earlier)


def finish_kernel(counts, *refs):
    flat = [count for chunk in counts for count in chunk]
    blocks, (result,) = split_refs(flat, refs)
    at = 0
    for chunk in counts:
        total = 0.0
        for pieces in blocks[: len(chunk)]:
            whole = jnp.concatenate([ref[...] for ref in pieces], 1)
            total = total + whole.astype(jnp.float32)
        blocks = blocks[len(chunk) :]
        result[at : at + total.shape[0]] = total.astype(result.dtype)
        at += total.shape[0]


def finish(chunks, earlier):
    flat = [piece for chunk in chunks for pieces in chunk for piece in pieces]
    rows = sum(chunk[0][0].shape[0] for chunk in chunks)
    width = sum(piece.shape[1] for piece in chunks[0][0])
    shape = jax.ShapeDtypeStruct((rows, width), jnp.bfloat16)
    kernel = functools.partial(finish_kernel, [[len(pieces) for pieces in c] for c in chunks])
    return call(kernel, [shape], flat, 8, 0, 0, "finish", earlier)[0]


def shards(
    tokens,
    norm_gain,
    w_query,
    w_key,
    w_value,
    w_out,
    keys_cache,
    values_cache,
    cached_lengths,
    rope_offsets,
):
    rows, width = tokens.shape
    requests = cached_lengths.shape[0]
    groups = lax.axis_size("seq") // requests
    heads = lax.axis_size("head")
    chips = heads // CORES
    gain = norm_gain.reshape(heads, 1, width)
    sizes = [rows * units // sum(CHUNK_UNITS) for units in CHUNK_UNITS]
    starts = [sum(sizes[:chunk]) for chunk in range(len(sizes))]
    cuts = [tokens[at : at + size] for at, size in zip(starts, sizes)]
    weights = [w_query, w_key, w_value]

    from_chips = [other_chips(cuts[0])]
    crossed = other_core(tokens)
    mark = marks(keys_cache.shape[0])
    tables = rope_tables(cached_lengths, rope_offsets, groups, rows, [mark])
    earlier = [tables[0]]
    for cut in cuts[1:]:
        (late,) = relay([cut], cut.shape[:1], earlier)
        from_chips.append(other_chips(late))
        earlier = [late]
    wides = widen(keys_cache, values_cache, mark, cached_lengths, earlier)
    earlier = [wides[0]]

    def project_chunk(chunk, earlier):
        at, count = starts[chunk], sizes[chunk]
        passed = [relay([piece], [count], earlier)[0] for piece in from_chips[chunk]]
        pieces = [[tokens]] + [[piece] for piece in passed]
        pieces += [[crossed]] + [[other_core(piece)] for piece in passed]
        queries, *new = project_rows(pieces, gain, weights, tables, at, count, passed)
        return queries, new

    def send(piece, sign):
        return [shifted(piece, "seq", sign * turn * requests) for turn in range(1, groups)]

    queries, new = project_chunk(0, earlier)
    own_queries, new_rows = [queries], [new]
    asked = [send(queries, 1)]
    own_parts = []
    for chunk in range(1, len(sizes)):
        queries, new = project_chunk(chunk, [queries])
        own_queries.append(queries)
        new_rows.append(new)
        own_parts.append(attend_own(own_queries[chunk - 1], wides, mark, new_rows[:chunk], [queries]))
        (late,) = relay([queries], [sizes[chunk]], own_parts[-1][:1])
        asked.append(send(late, 1))
        earlier = [late]
    answered = []
    for chunk in range(len(sizes)):
        answers = []
        for turn in range(1, groups):
            answer = attend(
                requests, groups, turn, asked[chunk][turn - 1], wides, mark, new_rows, earlier
            )
            answers.append(shifted(answer, "seq", -turn * requests))
            earlier = [answer]
        answered.append(answers)
        if chunk == len(sizes) - 2:
            own_parts.append(attend_own(own_queries[-1], wides, mark, new_rows, earlier))
            earlier = own_parts[-1][:1]

    parts = []
    landed = []
    for chunk in range(len(sizes)):
        last = chunk == len(sizes) - 1
        merged, fars = combine(own_parts[chunk], answered[chunk], w_out, heads, earlier)
        fars = [[other_core(part) for part in far] for far in fars]
        far, near = project_near(merged, w_out, heads)
        far = [other_core(part) for part in far]
        waited = landed + ([near[0]] if last else far)
        sums = [
            sum_cores(one, parts_far, PIECES if last else 1, waited)
            for one, parts_far in zip(near[1:], fars)
        ]
        arrived = [
            [shifted(piece, "head", CORES * k) for piece in pieces]
            for k, pieces in enumerate(sums, 1)
        ]
        parts.append([[near[0]], far, *arrived])
        landed = [pieces[0] for pieces in arrived]
        earlier = [pieces[0] for pieces in sums]
        if chunk == 0:
            pairs = send(pair_rows(new_rows, earlier), 1)
    keys_updated, values_updated, done = update(
        cached_lengths, new_rows, pairs, keys_cache, values_cache, earlier
    )
    return (finish(parts, [done]), keys_updated, values_updated)


def solution(mesh):
    return jax.shard_map(
        shards,
        mesh=mesh,
        in_specs=(
            P("seq", "head"),
            P(),
            P(None, "head"),
            P(None, "head"),
            P(None, "head"),
            P("head", None),
            P("seq", "head"),
            P("seq", "head"),
            P(),
            P(),
        ),
        out_specs=(P("seq", "head"), P("seq", "head"), P("seq", "head")),
        check_vma=False,
    )
```

```python
import functools
import math

import jax
import jax.numpy as jnp
from jax import lax
from jax.experimental import pallas as pl
from jax.experimental.pallas import tpu as pltpu
from jax.sharding import PartitionSpec as P

HD = 128
LANES = 128
STAT_ROWS = 8
ROW_TILE = 16
CORES = 2
CHUNKS = 2
COST_WEIGHT = 0.0005
FIRST_MICROS = 2
FLOPS_PER_MICRO = 1_000_000_000
MIB = 1 << 20

rope_base = 500000.0
neg_large = -1e30
log2_scale = math.log2(math.e) / math.sqrt(HD)

VMEM = pl.BlockSpec(memory_space=pltpu.VMEM)
ANY = pl.BlockSpec(memory_space=pl.ANY)


def shifted(shard, axis, by):
    devices = lax.axis_size(axis)
    return lax.ppermute(shard, axis, [(i, (i + by) % devices) for i in range(devices)])


def other_core(shard):
    devices = lax.axis_size("head")
    return lax.ppermute(shard, "head", [(i, i ^ 1) for i in range(devices)])


def other_chips(own):
    chips = lax.axis_size("head") // CORES
    return [shifted(own, "head", CORES * k) for k in range(1, chips)]


def place_of(requests):
    member = lax.axis_index("seq")
    return lax.rem(member, requests), lax.div(member, requests)


def source_of(position_in, turn, groups):
    return lax.rem(position_in + (groups - turn), groups)


def dot(left, right):
    return jnp.dot(left, right, preferred_element_type=jnp.float32)


def dot_transposed(left, right):
    return lax.dot_general(
        left, right, (((1,), (1,)), ((), ())), preferred_element_type=jnp.float32
    )


def call(
    kernel, out_shape, arrays, limit, flops, transcendentals, name, earlier=(),
    scratch=(), micros=0,
):
    moved = sum(a.size * a.dtype.itemsize for a in arrays)
    moved += sum(math.prod(s.shape) * s.dtype.itemsize for s in out_shape)
    read = len(arrays)
    skipped = len(earlier)

    def body(*refs):
        kernel(*refs[:read], *refs[read + skipped :])

    return pl.pallas_call(
        body,
        out_shape=out_shape,
        in_specs=[VMEM] * len(arrays) + [ANY] * skipped,
        out_specs=[VMEM] * len(out_shape),
        scratch_shapes=scratch,
        compiler_params=pltpu.CompilerParams(vmem_limit_bytes=limit * MIB),
        cost_estimate=pl.CostEstimate(
            flops=max(int(COST_WEIGHT * flops), micros * FLOPS_PER_MICRO),
            bytes_accessed=int(COST_WEIGHT * moved),
            transcendentals=int(COST_WEIGHT * transcendentals),
        ),
        name=name,
    )(*arrays, *earlier)


def whole_of(blocks):
    parts = [block[...] for block in blocks]
    return jnp.concatenate(parts, 0) if len(parts) > 1 else parts[0]


def relay_kernel(count, *refs):
    whole = whole_of(refs[:count])
    at = 0
    for ref in refs[count:]:
        ref[...] = whole[at : at + ref.shape[0]]
        at = (at + ref.shape[0]) % whole.shape[0]


def relay(blocks, sizes, earlier):
    shapes = [jax.ShapeDtypeStruct((size, *blocks[0].shape[1:]), blocks[0].dtype) for size in sizes]
    kernel = functools.partial(relay_kernel, len(blocks))
    return call(kernel, shapes, [*blocks], 4, 0, 0, "relay", earlier)


def mark_kernel(mark):
    lane = lax.broadcasted_iota(jnp.int32, mark.shape, 1)
    mark[...] = jnp.where(lane == 0, 1.0, 0.0).astype(mark.dtype)


def marks(rows):
    shape = jax.ShapeDtypeStruct((rows, LANES), jnp.bfloat16)
    return call(mark_kernel, [shape], [], 4, 0, 0, "marks", micros=FIRST_MICROS)[0]


def tables_kernel(groups, lengths_in, offsets_in, cosine, sine, *scratch):
    lengths, offsets, semaphores = scratch
    numbers = [
        pltpu.make_async_copy(lengths_in, lengths, semaphores.at[0]),
        pltpu.make_async_copy(offsets_in, offsets, semaphores.at[1]),
    ]
    for copy in numbers:
        copy.start()
    rows = cosine.shape[0] // groups
    for copy in numbers:
        copy.wait()
    request, position_in = place_of(lengths.shape[0])
    lane = lax.broadcasted_iota(jnp.int32, (rows, LANES), 1)
    row = lax.broadcasted_iota(jnp.int32, (rows, LANES), 0)
    half = lax.rem(lane, HD // 2).astype(jnp.float32)
    frequency = jnp.exp2(half * (-2.0 / HD * math.log2(rope_base)))
    sign = jnp.where(lane < HD // 2, -1.0, 1.0)
    for turn in range(groups):
        first = source_of(position_in, turn, groups) * rows
        first = first + offsets[request] + lengths[request]
        angles = (row + first).astype(jnp.float32) * frequency
        part = slice(turn * rows, (turn + 1) * rows)
        cosine[part] = jnp.cos(angles)
        sine[part] = jnp.sin(angles) * sign


def rope_tables(lengths, offsets, groups, rows, earlier):
    table = jax.ShapeDtypeStruct((groups * rows, LANES), jnp.float32)
    return call(
        functools.partial(tables_kernel, groups),
        [table, table],
        [lengths, offsets],
        12,
        0,
        0,
        "rope_tables",
        earlier,
        [
            pltpu.SMEM(lengths.shape, lengths.dtype),
            pltpu.SMEM(offsets.shape, offsets.dtype),
            pltpu.SemaphoreType.DMA((2,)),
        ],
    )


def widen_kernel(keys, values, mark, lengths_in, wide_keys, wide_values, lengths, semaphore):
    number = pltpu.make_async_copy(lengths_in, lengths, semaphore)
    number.start()
    slots = keys.shape[0]
    heads = keys.shape[1] // HD
    for head in range(heads):
        own = slice(head * HD, (head + 1) * HD)
        wide_keys[head, :, :HD] = keys[:, own]
        wide_values[head, :, :HD] = values[:, own]
        wide_values[head, :, HD:] = mark[:slots]
    number.wait()
    request, position_in = place_of(lengths.shape[0])
    slot = lax.broadcasted_iota(jnp.int32, (slots, LANES), 0) + position_in * slots
    lane = lax.broadcasted_iota(jnp.int32, (slots, LANES), 1)
    bias = jnp.where((lane == 0) & (slot >= lengths[request]), neg_large, 0.0).astype(jnp.bfloat16)
    for head in range(heads):
        wide_keys[head, :, HD:] = bias


def widen(keys, values, mark, lengths, earlier):
    slots, width = keys.shape
    wide = jax.ShapeDtypeStruct((width // HD, slots, HD + LANES), jnp.bfloat16)
    return call(
        widen_kernel,
        [wide, wide],
        [keys, values, mark, lengths],
        12,
        0,
        0,
        "widen_caches",
        earlier,
        [pltpu.SMEM(lengths.shape, lengths.dtype), pltpu.SemaphoreType.DMA],
    )


def rotate(vectors, cosine, sine):
    return vectors * cosine + pltpu.roll(vectors, HD // 2, 1) * sine


def project_normed(pieces, gain, weights):
    heads = gain.shape[0]
    width = gain.shape[2]
    me = lax.axis_index("head")
    squares = 0.0
    sums = [0.0] * len(weights)
    for index, piece in enumerate(pieces):
        owner = lax.rem(me + (heads - CORES * (index % (heads // CORES))), heads)
        if index >= heads // CORES:
            owner = owner ^ 1
        wide = piece.astype(jnp.float32)
        scaled = (wide * gain[owner]).astype(jnp.bfloat16)
        along = pl.ds(pl.multiple_of(owner * width, LANES), width)
        for place, weight in enumerate(weights):
            sums[place] = sums[place] + dot(scaled, weight[along, :])
        squares = squares + jnp.sum(wide * wide, -1, keepdims=True)
    factor = lax.rsqrt(squares / (heads * width) + 1e-05)
    return [total * factor for total in sums]


def stat_rows(columns, rows):
    lane = lax.broadcasted_iota(jnp.int32, (rows, LANES), 1)
    table = jnp.zeros((rows, LANES), jnp.float32)
    for index, column in enumerate(columns):
        table = jnp.where(lane == index, column, table)
    return table.T[:STAT_ROWS]


def split_refs(counts, refs):
    parts = []
    for count in counts:
        parts.append(refs[:count])
        refs = refs[count:]
    return parts, refs


def rows_of(blocks, row_at, rows):
    parts = []
    at = 0
    for block in blocks:
        size = block.shape[0]
        low, high = max(row_at - at, 0), min(row_at + rows - at, size)
        if low < high:
            parts.append(block[low:high])
        at += size
    return jnp.concatenate(parts, 0) if len(parts) > 1 else parts[0]


def attend_kernel(counts, own, row_at, rows, table_at, *refs):
    blocks, refs = split_refs(counts, refs)
    gain, w_query, cosine, sine, wide_keys, wide_values, mark, *outputs = refs
    pieces = [rows_of(one, row_at, rows) for one in blocks]
    (product,) = project_normed(pieces, gain, [w_query])
    cosine = cosine[table_at : table_at + rows]
    sine = sine[table_at : table_at + rows]
    kv_heads = wide_keys.shape[0]
    repeat = product.shape[1] // HD // kv_heads
    queries = [
        (rotate(product[:, head * HD : (head + 1) * HD], cosine, sine) * log2_scale).astype(
            jnp.bfloat16
        )
        for head in range(kv_heads * repeat)
    ]
    step = min(rows, LANES)
    mark = mark[: repeat * step]
    tiles = [(head, at) for head in range(kv_heads) for at in range(0, rows, step)]

    def scores_of(head, at):
        stacked = jnp.concatenate(
            [query[at : at + step] for query in queries[head * repeat : (head + 1) * repeat]], 0
        )
        return dot_transposed(jnp.concatenate([stacked, mark], 1), wide_keys[head])

    columns = {}
    following = scores_of(*tiles[0])
    for index, (head, at) in enumerate(tiles):
        scores = following
        if index + 1 < len(tiles):
            following = scores_of(*tiles[index + 1])
        largest = jnp.max(scores, -1, keepdims=True)
        weights = jnp.exp2(scores - largest).astype(jnp.bfloat16)
        summed = dot(weights, wide_values[head])
        denominator = summed[:, HD : HD + 1]
        result = summed[:, :HD] / denominator
        logs = largest + jnp.log2(denominator)
        for turn in range(repeat):
            part = slice(turn * step, (turn + 1) * step)
            to = slice((head * repeat + turn) * HD, (head * repeat + turn + 1) * HD)
            outputs[0][at : at + step, to] = result[part].astype(outputs[0].dtype)
            columns.setdefault(head * repeat + turn, []).append(logs[part])
    stats = stat_rows([jnp.concatenate(parts, 0) for parts in columns.values()], rows)
    if own:
        outputs[1][...] = stats
        outputs[2][...] = jnp.concatenate(queries, 1)
        return
    outputs[0][rows:] = jnp.zeros((ROW_TILE, outputs[0].shape[1]), jnp.bfloat16)
    rest = jnp.concatenate([stats, jnp.zeros((ROW_TILE - STAT_ROWS, rows), jnp.float32)], 0)
    for part in range(3):
        rounded = rest.astype(jnp.bfloat16)
        outputs[0][rows:, part * rows : (part + 1) * rows] = rounded
        rest = rest - rounded.astype(jnp.float32)


def attend(
    pieces, gain, w_query, tables, wide_keys, wide_values, mark, own, row_at, rows, table_at,
    earlier,
):
    counts = [len(blocks) for blocks in pieces]
    flat = [block for blocks in pieces for block in blocks]
    out_width = w_query.shape[1]
    slots = wide_keys.shape[1]
    if own:
        out_shape = [
            jax.ShapeDtypeStruct((rows, out_width), jnp.float32),
            jax.ShapeDtypeStruct((STAT_ROWS, rows), jnp.float32),
            jax.ShapeDtypeStruct((rows, out_width), jnp.bfloat16),
        ]
    else:
        out_shape = [jax.ShapeDtypeStruct((rows + ROW_TILE, out_width), jnp.bfloat16)]
    return call(
        functools.partial(attend_kernel, counts, own, row_at, rows, table_at),
        out_shape,
        [*flat, gain, w_query, *tables, wide_keys, wide_values, mark],
        28,
        2 * rows * out_width * (w_query.shape[0] + 4 * slots),
        rows * out_width // HD * slots,
        "attend_own" if own else "attend_partner",
        earlier,
    )


def fresh_kernel(counts, table_at, *refs):
    blocks, refs = split_refs(counts, refs)
    gain, w_key, w_value, cosine, sine, new_keys, new_values = refs
    rows = new_keys.shape[0]
    pieces = [whole_of(one) for one in blocks]
    keys, values = project_normed(pieces, gain, [w_key, w_value])
    cosine = cosine[table_at : table_at + rows]
    sine = sine[table_at : table_at + rows]
    for head in range(keys.shape[1] // HD):
        own = slice(head * HD, (head + 1) * HD)
        new_keys[:, own] = rotate(keys[:, own], cosine, sine).astype(jnp.bfloat16)
    new_values[...] = values.astype(jnp.bfloat16)


def fresh(pieces, gain, w_key, w_value, tables, table_at, earlier):
    flat = [block for blocks in pieces for block in blocks]
    rows = sum(block.shape[0] for block in pieces[0])
    shape = jax.ShapeDtypeStruct((rows, w_key.shape[1]), jnp.bfloat16)
    return call(
        functools.partial(fresh_kernel, [len(blocks) for blocks in pieces], table_at),
        [shape, shape],
        [*flat, gain, w_key, w_value, *tables],
        20,
        4 * rows * w_key.size,
        0,
        "fresh_kv",
        earlier,
    )


def write_rows(target, fresh_rows, first):
    rows = fresh_rows.shape[0]
    slab_rows = target.shape[0]
    span = rows + ROW_TILE
    start = jnp.clip(first, 0, slab_rows - span)
    start = start - lax.rem(start, ROW_TILE)
    window = pl.ds(pl.multiple_of(start, ROW_TILE), span)
    shift = start - first
    place = lax.broadcasted_iota(jnp.int32, (span, rows), 0) + shift
    chosen = place == lax.broadcasted_iota(jnp.int32, (span, rows), 1)
    moved = dot(chosen.astype(jnp.bfloat16), fresh_rows)
    row = lax.broadcasted_iota(jnp.int32, (span, target.shape[1]), 0) + shift
    inside = (row >= 0) & (row < rows)
    old = target[window, :].astype(jnp.float32)
    target[window, :] = jnp.where(inside, moved, old).astype(jnp.bfloat16)


def attend_fresh_kernel(groups, requests, *refs):
    query_refs, refs = refs[:CHUNKS], refs[CHUNKS:]
    key_refs, value_refs, refs = refs[:groups], refs[groups : 2 * groups], refs[2 * groups :]
    partial, stats = refs
    position_in = place_of(requests)[1]
    rows, width = partial.shape
    kv_heads = key_refs[0].shape[1] // HD
    repeat = width // HD // kv_heads
    queries = whole_of(query_refs)
    token = lax.broadcasted_iota(jnp.int32, (rows, rows), 0)
    within = lax.broadcasted_iota(jnp.int32, (rows, rows), 1)
    causal = jnp.where(within <= token, 0.0, neg_large)
    causal = jnp.concatenate([causal] * repeat, 0)
    lane = lax.broadcasted_iota(jnp.int32, (rows, LANES), 1)
    ones = jnp.where(lane == 0, 1.0, 0.0).astype(jnp.bfloat16)
    hidden = [jnp.zeros((rows, LANES), jnp.bfloat16)]
    for turn in range(1, groups):
        later = source_of(position_in, turn, groups) > position_in
        hidden.append(jnp.where((lane == 0) & later, neg_large, 0.0).astype(jnp.bfloat16))
    columns = []
    for head in range(kv_heads):
        own = [
            slice((head * repeat + turn) * HD, (head * repeat + turn + 1) * HD)
            for turn in range(repeat)
        ]
        shared = slice(head * HD, (head + 1) * HD)
        stacked = jnp.concatenate([queries[:, one] for one in own], 0)
        stacked = jnp.concatenate([stacked, jnp.concatenate([ones] * repeat, 0)], 1)
        scores = [
            dot_transposed(stacked, jnp.concatenate([ref[:, shared], bias], 1))
            for ref, bias in zip(key_refs, hidden)
        ]
        scores = jnp.concatenate([scores[0] + causal] + scores[1:], 1)
        largest = jnp.max(scores, -1, keepdims=True)
        weights = jnp.exp2(scores - largest).astype(jnp.bfloat16)
        wide_values = [jnp.concatenate([ref[:, shared], ones], 1) for ref in value_refs]
        summed = dot(weights, jnp.concatenate(wide_values, 0))
        denominator = summed[:, HD : HD + 1]
        result = summed[:, :HD] / denominator
        logs = largest + jnp.log2(denominator)
        for turn, one in enumerate(own):
            part = slice(turn * rows, (turn + 1) * rows)
            partial[:, one] = result[part]
            columns.append(logs[part])
    stats[...] = stat_rows(columns, rows)


def attend_fresh(requests, queries, new_keys, new_values):
    groups = len(new_keys)
    rows = new_keys[0].shape[0]
    width = queries[0].shape[1]
    return call(
        functools.partial(attend_fresh_kernel, groups, requests),
        [
            jax.ShapeDtypeStruct((rows, width), jnp.float32),
            jax.ShapeDtypeStruct((STAT_ROWS, rows), jnp.float32),
        ],
        [*queries, *new_keys, *new_values],
        24,
        4 * rows * width * rows * groups,
        rows * width // HD * rows * groups,
        "attend_fresh",
    )


def update_kernel(groups, *refs):
    key_refs, value_refs, refs = refs[:groups], refs[groups : 2 * groups], refs[2 * groups :]
    keys, values, lengths_in, keys_updated, values_updated, done, lengths, semaphore = refs
    number = pltpu.make_async_copy(lengths_in, lengths, semaphore)
    number.start()
    keys_updated[...] = keys[...]
    values_updated[...] = values[...]
    done[...] = jnp.zeros(done.shape, done.dtype)
    number.wait()
    request, position_in = place_of(lengths.shape[0])
    rows = key_refs[0].shape[0]
    for turn in range(groups):
        source = source_of(position_in, turn, groups)
        first = lengths[request] + source * rows - position_in * keys.shape[0]
        write_rows(keys_updated, key_refs[turn][...], first)
        write_rows(values_updated, value_refs[turn][...], first)


def update(lengths, new_keys, new_values, keys, values, earlier):
    groups = len(new_keys)
    slab = jax.ShapeDtypeStruct(keys.shape, keys.dtype)
    return call(
        functools.partial(update_kernel, groups),
        [slab, slab, jax.ShapeDtypeStruct((STAT_ROWS, LANES), jnp.float32)],
        [*new_keys, *new_values, keys, values, lengths],
        20,
        4 * new_keys[0].size * new_keys[0].shape[0] * groups,
        0,
        "update_caches",
        earlier,
        [pltpu.SMEM(lengths.shape, lengths.dtype), pltpu.SemaphoreType.DMA],
    )


def combine_kernel(row_at, own_partial, own_stats, fresh_partial, fresh_stats, *refs):
    heads = lax.axis_size("head")
    chips = heads // CORES
    outputs = 2 * chips - 1
    received = refs[: -1 - outputs]
    w_out, merged_rows = refs[-1 - outputs], refs[-outputs]
    far = refs[1 - outputs :]
    width = own_partial.shape[1]
    rows = merged_rows.shape[0]
    part = slice(row_at, row_at + rows)
    padding = jnp.zeros((LANES - STAT_ROWS, rows), jnp.float32)
    stats = [own_stats[...], fresh_stats[:, part]]
    for ref in received:
        stats.append(
            sum(
                ref[rows:, turn * rows : (turn + 1) * rows].astype(jnp.float32)
                for turn in range(3)
            )[:STAT_ROWS]
        )
    logs = [jnp.concatenate([stat, padding], 0).T for stat in stats]
    largest = functools.reduce(jnp.maximum, logs)
    shares = [jnp.exp2(log - largest) for log in logs]
    total = functools.reduce(jnp.add, shares)
    shares = [share / total for share in shares]
    attended = []
    for head in range(width // HD):
        own = slice(head * HD, (head + 1) * HD)
        column = slice(head, head + 1)
        merged = own_partial[:, own] * shares[0][:, column]
        merged = merged + fresh_partial[part, own] * shares[1][:, column]
        for ref, share in zip(received, shares[2:]):
            merged = merged + ref[:rows, own].astype(jnp.float32) * share[:, column]
        attended.append(merged.astype(jnp.bfloat16))
    attended = jnp.concatenate(attended, 1)
    merged_rows[...] = attended
    for ahead in range(1, chips):
        result = block_product(attended, w_out, ahead, 1)
        middle = result.shape[1] // 2
        far[2 * ahead - 2][...] = result[:, :middle]
        far[2 * ahead - 1][...] = result[:, middle:]


def block_product(attended, w_out, ahead, flip):
    heads = lax.axis_size("head")
    block_width = w_out.shape[1] // heads
    block = lax.rem(lax.axis_index("head") + CORES * ahead, heads) ^ flip
    along = pl.ds(pl.multiple_of(block * block_width, LANES), block_width)
    return dot(attended, w_out[:, along]).astype(jnp.bfloat16)


def project_kernel(merged_rows, w_out, far, *near):
    attended = merged_rows[...]
    far[...] = block_product(attended, w_out, 0, 1)
    for ahead, target in enumerate(near):
        target[...] = block_product(attended, w_out, ahead, 0)


def combine(row_at, rows, own, fresh_part, received, w_out, heads, earlier):
    chips = heads // CORES
    width = w_out.shape[1] // heads
    merged = jax.ShapeDtypeStruct((rows, own[0].shape[1]), jnp.bfloat16)
    half = jax.ShapeDtypeStruct((rows, width // 2), jnp.bfloat16)
    merged, *far = call(
        functools.partial(combine_kernel, row_at),
        [merged] + [half] * (2 * chips - 2),
        [*own, *fresh_part, *received, w_out],
        20,
        rows * w_out.size,
        0,
        "combine",
        earlier,
    )
    return merged, [far[2 * k : 2 * k + 2] for k in range(chips - 1)]


def project(merged, w_out, heads):
    block = jax.ShapeDtypeStruct((merged.shape[0], w_out.shape[1] // heads), jnp.bfloat16)
    far, *near = call(
        project_kernel,
        [block] * (1 + heads // CORES),
        [merged, w_out],
        20,
        2 * merged.shape[0] * w_out.size,
        0,
        "project",
    )
    return far, near


def sum_kernel(count, *refs):
    total = refs[0][...].astype(jnp.float32)
    total = total + jnp.concatenate([ref[...] for ref in refs[1:count]], 1).astype(jnp.float32)
    refs[count][...] = total.astype(jnp.bfloat16)


def sum_cores(near, far, earlier):
    return call(
        functools.partial(sum_kernel, 1 + len(far)),
        [jax.ShapeDtypeStruct(near.shape, near.dtype)],
        [near, *far],
        8,
        near.size,
        0,
        "sum_cores",
        earlier,
    )[0]


def finish_kernel(*refs):
    *parts, result = refs
    count = len(parts) // CHUNKS
    rows = parts[0].shape[0]
    for chunk in range(CHUNKS):
        total = 0.0
        for ref in parts[chunk * count : (chunk + 1) * count]:
            total = total + ref[...].astype(jnp.float32)
        result[chunk * rows : (chunk + 1) * rows] = total.astype(jnp.bfloat16)


def finish(parts, earlier):
    rows, width = parts[0].shape
    shape = jax.ShapeDtypeStruct((CHUNKS * rows, width), jnp.bfloat16)
    flops = CHUNKS * rows * width
    return call(finish_kernel, [shape], parts, 8, flops, 0, "finish", earlier)[0]


def shards(
    tokens,
    norm_gain,
    w_query,
    w_key,
    w_value,
    w_out,
    keys_cache,
    values_cache,
    cached_lengths,
    rope_offsets,
):
    rows, width = tokens.shape
    requests = cached_lengths.shape[0]
    groups = lax.axis_size("seq") // requests
    heads = lax.axis_size("head")
    chips = heads // CORES
    chunk_rows = rows // CHUNKS
    gain = norm_gain.reshape(heads, 1, width)

    mark = marks(keys_cache.shape[0])
    tables = rope_tables(cached_lengths, rope_offsets, groups, rows, [mark])
    wide_keys, wide_values = widen(keys_cache, values_cache, mark, cached_lengths, tables[:1])

    def attend_rows(pieces, own, chunk, turn, earlier):
        at = chunk * chunk_rows
        return attend(
            pieces, gain, w_query, tables, wide_keys, wide_values, mark, own, at if own else 0,
            chunk_rows, turn * rows + at, earlier,
        )

    half = chunk_rows // 2
    own, *own_halves = relay([tokens], [rows, chunk_rows, rows - chunk_rows], [mark])
    first = [shifted(own_halves[0], "seq", turn * requests) for turn in range(1, groups)]
    from_chips = list(zip(*[other_chips(part) for part in own_halves]))
    crossed = other_core(own)
    (late,) = relay(own_halves[1:], [rows - chunk_rows], [wide_keys])
    second = [shifted(late, "seq", turn * requests) for turn in range(1, groups)]
    first = [relay([piece], [chunk_rows], [late])[0] for piece in first]
    first_from_chips = [other_chips(piece) for piece in first]
    own_cuts = [relay(pair, [rows, half, half, rows - chunk_rows], first) for pair in from_chips]
    own_pieces = [[own]] + [[cut[0]] for cut in own_cuts] + [[crossed]]
    own_pieces += [[other_core(block) for block in cut[1:]] for cut in own_cuts]
    own_early = [
        blocks if len(blocks) == 1 else blocks[: len(blocks) - 1] for blocks in own_pieces
    ]
    earlier = [cut[0] for cut in own_cuts]

    *own_part, queries = attend_rows(own_early, True, 0, 0, earlier)
    own_queries = [queries]
    earlier = [queries]
    second = [relay([piece], [rows - chunk_rows], earlier)[0] for piece in second]
    second_from_chips = [other_chips(piece) for piece in second]
    earlier = second

    def gather_cores(piece, from_chips, earlier):
        size = piece.shape[0]
        passed = [relay([one], [size, size // 2, size // 2], earlier) for one in from_chips]
        blocks = [[piece]] + [[one[0]] for one in passed] + [[other_core(piece)]]
        blocks += [[other_core(part) for part in one[1:]] for one in passed]
        return blocks, [one[0] for one in passed]

    gathered = []
    for piece, from_chips in zip(first, first_from_chips):
        blocks, passed = gather_cores(piece, from_chips, earlier)
        gathered.append([blocks])
        earlier = earlier + passed
    received = [[] for _ in range(CHUNKS)]
    for turn in range(1, groups):
        (packed,) = attend_rows(gathered[turn - 1][0], False, 0, turn, earlier)
        received[0].append(shifted(packed, "seq", -turn * requests))
        earlier = [packed]
    for blocks, piece, from_chips in zip(gathered, second, second_from_chips):
        along, passed = gather_cores(piece, from_chips, earlier)
        blocks.append(along)
        earlier = earlier + passed
    for turn in range(1, groups):
        (packed,) = attend_rows(gathered[turn - 1][1], False, 1, turn, earlier)
        received[1].append(shifted(packed, "seq", -turn * requests))
        earlier = [packed]
    *late_part, queries = attend_rows(own_pieces, True, 1, 0, earlier)
    own_part += late_part
    own_queries.append(queries)
    new_rows = [fresh(own_pieces, gain, w_key, w_value, tables, 0, [queries])]
    earlier = [new_rows[0][0]]
    for turn in range(1, groups):
        pieces = [sum(blocks, []) for blocks in zip(*gathered[turn - 1])]
        new_rows.append(fresh(pieces, gain, w_key, w_value, tables, turn * rows, earlier))
    new_keys, new_values = zip(*new_rows)
    fresh_part = attend_fresh(requests, own_queries, new_keys, new_values)

    parts = []
    earlier = before_sums = []
    for chunk in range(CHUNKS):
        merged, fars = combine(
            chunk * chunk_rows, chunk_rows, own_part[2 * chunk : 2 * chunk + 2], fresh_part,
            received[chunk], w_out, heads, earlier,
        )
        fars = [[other_core(part) for part in far] for far in fars]
        far, near = project(merged, w_out, heads)
        earlier = [far] + before_sums
        sums = [sum_cores(one, parts_far, earlier) for one, parts_far in zip(near[1:], fars)]
        from_chips = [shifted(one, "head", CORES * k) for k, one in enumerate(sums, 1)]
        parts += [near[0], other_core(far), *from_chips]
        earlier, before_sums = sums, from_chips
    keys_updated, values_updated, done = update(
        cached_lengths, new_keys, new_values, keys_cache, values_cache, earlier
    )
    return (finish(parts, [done]), keys_updated, values_updated)


def solution(mesh):
    return jax.shard_map(
        shards,
        mesh=mesh,
        in_specs=(
            P("seq", "head"),
            P(),
            P(None, "head"),
            P(None, "head"),
            P(None, "head"),
            P("head", None),
            P("seq", "head"),
            P("seq", "head"),
            P(),
            P(),
        ),
        out_specs=(P("seq", "head"), P("seq", "head"), P("seq", "head")),
        check_vma=False,
    )
```

```python
import functools
import math

import jax
import jax.numpy as jnp
from jax import lax
from jax.experimental import pallas as pl
from jax.experimental.pallas import tpu as pltpu
from jax.sharding import PartitionSpec as P

HD = 128
LANES = 128
STAT_ROWS = 8
ROW_TILE = 16
CORES = 2
CHUNKS = 2
COST_WEIGHT = 0.0005
FIRST_MICROS = 2
FLOPS_PER_MICRO = 1_000_000_000
MIB = 1 << 20

rope_base = 500000.0
neg_large = -1e30
log2_scale = math.log2(math.e) / math.sqrt(HD)

VMEM = pl.BlockSpec(memory_space=pltpu.VMEM)
ANY = pl.BlockSpec(memory_space=pl.ANY)


def shifted(shard, axis, by):
    devices = lax.axis_size(axis)
    return lax.ppermute(shard, axis, [(i, (i + by) % devices) for i in range(devices)])


def other_core(shard):
    devices = lax.axis_size("head")
    return lax.ppermute(shard, "head", [(i, i ^ 1) for i in range(devices)])


def other_chips(own):
    chips = lax.axis_size("head") // CORES
    return [shifted(own, "head", CORES * k) for k in range(1, chips)]


def place_of(requests):
    member = lax.axis_index("seq")
    return lax.rem(member, requests), lax.div(member, requests)


def source_of(position_in, turn, groups):
    return lax.rem(position_in + (groups - turn), groups)


def dot(left, right):
    return jnp.dot(left, right, preferred_element_type=jnp.float32)


def dot_transposed(left, right):
    return lax.dot_general(
        left, right, (((1,), (1,)), ((), ())), preferred_element_type=jnp.float32
    )


def call(
    kernel, out_shape, arrays, limit, flops, transcendentals, name, earlier=(),
    scratch=(), micros=0,
):
    moved = sum(a.size * a.dtype.itemsize for a in arrays)
    moved += sum(math.prod(s.shape) * s.dtype.itemsize for s in out_shape)
    read = len(arrays)
    skipped = len(earlier)

    def body(*refs):
        kernel(*refs[:read], *refs[read + skipped :])

    return pl.pallas_call(
        body,
        out_shape=out_shape,
        in_specs=[VMEM] * len(arrays) + [ANY] * skipped,
        out_specs=[VMEM] * len(out_shape),
        scratch_shapes=scratch,
        compiler_params=pltpu.CompilerParams(vmem_limit_bytes=limit * MIB),
        cost_estimate=pl.CostEstimate(
            flops=max(int(COST_WEIGHT * flops), micros * FLOPS_PER_MICRO),
            bytes_accessed=int(COST_WEIGHT * moved),
            transcendentals=int(COST_WEIGHT * transcendentals),
        ),
        name=name,
    )(*arrays, *earlier)


def whole_of(blocks):
    parts = [block[...] for block in blocks]
    return jnp.concatenate(parts, 0) if len(parts) > 1 else parts[0]


def relay_kernel(count, *refs):
    whole = whole_of(refs[:count])
    at = 0
    for ref in refs[count:]:
        ref[...] = whole[at : at + ref.shape[0]]
        at = (at + ref.shape[0]) % whole.shape[0]


def relay(blocks, sizes, earlier):
    shapes = [jax.ShapeDtypeStruct((size, *blocks[0].shape[1:]), blocks[0].dtype) for size in sizes]
    kernel = functools.partial(relay_kernel, len(blocks))
    return call(kernel, shapes, [*blocks], 4, 0, 0, "relay", earlier)


def mark_kernel(mark):
    lane = lax.broadcasted_iota(jnp.int32, mark.shape, 1)
    mark[...] = jnp.where(lane == 0, 1.0, 0.0).astype(mark.dtype)


def marks(rows):
    shape = jax.ShapeDtypeStruct((rows, LANES), jnp.bfloat16)
    return call(mark_kernel, [shape], [], 4, 0, 0, "marks", micros=FIRST_MICROS)[0]


def tables_kernel(groups, lengths_in, offsets_in, cosine, sine, *scratch):
    lengths, offsets, semaphores = scratch
    numbers = [
        pltpu.make_async_copy(lengths_in, lengths, semaphores.at[0]),
        pltpu.make_async_copy(offsets_in, offsets, semaphores.at[1]),
    ]
    for copy in numbers:
        copy.start()
    rows = cosine.shape[0] // groups
    for copy in numbers:
        copy.wait()
    request, position_in = place_of(lengths.shape[0])
    lane = lax.broadcasted_iota(jnp.int32, (rows, LANES), 1)
    row = lax.broadcasted_iota(jnp.int32, (rows, LANES), 0)
    half = lax.rem(lane, HD // 2).astype(jnp.float32)
    frequency = jnp.exp2(half * (-2.0 / HD * math.log2(rope_base)))
    sign = jnp.where(lane < HD // 2, -1.0, 1.0)
    for turn in range(groups):
        first = source_of(position_in, turn, groups) * rows
        first = first + offsets[request] + lengths[request]
        angles = (row + first).astype(jnp.float32) * frequency
        part = slice(turn * rows, (turn + 1) * rows)
        cosine[part] = jnp.cos(angles)
        sine[part] = jnp.sin(angles) * sign


def rope_tables(lengths, offsets, groups, rows, earlier):
    table = jax.ShapeDtypeStruct((groups * rows, LANES), jnp.float32)
    return call(
        functools.partial(tables_kernel, groups),
        [table, table],
        [lengths, offsets],
        12,
        0,
        0,
        "rope_tables",
        earlier,
        [
            pltpu.SMEM(lengths.shape, lengths.dtype),
            pltpu.SMEM(offsets.shape, offsets.dtype),
            pltpu.SemaphoreType.DMA((2,)),
        ],
    )


def widen_kernel(keys, values, mark, lengths_in, wide_keys, wide_values, lengths, semaphore):
    number = pltpu.make_async_copy(lengths_in, lengths, semaphore)
    number.start()
    slots = keys.shape[0]
    heads = keys.shape[1] // HD
    for head in range(heads):
        own = slice(head * HD, (head + 1) * HD)
        wide_keys[head, :, :HD] = keys[:, own]
        wide_values[head, :, :HD] = values[:, own]
        wide_values[head, :, HD:] = mark[:slots]
    number.wait()
    request, position_in = place_of(lengths.shape[0])
    slot = lax.broadcasted_iota(jnp.int32, (slots, LANES), 0) + position_in * slots
    lane = lax.broadcasted_iota(jnp.int32, (slots, LANES), 1)
    bias = jnp.where((lane == 0) & (slot >= lengths[request]), neg_large, 0.0).astype(jnp.bfloat16)
    for head in range(heads):
        wide_keys[head, :, HD:] = bias


def widen(keys, values, mark, lengths, earlier):
    slots, width = keys.shape
    wide = jax.ShapeDtypeStruct((width // HD, slots, HD + LANES), jnp.bfloat16)
    return call(
        widen_kernel,
        [wide, wide],
        [keys, values, mark, lengths],
        12,
        0,
        0,
        "widen_caches",
        earlier,
        [pltpu.SMEM(lengths.shape, lengths.dtype), pltpu.SemaphoreType.DMA],
    )


def rotate(vectors, cosine, sine):
    return vectors * cosine + pltpu.roll(vectors, HD // 2, 1) * sine


def project_normed(pieces, gain, weights):
    heads = gain.shape[0]
    width = gain.shape[2]
    me = lax.axis_index("head")
    squares = 0.0
    sums = [0.0] * len(weights)
    for index, piece in enumerate(pieces):
        owner = lax.rem(me + (heads - CORES * (index % (heads // CORES))), heads)
        if index >= heads // CORES:
            owner = owner ^ 1
        wide = piece.astype(jnp.float32)
        scaled = (wide * gain[owner]).astype(jnp.bfloat16)
        along = pl.ds(pl.multiple_of(owner * width, LANES), width)
        for place, weight in enumerate(weights):
            sums[place] = sums[place] + dot(scaled, weight[along, :])
        squares = squares + jnp.sum(wide * wide, -1, keepdims=True)
    factor = lax.rsqrt(squares / (heads * width) + 1e-05)
    return [total * factor for total in sums]


def stat_rows(columns, rows):
    lane = lax.broadcasted_iota(jnp.int32, (rows, LANES), 1)
    table = jnp.zeros((rows, LANES), jnp.float32)
    for index, column in enumerate(columns):
        table = jnp.where(lane == index, column, table)
    return table.T[:STAT_ROWS]


def split_refs(counts, refs):
    parts = []
    for count in counts:
        parts.append(refs[:count])
        refs = refs[count:]
    return parts, refs


def rows_of(blocks, row_at, rows):
    parts = []
    at = 0
    for block in blocks:
        size = block.shape[0]
        low, high = max(row_at - at, 0), min(row_at + rows - at, size)
        if low < high:
            parts.append(block[low:high])
        at += size
    return jnp.concatenate(parts, 0) if len(parts) > 1 else parts[0]


def attend_kernel(counts, own, row_at, rows, table_at, *refs):
    blocks, refs = split_refs(counts, refs)
    gain, w_query, cosine, sine, wide_keys, wide_values, mark, *outputs = refs
    pieces = [rows_of(one, row_at, rows) for one in blocks]
    (product,) = project_normed(pieces, gain, [w_query])
    cosine = cosine[table_at : table_at + rows]
    sine = sine[table_at : table_at + rows]
    kv_heads = wide_keys.shape[0]
    repeat = product.shape[1] // HD // kv_heads
    queries = [
        (rotate(product[:, head * HD : (head + 1) * HD], cosine, sine) * log2_scale).astype(
            jnp.bfloat16
        )
        for head in range(kv_heads * repeat)
    ]
    step = min(rows, LANES)
    mark = mark[: repeat * step]
    tiles = [(head, at) for head in range(kv_heads) for at in range(0, rows, step)]

    def scores_of(head, at):
        stacked = jnp.concatenate(
            [query[at : at + step] for query in queries[head * repeat : (head + 1) * repeat]], 0
        )
        return dot_transposed(jnp.concatenate([stacked, mark], 1), wide_keys[head])

    columns = {}
    following = scores_of(*tiles[0])
    for index, (head, at) in enumerate(tiles):
        scores = following
        if index + 1 < len(tiles):
            following = scores_of(*tiles[index + 1])
        largest = jnp.max(scores, -1, keepdims=True)
        weights = jnp.exp2(scores - largest).astype(jnp.bfloat16)
        summed = dot(weights, wide_values[head])
        denominator = summed[:, HD : HD + 1]
        result = summed[:, :HD] / denominator
        logs = largest + jnp.log2(denominator)
        for turn in range(repeat):
            part = slice(turn * step, (turn + 1) * step)
            to = slice((head * repeat + turn) * HD, (head * repeat + turn + 1) * HD)
            outputs[0][at : at + step, to] = result[part].astype(outputs[0].dtype)
            columns.setdefault(head * repeat + turn, []).append(logs[part])
    stats = stat_rows([jnp.concatenate(parts, 0) for parts in columns.values()], rows)
    if own:
        outputs[1][...] = stats
        outputs[2][...] = jnp.concatenate(queries, 1)
        return
    outputs[0][rows:] = jnp.zeros((ROW_TILE, outputs[0].shape[1]), jnp.bfloat16)
    rest = jnp.concatenate([stats, jnp.zeros((ROW_TILE - STAT_ROWS, rows), jnp.float32)], 0)
    for part in range(3):
        rounded = rest.astype(jnp.bfloat16)
        outputs[0][rows:, part * rows : (part + 1) * rows] = rounded
        rest = rest - rounded.astype(jnp.float32)


def attend(
    pieces, gain, w_query, tables, wide_keys, wide_values, mark, own, row_at, rows, table_at,
    earlier,
):
    counts = [len(blocks) for blocks in pieces]
    flat = [block for blocks in pieces for block in blocks]
    out_width = w_query.shape[1]
    slots = wide_keys.shape[1]
    if own:
        out_shape = [
            jax.ShapeDtypeStruct((rows, out_width), jnp.float32),
            jax.ShapeDtypeStruct((STAT_ROWS, rows), jnp.float32),
            jax.ShapeDtypeStruct((rows, out_width), jnp.bfloat16),
        ]
    else:
        out_shape = [jax.ShapeDtypeStruct((rows + ROW_TILE, out_width), jnp.bfloat16)]
    return call(
        functools.partial(attend_kernel, counts, own, row_at, rows, table_at),
        out_shape,
        [*flat, gain, w_query, *tables, wide_keys, wide_values, mark],
        28,
        2 * rows * out_width * (w_query.shape[0] + 4 * slots),
        rows * out_width // HD * slots,
        "attend_own" if own else "attend_partner",
        earlier,
    )


def fresh_kernel(counts, table_at, *refs):
    blocks, refs = split_refs(counts, refs)
    gain, w_key, w_value, cosine, sine, new_keys, new_values = refs
    rows = new_keys.shape[0]
    pieces = [whole_of(one) for one in blocks]
    keys, values = project_normed(pieces, gain, [w_key, w_value])
    cosine = cosine[table_at : table_at + rows]
    sine = sine[table_at : table_at + rows]
    for head in range(keys.shape[1] // HD):
        own = slice(head * HD, (head + 1) * HD)
        new_keys[:, own] = rotate(keys[:, own], cosine, sine).astype(jnp.bfloat16)
    new_values[...] = values.astype(jnp.bfloat16)


def fresh(pieces, gain, w_key, w_value, tables, table_at, earlier):
    flat = [block for blocks in pieces for block in blocks]
    rows = sum(block.shape[0] for block in pieces[0])
    shape = jax.ShapeDtypeStruct((rows, w_key.shape[1]), jnp.bfloat16)
    return call(
        functools.partial(fresh_kernel, [len(blocks) for blocks in pieces], table_at),
        [shape, shape],
        [*flat, gain, w_key, w_value, *tables],
        20,
        4 * rows * w_key.size,
        0,
        "fresh_kv",
        earlier,
    )


def write_rows(target, fresh_rows, first):
    rows = fresh_rows.shape[0]
    slab_rows = target.shape[0]
    span = rows + ROW_TILE
    start = jnp.clip(first, 0, slab_rows - span)
    start = start - lax.rem(start, ROW_TILE)
    window = pl.ds(pl.multiple_of(start, ROW_TILE), span)
    shift = start - first
    place = lax.broadcasted_iota(jnp.int32, (span, rows), 0) + shift
    chosen = place == lax.broadcasted_iota(jnp.int32, (span, rows), 1)
    moved = dot(chosen.astype(jnp.bfloat16), fresh_rows)
    row = lax.broadcasted_iota(jnp.int32, (span, target.shape[1]), 0) + shift
    inside = (row >= 0) & (row < rows)
    old = target[window, :].astype(jnp.float32)
    target[window, :] = jnp.where(inside, moved, old).astype(jnp.bfloat16)


def attend_fresh_kernel(groups, requests, *refs):
    query_refs, refs = refs[:CHUNKS], refs[CHUNKS:]
    key_refs, value_refs, refs = refs[:groups], refs[groups : 2 * groups], refs[2 * groups :]
    partial, stats = refs
    position_in = place_of(requests)[1]
    rows, width = partial.shape
    kv_heads = key_refs[0].shape[1] // HD
    repeat = width // HD // kv_heads
    queries = whole_of(query_refs)
    token = lax.broadcasted_iota(jnp.int32, (rows, rows), 0)
    within = lax.broadcasted_iota(jnp.int32, (rows, rows), 1)
    causal = jnp.where(within <= token, 0.0, neg_large)
    causal = jnp.concatenate([causal] * repeat, 0)
    lane = lax.broadcasted_iota(jnp.int32, (rows, LANES), 1)
    ones = jnp.where(lane == 0, 1.0, 0.0).astype(jnp.bfloat16)
    hidden = [jnp.zeros((rows, LANES), jnp.bfloat16)]
    for turn in range(1, groups):
        later = source_of(position_in, turn, groups) > position_in
        hidden.append(jnp.where((lane == 0) & later, neg_large, 0.0).astype(jnp.bfloat16))
    columns = []
    for head in range(kv_heads):
        own = [
            slice((head * repeat + turn) * HD, (head * repeat + turn + 1) * HD)
            for turn in range(repeat)
        ]
        shared = slice(head * HD, (head + 1) * HD)
        stacked = jnp.concatenate([queries[:, one] for one in own], 0)
        stacked = jnp.concatenate([stacked, jnp.concatenate([ones] * repeat, 0)], 1)
        scores = [
            dot_transposed(stacked, jnp.concatenate([ref[:, shared], bias], 1))
            for ref, bias in zip(key_refs, hidden)
        ]
        scores = jnp.concatenate([scores[0] + causal] + scores[1:], 1)
        largest = jnp.max(scores, -1, keepdims=True)
        weights = jnp.exp2(scores - largest).astype(jnp.bfloat16)
        wide_values = [jnp.concatenate([ref[:, shared], ones], 1) for ref in value_refs]
        summed = dot(weights, jnp.concatenate(wide_values, 0))
        denominator = summed[:, HD : HD + 1]
        result = summed[:, :HD] / denominator
        logs = largest + jnp.log2(denominator)
        for turn, one in enumerate(own):
            part = slice(turn * rows, (turn + 1) * rows)
            partial[:, one] = result[part]
            columns.append(logs[part])
    stats[...] = stat_rows(columns, rows)


def attend_fresh(requests, queries, new_keys, new_values):
    groups = len(new_keys)
    rows = new_keys[0].shape[0]
    width = queries[0].shape[1]
    return call(
        functools.partial(attend_fresh_kernel, groups, requests),
        [
            jax.ShapeDtypeStruct((rows, width), jnp.float32),
            jax.ShapeDtypeStruct((STAT_ROWS, rows), jnp.float32),
        ],
        [*queries, *new_keys, *new_values],
        24,
        4 * rows * width * rows * groups,
        rows * width // HD * rows * groups,
        "attend_fresh",
    )


def update_kernel(groups, *refs):
    key_refs, value_refs, refs = refs[:groups], refs[groups : 2 * groups], refs[2 * groups :]
    keys, values, lengths_in, keys_updated, values_updated, done, lengths, semaphore = refs
    number = pltpu.make_async_copy(lengths_in, lengths, semaphore)
    number.start()
    keys_updated[...] = keys[...]
    values_updated[...] = values[...]
    done[...] = jnp.zeros(done.shape, done.dtype)
    number.wait()
    request, position_in = place_of(lengths.shape[0])
    rows = key_refs[0].shape[0]
    for turn in range(groups):
        source = source_of(position_in, turn, groups)
        first = lengths[request] + source * rows - position_in * keys.shape[0]
        write_rows(keys_updated, key_refs[turn][...], first)
        write_rows(values_updated, value_refs[turn][...], first)


def update(lengths, new_keys, new_values, keys, values, earlier):
    groups = len(new_keys)
    slab = jax.ShapeDtypeStruct(keys.shape, keys.dtype)
    return call(
        functools.partial(update_kernel, groups),
        [slab, slab, jax.ShapeDtypeStruct((STAT_ROWS, LANES), jnp.float32)],
        [*new_keys, *new_values, keys, values, lengths],
        20,
        4 * new_keys[0].size * new_keys[0].shape[0] * groups,
        0,
        "update_caches",
        earlier,
        [pltpu.SMEM(lengths.shape, lengths.dtype), pltpu.SemaphoreType.DMA],
    )


def combine_kernel(row_at, own_partial, own_stats, fresh_partial, fresh_stats, *refs):
    heads = lax.axis_size("head")
    chips = heads // CORES
    outputs = 2 * chips - 1
    received = refs[: -1 - outputs]
    w_out, merged_rows = refs[-1 - outputs], refs[-outputs]
    far = refs[1 - outputs :]
    width = own_partial.shape[1]
    rows = merged_rows.shape[0]
    part = slice(row_at, row_at + rows)
    padding = jnp.zeros((LANES - STAT_ROWS, rows), jnp.float32)
    stats = [own_stats[...], fresh_stats[:, part]]
    for ref in received:
        stats.append(
            sum(
                ref[rows:, turn * rows : (turn + 1) * rows].astype(jnp.float32)
                for turn in range(3)
            )[:STAT_ROWS]
        )
    logs = [jnp.concatenate([stat, padding], 0).T for stat in stats]
    largest = functools.reduce(jnp.maximum, logs)
    shares = [jnp.exp2(log - largest) for log in logs]
    total = functools.reduce(jnp.add, shares)
    shares = [share / total for share in shares]
    attended = []
    for head in range(width // HD):
        own = slice(head * HD, (head + 1) * HD)
        column = slice(head, head + 1)
        merged = own_partial[:, own] * shares[0][:, column]
        merged = merged + fresh_partial[part, own] * shares[1][:, column]
        for ref, share in zip(received, shares[2:]):
            merged = merged + ref[:rows, own].astype(jnp.float32) * share[:, column]
        attended.append(merged.astype(jnp.bfloat16))
    attended = jnp.concatenate(attended, 1)
    merged_rows[...] = attended
    for ahead in range(1, chips):
        result = block_product(attended, w_out, ahead, 1)
        middle = result.shape[1] // 2
        far[2 * ahead - 2][...] = result[:, :middle]
        far[2 * ahead - 1][...] = result[:, middle:]


def block_product(attended, w_out, ahead, flip):
    heads = lax.axis_size("head")
    block_width = w_out.shape[1] // heads
    block = lax.rem(lax.axis_index("head") + CORES * ahead, heads) ^ flip
    along = pl.ds(pl.multiple_of(block * block_width, LANES), block_width)
    return dot(attended, w_out[:, along]).astype(jnp.bfloat16)


def project_kernel(merged_rows, w_out, far, *near):
    attended = merged_rows[...]
    far[...] = block_product(attended, w_out, 0, 1)
    for ahead, target in enumerate(near):
        target[...] = block_product(attended, w_out, ahead, 0)


def combine(row_at, rows, own, fresh_part, received, w_out, heads, earlier):
    chips = heads // CORES
    width = w_out.shape[1] // heads
    merged = jax.ShapeDtypeStruct((rows, own[0].shape[1]), jnp.bfloat16)
    half = jax.ShapeDtypeStruct((rows, width // 2), jnp.bfloat16)
    merged, *far = call(
        functools.partial(combine_kernel, row_at),
        [merged] + [half] * (2 * chips - 2),
        [*own, *fresh_part, *received, w_out],
        20,
        rows * w_out.size,
        0,
        "combine",
        earlier,
    )
    return merged, [far[2 * k : 2 * k + 2] for k in range(chips - 1)]


def project(merged, w_out, heads):
    block = jax.ShapeDtypeStruct((merged.shape[0], w_out.shape[1] // heads), jnp.bfloat16)
    far, *near = call(
        project_kernel,
        [block] * (1 + heads // CORES),
        [merged, w_out],
        20,
        2 * merged.shape[0] * w_out.size,
        0,
        "project",
    )
    return far, near


def sum_kernel(count, *refs):
    total = refs[0][...].astype(jnp.float32)
    total = total + jnp.concatenate([ref[...] for ref in refs[1:count]], 1).astype(jnp.float32)
    refs[count][...] = total.astype(jnp.bfloat16)


def sum_cores(near, far, earlier):
    return call(
        functools.partial(sum_kernel, 1 + len(far)),
        [jax.ShapeDtypeStruct(near.shape, near.dtype)],
        [near, *far],
        8,
        near.size,
        0,
        "sum_cores",
        earlier,
    )[0]


def finish_kernel(*refs):
    *parts, result = refs
    count = len(parts) // CHUNKS
    rows = parts[0].shape[0]
    for chunk in range(CHUNKS):
        total = 0.0
        for ref in parts[chunk * count : (chunk + 1) * count]:
            total = total + ref[...].astype(jnp.float32)
        result[chunk * rows : (chunk + 1) * rows] = total.astype(jnp.bfloat16)


def finish(parts, earlier):
    rows, width = parts[0].shape
    shape = jax.ShapeDtypeStruct((CHUNKS * rows, width), jnp.bfloat16)
    flops = CHUNKS * rows * width
    return call(finish_kernel, [shape], parts, 8, flops, 0, "finish", earlier)[0]


def shards(
    tokens,
    norm_gain,
    w_query,
    w_key,
    w_value,
    w_out,
    keys_cache,
    values_cache,
    cached_lengths,
    rope_offsets,
):
    rows, width = tokens.shape
    requests = cached_lengths.shape[0]
    groups = lax.axis_size("seq") // requests
    heads = lax.axis_size("head")
    chips = heads // CORES
    chunk_rows = rows // CHUNKS
    gain = norm_gain.reshape(heads, 1, width)

    mark = marks(keys_cache.shape[0])
    tables = rope_tables(cached_lengths, rope_offsets, groups, rows, [mark])
    wide_keys, wide_values = widen(keys_cache, values_cache, mark, cached_lengths, tables[:1])

    def attend_rows(pieces, own, chunk, turn, earlier):
        at = chunk * chunk_rows
        return attend(
            pieces, gain, w_query, tables, wide_keys, wide_values, mark, own, at if own else 0,
            chunk_rows, turn * rows + at, earlier,
        )

    half = chunk_rows // 2
    from_chips = other_chips(tokens)
    crossed = other_core(tokens)
    own, early, late = relay([tokens], [rows, chunk_rows, rows - chunk_rows], [])
    first = [shifted(early, "seq", turn * requests) for turn in range(1, groups)]
    (late,) = relay([late], [rows - chunk_rows], from_chips + [wide_keys])
    second = [shifted(late, "seq", turn * requests) for turn in range(1, groups)]
    own_cuts = [relay([piece], [rows, half, half, rows - chunk_rows], [late]) for piece in from_chips]
    own_pieces = [[own]] + [[cut[0]] for cut in own_cuts] + [[crossed]]
    own_pieces += [[other_core(block) for block in cut[1:]] for cut in own_cuts]
    own_early = [
        blocks if len(blocks) == 1 else blocks[: len(blocks) - 1] for blocks in own_pieces
    ]
    earlier = [cut[0] for cut in own_cuts]
    first = [relay([piece], [chunk_rows], earlier)[0] for piece in first]
    first_from_chips = [other_chips(piece) for piece in first]
    *own_part, queries = attend_rows(own_early, True, 0, 0, first)
    own_queries = [queries]
    new_rows = [fresh(own_pieces, gain, w_key, w_value, tables, 0, [queries])]
    earlier = [new_rows[0][0]]
    second = [relay([piece], [rows - chunk_rows], earlier)[0] for piece in second]
    second_from_chips = [other_chips(piece) for piece in second]
    earlier = second

    def gather_cores(piece, from_chips, earlier):
        size = piece.shape[0]
        passed = [relay([one], [size, size // 2, size // 2], earlier) for one in from_chips]
        blocks = [[piece]] + [[one[0]] for one in passed] + [[other_core(piece)]]
        blocks += [[other_core(part) for part in one[1:]] for one in passed]
        return blocks, [one[0] for one in passed]

    gathered = []
    for piece, from_chips in zip(first, first_from_chips):
        blocks, passed = gather_cores(piece, from_chips, earlier)
        gathered.append([blocks])
        earlier = earlier + passed
    received = [[] for _ in range(CHUNKS)]
    for turn in range(1, groups):
        (packed,) = attend_rows(gathered[turn - 1][0], False, 0, turn, earlier)
        received[0].append(shifted(packed, "seq", -turn * requests))
        earlier = [packed]
    *late_part, queries = attend_rows(own_pieces, True, 1, 0, earlier)
    own_part += late_part
    own_queries.append(queries)
    earlier = [queries]
    for blocks, piece, from_chips in zip(gathered, second, second_from_chips):
        along, passed = gather_cores(piece, from_chips, earlier)
        blocks.append(along)
        earlier = earlier + passed
    for turn in range(1, groups):
        (packed,) = attend_rows(gathered[turn - 1][1], False, 1, turn, earlier)
        received[1].append(shifted(packed, "seq", -turn * requests))
        earlier = [packed]
    for turn in range(1, groups):
        pieces = [sum(blocks, []) for blocks in zip(*gathered[turn - 1])]
        new_rows.append(fresh(pieces, gain, w_key, w_value, tables, turn * rows, earlier))
    new_keys, new_values = zip(*new_rows)
    fresh_part = attend_fresh(requests, own_queries, new_keys, new_values)

    parts = []
    earlier = before_sums = []
    for chunk in range(CHUNKS):
        merged, fars = combine(
            chunk * chunk_rows, chunk_rows, own_part[2 * chunk : 2 * chunk + 2], fresh_part,
            received[chunk], w_out, heads, earlier,
        )
        fars = [[other_core(part) for part in far] for far in fars]
        far, near = project(merged, w_out, heads)
        earlier = [far] + before_sums
        sums = [sum_cores(one, parts_far, earlier) for one, parts_far in zip(near[1:], fars)]
        from_chips = [shifted(one, "head", CORES * k) for k, one in enumerate(sums, 1)]
        parts += [near[0], other_core(far), *from_chips]
        earlier, before_sums = sums, from_chips
    keys_updated, values_updated, done = update(
        cached_lengths, new_keys, new_values, keys_cache, values_cache, earlier
    )
    return (finish(parts, [done]), keys_updated, values_updated)


def solution(mesh):
    return jax.shard_map(
        shards,
        mesh=mesh,
        in_specs=(
            P("seq", "head"),
            P(),
            P(None, "head"),
            P(None, "head"),
            P(None, "head"),
            P("head", None),
            P("seq", "head"),
            P("seq", "head"),
            P(),
            P(),
        ),
        out_specs=(P("seq", "head"), P("seq", "head"), P("seq", "head")),
        check_vma=False,
    )
```

```python
import functools
import math

import jax
import jax.numpy as jnp
from jax import lax
from jax.experimental import pallas as pl
from jax.experimental.pallas import tpu as pltpu
from jax.sharding import PartitionSpec as P

HD = 128
LANES = 128
STAT_ROWS = 8
ROW_TILE = 16
CORES = 2
CHUNKS = 2
COST_WEIGHT = 0.0005
FIRST_MICROS = 2
FLOPS_PER_MICRO = 1_000_000_000
MIB = 1 << 20

rope_base = 500000.0
neg_large = -1e30
log2_scale = math.log2(math.e) / math.sqrt(HD)

VMEM = pl.BlockSpec(memory_space=pltpu.VMEM)
ANY = pl.BlockSpec(memory_space=pl.ANY)


def shifted(shard, axis, by):
    devices = lax.axis_size(axis)
    return lax.ppermute(shard, axis, [(i, (i + by) % devices) for i in range(devices)])


def other_core(shard):
    devices = lax.axis_size("head")
    return lax.ppermute(shard, "head", [(i, i ^ 1) for i in range(devices)])


def other_chips(own):
    chips = lax.axis_size("head") // CORES
    return [shifted(own, "head", CORES * k) for k in range(1, chips)]


def place_of(requests):
    member = lax.axis_index("seq")
    return lax.rem(member, requests), lax.div(member, requests)


def source_of(position_in, turn, groups):
    return lax.rem(position_in + (groups - turn), groups)


def dot(left, right):
    return jnp.dot(left, right, preferred_element_type=jnp.float32)


def dot_transposed(left, right):
    return lax.dot_general(
        left, right, (((1,), (1,)), ((), ())), preferred_element_type=jnp.float32
    )


def call(
    kernel, out_shape, arrays, limit, flops, transcendentals, name, earlier=(),
    scratch=(), micros=0,
):
    moved = sum(a.size * a.dtype.itemsize for a in arrays)
    moved += sum(math.prod(s.shape) * s.dtype.itemsize for s in out_shape)
    read = len(arrays)
    skipped = len(earlier)

    def body(*refs):
        kernel(*refs[:read], *refs[read + skipped :])

    return pl.pallas_call(
        body,
        out_shape=out_shape,
        in_specs=[VMEM] * len(arrays) + [ANY] * skipped,
        out_specs=[VMEM] * len(out_shape),
        scratch_shapes=scratch,
        compiler_params=pltpu.CompilerParams(vmem_limit_bytes=limit * MIB),
        cost_estimate=pl.CostEstimate(
            flops=max(int(COST_WEIGHT * flops), micros * FLOPS_PER_MICRO),
            bytes_accessed=int(COST_WEIGHT * moved),
            transcendentals=int(COST_WEIGHT * transcendentals),
        ),
        name=name,
    )(*arrays, *earlier)


def whole_of(blocks):
    parts = [block[...] for block in blocks]
    return jnp.concatenate(parts, 0) if len(parts) > 1 else parts[0]


def relay_kernel(count, *refs):
    whole = whole_of(refs[:count])
    at = 0
    for ref in refs[count:]:
        ref[...] = whole[at : at + ref.shape[0]]
        at = (at + ref.shape[0]) % whole.shape[0]


def relay(blocks, sizes, earlier):
    shapes = [jax.ShapeDtypeStruct((size, *blocks[0].shape[1:]), blocks[0].dtype) for size in sizes]
    kernel = functools.partial(relay_kernel, len(blocks))
    return call(kernel, shapes, [*blocks], 4, 0, 0, "relay", earlier)


def mark_kernel(mark):
    lane = lax.broadcasted_iota(jnp.int32, mark.shape, 1)
    mark[...] = jnp.where(lane == 0, 1.0, 0.0).astype(mark.dtype)


def marks(rows):
    shape = jax.ShapeDtypeStruct((rows, LANES), jnp.bfloat16)
    return call(mark_kernel, [shape], [], 4, 0, 0, "marks", micros=FIRST_MICROS)[0]


def tables_kernel(groups, lengths_in, offsets_in, cosine, sine, *scratch):
    lengths, offsets, semaphores = scratch
    numbers = [
        pltpu.make_async_copy(lengths_in, lengths, semaphores.at[0]),
        pltpu.make_async_copy(offsets_in, offsets, semaphores.at[1]),
    ]
    for copy in numbers:
        copy.start()
    rows = cosine.shape[0] // groups
    for copy in numbers:
        copy.wait()
    request, position_in = place_of(lengths.shape[0])
    lane = lax.broadcasted_iota(jnp.int32, (rows, LANES), 1)
    row = lax.broadcasted_iota(jnp.int32, (rows, LANES), 0)
    half = lax.rem(lane, HD // 2).astype(jnp.float32)
    frequency = jnp.exp2(half * (-2.0 / HD * math.log2(rope_base)))
    sign = jnp.where(lane < HD // 2, -1.0, 1.0)
    for turn in range(groups):
        first = source_of(position_in, turn, groups) * rows
        first = first + offsets[request] + lengths[request]
        angles = (row + first).astype(jnp.float32) * frequency
        part = slice(turn * rows, (turn + 1) * rows)
        cosine[part] = jnp.cos(angles)
        sine[part] = jnp.sin(angles) * sign


def rope_tables(lengths, offsets, groups, rows, earlier):
    table = jax.ShapeDtypeStruct((groups * rows, LANES), jnp.float32)
    return call(
        functools.partial(tables_kernel, groups),
        [table, table],
        [lengths, offsets],
        12,
        0,
        0,
        "rope_tables",
        earlier,
        [
            pltpu.SMEM(lengths.shape, lengths.dtype),
            pltpu.SMEM(offsets.shape, offsets.dtype),
            pltpu.SemaphoreType.DMA((2,)),
        ],
    )


def widen_kernel(keys, values, mark, lengths_in, wide_keys, wide_values, lengths, semaphore):
    number = pltpu.make_async_copy(lengths_in, lengths, semaphore)
    number.start()
    slots = keys.shape[0]
    heads = keys.shape[1] // HD
    for head in range(heads):
        own = slice(head * HD, (head + 1) * HD)
        wide_keys[head, :, :HD] = keys[:, own]
        wide_values[head, :, :HD] = values[:, own]
        wide_values[head, :, HD:] = mark[:slots]
    number.wait()
    request, position_in = place_of(lengths.shape[0])
    slot = lax.broadcasted_iota(jnp.int32, (slots, LANES), 0) + position_in * slots
    lane = lax.broadcasted_iota(jnp.int32, (slots, LANES), 1)
    bias = jnp.where((lane == 0) & (slot >= lengths[request]), neg_large, 0.0).astype(jnp.bfloat16)
    for head in range(heads):
        wide_keys[head, :, HD:] = bias


def widen(keys, values, mark, lengths, earlier):
    slots, width = keys.shape
    wide = jax.ShapeDtypeStruct((width // HD, slots, HD + LANES), jnp.bfloat16)
    return call(
        widen_kernel,
        [wide, wide],
        [keys, values, mark, lengths],
        12,
        0,
        0,
        "widen_caches",
        earlier,
        [pltpu.SMEM(lengths.shape, lengths.dtype), pltpu.SemaphoreType.DMA],
    )


def rotate(vectors, cosine, sine):
    return vectors * cosine + pltpu.roll(vectors, HD // 2, 1) * sine


def project_normed(pieces, gain, weights):
    heads = gain.shape[0]
    width = gain.shape[2]
    me = lax.axis_index("head")
    squares = 0.0
    sums = [0.0] * len(weights)
    for index, piece in enumerate(pieces):
        owner = lax.rem(me + (heads - CORES * (index % (heads // CORES))), heads)
        if index >= heads // CORES:
            owner = owner ^ 1
        wide = piece.astype(jnp.float32)
        scaled = (wide * gain[owner]).astype(jnp.bfloat16)
        along = pl.ds(pl.multiple_of(owner * width, LANES), width)
        for place, weight in enumerate(weights):
            sums[place] = sums[place] + dot(scaled, weight[along, :])
        squares = squares + jnp.sum(wide * wide, -1, keepdims=True)
    factor = lax.rsqrt(squares / (heads * width) + 1e-05)
    return [total * factor for total in sums]


def stat_rows(columns, rows):
    lane = lax.broadcasted_iota(jnp.int32, (rows, LANES), 1)
    table = jnp.zeros((rows, LANES), jnp.float32)
    for index, column in enumerate(columns):
        table = jnp.where(lane == index, column, table)
    return table.T[:STAT_ROWS]


def split_refs(counts, refs):
    parts = []
    for count in counts:
        parts.append(refs[:count])
        refs = refs[count:]
    return parts, refs


def rows_of(blocks, row_at, rows):
    parts = []
    at = 0
    for block in blocks:
        size = block.shape[0]
        low, high = max(row_at - at, 0), min(row_at + rows - at, size)
        if low < high:
            parts.append(block[low:high])
        at += size
    return jnp.concatenate(parts, 0) if len(parts) > 1 else parts[0]


def head_queries(product, cosine, sine):
    return [
        (rotate(product[:, at : at + HD], cosine, sine) * log2_scale).astype(jnp.bfloat16)
        for at in range(0, product.shape[1], HD)
    ]


def weigh(scores, values):
    largest = functools.reduce(
        jnp.maximum, [jnp.max(score, -1, keepdims=True) for score in scores]
    )
    summed = 0.0
    for score, value in zip(scores, values):
        weights = jnp.exp2(score - largest).astype(jnp.bfloat16)
        summed = summed + dot(weights, value)
    denominator = summed[:, HD : HD + 1]
    return summed[:, :HD] / denominator, largest + jnp.log2(denominator)


def attend_heads(queries, wide_keys, wide_values, mark, fresh, store):
    rows = queries.shape[0]
    kv_heads = wide_keys.shape[0]
    repeat = queries.shape[1] // HD // kv_heads
    marked = mark[: repeat * rows]
    scores = []
    values = []
    for head in range(kv_heads):
        shared = slice(head * HD, (head + 1) * HD)
        stacked = jnp.concatenate(
            [
                queries[:, (head * repeat + turn) * HD : (head * repeat + turn + 1) * HD]
                for turn in range(repeat)
            ],
            0,
        )
        wide = jnp.concatenate([stacked, marked], 1)
        found = [dot_transposed(wide, wide_keys[head])]
        held = [wide_values[head]]
        for keys, new_values, column, bias in fresh:
            if bias is None:
                added = jnp.concatenate([keys[:, shared], column], 1)
                found.append(dot_transposed(wide, added))
            else:
                bias = jnp.concatenate([bias] * repeat, 0)
                found.append(dot_transposed(stacked, keys[:, shared]) + bias)
            held.append(jnp.concatenate([new_values[:, shared], mark[: keys.shape[0]]], 1))
        scores.append(found)
        values.append(held)
    columns = []
    for head in range(kv_heads):
        result, logs = weigh(scores[head], values[head])
        for turn in range(repeat):
            part = slice(turn * rows, (turn + 1) * rows)
            store((head * repeat + turn) * HD, result[part])
            columns.append(logs[part])
    return stat_rows(columns, rows)


def attend_kernel(counts, groups, requests, turn, row_at, rows, table_at, *refs):
    blocks, refs = split_refs(counts, refs)
    gain, w_query, cosine, sine, wide_keys, wide_values, mark, keys, values, *outputs = refs
    pieces = [rows_of(one, row_at, rows) for one in blocks]
    (product,) = project_normed(pieces, gain, [w_query])
    part = slice(table_at, table_at + rows)
    queries = jnp.concatenate(head_queries(product, cosine[part], sine[part]), 1)
    target = outputs[0]

    def store(at, result):
        target[:rows, at : at + HD] = result.astype(target.dtype)

    if turn:
        position_in = place_of(requests)[1]
        hidden = position_in > source_of(position_in, turn, groups)
        bias = mark[: keys.shape[0]].astype(jnp.float32) * neg_large
        bias = jnp.where(hidden, bias, 0.0).astype(jnp.bfloat16)
        fresh = [(keys[...], values[...], bias, None)]
    else:
        fresh = []
        if row_at:
            fresh.append((keys[:row_at], values[:row_at], jnp.zeros((row_at, LANES), jnp.bfloat16), None))
        token = lax.broadcasted_iota(jnp.int32, (rows, rows), 0)
        within = lax.broadcasted_iota(jnp.int32, (rows, rows), 1)
        causal = jnp.where(within <= token, 0.0, neg_large)
        own = slice(row_at, row_at + rows)
        fresh.append((keys[own], values[own], None, causal))
    stats = attend_heads(queries, wide_keys, wide_values, mark, fresh, store)
    if not turn:
        outputs[1][...] = stats
        return
    target[rows:] = jnp.zeros((ROW_TILE, target.shape[1]), target.dtype)
    rest = jnp.concatenate([stats, jnp.zeros((ROW_TILE - STAT_ROWS, rows), jnp.float32)], 0)
    for index in range(3):
        rounded = rest.astype(target.dtype)
        target[rows:, index * rows : (index + 1) * rows] = rounded
        rest = rest - rounded.astype(jnp.float32)


def attend(
    pieces, gain, w_query, tables, wides, mark, new_rows, place, turn, row_at, rows, table_at,
    earlier,
):
    counts = [len(blocks) for blocks in pieces]
    flat = [block for blocks in pieces for block in blocks]
    width = w_query.shape[1]
    slots = wides[0].shape[1]
    if turn:
        out_shape = [jax.ShapeDtypeStruct((rows + ROW_TILE, width), jnp.bfloat16)]
    else:
        out_shape = [
            jax.ShapeDtypeStruct((rows, width), jnp.float32),
            jax.ShapeDtypeStruct((STAT_ROWS, rows), jnp.float32),
        ]
    return call(
        functools.partial(attend_kernel, counts, *place, turn, row_at, rows, table_at),
        out_shape,
        [*flat, gain, w_query, *tables, *wides, mark, *new_rows],
        28,
        2 * rows * width * (w_query.shape[0] + 4 * slots),
        rows * width // HD * slots,
        "attend_partner" if turn else "attend_own",
        earlier,
    )


def fresh_kernel(counts, table_at, *refs):
    blocks, refs = split_refs(counts, refs)
    gain, w_key, w_value, cosine, sine, new_keys, new_values = refs
    rows = new_keys.shape[0]
    pieces = [whole_of(one) for one in blocks]
    keys, values = project_normed(pieces, gain, [w_key, w_value])
    cosine = cosine[table_at : table_at + rows]
    sine = sine[table_at : table_at + rows]
    for head in range(keys.shape[1] // HD):
        own = slice(head * HD, (head + 1) * HD)
        new_keys[:, own] = rotate(keys[:, own], cosine, sine).astype(jnp.bfloat16)
    new_values[...] = values.astype(jnp.bfloat16)


def fresh(pieces, gain, w_key, w_value, tables, table_at, earlier):
    flat = [block for blocks in pieces for block in blocks]
    rows = sum(block.shape[0] for block in pieces[0])
    shape = jax.ShapeDtypeStruct((rows, w_key.shape[1]), jnp.bfloat16)
    return call(
        functools.partial(fresh_kernel, [len(blocks) for blocks in pieces], table_at),
        [shape, shape],
        [*flat, gain, w_key, w_value, *tables],
        20,
        4 * rows * w_key.size,
        0,
        "fresh_kv",
        earlier,
    )


def write_rows(target, fresh_rows, first):
    rows = fresh_rows.shape[0]
    slab_rows = target.shape[0]
    span = rows + ROW_TILE
    start = jnp.clip(first, 0, slab_rows - span)
    start = start - lax.rem(start, ROW_TILE)
    window = pl.ds(pl.multiple_of(start, ROW_TILE), span)
    shift = start - first
    place = lax.broadcasted_iota(jnp.int32, (span, rows), 0) + shift
    chosen = place == lax.broadcasted_iota(jnp.int32, (span, rows), 1)
    moved = dot(chosen.astype(jnp.bfloat16), fresh_rows)
    row = lax.broadcasted_iota(jnp.int32, (span, target.shape[1]), 0) + shift
    inside = (row >= 0) & (row < rows)
    old = target[window, :].astype(jnp.float32)
    target[window, :] = jnp.where(inside, moved, old).astype(jnp.bfloat16)


def update_kernel(groups, *refs):
    key_refs, value_refs, refs = refs[:groups], refs[groups : 2 * groups], refs[2 * groups :]
    keys, values, lengths_in, keys_updated, values_updated, done, lengths, semaphore = refs
    number = pltpu.make_async_copy(lengths_in, lengths, semaphore)
    number.start()
    keys_updated[...] = keys[...]
    values_updated[...] = values[...]
    done[...] = jnp.zeros(done.shape, done.dtype)
    number.wait()
    request, position_in = place_of(lengths.shape[0])
    rows = key_refs[0].shape[0]
    for turn in range(groups):
        source = source_of(position_in, turn, groups)
        first = lengths[request] + source * rows - position_in * keys.shape[0]
        write_rows(keys_updated, key_refs[turn][...], first)
        write_rows(values_updated, value_refs[turn][...], first)


def update(lengths, new_keys, new_values, keys, values, earlier):
    groups = len(new_keys)
    slab = jax.ShapeDtypeStruct(keys.shape, keys.dtype)
    return call(
        functools.partial(update_kernel, groups),
        [slab, slab, jax.ShapeDtypeStruct((STAT_ROWS, LANES), jnp.float32)],
        [*new_keys, *new_values, keys, values, lengths],
        20,
        4 * new_keys[0].size * new_keys[0].shape[0] * groups,
        0,
        "update_caches",
        earlier,
        [pltpu.SMEM(lengths.shape, lengths.dtype), pltpu.SemaphoreType.DMA],
    )


def combine_kernel(own_partial, own_stats, *refs):
    heads = lax.axis_size("head")
    chips = heads // CORES
    outputs = 2 * chips - 1
    received = refs[: -1 - outputs]
    w_out, merged_rows = refs[-1 - outputs], refs[-outputs]
    far = refs[1 - outputs :]
    rows, width = own_partial.shape
    padding = jnp.zeros((LANES - STAT_ROWS, rows), jnp.float32)
    stats = [own_stats[...]]
    for ref in received:
        stats.append(
            sum(
                ref[rows:, turn * rows : (turn + 1) * rows].astype(jnp.float32)
                for turn in range(3)
            )[:STAT_ROWS]
        )
    logs = [jnp.concatenate([stat, padding], 0).T for stat in stats]
    largest = functools.reduce(jnp.maximum, logs)
    shares = [jnp.exp2(log - largest) for log in logs]
    total = functools.reduce(jnp.add, shares)
    shares = [share / total for share in shares]
    attended = []
    for head in range(width // HD):
        own = slice(head * HD, (head + 1) * HD)
        column = slice(head, head + 1)
        merged = own_partial[:, own] * shares[0][:, column]
        for ref, share in zip(received, shares[1:]):
            merged = merged + ref[:rows, own].astype(jnp.float32) * share[:, column]
        attended.append(merged.astype(jnp.bfloat16))
    attended = jnp.concatenate(attended, 1)
    merged_rows[...] = attended
    for ahead in range(1, chips):
        result = block_product(attended, w_out, ahead, 1)
        middle = result.shape[1] // 2
        far[2 * ahead - 2][...] = result[:, :middle]
        far[2 * ahead - 1][...] = result[:, middle:]


def block_product(attended, w_out, ahead, flip):
    heads = lax.axis_size("head")
    block_width = w_out.shape[1] // heads
    block = lax.rem(lax.axis_index("head") + CORES * ahead, heads) ^ flip
    along = pl.ds(pl.multiple_of(block * block_width, LANES), block_width)
    return dot(attended, w_out[:, along]).astype(jnp.bfloat16)


def project_kernel(merged_rows, w_out, far, *near):
    attended = merged_rows[...]
    far[...] = block_product(attended, w_out, 0, 1)
    for ahead, target in enumerate(near):
        target[...] = block_product(attended, w_out, ahead, 0)


def combine(own, received, w_out, heads, earlier):
    chips = heads // CORES
    rows = own[0].shape[0]
    width = w_out.shape[1] // heads
    merged = jax.ShapeDtypeStruct((rows, own[0].shape[1]), jnp.bfloat16)
    half = jax.ShapeDtypeStruct((rows, width // 2), jnp.bfloat16)
    merged, *far = call(
        combine_kernel,
        [merged] + [half] * (2 * chips - 2),
        [*own, *received, w_out],
        20,
        rows * w_out.size,
        0,
        "combine",
        earlier,
    )
    return merged, [far[2 * k : 2 * k + 2] for k in range(chips - 1)]


def project(merged, w_out, heads):
    block = jax.ShapeDtypeStruct((merged.shape[0], w_out.shape[1] // heads), jnp.bfloat16)
    far, *near = call(
        project_kernel,
        [block] * (1 + heads // CORES),
        [merged, w_out],
        20,
        2 * merged.shape[0] * w_out.size,
        0,
        "project",
    )
    return far, near


def sum_kernel(count, *refs):
    total = refs[0][...].astype(jnp.float32)
    total = total + jnp.concatenate([ref[...] for ref in refs[1:count]], 1).astype(jnp.float32)
    refs[count][...] = total.astype(jnp.bfloat16)


def sum_cores(near, far, earlier):
    return call(
        functools.partial(sum_kernel, 1 + len(far)),
        [jax.ShapeDtypeStruct(near.shape, near.dtype)],
        [near, *far],
        8,
        near.size,
        0,
        "sum_cores",
        earlier,
    )[0]


def finish_kernel(*refs):
    *parts, result = refs
    count = len(parts) // CHUNKS
    rows = parts[0].shape[0]
    for chunk in range(CHUNKS):
        total = 0.0
        for ref in parts[chunk * count : (chunk + 1) * count]:
            total = total + ref[...].astype(jnp.float32)
        result[chunk * rows : (chunk + 1) * rows] = total.astype(jnp.bfloat16)


def finish(parts, earlier):
    rows, width = parts[0].shape
    shape = jax.ShapeDtypeStruct((CHUNKS * rows, width), jnp.bfloat16)
    flops = CHUNKS * rows * width
    return call(finish_kernel, [shape], parts, 8, flops, 0, "finish", earlier)[0]


def shards(
    tokens,
    norm_gain,
    w_query,
    w_key,
    w_value,
    w_out,
    keys_cache,
    values_cache,
    cached_lengths,
    rope_offsets,
):
    rows, width = tokens.shape
    requests = cached_lengths.shape[0]
    groups = lax.axis_size("seq") // requests
    heads = lax.axis_size("head")
    chips = heads // CORES
    chunk_rows = rows // CHUNKS
    gain = norm_gain.reshape(heads, 1, width)

    mark = marks(keys_cache.shape[0])
    tables = rope_tables(cached_lengths, rope_offsets, groups, rows, [mark])
    wide_keys, wide_values = widen(keys_cache, values_cache, mark, cached_lengths, tables[:1])

    def attend_rows(pieces, turn, chunk, earlier):
        at = chunk * chunk_rows
        return attend(
            pieces, gain, w_query, tables, [wide_keys, wide_values], mark, new_rows[0],
            (groups, requests), turn, 0 if turn else at, chunk_rows, turn * rows + at, earlier,
        )

    half = chunk_rows // 2
    from_chips = other_chips(tokens)
    crossed = other_core(tokens)
    own, early, late = relay([tokens], [rows, chunk_rows, rows - chunk_rows], [])
    first = [shifted(early, "seq", turn * requests) for turn in range(1, groups)]
    (late,) = relay([late], [rows - chunk_rows], from_chips + [wide_keys])
    second = [shifted(late, "seq", turn * requests) for turn in range(1, groups)]
    own_cuts = [relay([piece], [rows, half, half, rows - chunk_rows], [late]) for piece in from_chips]
    own_pieces = [[own]] + [[cut[0]] for cut in own_cuts] + [[crossed]]
    own_pieces += [[other_core(block) for block in cut[1:]] for cut in own_cuts]
    own_early = [
        blocks if len(blocks) == 1 else blocks[: len(blocks) - 1] for blocks in own_pieces
    ]
    earlier = [cut[0] for cut in own_cuts]
    first = [relay([piece], [chunk_rows], earlier)[0] for piece in first]
    first_from_chips = [other_chips(piece) for piece in first]
    new_rows = [fresh(own_pieces, gain, w_key, w_value, tables, 0, first)]
    own_part = attend_rows(own_early, 0, 0, [new_rows[0][0]])
    earlier = own_part[:1]
    second = [relay([piece], [rows - chunk_rows], earlier)[0] for piece in second]
    second_from_chips = [other_chips(piece) for piece in second]
    earlier = second

    def gather_cores(piece, from_chips, earlier):
        size = piece.shape[0]
        passed = [relay([one], [size, size // 2, size // 2], earlier) for one in from_chips]
        blocks = [[piece]] + [[one[0]] for one in passed] + [[other_core(piece)]]
        blocks += [[other_core(part) for part in one[1:]] for one in passed]
        return blocks, [one[0] for one in passed]

    gathered = []
    for piece, from_chips in zip(first, first_from_chips):
        blocks, passed = gather_cores(piece, from_chips, earlier)
        gathered.append([blocks])
        earlier = earlier + passed
    received = [[] for _ in range(CHUNKS)]
    for turn in range(1, groups):
        (packed,) = attend_rows(gathered[turn - 1][0], turn, 0, earlier)
        received[0].append(shifted(packed, "seq", -turn * requests))
        earlier = [packed]
    for blocks, piece, from_chips in zip(gathered, second, second_from_chips):
        along, passed = gather_cores(piece, from_chips, earlier)
        blocks.append(along)
        earlier = earlier + passed
    for turn in range(1, groups):
        (packed,) = attend_rows(gathered[turn - 1][1], turn, 1, earlier)
        received[1].append(shifted(packed, "seq", -turn * requests))
        earlier = [packed]
    own_part = [own_part, attend_rows(own_pieces, 0, 1, earlier)]

    parts = []
    earlier, before_sums = own_part[1][:1], []
    for chunk in range(CHUNKS):
        merged, fars = combine(own_part[chunk], received[chunk], w_out, heads, earlier)
        fars = [[other_core(part) for part in far] for far in fars]
        far, near = project(merged, w_out, heads)
        earlier = [far] + before_sums
        sums = [sum_cores(one, parts_far, earlier) for one, parts_far in zip(near[1:], fars)]
        from_chips = [shifted(one, "head", CORES * k) for k, one in enumerate(sums, 1)]
        parts += [near[0], other_core(far), *from_chips]
        earlier, before_sums = sums, from_chips
    for turn in range(1, groups):
        pieces = [sum(blocks, []) for blocks in zip(*gathered[turn - 1])]
        new_rows.append(fresh(pieces, gain, w_key, w_value, tables, turn * rows, earlier))
        earlier = [new_rows[-1][0]]
    new_keys, new_values = zip(*new_rows)
    keys_updated, values_updated, done = update(
        cached_lengths, new_keys, new_values, keys_cache, values_cache, earlier
    )
    return (finish(parts, [done]), keys_updated, values_updated)


def solution(mesh):
    return jax.shard_map(
        shards,
        mesh=mesh,
        in_specs=(
            P("seq", "head"),
            P(),
            P(None, "head"),
            P(None, "head"),
            P(None, "head"),
            P("head", None),
            P("seq", "head"),
            P("seq", "head"),
            P(),
            P(),
        ),
        out_specs=(P("seq", "head"), P("seq", "head"), P("seq", "head")),
        check_vma=False,
    )
```

```python
import functools
import math

import jax
import jax.numpy as jnp
from jax import lax
from jax.experimental import pallas as pl
from jax.experimental.pallas import tpu as pltpu
from jax.sharding import PartitionSpec as P

HD = 128
LANES = 128
STAT_ROWS = 8
ROW_TILE = 16
CORES = 2
CHUNKS = 2
SLOT_TILES = 2
COST_WEIGHT = 0.0005
FIRST_MICROS = 2
FLOPS_PER_MICRO = 1_000_000_000
MIB = 1 << 20

rope_base = 500000.0
neg_large = -1e30
log2_scale = math.log2(math.e) / math.sqrt(HD)

VMEM = pl.BlockSpec(memory_space=pltpu.VMEM)
ANY = pl.BlockSpec(memory_space=pl.ANY)


def shifted(shard, axis, by):
    devices = lax.axis_size(axis)
    return lax.ppermute(shard, axis, [(i, (i + by) % devices) for i in range(devices)])


def other_core(shard):
    devices = lax.axis_size("head")
    return lax.ppermute(shard, "head", [(i, i ^ 1) for i in range(devices)])


def other_chips(own):
    chips = lax.axis_size("head") // CORES
    return [shifted(own, "head", CORES * k) for k in range(1, chips)]


def place_of(requests):
    member = lax.axis_index("seq")
    return lax.rem(member, requests), lax.div(member, requests)


def source_of(position_in, turn, groups):
    return lax.rem(position_in + (groups - turn), groups)


def dot(left, right):
    return jnp.dot(left, right, preferred_element_type=jnp.float32)


def dot_transposed(left, right):
    return lax.dot_general(
        left, right, (((1,), (1,)), ((), ())), preferred_element_type=jnp.float32
    )


def call(
    kernel, out_shape, arrays, limit, flops, transcendentals, name, earlier=(),
    scratch=(), micros=0,
):
    moved = sum(a.size * a.dtype.itemsize for a in arrays)
    moved += sum(math.prod(s.shape) * s.dtype.itemsize for s in out_shape)
    read = len(arrays)
    skipped = len(earlier)

    def body(*refs):
        kernel(*refs[:read], *refs[read + skipped :])

    return pl.pallas_call(
        body,
        out_shape=out_shape,
        in_specs=[VMEM] * len(arrays) + [ANY] * skipped,
        out_specs=[VMEM] * len(out_shape),
        scratch_shapes=scratch,
        compiler_params=pltpu.CompilerParams(vmem_limit_bytes=limit * MIB),
        cost_estimate=pl.CostEstimate(
            flops=max(int(COST_WEIGHT * flops), micros * FLOPS_PER_MICRO),
            bytes_accessed=int(COST_WEIGHT * moved),
            transcendentals=int(COST_WEIGHT * transcendentals),
        ),
        name=name,
    )(*arrays, *earlier)


def whole_of(blocks):
    parts = [block[...] for block in blocks]
    return jnp.concatenate(parts, 0) if len(parts) > 1 else parts[0]


def relay_kernel(count, *refs):
    whole = whole_of(refs[:count])
    at = 0
    for ref in refs[count:]:
        ref[...] = whole[at : at + ref.shape[0]]
        at = (at + ref.shape[0]) % whole.shape[0]


def relay(blocks, sizes, earlier):
    shapes = [jax.ShapeDtypeStruct((size, *blocks[0].shape[1:]), blocks[0].dtype) for size in sizes]
    kernel = functools.partial(relay_kernel, len(blocks))
    return call(kernel, shapes, [*blocks], 4, 0, 0, "relay", earlier)


def mark_kernel(mark):
    lane = lax.broadcasted_iota(jnp.int32, mark.shape, 1)
    mark[...] = jnp.where(lane == 0, 1.0, 0.0).astype(mark.dtype)


def marks(rows):
    shape = jax.ShapeDtypeStruct((rows, LANES), jnp.bfloat16)
    return call(mark_kernel, [shape], [], 4, 0, 0, "marks", micros=FIRST_MICROS)[0]


def tables_kernel(groups, lengths_in, offsets_in, cosine, sine, *scratch):
    lengths, offsets, semaphores = scratch
    numbers = [
        pltpu.make_async_copy(lengths_in, lengths, semaphores.at[0]),
        pltpu.make_async_copy(offsets_in, offsets, semaphores.at[1]),
    ]
    for copy in numbers:
        copy.start()
    rows = cosine.shape[0] // groups
    for copy in numbers:
        copy.wait()
    request, position_in = place_of(lengths.shape[0])
    lane = lax.broadcasted_iota(jnp.int32, (rows, LANES), 1)
    row = lax.broadcasted_iota(jnp.int32, (rows, LANES), 0)
    half = lax.rem(lane, HD // 2).astype(jnp.float32)
    frequency = jnp.exp2(half * (-2.0 / HD * math.log2(rope_base)))
    sign = jnp.where(lane < HD // 2, -1.0, 1.0)
    for turn in range(groups):
        first = source_of(position_in, turn, groups) * rows
        first = first + offsets[request] + lengths[request]
        angles = (row + first).astype(jnp.float32) * frequency
        part = slice(turn * rows, (turn + 1) * rows)
        cosine[part] = jnp.cos(angles)
        sine[part] = jnp.sin(angles) * sign


def rope_tables(lengths, offsets, groups, rows, earlier):
    table = jax.ShapeDtypeStruct((groups * rows, LANES), jnp.float32)
    return call(
        functools.partial(tables_kernel, groups),
        [table, table],
        [lengths, offsets],
        12,
        0,
        0,
        "rope_tables",
        earlier,
        [
            pltpu.SMEM(lengths.shape, lengths.dtype),
            pltpu.SMEM(offsets.shape, offsets.dtype),
            pltpu.SemaphoreType.DMA((2,)),
        ],
    )


def widen_kernel(keys, values, mark, lengths_in, wide_keys, wide_values, lengths, semaphore):
    number = pltpu.make_async_copy(lengths_in, lengths, semaphore)
    number.start()
    slots = keys.shape[0]
    heads = keys.shape[1] // HD
    for head in range(heads):
        own = slice(head * HD, (head + 1) * HD)
        wide_keys[head, :, :HD] = keys[:, own]
        wide_values[head, :, :HD] = values[:, own]
        wide_values[head, :, HD:] = mark[:slots]
    number.wait()
    request, position_in = place_of(lengths.shape[0])
    slot = lax.broadcasted_iota(jnp.int32, (slots, LANES), 0) + position_in * slots
    lane = lax.broadcasted_iota(jnp.int32, (slots, LANES), 1)
    bias = jnp.where((lane == 0) & (slot >= lengths[request]), neg_large, 0.0).astype(jnp.bfloat16)
    for head in range(heads):
        wide_keys[head, :, HD:] = bias


def widen(keys, values, mark, lengths, earlier):
    slots, width = keys.shape
    wide = jax.ShapeDtypeStruct((width // HD, slots, HD + LANES), jnp.bfloat16)
    return call(
        widen_kernel,
        [wide, wide],
        [keys, values, mark, lengths],
        12,
        0,
        0,
        "widen_caches",
        earlier,
        [pltpu.SMEM(lengths.shape, lengths.dtype), pltpu.SemaphoreType.DMA],
    )


def rotate(vectors, cosine, sine):
    return vectors * cosine + pltpu.roll(vectors, HD // 2, 1) * sine


def project_normed(pieces, gain, weights):
    heads = gain.shape[0]
    width = gain.shape[2]
    me = lax.axis_index("head")
    squares = 0.0
    sums = [0.0] * len(weights)
    for index, piece in enumerate(pieces):
        owner = lax.rem(me + (heads - CORES * (index % (heads // CORES))), heads)
        if index >= heads // CORES:
            owner = owner ^ 1
        wide = piece.astype(jnp.float32)
        scaled = (wide * gain[owner]).astype(jnp.bfloat16)
        along = pl.ds(pl.multiple_of(owner * width, LANES), width)
        for place, weight in enumerate(weights):
            sums[place] = sums[place] + dot(scaled, weight[along, :])
        squares = squares + jnp.sum(wide * wide, -1, keepdims=True)
    factor = lax.rsqrt(squares / (heads * width) + 1e-05)
    return [total * factor for total in sums]


def stat_rows(columns, rows):
    lane = lax.broadcasted_iota(jnp.int32, (rows, LANES), 1)
    table = jnp.zeros((rows, LANES), jnp.float32)
    for index, column in enumerate(columns):
        table = jnp.where(lane == index, column, table)
    return table.T[:STAT_ROWS]


def split_refs(counts, refs):
    parts = []
    for count in counts:
        parts.append(refs[:count])
        refs = refs[count:]
    return parts, refs


def rows_of(blocks, row_at, rows):
    parts = []
    at = 0
    for block in blocks:
        size = block.shape[0]
        low, high = max(row_at - at, 0), min(row_at + rows - at, size)
        if low < high:
            parts.append(block[low:high])
        at += size
    return jnp.concatenate(parts, 0) if len(parts) > 1 else parts[0]


def attend_kernel(counts, own, row_at, rows, table_at, *refs):
    blocks, refs = split_refs(counts, refs)
    gain, w_query, cosine, sine, wide_keys, wide_values, mark, *outputs = refs
    pieces = [rows_of(one, row_at, rows) for one in blocks]
    (product,) = project_normed(pieces, gain, [w_query])
    cosine = cosine[table_at : table_at + rows]
    sine = sine[table_at : table_at + rows]
    kv_heads = wide_keys.shape[0]
    repeat = product.shape[1] // HD // kv_heads
    queries = [
        (rotate(product[:, head * HD : (head + 1) * HD], cosine, sine) * log2_scale).astype(
            jnp.bfloat16
        )
        for head in range(kv_heads * repeat)
    ]
    mark = mark[: repeat * rows]
    slots = wide_keys.shape[1] // SLOT_TILES
    tiles = [(head, at) for head in range(kv_heads) for at in range(0, slots * SLOT_TILES, slots)]

    def scores_of(head, at):
        stacked = jnp.concatenate(queries[head * repeat : (head + 1) * repeat], 0)
        wide = jnp.concatenate([stacked, mark], 1)
        return dot_transposed(wide, wide_keys[head, at : at + slots])

    columns = []
    found = []
    following = scores_of(*tiles[0])
    for index, (head, at) in enumerate(tiles):
        scores = following
        if index + 1 < len(tiles):
            following = scores_of(*tiles[index + 1])
        largest = jnp.max(scores, -1, keepdims=True)
        weights = jnp.exp2(scores - largest).astype(jnp.bfloat16)
        found.append((largest, dot(weights, wide_values[head, at : at + slots])))
        if len(found) < SLOT_TILES:
            continue
        largest = functools.reduce(jnp.maximum, [tile[0] for tile in found])
        summed = sum(tile[1] * jnp.exp2(tile[0] - largest) for tile in found)
        found = []
        denominator = summed[:, HD : HD + 1]
        result = summed[:, :HD] / denominator
        logs = largest + jnp.log2(denominator)
        for turn in range(repeat):
            part = slice(turn * rows, (turn + 1) * rows)
            to = slice((head * repeat + turn) * HD, (head * repeat + turn + 1) * HD)
            outputs[0][:rows, to] = result[part].astype(outputs[0].dtype)
            columns.append(logs[part])
    stats = stat_rows(columns, rows)
    if own:
        outputs[1][...] = stats
        outputs[2][...] = jnp.concatenate(queries, 1)
        return
    outputs[0][rows:] = jnp.zeros((ROW_TILE, outputs[0].shape[1]), jnp.bfloat16)
    rest = jnp.concatenate([stats, jnp.zeros((ROW_TILE - STAT_ROWS, rows), jnp.float32)], 0)
    for part in range(3):
        rounded = rest.astype(jnp.bfloat16)
        outputs[0][rows:, part * rows : (part + 1) * rows] = rounded
        rest = rest - rounded.astype(jnp.float32)


def attend(
    pieces, gain, w_query, tables, wide_keys, wide_values, mark, own, row_at, rows, table_at,
    earlier,
):
    counts = [len(blocks) for blocks in pieces]
    flat = [block for blocks in pieces for block in blocks]
    out_width = w_query.shape[1]
    slots = wide_keys.shape[1]
    if own:
        out_shape = [
            jax.ShapeDtypeStruct((rows, out_width), jnp.float32),
            jax.ShapeDtypeStruct((STAT_ROWS, rows), jnp.float32),
            jax.ShapeDtypeStruct((rows, out_width), jnp.bfloat16),
        ]
    else:
        out_shape = [jax.ShapeDtypeStruct((rows + ROW_TILE, out_width), jnp.bfloat16)]
    return call(
        functools.partial(attend_kernel, counts, own, row_at, rows, table_at),
        out_shape,
        [*flat, gain, w_query, *tables, wide_keys, wide_values, mark],
        28,
        2 * rows * out_width * (w_query.shape[0] + 4 * slots),
        rows * out_width // HD * slots,
        "attend_own" if own else "attend_partner",
        earlier,
    )


def fresh_kernel(counts, table_at, *refs):
    blocks, refs = split_refs(counts, refs)
    gain, w_key, w_value, cosine, sine, new_keys, new_values = refs
    rows = new_keys.shape[0]
    pieces = [whole_of(one) for one in blocks]
    keys, values = project_normed(pieces, gain, [w_key, w_value])
    cosine = cosine[table_at : table_at + rows]
    sine = sine[table_at : table_at + rows]
    for head in range(keys.shape[1] // HD):
        own = slice(head * HD, (head + 1) * HD)
        new_keys[:, own] = rotate(keys[:, own], cosine, sine).astype(jnp.bfloat16)
    new_values[...] = values.astype(jnp.bfloat16)


def fresh(pieces, gain, w_key, w_value, tables, table_at, earlier):
    flat = [block for blocks in pieces for block in blocks]
    rows = sum(block.shape[0] for block in pieces[0])
    shape = jax.ShapeDtypeStruct((rows, w_key.shape[1]), jnp.bfloat16)
    return call(
        functools.partial(fresh_kernel, [len(blocks) for blocks in pieces], table_at),
        [shape, shape],
        [*flat, gain, w_key, w_value, *tables],
        20,
        4 * rows * w_key.size,
        0,
        "fresh_kv",
        earlier,
    )


def write_rows(target, fresh_rows, first):
    rows = fresh_rows.shape[0]
    slab_rows = target.shape[0]
    span = rows + ROW_TILE
    start = jnp.clip(first, 0, slab_rows - span)
    start = start - lax.rem(start, ROW_TILE)
    window = pl.ds(pl.multiple_of(start, ROW_TILE), span)
    shift = start - first
    place = lax.broadcasted_iota(jnp.int32, (span, rows), 0) + shift
    chosen = place == lax.broadcasted_iota(jnp.int32, (span, rows), 1)
    moved = dot(chosen.astype(jnp.bfloat16), fresh_rows)
    row = lax.broadcasted_iota(jnp.int32, (span, target.shape[1]), 0) + shift
    inside = (row >= 0) & (row < rows)
    old = target[window, :].astype(jnp.float32)
    target[window, :] = jnp.where(inside, moved, old).astype(jnp.bfloat16)


def attend_fresh_kernel(groups, requests, *refs):
    query_refs, refs = refs[:CHUNKS], refs[CHUNKS:]
    key_refs, value_refs, refs = refs[:groups], refs[groups : 2 * groups], refs[2 * groups :]
    partial, stats = refs
    position_in = place_of(requests)[1]
    rows, width = partial.shape
    kv_heads = key_refs[0].shape[1] // HD
    repeat = width // HD // kv_heads
    queries = whole_of(query_refs)
    token = lax.broadcasted_iota(jnp.int32, (rows, rows), 0)
    within = lax.broadcasted_iota(jnp.int32, (rows, rows), 1)
    causal = jnp.where(within <= token, 0.0, neg_large)
    causal = jnp.concatenate([causal] * repeat, 0)
    lane = lax.broadcasted_iota(jnp.int32, (rows, LANES), 1)
    ones = jnp.where(lane == 0, 1.0, 0.0).astype(jnp.bfloat16)
    hidden = [jnp.zeros((rows, LANES), jnp.bfloat16)]
    for turn in range(1, groups):
        later = source_of(position_in, turn, groups) > position_in
        hidden.append(jnp.where((lane == 0) & later, neg_large, 0.0).astype(jnp.bfloat16))
    columns = []
    for head in range(kv_heads):
        own = [
            slice((head * repeat + turn) * HD, (head * repeat + turn + 1) * HD)
            for turn in range(repeat)
        ]
        shared = slice(head * HD, (head + 1) * HD)
        stacked = jnp.concatenate([queries[:, one] for one in own], 0)
        stacked = jnp.concatenate([stacked, jnp.concatenate([ones] * repeat, 0)], 1)
        scores = [
            dot_transposed(stacked, jnp.concatenate([ref[:, shared], bias], 1))
            for ref, bias in zip(key_refs, hidden)
        ]
        scores = jnp.concatenate([scores[0] + causal] + scores[1:], 1)
        largest = jnp.max(scores, -1, keepdims=True)
        weights = jnp.exp2(scores - largest).astype(jnp.bfloat16)
        wide_values = [jnp.concatenate([ref[:, shared], ones], 1) for ref in value_refs]
        summed = dot(weights, jnp.concatenate(wide_values, 0))
        denominator = summed[:, HD : HD + 1]
        result = summed[:, :HD] / denominator
        logs = largest + jnp.log2(denominator)
        for turn, one in enumerate(own):
            part = slice(turn * rows, (turn + 1) * rows)
            partial[:, one] = result[part]
            columns.append(logs[part])
    stats[...] = stat_rows(columns, rows)


def attend_fresh(requests, queries, new_keys, new_values):
    groups = len(new_keys)
    rows = new_keys[0].shape[0]
    width = queries[0].shape[1]
    return call(
        functools.partial(attend_fresh_kernel, groups, requests),
        [
            jax.ShapeDtypeStruct((rows, width), jnp.float32),
            jax.ShapeDtypeStruct((STAT_ROWS, rows), jnp.float32),
        ],
        [*queries, *new_keys, *new_values],
        24,
        4 * rows * width * rows * groups,
        rows * width // HD * rows * groups,
        "attend_fresh",
    )


def update_kernel(groups, *refs):
    key_refs, value_refs, refs = refs[:groups], refs[groups : 2 * groups], refs[2 * groups :]
    keys, values, lengths_in, keys_updated, values_updated, done, lengths, semaphore = refs
    number = pltpu.make_async_copy(lengths_in, lengths, semaphore)
    number.start()
    keys_updated[...] = keys[...]
    values_updated[...] = values[...]
    done[...] = jnp.zeros(done.shape, done.dtype)
    number.wait()
    request, position_in = place_of(lengths.shape[0])
    rows = key_refs[0].shape[0]
    for turn in range(groups):
        source = source_of(position_in, turn, groups)
        first = lengths[request] + source * rows - position_in * keys.shape[0]
        write_rows(keys_updated, key_refs[turn][...], first)
        write_rows(values_updated, value_refs[turn][...], first)


def update(lengths, new_keys, new_values, keys, values, earlier):
    groups = len(new_keys)
    slab = jax.ShapeDtypeStruct(keys.shape, keys.dtype)
    return call(
        functools.partial(update_kernel, groups),
        [slab, slab, jax.ShapeDtypeStruct((STAT_ROWS, LANES), jnp.float32)],
        [*new_keys, *new_values, keys, values, lengths],
        20,
        4 * new_keys[0].size * new_keys[0].shape[0] * groups,
        0,
        "update_caches",
        earlier,
        [pltpu.SMEM(lengths.shape, lengths.dtype), pltpu.SemaphoreType.DMA],
    )


def combine_kernel(row_at, own_partial, own_stats, fresh_partial, fresh_stats, *refs):
    heads = lax.axis_size("head")
    chips = heads // CORES
    outputs = 2 * chips - 1
    received = refs[: -1 - outputs]
    w_out, merged_rows = refs[-1 - outputs], refs[-outputs]
    far = refs[1 - outputs :]
    width = own_partial.shape[1]
    rows = merged_rows.shape[0]
    part = slice(row_at, row_at + rows)
    padding = jnp.zeros((LANES - STAT_ROWS, rows), jnp.float32)
    stats = [own_stats[...], fresh_stats[:, part]]
    for ref in received:
        stats.append(
            sum(
                ref[rows:, turn * rows : (turn + 1) * rows].astype(jnp.float32)
                for turn in range(3)
            )[:STAT_ROWS]
        )
    logs = [jnp.concatenate([stat, padding], 0).T for stat in stats]
    largest = functools.reduce(jnp.maximum, logs)
    shares = [jnp.exp2(log - largest) for log in logs]
    total = functools.reduce(jnp.add, shares)
    shares = [share / total for share in shares]
    attended = []
    for head in range(width // HD):
        own = slice(head * HD, (head + 1) * HD)
        column = slice(head, head + 1)
        merged = own_partial[:, own] * shares[0][:, column]
        merged = merged + fresh_partial[part, own] * shares[1][:, column]
        for ref, share in zip(received, shares[2:]):
            merged = merged + ref[:rows, own].astype(jnp.float32) * share[:, column]
        attended.append(merged.astype(jnp.bfloat16))
    attended = jnp.concatenate(attended, 1)
    merged_rows[...] = attended
    for ahead in range(1, chips):
        result = block_product(attended, w_out, ahead, 1)
        middle = result.shape[1] // 2
        far[2 * ahead - 2][...] = result[:, :middle]
        far[2 * ahead - 1][...] = result[:, middle:]


def block_product(attended, w_out, ahead, flip):
    heads = lax.axis_size("head")
    block_width = w_out.shape[1] // heads
    block = lax.rem(lax.axis_index("head") + CORES * ahead, heads) ^ flip
    along = pl.ds(pl.multiple_of(block * block_width, LANES), block_width)
    return dot(attended, w_out[:, along]).astype(jnp.bfloat16)


def project_kernel(merged_rows, w_out, far, *near):
    attended = merged_rows[...]
    far[...] = block_product(attended, w_out, 0, 1)
    for ahead, target in enumerate(near):
        target[...] = block_product(attended, w_out, ahead, 0)


def combine(row_at, rows, own, fresh_part, received, w_out, heads, earlier):
    chips = heads // CORES
    width = w_out.shape[1] // heads
    merged = jax.ShapeDtypeStruct((rows, own[0].shape[1]), jnp.bfloat16)
    half = jax.ShapeDtypeStruct((rows, width // 2), jnp.bfloat16)
    merged, *far = call(
        functools.partial(combine_kernel, row_at),
        [merged] + [half] * (2 * chips - 2),
        [*own, *fresh_part, *received, w_out],
        20,
        rows * w_out.size,
        0,
        "combine",
        earlier,
    )
    return merged, [far[2 * k : 2 * k + 2] for k in range(chips - 1)]


def project(merged, w_out, heads):
    block = jax.ShapeDtypeStruct((merged.shape[0], w_out.shape[1] // heads), jnp.bfloat16)
    far, *near = call(
        project_kernel,
        [block] * (1 + heads // CORES),
        [merged, w_out],
        20,
        2 * merged.shape[0] * w_out.size,
        0,
        "project",
    )
    return far, near


def sum_kernel(count, *refs):
    total = refs[0][...].astype(jnp.float32)
    total = total + jnp.concatenate([ref[...] for ref in refs[1:count]], 1).astype(jnp.float32)
    refs[count][...] = total.astype(jnp.bfloat16)


def sum_cores(near, far, earlier):
    return call(
        functools.partial(sum_kernel, 1 + len(far)),
        [jax.ShapeDtypeStruct(near.shape, near.dtype)],
        [near, *far],
        8,
        near.size,
        0,
        "sum_cores",
        earlier,
    )[0]


def finish_kernel(*refs):
    *parts, result = refs
    count = len(parts) // CHUNKS
    rows = parts[0].shape[0]
    for chunk in range(CHUNKS):
        total = 0.0
        for ref in parts[chunk * count : (chunk + 1) * count]:
            total = total + ref[...].astype(jnp.float32)
        result[chunk * rows : (chunk + 1) * rows] = total.astype(jnp.bfloat16)


def finish(parts, earlier):
    rows, width = parts[0].shape
    shape = jax.ShapeDtypeStruct((CHUNKS * rows, width), jnp.bfloat16)
    flops = CHUNKS * rows * width
    return call(finish_kernel, [shape], parts, 8, flops, 0, "finish", earlier)[0]


def shards(
    tokens,
    norm_gain,
    w_query,
    w_key,
    w_value,
    w_out,
    keys_cache,
    values_cache,
    cached_lengths,
    rope_offsets,
):
    rows, width = tokens.shape
    requests = cached_lengths.shape[0]
    groups = lax.axis_size("seq") // requests
    heads = lax.axis_size("head")
    chips = heads // CORES
    chunk_rows = rows // CHUNKS
    gain = norm_gain.reshape(heads, 1, width)

    mark = marks(keys_cache.shape[0])
    tables = rope_tables(cached_lengths, rope_offsets, groups, rows, [mark])
    wide_keys, wide_values = widen(keys_cache, values_cache, mark, cached_lengths, tables[:1])

    def attend_rows(pieces, own, chunk, turn, earlier):
        at = chunk * chunk_rows
        return attend(
            pieces, gain, w_query, tables, wide_keys, wide_values, mark, own, at if own else 0,
            chunk_rows, turn * rows + at, earlier,
        )

    half = chunk_rows // 2
    from_chips = other_chips(tokens)
    crossed = other_core(tokens)
    own, early, late = relay([tokens], [rows, chunk_rows, rows - chunk_rows], [])
    first = [shifted(early, "seq", turn * requests) for turn in range(1, groups)]
    (late,) = relay([late], [rows - chunk_rows], from_chips + [wide_keys])
    second = [shifted(late, "seq", turn * requests) for turn in range(1, groups)]
    own_cuts = [relay([piece], [rows, half, half, half, half], [late]) for piece in from_chips]
    own_pieces = [[own]] + [[cut[0]] for cut in own_cuts] + [[crossed]]
    own_pieces += [[other_core(block) for block in cut[1:]] for cut in own_cuts]
    own_early = [
        blocks if len(blocks) == 1 else blocks[:2] for blocks in own_pieces
    ]
    earlier = [cut[0] for cut in own_cuts]
    first = [relay([piece], [chunk_rows], earlier)[0] for piece in first]
    first_from_chips = [other_chips(piece) for piece in first]
    *own_part, queries = attend_rows(own_early, True, 0, 0, first)
    own_queries = [queries]
    new_rows = [fresh(own_pieces, gain, w_key, w_value, tables, 0, [queries])]
    earlier = [new_rows[0][0]]
    second = [relay([piece], [rows - chunk_rows], earlier)[0] for piece in second]
    second_from_chips = [other_chips(piece) for piece in second]
    earlier = second

    def gather_cores(piece, from_chips, earlier):
        size = piece.shape[0]
        passed = [relay([one], [size, size // 2, size // 2], earlier) for one in from_chips]
        blocks = [[piece]] + [[one[0]] for one in passed] + [[other_core(piece)]]
        blocks += [[other_core(part) for part in one[1:]] for one in passed]
        return blocks, [one[0] for one in passed]

    gathered = []
    for piece, from_chips in zip(first, first_from_chips):
        blocks, passed = gather_cores(piece, from_chips, earlier)
        gathered.append([blocks])
        earlier = earlier + passed
    received = [[] for _ in range(CHUNKS)]
    for turn in range(1, groups):
        (packed,) = attend_rows(gathered[turn - 1][0], False, 0, turn, earlier)
        received[0].append(shifted(packed, "seq", -turn * requests))
        earlier = [packed]
    *late_part, queries = attend_rows(own_pieces, True, 1, 0, earlier)
    own_part += late_part
    own_queries.append(queries)
    earlier = [queries]
    for blocks, piece, from_chips in zip(gathered, second, second_from_chips):
        along, passed = gather_cores(piece, from_chips, earlier)
        blocks.append(along)
        earlier = earlier + passed
    for turn in range(1, groups):
        (packed,) = attend_rows(gathered[turn - 1][1], False, 1, turn, earlier)
        received[1].append(shifted(packed, "seq", -turn * requests))
        earlier = [packed]
    for turn in range(1, groups):
        pieces = [sum(blocks, []) for blocks in zip(*gathered[turn - 1])]
        new_rows.append(fresh(pieces, gain, w_key, w_value, tables, turn * rows, earlier))
    new_keys, new_values = zip(*new_rows)
    fresh_part = attend_fresh(requests, own_queries, new_keys, new_values)

    parts = []
    earlier = before_sums = []
    for chunk in range(CHUNKS):
        merged, fars = combine(
            chunk * chunk_rows, chunk_rows, own_part[2 * chunk : 2 * chunk + 2], fresh_part,
            received[chunk], w_out, heads, earlier,
        )
        fars = [[other_core(part) for part in far] for far in fars]
        far, near = project(merged, w_out, heads)
        earlier = [far] + before_sums
        sums = [sum_cores(one, parts_far, earlier) for one, parts_far in zip(near[1:], fars)]
        from_chips = [shifted(one, "head", CORES * k) for k, one in enumerate(sums, 1)]
        parts += [near[0], other_core(far), *from_chips]
        earlier, before_sums = sums, from_chips
    keys_updated, values_updated, done = update(
        cached_lengths, new_keys, new_values, keys_cache, values_cache, earlier
    )
    return (finish(parts, [done]), keys_updated, values_updated)


def solution(mesh):
    return jax.shard_map(
        shards,
        mesh=mesh,
        in_specs=(
            P("seq", "head"),
            P(),
            P(None, "head"),
            P(None, "head"),
            P(None, "head"),
            P("head", None),
            P("seq", "head"),
            P("seq", "head"),
            P(),
            P(),
        ),
        out_specs=(P("seq", "head"), P("seq", "head"), P("seq", "head")),
        check_vma=False,
    )
```

```python
import functools
import math

import jax
import jax.numpy as jnp
from jax import lax
from jax.experimental import pallas as pl
from jax.experimental.pallas import tpu as pltpu
from jax.sharding import PartitionSpec as P

HD = 128
LANES = 128
STAT_ROWS = 8
ROW_TILE = 16
CORES = 2
CHUNKS = 2
SLOT_TILES = 4
COST_WEIGHT = 0.0005
FIRST_MICROS = 2
FLOPS_PER_MICRO = 1_000_000_000
MIB = 1 << 20

rope_base = 500000.0
neg_large = -1e30
least_sum = 2.0**-90
log2_scale = math.log2(math.e) / math.sqrt(HD)

VMEM = pl.BlockSpec(memory_space=pltpu.VMEM)
ANY = pl.BlockSpec(memory_space=pl.ANY)


def shifted(shard, axis, by):
    devices = lax.axis_size(axis)
    return lax.ppermute(shard, axis, [(i, (i + by) % devices) for i in range(devices)])


def other_core(shard):
    devices = lax.axis_size("head")
    return lax.ppermute(shard, "head", [(i, i ^ 1) for i in range(devices)])


def other_chips(own):
    chips = lax.axis_size("head") // CORES
    return [shifted(own, "head", CORES * k) for k in range(1, chips)]


def place_of(requests):
    member = lax.axis_index("seq")
    return lax.rem(member, requests), lax.div(member, requests)


def source_of(position_in, turn, groups):
    return lax.rem(position_in + (groups - turn), groups)


def dot(left, right):
    return jnp.dot(left, right, preferred_element_type=jnp.float32)


def dot_transposed(left, right):
    return lax.dot_general(
        left, right, (((1,), (1,)), ((), ())), preferred_element_type=jnp.float32
    )


def call(
    kernel, out_shape, arrays, limit, flops, transcendentals, name, earlier=(),
    scratch=(), micros=0,
):
    moved = sum(a.size * a.dtype.itemsize for a in arrays)
    moved += sum(math.prod(s.shape) * s.dtype.itemsize for s in out_shape)
    read = len(arrays)
    skipped = len(earlier)

    def body(*refs):
        kernel(*refs[:read], *refs[read + skipped :])

    return pl.pallas_call(
        body,
        out_shape=out_shape,
        in_specs=[VMEM] * len(arrays) + [ANY] * skipped,
        out_specs=[VMEM] * len(out_shape),
        scratch_shapes=scratch,
        compiler_params=pltpu.CompilerParams(vmem_limit_bytes=limit * MIB),
        cost_estimate=pl.CostEstimate(
            flops=max(int(COST_WEIGHT * flops), micros * FLOPS_PER_MICRO),
            bytes_accessed=int(COST_WEIGHT * moved),
            transcendentals=int(COST_WEIGHT * transcendentals),
        ),
        name=name,
    )(*arrays, *earlier)


def whole_of(blocks):
    parts = [block[...] for block in blocks]
    return jnp.concatenate(parts, 0) if len(parts) > 1 else parts[0]


def relay_kernel(count, *refs):
    whole = whole_of(refs[:count])
    at = 0
    for ref in refs[count:]:
        ref[...] = whole[at : at + ref.shape[0]]
        at = (at + ref.shape[0]) % whole.shape[0]


def relay(blocks, sizes, earlier):
    shapes = [jax.ShapeDtypeStruct((size, *blocks[0].shape[1:]), blocks[0].dtype) for size in sizes]
    kernel = functools.partial(relay_kernel, len(blocks))
    return call(kernel, shapes, [*blocks], 4, 0, 0, "relay", earlier)


def mark_kernel(mark):
    lane = lax.broadcasted_iota(jnp.int32, mark.shape, 1)
    mark[...] = jnp.where(lane == 0, 1.0, 0.0).astype(mark.dtype)


def marks(rows):
    shape = jax.ShapeDtypeStruct((rows, LANES), jnp.bfloat16)
    return call(mark_kernel, [shape], [], 4, 0, 0, "marks", micros=FIRST_MICROS)[0]


def tables_kernel(groups, lengths_in, offsets_in, cosine, sine, *scratch):
    lengths, offsets, semaphores = scratch
    numbers = [
        pltpu.make_async_copy(lengths_in, lengths, semaphores.at[0]),
        pltpu.make_async_copy(offsets_in, offsets, semaphores.at[1]),
    ]
    for copy in numbers:
        copy.start()
    rows = cosine.shape[0] // groups
    for copy in numbers:
        copy.wait()
    request, position_in = place_of(lengths.shape[0])
    lane = lax.broadcasted_iota(jnp.int32, (rows, LANES), 1)
    row = lax.broadcasted_iota(jnp.int32, (rows, LANES), 0)
    half = lax.rem(lane, HD // 2).astype(jnp.float32)
    frequency = jnp.exp2(half * (-2.0 / HD * math.log2(rope_base)))
    sign = jnp.where(lane < HD // 2, -1.0, 1.0)
    for turn in range(groups):
        first = source_of(position_in, turn, groups) * rows
        first = first + offsets[request] + lengths[request]
        angles = (row + first).astype(jnp.float32) * frequency
        part = slice(turn * rows, (turn + 1) * rows)
        cosine[part] = jnp.cos(angles)
        sine[part] = jnp.sin(angles) * sign


def rope_tables(lengths, offsets, groups, rows, earlier):
    table = jax.ShapeDtypeStruct((groups * rows, LANES), jnp.float32)
    return call(
        functools.partial(tables_kernel, groups),
        [table, table],
        [lengths, offsets],
        12,
        0,
        0,
        "rope_tables",
        earlier,
        [
            pltpu.SMEM(lengths.shape, lengths.dtype),
            pltpu.SMEM(offsets.shape, offsets.dtype),
            pltpu.SemaphoreType.DMA((2,)),
        ],
    )


def widen_kernel(keys, values, mark, lengths_in, wide_keys, wide_values, norms, *scratch):
    lengths, semaphore = scratch
    number = pltpu.make_async_copy(lengths_in, lengths, semaphore)
    number.start()
    slots = keys.shape[0]
    heads = keys.shape[1] // HD
    for head in range(heads):
        own = slice(head * HD, (head + 1) * HD)
        wide_keys[head, :, :HD] = keys[:, own]
        wide_values[head, :, :HD] = values[:, own]
        wide_values[head, :, HD:] = mark[:slots]
    number.wait()
    request, position_in = place_of(lengths.shape[0])
    slot = lax.broadcasted_iota(jnp.int32, (slots, LANES), 0) + position_in * slots
    lane = lax.broadcasted_iota(jnp.int32, (slots, LANES), 1)
    bias = jnp.where((lane == 0) & (slot >= lengths[request]), neg_large, 0.0)
    bias = jnp.where(lane == 1, 1.0, bias).astype(jnp.bfloat16)
    visible = slot[:, :1] < lengths[request]
    norms[...] = jnp.full(norms.shape, -1.0, norms.dtype)
    for head in range(heads):
        wide_keys[head, :, HD:] = bias
        key = keys[:, head * HD : (head + 1) * HD].astype(jnp.float32)
        squares = jnp.where(visible, jnp.sum(key * key, -1, keepdims=True), -1.0)
        largest = jnp.max(squares, 0, keepdims=True)
        norms[head : head + 1] = jnp.broadcast_to(largest, (1, LANES))


def widen(keys, values, mark, lengths, earlier):
    slots, width = keys.shape
    wide = jax.ShapeDtypeStruct((width // HD, slots, HD + LANES), jnp.bfloat16)
    return call(
        widen_kernel,
        [wide, wide, jax.ShapeDtypeStruct((STAT_ROWS, LANES), jnp.float32)],
        [keys, values, mark, lengths],
        12,
        0,
        0,
        "widen_caches",
        earlier,
        [pltpu.SMEM(lengths.shape, lengths.dtype), pltpu.SemaphoreType.DMA],
    )


def rotate(vectors, cosine, sine):
    return vectors * cosine + pltpu.roll(vectors, HD // 2, 1) * sine


def project_normed(pieces, gain, weights):
    heads = gain.shape[0]
    width = gain.shape[2]
    me = lax.axis_index("head")
    squares = 0.0
    sums = [0.0] * len(weights)
    for index, piece in enumerate(pieces):
        owner = lax.rem(me + (heads - CORES * (index % (heads // CORES))), heads)
        if index >= heads // CORES:
            owner = owner ^ 1
        wide = piece.astype(jnp.float32)
        scaled = (wide * gain[owner]).astype(jnp.bfloat16)
        along = pl.ds(pl.multiple_of(owner * width, LANES), width)
        for place, weight in enumerate(weights):
            sums[place] = sums[place] + dot(scaled, weight[along, :])
        squares = squares + jnp.sum(wide * wide, -1, keepdims=True)
    factor = lax.rsqrt(squares / (heads * width) + 1e-05)
    return [total * factor for total in sums]


def stat_rows(columns, rows):
    lane = lax.broadcasted_iota(jnp.int32, (rows, LANES), 1)
    table = jnp.zeros((rows, LANES), jnp.float32)
    for index, column in enumerate(columns):
        table = jnp.where(lane == index, column, table)
    return table.T[:STAT_ROWS]


def split_refs(counts, refs):
    parts = []
    for count in counts:
        parts.append(refs[:count])
        refs = refs[count:]
    return parts, refs


def rows_of(blocks, row_at, rows):
    parts = []
    at = 0
    for block in blocks:
        size = block.shape[0]
        low, high = max(row_at - at, 0), min(row_at + rows - at, size)
        if low < high:
            parts.append(block[low:high])
        at += size
    return jnp.concatenate(parts, 0) if len(parts) > 1 else parts[0]


def attend_kernel(counts, own, row_at, rows, table_at, *refs):
    blocks, refs = split_refs(counts, refs)
    gain, w_query, cosine, sine, wide_keys, wide_values, norms, mark, *outputs = refs
    pieces = [rows_of(one, row_at, rows) for one in blocks]
    (product,) = project_normed(pieces, gain, [w_query])
    cosine = cosine[table_at : table_at + rows]
    sine = sine[table_at : table_at + rows]
    kv_heads = wide_keys.shape[0]
    repeat = product.shape[1] // HD // kv_heads
    queries = [
        (rotate(product[:, head * HD : (head + 1) * HD], cosine, sine) * log2_scale).astype(
            jnp.bfloat16
        )
        for head in range(kv_heads * repeat)
    ]
    if own:
        outputs[2][...] = jnp.concatenate(queries, 1)
    ones = mark[: repeat * rows]
    second = lax.broadcasted_iota(jnp.int32, ones.shape, 1) == 1
    stacked = [
        jnp.concatenate(queries[head * repeat : (head + 1) * repeat], 0) for head in range(kv_heads)
    ]

    def store(summed, shifts):
        columns = []
        for head in range(kv_heads):
            denominator = summed[head][:, HD : HD + 1]
            seen = denominator > 0.0
            result = summed[head][:, :HD] / jnp.where(seen, denominator, 1.0)
            logs = shifts[head] + jnp.log2(jnp.where(seen, denominator, 1.0))
            logs = jnp.where(seen, logs, neg_large)
            for turn in range(repeat):
                part = slice(turn * rows, (turn + 1) * rows)
                at = (head * repeat + turn) * HD
                outputs[0][:rows, at : at + HD] = result[part].astype(outputs[0].dtype)
                columns.append(logs[part])
        stats = stat_rows(columns, rows)
        if own:
            outputs[1][...] = stats
            return
        outputs[0][rows:] = jnp.zeros((ROW_TILE, outputs[0].shape[1]), jnp.bfloat16)
        rest = jnp.concatenate([stats, jnp.zeros((ROW_TILE - STAT_ROWS, rows), jnp.float32)], 0)
        for part in range(3):
            rounded = rest.astype(jnp.bfloat16)
            outputs[0][rows:, part * rows : (part + 1) * rows] = rounded
            rest = rest - rounded.astype(jnp.float32)

    summed = []
    shifts = []
    slots = wide_keys.shape[1] // SLOT_TILES
    for head in range(kv_heads):
        wide = stacked[head].astype(jnp.float32)
        square = jnp.sum(wide * wide, -1, keepdims=True)
        bound = jnp.sqrt(square * jnp.maximum(norms[head : head + 1, :1], 0.0))
        shift = bound.astype(jnp.bfloat16).astype(jnp.float32)
        added = jnp.where(second, -shift, ones.astype(jnp.float32)).astype(jnp.bfloat16)
        wide = jnp.concatenate([stacked[head], added], 1)
        total = 0.0
        for at in range(0, slots * SLOT_TILES, slots):
            scores = dot_transposed(wide, wide_keys[head, at : at + slots])
            weights = jnp.exp2(scores).astype(jnp.bfloat16)
            total = total + dot(weights, wide_values[head, at : at + slots])
        summed.append(total)
        shifts.append(shift)
    store(summed, shifts)
    least = functools.reduce(
        jnp.minimum, [jnp.min(total[:, HD : HD + 1]) for total in summed]
    )

    @pl.when((least < least_sum) & (jnp.max(norms[...]) >= 0.0))
    def _():
        exact = []
        largest = []
        for head in range(kv_heads):
            scores = dot_transposed(jnp.concatenate([stacked[head], ones], 1), wide_keys[head])
            largest.append(jnp.max(scores, -1, keepdims=True))
            weights = jnp.exp2(scores - largest[head]).astype(jnp.bfloat16)
            exact.append(dot(weights, wide_values[head]))
        store(exact, largest)


def attend(
    pieces, gain, w_query, tables, wides, mark, own, row_at, rows, table_at,
    earlier,
):
    counts = [len(blocks) for blocks in pieces]
    flat = [block for blocks in pieces for block in blocks]
    out_width = w_query.shape[1]
    slots = wides[0].shape[1]
    if own:
        out_shape = [
            jax.ShapeDtypeStruct((rows, out_width), jnp.float32),
            jax.ShapeDtypeStruct((STAT_ROWS, rows), jnp.float32),
            jax.ShapeDtypeStruct((rows, out_width), jnp.bfloat16),
        ]
    else:
        out_shape = [jax.ShapeDtypeStruct((rows + ROW_TILE, out_width), jnp.bfloat16)]
    return call(
        functools.partial(attend_kernel, counts, own, row_at, rows, table_at),
        out_shape,
        [*flat, gain, w_query, *tables, *wides, mark],
        28,
        2 * rows * out_width * (w_query.shape[0] + 4 * slots),
        rows * out_width // HD * slots,
        "attend_own" if own else "attend_partner",
        earlier,
    )


def fresh_kernel(counts, table_at, *refs):
    blocks, refs = split_refs(counts, refs)
    gain, w_key, w_value, cosine, sine, new_keys, new_values = refs
    rows = new_keys.shape[0]
    pieces = [whole_of(one) for one in blocks]
    keys, values = project_normed(pieces, gain, [w_key, w_value])
    cosine = cosine[table_at : table_at + rows]
    sine = sine[table_at : table_at + rows]
    for head in range(keys.shape[1] // HD):
        own = slice(head * HD, (head + 1) * HD)
        new_keys[:, own] = rotate(keys[:, own], cosine, sine).astype(jnp.bfloat16)
    new_values[...] = values.astype(jnp.bfloat16)


def fresh(pieces, gain, w_key, w_value, tables, table_at, earlier):
    flat = [block for blocks in pieces for block in blocks]
    rows = sum(block.shape[0] for block in pieces[0])
    shape = jax.ShapeDtypeStruct((rows, w_key.shape[1]), jnp.bfloat16)
    return call(
        functools.partial(fresh_kernel, [len(blocks) for blocks in pieces], table_at),
        [shape, shape],
        [*flat, gain, w_key, w_value, *tables],
        20,
        4 * rows * w_key.size,
        0,
        "fresh_kv",
        earlier,
    )


def write_rows(target, fresh_rows, first):
    rows = fresh_rows.shape[0]
    slab_rows = target.shape[0]
    span = rows + ROW_TILE
    start = jnp.clip(first, 0, slab_rows - span)
    start = start - lax.rem(start, ROW_TILE)
    window = pl.ds(pl.multiple_of(start, ROW_TILE), span)
    shift = start - first
    place = lax.broadcasted_iota(jnp.int32, (span, rows), 0) + shift
    chosen = place == lax.broadcasted_iota(jnp.int32, (span, rows), 1)
    moved = dot(chosen.astype(jnp.bfloat16), fresh_rows)
    row = lax.broadcasted_iota(jnp.int32, (span, target.shape[1]), 0) + shift
    inside = (row >= 0) & (row < rows)
    old = target[window, :].astype(jnp.float32)
    target[window, :] = jnp.where(inside, moved, old).astype(jnp.bfloat16)


def attend_fresh_kernel(groups, requests, *refs):
    query_refs, refs = refs[:CHUNKS], refs[CHUNKS:]
    key_refs, value_refs, refs = refs[:groups], refs[groups : 2 * groups], refs[2 * groups :]
    partial, stats = refs
    position_in = place_of(requests)[1]
    rows, width = partial.shape
    kv_heads = key_refs[0].shape[1] // HD
    repeat = width // HD // kv_heads
    queries = whole_of(query_refs)
    token = lax.broadcasted_iota(jnp.int32, (rows, rows), 0)
    within = lax.broadcasted_iota(jnp.int32, (rows, rows), 1)
    causal = jnp.where(within <= token, 0.0, neg_large)
    causal = jnp.concatenate([causal] * repeat, 0)
    lane = lax.broadcasted_iota(jnp.int32, (rows, LANES), 1)
    ones = jnp.where(lane == 0, 1.0, 0.0).astype(jnp.bfloat16)
    hidden = [jnp.zeros((rows, LANES), jnp.bfloat16)]
    for turn in range(1, groups):
        later = source_of(position_in, turn, groups) > position_in
        hidden.append(jnp.where((lane == 0) & later, neg_large, 0.0).astype(jnp.bfloat16))
    columns = []
    for head in range(kv_heads):
        own = [
            slice((head * repeat + turn) * HD, (head * repeat + turn + 1) * HD)
            for turn in range(repeat)
        ]
        shared = slice(head * HD, (head + 1) * HD)
        stacked = jnp.concatenate([queries[:, one] for one in own], 0)
        stacked = jnp.concatenate([stacked, jnp.concatenate([ones] * repeat, 0)], 1)
        scores = [
            dot_transposed(stacked, jnp.concatenate([ref[:, shared], bias], 1))
            for ref, bias in zip(key_refs, hidden)
        ]
        scores = jnp.concatenate([scores[0] + causal] + scores[1:], 1)
        largest = jnp.max(scores, -1, keepdims=True)
        weights = jnp.exp2(scores - largest).astype(jnp.bfloat16)
        wide_values = [jnp.concatenate([ref[:, shared], ones], 1) for ref in value_refs]
        summed = dot(weights, jnp.concatenate(wide_values, 0))
        denominator = summed[:, HD : HD + 1]
        result = summed[:, :HD] / denominator
        logs = largest + jnp.log2(denominator)
        for turn, one in enumerate(own):
            part = slice(turn * rows, (turn + 1) * rows)
            partial[:, one] = result[part]
            columns.append(logs[part])
    stats[...] = stat_rows(columns, rows)


def attend_fresh(requests, queries, new_keys, new_values):
    groups = len(new_keys)
    rows = new_keys[0].shape[0]
    width = queries[0].shape[1]
    return call(
        functools.partial(attend_fresh_kernel, groups, requests),
        [
            jax.ShapeDtypeStruct((rows, width), jnp.float32),
            jax.ShapeDtypeStruct((STAT_ROWS, rows), jnp.float32),
        ],
        [*queries, *new_keys, *new_values],
        24,
        4 * rows * width * rows * groups,
        rows * width // HD * rows * groups,
        "attend_fresh",
    )


def update_kernel(groups, *refs):
    key_refs, value_refs, refs = refs[:groups], refs[groups : 2 * groups], refs[2 * groups :]
    keys, values, lengths_in, keys_updated, values_updated, done, lengths, semaphore = refs
    number = pltpu.make_async_copy(lengths_in, lengths, semaphore)
    number.start()
    keys_updated[...] = keys[...]
    values_updated[...] = values[...]
    done[...] = jnp.zeros(done.shape, done.dtype)
    number.wait()
    request, position_in = place_of(lengths.shape[0])
    rows = key_refs[0].shape[0]
    for turn in range(groups):
        source = source_of(position_in, turn, groups)
        first = lengths[request] + source * rows - position_in * keys.shape[0]
        write_rows(keys_updated, key_refs[turn][...], first)
        write_rows(values_updated, value_refs[turn][...], first)


def update(lengths, new_keys, new_values, keys, values, earlier):
    groups = len(new_keys)
    slab = jax.ShapeDtypeStruct(keys.shape, keys.dtype)
    return call(
        functools.partial(update_kernel, groups),
        [slab, slab, jax.ShapeDtypeStruct((STAT_ROWS, LANES), jnp.float32)],
        [*new_keys, *new_values, keys, values, lengths],
        20,
        4 * new_keys[0].size * new_keys[0].shape[0] * groups,
        0,
        "update_caches",
        earlier,
        [pltpu.SMEM(lengths.shape, lengths.dtype), pltpu.SemaphoreType.DMA],
    )


def combine_kernel(row_at, own_partial, own_stats, fresh_partial, fresh_stats, *refs):
    heads = lax.axis_size("head")
    chips = heads // CORES
    outputs = 2 * chips - 1
    received = refs[: -1 - outputs]
    w_out, merged_rows = refs[-1 - outputs], refs[-outputs]
    far = refs[1 - outputs :]
    width = own_partial.shape[1]
    rows = merged_rows.shape[0]
    part = slice(row_at, row_at + rows)
    padding = jnp.zeros((LANES - STAT_ROWS, rows), jnp.float32)
    stats = [own_stats[...], fresh_stats[:, part]]
    for ref in received:
        stats.append(
            sum(
                ref[rows:, turn * rows : (turn + 1) * rows].astype(jnp.float32)
                for turn in range(3)
            )[:STAT_ROWS]
        )
    logs = [jnp.concatenate([stat, padding], 0).T for stat in stats]
    largest = functools.reduce(jnp.maximum, logs)
    shares = [jnp.exp2(log - largest) for log in logs]
    total = functools.reduce(jnp.add, shares)
    shares = [share / total for share in shares]
    attended = []
    for head in range(width // HD):
        own = slice(head * HD, (head + 1) * HD)
        column = slice(head, head + 1)
        merged = own_partial[:, own] * shares[0][:, column]
        merged = merged + fresh_partial[part, own] * shares[1][:, column]
        for ref, share in zip(received, shares[2:]):
            merged = merged + ref[:rows, own].astype(jnp.float32) * share[:, column]
        attended.append(merged.astype(jnp.bfloat16))
    attended = jnp.concatenate(attended, 1)
    merged_rows[...] = attended
    for ahead in range(1, chips):
        result = block_product(attended, w_out, ahead, 1)
        middle = result.shape[1] // 2
        far[2 * ahead - 2][...] = result[:, :middle]
        far[2 * ahead - 1][...] = result[:, middle:]


def block_product(attended, w_out, ahead, flip):
    heads = lax.axis_size("head")
    block_width = w_out.shape[1] // heads
    block = lax.rem(lax.axis_index("head") + CORES * ahead, heads) ^ flip
    along = pl.ds(pl.multiple_of(block * block_width, LANES), block_width)
    return dot(attended, w_out[:, along]).astype(jnp.bfloat16)


def project_kernel(merged_rows, w_out, far, *near):
    attended = merged_rows[...]
    far[...] = block_product(attended, w_out, 0, 1)
    for ahead, target in enumerate(near):
        target[...] = block_product(attended, w_out, ahead, 0)


def combine(row_at, rows, own, fresh_part, received, w_out, heads, earlier):
    chips = heads // CORES
    width = w_out.shape[1] // heads
    merged = jax.ShapeDtypeStruct((rows, own[0].shape[1]), jnp.bfloat16)
    half = jax.ShapeDtypeStruct((rows, width // 2), jnp.bfloat16)
    merged, *far = call(
        functools.partial(combine_kernel, row_at),
        [merged] + [half] * (2 * chips - 2),
        [*own, *fresh_part, *received, w_out],
        20,
        rows * w_out.size,
        0,
        "combine",
        earlier,
    )
    return merged, [far[2 * k : 2 * k + 2] for k in range(chips - 1)]


def project(merged, w_out, heads):
    block = jax.ShapeDtypeStruct((merged.shape[0], w_out.shape[1] // heads), jnp.bfloat16)
    far, *near = call(
        project_kernel,
        [block] * (1 + heads // CORES),
        [merged, w_out],
        20,
        2 * merged.shape[0] * w_out.size,
        0,
        "project",
    )
    return far, near


def sum_kernel(count, *refs):
    total = refs[0][...].astype(jnp.float32)
    total = total + jnp.concatenate([ref[...] for ref in refs[1:count]], 1).astype(jnp.float32)
    refs[count][...] = total.astype(jnp.bfloat16)


def sum_cores(near, far, earlier):
    return call(
        functools.partial(sum_kernel, 1 + len(far)),
        [jax.ShapeDtypeStruct(near.shape, near.dtype)],
        [near, *far],
        8,
        near.size,
        0,
        "sum_cores",
        earlier,
    )[0]


def finish_kernel(*refs):
    *parts, result = refs
    count = len(parts) // CHUNKS
    rows = parts[0].shape[0]
    for chunk in range(CHUNKS):
        total = 0.0
        for ref in parts[chunk * count : (chunk + 1) * count]:
            total = total + ref[...].astype(jnp.float32)
        result[chunk * rows : (chunk + 1) * rows] = total.astype(jnp.bfloat16)


def finish(parts, earlier):
    rows, width = parts[0].shape
    shape = jax.ShapeDtypeStruct((CHUNKS * rows, width), jnp.bfloat16)
    flops = CHUNKS * rows * width
    return call(finish_kernel, [shape], parts, 8, flops, 0, "finish", earlier)[0]


def shards(
    tokens,
    norm_gain,
    w_query,
    w_key,
    w_value,
    w_out,
    keys_cache,
    values_cache,
    cached_lengths,
    rope_offsets,
):
    rows, width = tokens.shape
    requests = cached_lengths.shape[0]
    groups = lax.axis_size("seq") // requests
    heads = lax.axis_size("head")
    chips = heads // CORES
    chunk_rows = rows // CHUNKS
    gain = norm_gain.reshape(heads, 1, width)

    mark = marks(keys_cache.shape[0])
    tables = rope_tables(cached_lengths, rope_offsets, groups, rows, [mark])
    wides = widen(keys_cache, values_cache, mark, cached_lengths, tables[:1])

    def attend_rows(pieces, own, chunk, turn, earlier):
        at = chunk * chunk_rows
        return attend(
            pieces, gain, w_query, tables, wides, mark, own, at if own else 0,
            chunk_rows, turn * rows + at, earlier,
        )

    half = chunk_rows // 2
    from_chips = other_chips(tokens)
    crossed = other_core(tokens)
    own, early, late = relay([tokens], [rows, chunk_rows, rows - chunk_rows], [])
    first = [shifted(early, "seq", turn * requests) for turn in range(1, groups)]
    (late,) = relay([late], [rows - chunk_rows], from_chips + [wides[0]])
    second = [shifted(late, "seq", turn * requests) for turn in range(1, groups)]
    own_cuts = [relay([piece], [rows, half, half, rows - chunk_rows], [late]) for piece in from_chips]
    own_pieces = [[own]] + [[cut[0]] for cut in own_cuts] + [[crossed]]
    own_pieces += [[other_core(block) for block in cut[1:]] for cut in own_cuts]
    own_early = [
        blocks if len(blocks) == 1 else blocks[: len(blocks) - 1] for blocks in own_pieces
    ]
    earlier = [cut[0] for cut in own_cuts]
    first = [relay([piece], [chunk_rows], earlier)[0] for piece in first]
    first_from_chips = [other_chips(piece) for piece in first]
    *own_part, queries = attend_rows(own_early, True, 0, 0, first)
    own_queries = [queries]
    new_rows = [fresh(own_pieces, gain, w_key, w_value, tables, 0, [queries])]
    earlier = [new_rows[0][0]]
    second = [relay([piece], [rows - chunk_rows], earlier)[0] for piece in second]
    second_from_chips = [other_chips(piece) for piece in second]
    earlier = second

    def gather_cores(piece, from_chips, earlier):
        size = piece.shape[0]
        passed = [relay([one], [size, size // 2, size // 2], earlier) for one in from_chips]
        blocks = [[piece]] + [[one[0]] for one in passed] + [[other_core(piece)]]
        blocks += [[other_core(part) for part in one[1:]] for one in passed]
        return blocks, [one[0] for one in passed]

    gathered = []
    for piece, from_chips in zip(first, first_from_chips):
        blocks, passed = gather_cores(piece, from_chips, earlier)
        gathered.append([blocks])
        earlier = earlier + passed
    received = [[] for _ in range(CHUNKS)]
    for turn in range(1, groups):
        (packed,) = attend_rows(gathered[turn - 1][0], False, 0, turn, earlier)
        received[0].append(shifted(packed, "seq", -turn * requests))
        earlier = [packed]
    *late_part, queries = attend_rows(own_pieces, True, 1, 0, earlier)
    own_part += late_part
    own_queries.append(queries)
    earlier = [queries]
    for blocks, piece, from_chips in zip(gathered, second, second_from_chips):
        along, passed = gather_cores(piece, from_chips, earlier)
        blocks.append(along)
        earlier = earlier + passed
    for turn in range(1, groups):
        (packed,) = attend_rows(gathered[turn - 1][1], False, 1, turn, earlier)
        received[1].append(shifted(packed, "seq", -turn * requests))
        earlier = [packed]
    for turn in range(1, groups):
        pieces = [sum(blocks, []) for blocks in zip(*gathered[turn - 1])]
        new_rows.append(fresh(pieces, gain, w_key, w_value, tables, turn * rows, earlier))
    new_keys, new_values = zip(*new_rows)
    fresh_part = attend_fresh(requests, own_queries, new_keys, new_values)

    parts = []
    earlier = before_sums = []
    for chunk in range(CHUNKS):
        merged, fars = combine(
            chunk * chunk_rows, chunk_rows, own_part[2 * chunk : 2 * chunk + 2], fresh_part,
            received[chunk], w_out, heads, earlier,
        )
        fars = [[other_core(part) for part in far] for far in fars]
        far, near = project(merged, w_out, heads)
        earlier = [far] + before_sums
        sums = [sum_cores(one, parts_far, earlier) for one, parts_far in zip(near[1:], fars)]
        from_chips = [shifted(one, "head", CORES * k) for k, one in enumerate(sums, 1)]
        parts += [near[0], other_core(far), *from_chips]
        earlier, before_sums = sums, from_chips
    keys_updated, values_updated, done = update(
        cached_lengths, new_keys, new_values, keys_cache, values_cache, earlier
    )
    return (finish(parts, [done]), keys_updated, values_updated)


def solution(mesh):
    return jax.shard_map(
        shards,
        mesh=mesh,
        in_specs=(
            P("seq", "head"),
            P(),
            P(None, "head"),
            P(None, "head"),
            P(None, "head"),
            P("head", None),
            P("seq", "head"),
            P("seq", "head"),
            P(),
            P(),
        ),
        out_specs=(P("seq", "head"), P("seq", "head"), P("seq", "head")),
        check_vma=False,
    )
```

```python
import functools
import math

import jax
import jax.numpy as jnp
from jax import lax
from jax.experimental import pallas as pl
from jax.experimental.pallas import tpu as pltpu
from jax.sharding import PartitionSpec as P

HD = 128
LANES = 128
STAT_ROWS = 8
ROW_TILE = 16
CORES = 2
CHUNKS = 2
COST_WEIGHT = 0.0005
FIRST_MICROS = 2
FLOPS_PER_MICRO = 1_000_000_000
MIB = 1 << 20

rope_base = 500000.0
neg_large = -1e30
log2_scale = math.log2(math.e) / math.sqrt(HD)

VMEM = pl.BlockSpec(memory_space=pltpu.VMEM)
ANY = pl.BlockSpec(memory_space=pl.ANY)


def shifted(shard, axis, by):
    devices = lax.axis_size(axis)
    return lax.ppermute(shard, axis, [(i, (i + by) % devices) for i in range(devices)])


def other_core(shard):
    devices = lax.axis_size("head")
    return lax.ppermute(shard, "head", [(i, i ^ 1) for i in range(devices)])


def other_chips(own):
    chips = lax.axis_size("head") // CORES
    return [shifted(own, "head", CORES * k) for k in range(1, chips)]


def place_of(requests):
    member = lax.axis_index("seq")
    return lax.rem(member, requests), lax.div(member, requests)


def source_of(position_in, turn, groups):
    return lax.rem(position_in + (groups - turn), groups)


def dot(left, right):
    return jnp.dot(left, right, preferred_element_type=jnp.float32)


def dot_transposed(left, right):
    return lax.dot_general(
        left, right, (((1,), (1,)), ((), ())), preferred_element_type=jnp.float32
    )


def call(
    kernel, out_shape, arrays, limit, flops, transcendentals, name, earlier=(),
    scratch=(), micros=0,
):
    moved = sum(a.size * a.dtype.itemsize for a in arrays)
    moved += sum(math.prod(s.shape) * s.dtype.itemsize for s in out_shape)
    read = len(arrays)
    skipped = len(earlier)

    def body(*refs):
        kernel(*refs[:read], *refs[read + skipped :])

    return pl.pallas_call(
        body,
        out_shape=out_shape,
        in_specs=[VMEM] * len(arrays) + [ANY] * skipped,
        out_specs=[VMEM] * len(out_shape),
        scratch_shapes=scratch,
        compiler_params=pltpu.CompilerParams(vmem_limit_bytes=limit * MIB),
        cost_estimate=pl.CostEstimate(
            flops=max(int(COST_WEIGHT * flops), micros * FLOPS_PER_MICRO),
            bytes_accessed=int(COST_WEIGHT * moved),
            transcendentals=int(COST_WEIGHT * transcendentals),
        ),
        name=name,
    )(*arrays, *earlier)


def whole_of(blocks):
    parts = [block[...] for block in blocks]
    return jnp.concatenate(parts, 0) if len(parts) > 1 else parts[0]


def relay_kernel(count, *refs):
    whole = whole_of(refs[:count])
    at = 0
    for ref in refs[count:]:
        ref[...] = whole[at : at + ref.shape[0]]
        at = (at + ref.shape[0]) % whole.shape[0]


def relay(blocks, sizes, earlier):
    shapes = [jax.ShapeDtypeStruct((size, *blocks[0].shape[1:]), blocks[0].dtype) for size in sizes]
    kernel = functools.partial(relay_kernel, len(blocks))
    return call(kernel, shapes, [*blocks], 4, 0, 0, "relay", earlier)


def mark_kernel(mark):
    lane = lax.broadcasted_iota(jnp.int32, mark.shape, 1)
    mark[...] = jnp.where(lane == 0, 1.0, 0.0).astype(mark.dtype)


def marks(rows):
    shape = jax.ShapeDtypeStruct((rows, LANES), jnp.bfloat16)
    return call(mark_kernel, [shape], [], 4, 0, 0, "marks", micros=FIRST_MICROS)[0]


def tables_kernel(groups, lengths_in, offsets_in, cosine, sine, *scratch):
    lengths, offsets, semaphores = scratch
    numbers = [
        pltpu.make_async_copy(lengths_in, lengths, semaphores.at[0]),
        pltpu.make_async_copy(offsets_in, offsets, semaphores.at[1]),
    ]
    for copy in numbers:
        copy.start()
    rows = cosine.shape[0] // groups
    for copy in numbers:
        copy.wait()
    request, position_in = place_of(lengths.shape[0])
    lane = lax.broadcasted_iota(jnp.int32, (rows, LANES), 1)
    row = lax.broadcasted_iota(jnp.int32, (rows, LANES), 0)
    half = lax.rem(lane, HD // 2).astype(jnp.float32)
    frequency = jnp.exp2(half * (-2.0 / HD * math.log2(rope_base)))
    sign = jnp.where(lane < HD // 2, -1.0, 1.0)
    for turn in range(groups):
        first = source_of(position_in, turn, groups) * rows
        first = first + offsets[request] + lengths[request]
        angles = (row + first).astype(jnp.float32) * frequency
        part = slice(turn * rows, (turn + 1) * rows)
        cosine[part] = jnp.cos(angles)
        sine[part] = jnp.sin(angles) * sign


def rope_tables(lengths, offsets, groups, rows, earlier):
    table = jax.ShapeDtypeStruct((groups * rows, LANES), jnp.float32)
    return call(
        functools.partial(tables_kernel, groups),
        [table, table],
        [lengths, offsets],
        12,
        0,
        0,
        "rope_tables",
        earlier,
        [
            pltpu.SMEM(lengths.shape, lengths.dtype),
            pltpu.SMEM(offsets.shape, offsets.dtype),
            pltpu.SemaphoreType.DMA((2,)),
        ],
    )


def widen_kernel(keys, values, mark, lengths_in, wide_keys, wide_values, lengths, semaphore):
    number = pltpu.make_async_copy(lengths_in, lengths, semaphore)
    number.start()
    slots = keys.shape[0]
    heads = keys.shape[1] // HD
    for head in range(heads):
        own = slice(head * HD, (head + 1) * HD)
        wide_keys[head, :, :HD] = keys[:, own]
        wide_values[head, :, :HD] = values[:, own]
        wide_values[head, :, HD:] = mark[:slots]
    number.wait()
    request, position_in = place_of(lengths.shape[0])
    slot = lax.broadcasted_iota(jnp.int32, (slots, LANES), 0) + position_in * slots
    lane = lax.broadcasted_iota(jnp.int32, (slots, LANES), 1)
    bias = jnp.where((lane == 0) & (slot >= lengths[request]), neg_large, 0.0).astype(jnp.bfloat16)
    for head in range(heads):
        wide_keys[head, :, HD:] = bias


def widen(keys, values, mark, lengths, earlier):
    slots, width = keys.shape
    wide = jax.ShapeDtypeStruct((width // HD, slots, HD + LANES), jnp.bfloat16)
    return call(
        widen_kernel,
        [wide, wide],
        [keys, values, mark, lengths],
        12,
        0,
        0,
        "widen_caches",
        earlier,
        [pltpu.SMEM(lengths.shape, lengths.dtype), pltpu.SemaphoreType.DMA],
    )


def rotate(vectors, cosine, sine):
    return vectors * cosine + pltpu.roll(vectors, HD // 2, 1) * sine


def project_normed(pieces, gain, weights):
    heads = gain.shape[0]
    width = gain.shape[2]
    me = lax.axis_index("head")
    squares = 0.0
    sums = [0.0] * len(weights)
    for index, piece in enumerate(pieces):
        owner = lax.rem(me + (heads - CORES * (index % (heads // CORES))), heads)
        if index >= heads // CORES:
            owner = owner ^ 1
        wide = piece.astype(jnp.float32)
        scaled = (wide * gain[owner]).astype(jnp.bfloat16)
        along = pl.ds(pl.multiple_of(owner * width, LANES), width)
        for place, weight in enumerate(weights):
            sums[place] = sums[place] + dot(scaled, weight[along, :])
        squares = squares + jnp.sum(wide * wide, -1, keepdims=True)
    factor = lax.rsqrt(squares / (heads * width) + 1e-05)
    return [total * factor for total in sums]


def stat_rows(columns, rows):
    lane = lax.broadcasted_iota(jnp.int32, (rows, LANES), 1)
    table = jnp.zeros((rows, LANES), jnp.float32)
    for index, column in enumerate(columns):
        table = jnp.where(lane == index, column, table)
    return table.T[:STAT_ROWS]


def split_refs(counts, refs):
    parts = []
    for count in counts:
        parts.append(refs[:count])
        refs = refs[count:]
    return parts, refs


def rows_of(blocks, row_at, rows):
    parts = []
    at = 0
    for block in blocks:
        size = block.shape[0]
        low, high = max(row_at - at, 0), min(row_at + rows - at, size)
        if low < high:
            parts.append(block[low:high])
        at += size
    return jnp.concatenate(parts, 0) if len(parts) > 1 else parts[0]


def attend_kernel(counts, own, row_at, rows, table_at, *refs):
    blocks, refs = split_refs(counts, refs)
    gain, w_query, cosine, sine, wide_keys, wide_values, mark, *outputs = refs
    pieces = [rows_of(one, row_at, rows) for one in blocks]
    (product,) = project_normed(pieces, gain, [w_query])
    cosine = cosine[table_at : table_at + rows]
    sine = sine[table_at : table_at + rows]
    kv_heads = wide_keys.shape[0]
    repeat = product.shape[1] // HD // kv_heads
    queries = [
        (rotate(product[:, head * HD : (head + 1) * HD], cosine, sine) * log2_scale).astype(
            jnp.bfloat16
        )
        for head in range(kv_heads * repeat)
    ]
    step = min(rows, LANES)
    mark = mark[: repeat * step]
    tiles = [(head, at) for head in range(kv_heads) for at in range(0, rows, step)]

    def scores_of(head, at):
        stacked = jnp.concatenate(
            [query[at : at + step] for query in queries[head * repeat : (head + 1) * repeat]], 0
        )
        return dot_transposed(jnp.concatenate([stacked, mark], 1), wide_keys[head])

    columns = {}
    following = scores_of(*tiles[0])
    for index, (head, at) in enumerate(tiles):
        scores = following
        if index + 1 < len(tiles):
            following = scores_of(*tiles[index + 1])
        largest = jnp.max(scores, -1, keepdims=True)
        weights = jnp.exp2(scores - largest).astype(jnp.bfloat16)
        summed = dot(weights, wide_values[head])
        denominator = summed[:, HD : HD + 1]
        result = summed[:, :HD] / denominator
        logs = largest + jnp.log2(denominator)
        for turn in range(repeat):
            part = slice(turn * step, (turn + 1) * step)
            to = slice((head * repeat + turn) * HD, (head * repeat + turn + 1) * HD)
            outputs[0][at : at + step, to] = result[part].astype(outputs[0].dtype)
            columns.setdefault(head * repeat + turn, []).append(logs[part])
    stats = stat_rows([jnp.concatenate(parts, 0) for parts in columns.values()], rows)
    if own:
        outputs[1][...] = stats
        outputs[2][...] = jnp.concatenate(queries, 1)
        return
    outputs[0][rows:] = jnp.zeros((ROW_TILE, outputs[0].shape[1]), jnp.bfloat16)
    rest = jnp.concatenate([stats, jnp.zeros((ROW_TILE - STAT_ROWS, rows), jnp.float32)], 0)
    for part in range(3):
        rounded = rest.astype(jnp.bfloat16)
        outputs[0][rows:, part * rows : (part + 1) * rows] = rounded
        rest = rest - rounded.astype(jnp.float32)


def attend(
    pieces, gain, w_query, tables, wide_keys, wide_values, mark, own, row_at, rows, table_at,
    earlier,
):
    counts = [len(blocks) for blocks in pieces]
    flat = [block for blocks in pieces for block in blocks]
    out_width = w_query.shape[1]
    slots = wide_keys.shape[1]
    if own:
        out_shape = [
            jax.ShapeDtypeStruct((rows, out_width), jnp.float32),
            jax.ShapeDtypeStruct((STAT_ROWS, rows), jnp.float32),
            jax.ShapeDtypeStruct((rows, out_width), jnp.bfloat16),
        ]
    else:
        out_shape = [jax.ShapeDtypeStruct((rows + ROW_TILE, out_width), jnp.bfloat16)]
    return call(
        functools.partial(attend_kernel, counts, own, row_at, rows, table_at),
        out_shape,
        [*flat, gain, w_query, *tables, wide_keys, wide_values, mark],
        28,
        2 * rows * out_width * (w_query.shape[0] + 4 * slots),
        rows * out_width // HD * slots,
        "attend_own" if own else "attend_partner",
        earlier,
    )


def fresh_kernel(counts, table_at, *refs):
    blocks, refs = split_refs(counts, refs)
    gain, w_key, w_value, cosine, sine, new_keys, new_values = refs
    rows = new_keys.shape[0]
    pieces = [whole_of(one) for one in blocks]
    keys, values = project_normed(pieces, gain, [w_key, w_value])
    cosine = cosine[table_at : table_at + rows]
    sine = sine[table_at : table_at + rows]
    for head in range(keys.shape[1] // HD):
        own = slice(head * HD, (head + 1) * HD)
        new_keys[:, own] = rotate(keys[:, own], cosine, sine).astype(jnp.bfloat16)
    new_values[...] = values.astype(jnp.bfloat16)


def fresh(pieces, gain, w_key, w_value, tables, table_at, earlier):
    flat = [block for blocks in pieces for block in blocks]
    rows = sum(block.shape[0] for block in pieces[0])
    shape = jax.ShapeDtypeStruct((rows, w_key.shape[1]), jnp.bfloat16)
    return call(
        functools.partial(fresh_kernel, [len(blocks) for blocks in pieces], table_at),
        [shape, shape],
        [*flat, gain, w_key, w_value, *tables],
        20,
        4 * rows * w_key.size,
        0,
        "fresh_kv",
        earlier,
    )


def write_rows(target, fresh_rows, first):
    rows = fresh_rows.shape[0]
    slab_rows = target.shape[0]
    span = rows + ROW_TILE
    start = jnp.clip(first, 0, slab_rows - span)
    start = start - lax.rem(start, ROW_TILE)
    window = pl.ds(pl.multiple_of(start, ROW_TILE), span)
    shift = start - first
    place = lax.broadcasted_iota(jnp.int32, (span, rows), 0) + shift
    chosen = place == lax.broadcasted_iota(jnp.int32, (span, rows), 1)
    moved = dot(chosen.astype(jnp.bfloat16), fresh_rows)
    row = lax.broadcasted_iota(jnp.int32, (span, target.shape[1]), 0) + shift
    inside = (row >= 0) & (row < rows)
    old = target[window, :].astype(jnp.float32)
    target[window, :] = jnp.where(inside, moved, old).astype(jnp.bfloat16)


def attend_fresh_kernel(groups, requests, *refs):
    query_refs, refs = refs[:CHUNKS], refs[CHUNKS:]
    key_refs, value_refs, refs = refs[:groups], refs[groups : 2 * groups], refs[2 * groups :]
    partial, stats = refs
    position_in = place_of(requests)[1]
    rows, width = partial.shape
    kv_heads = key_refs[0].shape[1] // HD
    repeat = width // HD // kv_heads
    queries = whole_of(query_refs)
    token = lax.broadcasted_iota(jnp.int32, (rows, rows), 0)
    within = lax.broadcasted_iota(jnp.int32, (rows, rows), 1)
    causal = jnp.where(within <= token, 0.0, neg_large)
    causal = jnp.concatenate([causal] * repeat, 0)
    lane = lax.broadcasted_iota(jnp.int32, (rows, LANES), 1)
    ones = jnp.where(lane == 0, 1.0, 0.0).astype(jnp.bfloat16)
    hidden = [jnp.zeros((rows, LANES), jnp.bfloat16)]
    for turn in range(1, groups):
        later = source_of(position_in, turn, groups) > position_in
        hidden.append(jnp.where((lane == 0) & later, neg_large, 0.0).astype(jnp.bfloat16))
    columns = []
    for head in range(kv_heads):
        own = [
            slice((head * repeat + turn) * HD, (head * repeat + turn + 1) * HD)
            for turn in range(repeat)
        ]
        shared = slice(head * HD, (head + 1) * HD)
        stacked = jnp.concatenate([queries[:, one] for one in own], 0)
        stacked = jnp.concatenate([stacked, jnp.concatenate([ones] * repeat, 0)], 1)
        scores = [
            dot_transposed(stacked, jnp.concatenate([ref[:, shared], bias], 1))
            for ref, bias in zip(key_refs, hidden)
        ]
        scores = jnp.concatenate([scores[0] + causal] + scores[1:], 1)
        largest = jnp.max(scores, -1, keepdims=True)
        weights = jnp.exp2(scores - largest).astype(jnp.bfloat16)
        wide_values = [jnp.concatenate([ref[:, shared], ones], 1) for ref in value_refs]
        summed = dot(weights, jnp.concatenate(wide_values, 0))
        denominator = summed[:, HD : HD + 1]
        result = summed[:, :HD] / denominator
        logs = largest + jnp.log2(denominator)
        for turn, one in enumerate(own):
            part = slice(turn * rows, (turn + 1) * rows)
            partial[:, one] = result[part]
            columns.append(logs[part])
    stats[...] = stat_rows(columns, rows)


def attend_fresh(requests, queries, new_keys, new_values):
    groups = len(new_keys)
    rows = new_keys[0].shape[0]
    width = queries[0].shape[1]
    return call(
        functools.partial(attend_fresh_kernel, groups, requests),
        [
            jax.ShapeDtypeStruct((rows, width), jnp.float32),
            jax.ShapeDtypeStruct((STAT_ROWS, rows), jnp.float32),
        ],
        [*queries, *new_keys, *new_values],
        24,
        4 * rows * width * rows * groups,
        rows * width // HD * rows * groups,
        "attend_fresh",
    )


def update_kernel(groups, *refs):
    key_refs, value_refs, refs = refs[:groups], refs[groups : 2 * groups], refs[2 * groups :]
    keys, values, lengths_in, keys_updated, values_updated, done, lengths, semaphore = refs
    number = pltpu.make_async_copy(lengths_in, lengths, semaphore)
    number.start()
    keys_updated[...] = keys[...]
    values_updated[...] = values[...]
    done[...] = jnp.zeros(done.shape, done.dtype)
    number.wait()
    request, position_in = place_of(lengths.shape[0])
    rows = key_refs[0].shape[0]
    for turn in range(groups):
        source = source_of(position_in, turn, groups)
        first = lengths[request] + source * rows - position_in * keys.shape[0]
        write_rows(keys_updated, key_refs[turn][...], first)
        write_rows(values_updated, value_refs[turn][...], first)


def update(lengths, new_keys, new_values, keys, values, earlier):
    groups = len(new_keys)
    slab = jax.ShapeDtypeStruct(keys.shape, keys.dtype)
    return call(
        functools.partial(update_kernel, groups),
        [slab, slab, jax.ShapeDtypeStruct((STAT_ROWS, LANES), jnp.float32)],
        [*new_keys, *new_values, keys, values, lengths],
        20,
        4 * new_keys[0].size * new_keys[0].shape[0] * groups,
        0,
        "update_caches",
        earlier,
        [pltpu.SMEM(lengths.shape, lengths.dtype), pltpu.SemaphoreType.DMA],
    )


def combine_kernel(row_at, own_partial, own_stats, fresh_partial, fresh_stats, *refs):
    heads = lax.axis_size("head")
    chips = heads // CORES
    outputs = 3 * chips - 2
    received = refs[: -1 - outputs]
    w_out, merged_rows = refs[-1 - outputs], refs[-outputs]
    far = refs[1 - outputs :]
    near = far[2 * chips - 2 :]
    width = own_partial.shape[1]
    rows = merged_rows.shape[0]
    part = slice(row_at, row_at + rows)
    padding = jnp.zeros((LANES - STAT_ROWS, rows), jnp.float32)
    stats = [own_stats[...], fresh_stats[:, part]]
    for ref in received:
        stats.append(
            sum(
                ref[rows:, turn * rows : (turn + 1) * rows].astype(jnp.float32)
                for turn in range(3)
            )[:STAT_ROWS]
        )
    logs = [jnp.concatenate([stat, padding], 0).T for stat in stats]
    largest = functools.reduce(jnp.maximum, logs)
    shares = [jnp.exp2(log - largest) for log in logs]
    total = functools.reduce(jnp.add, shares)
    shares = [share / total for share in shares]
    attended = []
    for head in range(width // HD):
        own = slice(head * HD, (head + 1) * HD)
        column = slice(head, head + 1)
        merged = own_partial[:, own] * shares[0][:, column]
        merged = merged + fresh_partial[part, own] * shares[1][:, column]
        for ref, share in zip(received, shares[2:]):
            merged = merged + ref[:rows, own].astype(jnp.float32) * share[:, column]
        attended.append(merged.astype(jnp.bfloat16))
    attended = jnp.concatenate(attended, 1)
    merged_rows[...] = attended
    for ahead in range(1, chips):
        result = block_product(attended, w_out, ahead, 1)
        middle = result.shape[1] // 2
        far[2 * ahead - 2][...] = result[:, :middle]
        far[2 * ahead - 1][...] = result[:, middle:]
    for ahead in range(1, chips):
        near[ahead - 1][...] = block_product(attended, w_out, ahead, 0)


def block_product(attended, w_out, ahead, flip):
    heads = lax.axis_size("head")
    block_width = w_out.shape[1] // heads
    block = lax.rem(lax.axis_index("head") + CORES * ahead, heads) ^ flip
    along = pl.ds(pl.multiple_of(block * block_width, LANES), block_width)
    return dot(attended, w_out[:, along]).astype(jnp.bfloat16)


def project_kernel(merged_rows, w_out, left, right, near):
    attended = merged_rows[...]
    result = block_product(attended, w_out, 0, 1)
    middle = result.shape[1] // 2
    left[...] = result[:, :middle]
    right[...] = result[:, middle:]
    near[...] = block_product(attended, w_out, 0, 0)


def combine(row_at, rows, own, fresh_part, received, w_out, heads, earlier):
    chips = heads // CORES
    width = w_out.shape[1] // heads
    merged = jax.ShapeDtypeStruct((rows, own[0].shape[1]), jnp.bfloat16)
    half = jax.ShapeDtypeStruct((rows, width // 2), jnp.bfloat16)
    near = jax.ShapeDtypeStruct((rows, width), jnp.bfloat16)
    merged, *blocks = call(
        functools.partial(combine_kernel, row_at),
        [merged] + [half] * (2 * chips - 2) + [near] * (chips - 1),
        [*own, *fresh_part, *received, w_out],
        20,
        rows * w_out.size,
        0,
        "combine",
        earlier,
    )
    far = [blocks[2 * k : 2 * k + 2] for k in range(chips - 1)]
    return merged, far, blocks[2 * chips - 2 :]


def project(merged, w_out, heads, earlier):
    rows, width = merged.shape[0], w_out.shape[1] // heads
    half = jax.ShapeDtypeStruct((rows, width // 2), jnp.bfloat16)
    return call(
        project_kernel,
        [half, half, jax.ShapeDtypeStruct((rows, width), jnp.bfloat16)],
        [merged, w_out],
        20,
        merged.shape[0] * w_out.size,
        0,
        "project",
        earlier,
    )


def sum_kernel(count, *refs):
    total = refs[0][...].astype(jnp.float32)
    total = total + jnp.concatenate([ref[...] for ref in refs[1:count]], 1).astype(jnp.float32)
    refs[count][...] = total.astype(jnp.bfloat16)


def sum_cores(near, far, earlier):
    return call(
        functools.partial(sum_kernel, 1 + len(far)),
        [jax.ShapeDtypeStruct(near.shape, near.dtype)],
        [near, *far],
        8,
        near.size,
        0,
        "sum_cores",
        earlier,
    )[0]


def finish_kernel(counts, *refs):
    flat = [count for chunk in counts for count in chunk]
    blocks, (result,) = split_refs(flat, refs)
    at = 0
    for chunk in counts:
        total = 0.0
        for pieces in blocks[: len(chunk)]:
            whole = jnp.concatenate([ref[...] for ref in pieces], 1)
            total = total + whole.astype(jnp.float32)
        blocks = blocks[len(chunk) :]
        result[at : at + total.shape[0]] = total.astype(result.dtype)
        at += total.shape[0]


def finish(chunks, earlier):
    flat = [piece for chunk in chunks for pieces in chunk for piece in pieces]
    rows = sum(chunk[0][0].shape[0] for chunk in chunks)
    width = sum(piece.shape[1] for piece in chunks[0][0])
    shape = jax.ShapeDtypeStruct((rows, width), jnp.bfloat16)
    kernel = functools.partial(finish_kernel, [[len(pieces) for pieces in c] for c in chunks])
    return call(kernel, [shape], flat, 8, 0, 0, "finish", earlier)[0]


def shards(
    tokens,
    norm_gain,
    w_query,
    w_key,
    w_value,
    w_out,
    keys_cache,
    values_cache,
    cached_lengths,
    rope_offsets,
):
    rows, width = tokens.shape
    requests = cached_lengths.shape[0]
    groups = lax.axis_size("seq") // requests
    heads = lax.axis_size("head")
    chips = heads // CORES
    chunk_rows = rows // CHUNKS
    gain = norm_gain.reshape(heads, 1, width)

    mark = marks(keys_cache.shape[0])
    tables = rope_tables(cached_lengths, rope_offsets, groups, rows, [mark])
    wide_keys, wide_values = widen(keys_cache, values_cache, mark, cached_lengths, tables[:1])

    def attend_rows(pieces, own, chunk, turn, earlier):
        at = chunk * chunk_rows
        return attend(
            pieces, gain, w_query, tables, wide_keys, wide_values, mark, own, at if own else 0,
            chunk_rows, turn * rows + at, earlier,
        )

    half = chunk_rows // 2
    from_chips = other_chips(tokens)
    crossed = other_core(tokens)
    own, early, late = relay([tokens], [rows, chunk_rows, rows - chunk_rows], [])
    first = [shifted(early, "seq", turn * requests) for turn in range(1, groups)]
    (late,) = relay([late], [rows - chunk_rows], from_chips + [wide_keys])
    second = [shifted(late, "seq", turn * requests) for turn in range(1, groups)]
    own_cuts = [relay([piece], [rows, half, half, rows - chunk_rows], [late]) for piece in from_chips]
    own_pieces = [[own]] + [[cut[0]] for cut in own_cuts] + [[crossed]]
    own_pieces += [[other_core(block) for block in cut[1:]] for cut in own_cuts]
    own_early = [
        blocks if len(blocks) == 1 else blocks[: len(blocks) - 1] for blocks in own_pieces
    ]
    earlier = [cut[0] for cut in own_cuts]
    first = [relay([piece], [chunk_rows], earlier)[0] for piece in first]
    first_from_chips = [other_chips(piece) for piece in first]
    *own_part, queries = attend_rows(own_early, True, 0, 0, first)
    own_queries = [queries]
    new_rows = [fresh(own_pieces, gain, w_key, w_value, tables, 0, [queries])]
    earlier = [new_rows[0][0]]
    second = [relay([piece], [rows - chunk_rows], earlier)[0] for piece in second]
    second_from_chips = [other_chips(piece) for piece in second]
    earlier = second

    def gather_cores(piece, from_chips, earlier):
        size = piece.shape[0]
        passed = [relay([one], [size, size // 2, size // 2], earlier) for one in from_chips]
        blocks = [[piece]] + [[one[0]] for one in passed] + [[other_core(piece)]]
        blocks += [[other_core(part) for part in one[1:]] for one in passed]
        return blocks, [one[0] for one in passed]

    gathered = []
    for piece, from_chips in zip(first, first_from_chips):
        blocks, passed = gather_cores(piece, from_chips, earlier)
        gathered.append([blocks])
        earlier = earlier + passed
    received = [[] for _ in range(CHUNKS)]
    for turn in range(1, groups):
        (packed,) = attend_rows(gathered[turn - 1][0], False, 0, turn, earlier)
        received[0].append(shifted(packed, "seq", -turn * requests))
        earlier = [packed]
    *late_part, queries = attend_rows(own_pieces, True, 1, 0, earlier)
    own_part += late_part
    own_queries.append(queries)
    earlier = [queries]
    for blocks, piece, from_chips in zip(gathered, second, second_from_chips):
        along, passed = gather_cores(piece, from_chips, earlier)
        blocks.append(along)
        earlier = earlier + passed
    for turn in range(1, groups):
        (packed,) = attend_rows(gathered[turn - 1][1], False, 1, turn, earlier)
        received[1].append(shifted(packed, "seq", -turn * requests))
        earlier = [packed]
    for turn in range(1, groups):
        pieces = [sum(blocks, []) for blocks in zip(*gathered[turn - 1])]
        new_rows.append(fresh(pieces, gain, w_key, w_value, tables, turn * rows, earlier))
    new_keys, new_values = zip(*new_rows)
    fresh_part = attend_fresh(requests, own_queries, new_keys, new_values)

    parts = []
    earlier = before_sums = []
    for chunk in range(CHUNKS):
        merged, fars, nears = combine(
            chunk * chunk_rows, chunk_rows, own_part[2 * chunk : 2 * chunk + 2], fresh_part,
            received[chunk], w_out, heads, earlier,
        )
        fars = [[other_core(part) for part in far] for far in fars]
        sums = [sum_cores(one, far, [merged] + before_sums) for one, far in zip(nears, fars)]
        from_chips = [shifted(one, "head", CORES * k) for k, one in enumerate(sums, 1)]
        *far, near = project(merged, w_out, heads, sums)
        parts.append([[near], [other_core(part) for part in far], *[[one] for one in from_chips]])
        earlier, before_sums = [near], from_chips
    keys_updated, values_updated, done = update(
        cached_lengths, new_keys, new_values, keys_cache, values_cache, earlier
    )
    return (finish(parts, [done]), keys_updated, values_updated)


def solution(mesh):
    return jax.shard_map(
        shards,
        mesh=mesh,
        in_specs=(
            P("seq", "head"),
            P(),
            P(None, "head"),
            P(None, "head"),
            P(None, "head"),
            P("head", None),
            P("seq", "head"),
            P("seq", "head"),
            P(),
            P(),
        ),
        out_specs=(P("seq", "head"), P("seq", "head"), P("seq", "head")),
        check_vma=False,
    )
```

```python
import functools
import math

import jax
import jax.numpy as jnp
from jax import lax
from jax.experimental import pallas as pl
from jax.experimental.pallas import tpu as pltpu
from jax.sharding import PartitionSpec as P

HD = 128
LANES = 128
STAT_ROWS = 8
ROW_TILE = 16
CORES = 2
CHUNK_UNITS = (8, 8)
COST_WEIGHT = 0.0005
FIRST_MICROS = 2
FLOPS_PER_MICRO = 1_000_000_000
MIB = 1 << 20

rope_base = 500000.0
neg_large = -1e30
log2_scale = math.log2(math.e) / math.sqrt(HD)

VMEM = pl.BlockSpec(memory_space=pltpu.VMEM)
ANY = pl.BlockSpec(memory_space=pl.ANY)


def shifted(shard, axis, by):
    devices = lax.axis_size(axis)
    return lax.ppermute(shard, axis, [(i, (i + by) % devices) for i in range(devices)])


def other_core(shard):
    devices = lax.axis_size("head")
    return lax.ppermute(shard, "head", [(i, i ^ 1) for i in range(devices)])


def other_chips(own):
    chips = lax.axis_size("head") // CORES
    return [shifted(own, "head", CORES * k) for k in range(1, chips)]


def place_of(requests):
    member = lax.axis_index("seq")
    return lax.rem(member, requests), lax.div(member, requests)


def source_of(position_in, turn, groups):
    return lax.rem(position_in + (groups - turn), groups)


def dot(left, right):
    return jnp.dot(left, right, preferred_element_type=jnp.float32)


def dot_transposed(left, right):
    return lax.dot_general(
        left, right, (((1,), (1,)), ((), ())), preferred_element_type=jnp.float32
    )


def call(
    kernel, out_shape, arrays, limit, flops, transcendentals, name, earlier=(),
    scratch=(), micros=0,
):
    moved = sum(a.size * a.dtype.itemsize for a in arrays)
    moved += sum(math.prod(s.shape) * s.dtype.itemsize for s in out_shape)
    read = len(arrays)
    skipped = len(earlier)

    def body(*refs):
        kernel(*refs[:read], *refs[read + skipped :])

    return pl.pallas_call(
        body,
        out_shape=out_shape,
        in_specs=[VMEM] * len(arrays) + [ANY] * skipped,
        out_specs=[VMEM] * len(out_shape),
        scratch_shapes=scratch,
        compiler_params=pltpu.CompilerParams(vmem_limit_bytes=limit * MIB),
        cost_estimate=pl.CostEstimate(
            flops=max(int(COST_WEIGHT * flops), micros * FLOPS_PER_MICRO),
            bytes_accessed=int(COST_WEIGHT * moved),
            transcendentals=int(COST_WEIGHT * transcendentals),
        ),
        name=name,
    )(*arrays, *earlier)


def whole_of(blocks):
    parts = [block[...] for block in blocks]
    return jnp.concatenate(parts, 0) if len(parts) > 1 else parts[0]


def relay_kernel(count, *refs):
    whole = whole_of(refs[:count])
    at = 0
    for ref in refs[count:]:
        ref[...] = whole[at : at + ref.shape[0]]
        at = (at + ref.shape[0]) % whole.shape[0]


def relay(blocks, sizes, earlier):
    shapes = [jax.ShapeDtypeStruct((size, *blocks[0].shape[1:]), blocks[0].dtype) for size in sizes]
    kernel = functools.partial(relay_kernel, len(blocks))
    return call(kernel, shapes, [*blocks], 4, 0, 0, "relay", earlier)


def mark_kernel(mark):
    lane = lax.broadcasted_iota(jnp.int32, mark.shape, 1)
    mark[...] = jnp.where(lane == 0, 1.0, 0.0).astype(mark.dtype)


def marks(rows):
    shape = jax.ShapeDtypeStruct((rows, LANES), jnp.bfloat16)
    return call(mark_kernel, [shape], [], 4, 0, 0, "marks", micros=FIRST_MICROS)[0]


def tables_kernel(groups, lengths_in, offsets_in, cosine, sine, *scratch):
    lengths, offsets, semaphores = scratch
    numbers = [
        pltpu.make_async_copy(lengths_in, lengths, semaphores.at[0]),
        pltpu.make_async_copy(offsets_in, offsets, semaphores.at[1]),
    ]
    for copy in numbers:
        copy.start()
    rows = cosine.shape[0] // groups
    for copy in numbers:
        copy.wait()
    request, position_in = place_of(lengths.shape[0])
    lane = lax.broadcasted_iota(jnp.int32, (rows, LANES), 1)
    row = lax.broadcasted_iota(jnp.int32, (rows, LANES), 0)
    half = lax.rem(lane, HD // 2).astype(jnp.float32)
    frequency = jnp.exp2(half * (-2.0 / HD * math.log2(rope_base)))
    sign = jnp.where(lane < HD // 2, -1.0, 1.0)
    for turn in range(groups):
        first = source_of(position_in, turn, groups) * rows
        first = first + offsets[request] + lengths[request]
        angles = (row + first).astype(jnp.float32) * frequency
        part = slice(turn * rows, (turn + 1) * rows)
        cosine[part] = jnp.cos(angles)
        sine[part] = jnp.sin(angles) * sign


def rope_tables(lengths, offsets, groups, rows, earlier):
    table = jax.ShapeDtypeStruct((groups * rows, LANES), jnp.float32)
    return call(
        functools.partial(tables_kernel, groups),
        [table, table],
        [lengths, offsets],
        12,
        0,
        0,
        "rope_tables",
        earlier,
        [
            pltpu.SMEM(lengths.shape, lengths.dtype),
            pltpu.SMEM(offsets.shape, offsets.dtype),
            pltpu.SemaphoreType.DMA((2,)),
        ],
    )


def widen_kernel(keys, values, mark, lengths_in, wide_keys, wide_values, lengths, semaphore):
    number = pltpu.make_async_copy(lengths_in, lengths, semaphore)
    number.start()
    slots = keys.shape[0]
    heads = keys.shape[1] // HD
    for head in range(heads):
        own = slice(head * HD, (head + 1) * HD)
        wide_keys[head, :, :HD] = keys[:, own]
        wide_values[head, :, :HD] = values[:, own]
        wide_values[head, :, HD:] = mark[:slots]
    number.wait()
    request, position_in = place_of(lengths.shape[0])
    slot = lax.broadcasted_iota(jnp.int32, (slots, LANES), 0) + position_in * slots
    lane = lax.broadcasted_iota(jnp.int32, (slots, LANES), 1)
    bias = jnp.where((lane == 0) & (slot >= lengths[request]), neg_large, 0.0).astype(jnp.bfloat16)
    for head in range(heads):
        wide_keys[head, :, HD:] = bias


def widen(keys, values, mark, lengths, earlier):
    slots, width = keys.shape
    wide = jax.ShapeDtypeStruct((width // HD, slots, HD + LANES), jnp.bfloat16)
    return call(
        widen_kernel,
        [wide, wide],
        [keys, values, mark, lengths],
        12,
        0,
        0,
        "widen_caches",
        earlier,
        [pltpu.SMEM(lengths.shape, lengths.dtype), pltpu.SemaphoreType.DMA],
    )


def rotate(vectors, cosine, sine):
    return vectors * cosine + pltpu.roll(vectors, HD // 2, 1) * sine


def project_normed(pieces, gain, weights):
    heads = gain.shape[0]
    width = gain.shape[2]
    me = lax.axis_index("head")
    squares = 0.0
    sums = [0.0] * len(weights)
    for index, piece in enumerate(pieces):
        owner = lax.rem(me + (heads - CORES * (index % (heads // CORES))), heads)
        if index >= heads // CORES:
            owner = owner ^ 1
        wide = piece.astype(jnp.float32)
        scaled = (wide * gain[owner]).astype(jnp.bfloat16)
        along = pl.ds(pl.multiple_of(owner * width, LANES), width)
        for place, weight in enumerate(weights):
            sums[place] = sums[place] + dot(scaled, weight[along, :])
        squares = squares + jnp.sum(wide * wide, -1, keepdims=True)
    factor = lax.rsqrt(squares / (heads * width) + 1e-05)
    return [total * factor for total in sums]


def stat_rows(columns, rows):
    padded = -(-rows // LANES) * LANES
    lane = lax.broadcasted_iota(jnp.int32, (padded, LANES), 1)
    table = jnp.zeros((padded, LANES), jnp.float32)
    for index, column in enumerate(columns):
        if padded > rows:
            filler = jnp.zeros((padded - rows, 1), jnp.float32)
            column = jnp.concatenate([column, filler], 0)
        table = jnp.where(lane == index, column, table)
    return table.T[:STAT_ROWS]


def stat_columns(stats):
    padding = jnp.zeros((LANES - STAT_ROWS, stats.shape[1]), jnp.float32)
    return jnp.concatenate([stats, padding], 0).T


def stat_places(rows, width):
    lanes = -(-rows // LANES) * LANES
    in_row = width // lanes
    return [(part // in_row * ROW_TILE, part % in_row * lanes) for part in range(3)], lanes


def tail_rows(rows, width):
    return stat_places(rows, width)[0][-1][0] + ROW_TILE


def split_refs(counts, refs):
    parts = []
    for count in counts:
        parts.append(refs[:count])
        refs = refs[count:]
    return parts, refs


def rows_of(blocks, row_at, rows):
    parts = []
    at = 0
    for block in blocks:
        size = block.shape[0]
        low, high = max(row_at - at, 0), min(row_at + rows - at, size)
        if low < high:
            parts.append(block[low:high])
        at += size
    return jnp.concatenate(parts, 0) if len(parts) > 1 else parts[0]


def head_queries(product, cosine, sine):
    return [
        (rotate(product[:, at : at + HD], cosine, sine) * log2_scale).astype(jnp.bfloat16)
        for at in range(0, product.shape[1], HD)
    ]


def weigh(scores, values):
    largest = functools.reduce(
        jnp.maximum, [jnp.max(score, -1, keepdims=True) for score in scores]
    )
    summed = 0.0
    for score, value in zip(scores, values):
        weights = jnp.exp2(score - largest).astype(jnp.bfloat16)
        summed = summed + dot(weights, value)
    denominator = summed[:, HD : HD + 1]
    return summed[:, :HD] / denominator, largest + jnp.log2(denominator)


def attend_heads(queries, wide_keys, wide_values, mark, fresh, store):
    rows = queries.shape[0]
    kv_heads = wide_keys.shape[0]
    repeat = queries.shape[1] // HD // kv_heads
    marked = mark[: repeat * rows]
    scores = []
    values = []
    for head in range(kv_heads):
        shared = slice(head * HD, (head + 1) * HD)
        stacked = jnp.concatenate(
            [
                queries[:, (head * repeat + turn) * HD : (head * repeat + turn + 1) * HD]
                for turn in range(repeat)
            ],
            0,
        )
        wide = jnp.concatenate([stacked, marked], 1)
        found = [dot_transposed(wide, wide_keys[head])]
        held = [wide_values[head]]
        for keys, new_values, column, bias in fresh:
            if bias is None:
                added = jnp.concatenate([keys[:, shared], column], 1)
                found.append(dot_transposed(wide, added))
            else:
                bias = jnp.concatenate([bias] * repeat, 0)
                found.append(dot_transposed(stacked, keys[:, shared]) + bias)
            held.append(jnp.concatenate([new_values[:, shared], mark[: keys.shape[0]]], 1))
        scores.append(found)
        values.append(held)
    columns = []
    for head in range(kv_heads):
        result, logs = weigh(scores[head], values[head])
        for turn in range(repeat):
            part = slice(turn * rows, (turn + 1) * rows)
            store((head * repeat + turn) * HD, result[part])
            columns.append(logs[part])
    return stat_rows(columns, rows)


def attend_kernel(counts, groups, requests, turn, row_at, rows, table_at, *refs):
    blocks, refs = split_refs(counts, refs)
    gain, w_query, cosine, sine, wide_keys, wide_values, mark, keys, values, *outputs = refs
    pieces = [rows_of(one, row_at, rows) for one in blocks]
    (product,) = project_normed(pieces, gain, [w_query])
    part = slice(table_at, table_at + rows)
    queries = jnp.concatenate(head_queries(product, cosine[part], sine[part]), 1)
    target = outputs[0]

    def store(at, result):
        target[:rows, at : at + HD] = result.astype(target.dtype)

    if turn:
        position_in = place_of(requests)[1]
        hidden = position_in > source_of(position_in, turn, groups)
        bias = mark[: keys.shape[0]].astype(jnp.float32) * neg_large
        bias = jnp.where(hidden, bias, 0.0).astype(jnp.bfloat16)
        fresh = [(keys[...], values[...], bias, None)]
    else:
        fresh = []
        if row_at:
            fresh.append((keys[:row_at], values[:row_at], jnp.zeros((row_at, LANES), jnp.bfloat16), None))
        token = lax.broadcasted_iota(jnp.int32, (rows, rows), 0)
        within = lax.broadcasted_iota(jnp.int32, (rows, rows), 1)
        causal = jnp.where(within <= token, 0.0, neg_large)
        own = slice(row_at, row_at + rows)
        fresh.append((keys[own], values[own], None, causal))
    stats = attend_heads(queries, wide_keys, wide_values, mark, fresh, store)
    if not turn:
        outputs[1][...] = stats
        return
    target[rows:] = jnp.zeros((target.shape[0] - rows, target.shape[1]), target.dtype)
    places, lanes = stat_places(rows, target.shape[1])
    rest = jnp.concatenate([stats, jnp.zeros((ROW_TILE - STAT_ROWS, lanes), jnp.float32)], 0)
    for row, lane in places:
        rounded = rest.astype(target.dtype)
        target[rows + row : rows + row + ROW_TILE, lane : lane + lanes] = rounded
        rest = rest - rounded.astype(jnp.float32)


def attend(
    pieces, gain, w_query, tables, wides, mark, new_rows, place, turn, row_at, rows, table_at,
    earlier,
):
    counts = [len(blocks) for blocks in pieces]
    flat = [block for blocks in pieces for block in blocks]
    width = w_query.shape[1]
    slots = wides[0].shape[1]
    if turn:
        out_shape = [jax.ShapeDtypeStruct((rows + tail_rows(rows, width), width), jnp.bfloat16)]
    else:
        out_shape = [
            jax.ShapeDtypeStruct((rows, width), jnp.float32),
            jax.ShapeDtypeStruct((STAT_ROWS, -(-rows // LANES) * LANES), jnp.float32),
        ]
    return call(
        functools.partial(attend_kernel, counts, *place, turn, row_at, rows, table_at),
        out_shape,
        [*flat, gain, w_query, *tables, *wides, mark, *new_rows],
        28,
        2 * rows * width * (w_query.shape[0] + 4 * slots),
        rows * width // HD * slots,
        "attend_partner" if turn else "attend_own",
        earlier,
    )


def fresh_kernel(counts, table_at, *refs):
    blocks, refs = split_refs(counts, refs)
    gain, w_key, w_value, cosine, sine, new_keys, new_values = refs
    rows = new_keys.shape[0]
    pieces = [whole_of(one) for one in blocks]
    keys, values = project_normed(pieces, gain, [w_key, w_value])
    cosine = cosine[table_at : table_at + rows]
    sine = sine[table_at : table_at + rows]
    for head in range(keys.shape[1] // HD):
        own = slice(head * HD, (head + 1) * HD)
        new_keys[:, own] = rotate(keys[:, own], cosine, sine).astype(jnp.bfloat16)
    new_values[...] = values.astype(jnp.bfloat16)


def fresh(pieces, gain, w_key, w_value, tables, table_at, earlier):
    flat = [block for blocks in pieces for block in blocks]
    rows = sum(block.shape[0] for block in pieces[0])
    shape = jax.ShapeDtypeStruct((rows, w_key.shape[1]), jnp.bfloat16)
    return call(
        functools.partial(fresh_kernel, [len(blocks) for blocks in pieces], table_at),
        [shape, shape],
        [*flat, gain, w_key, w_value, *tables],
        20,
        4 * rows * w_key.size,
        0,
        "fresh_kv",
        earlier,
    )


def write_rows(target, fresh_rows, first):
    rows = fresh_rows.shape[0]
    slab_rows = target.shape[0]
    span = rows + ROW_TILE
    start = jnp.clip(first, 0, slab_rows - span)
    start = start - lax.rem(start, ROW_TILE)
    window = pl.ds(pl.multiple_of(start, ROW_TILE), span)
    shift = start - first
    place = lax.broadcasted_iota(jnp.int32, (span, rows), 0) + shift
    chosen = place == lax.broadcasted_iota(jnp.int32, (span, rows), 1)
    moved = dot(chosen.astype(jnp.bfloat16), fresh_rows)
    row = lax.broadcasted_iota(jnp.int32, (span, target.shape[1]), 0) + shift
    inside = (row >= 0) & (row < rows)
    old = target[window, :].astype(jnp.float32)
    target[window, :] = jnp.where(inside, moved, old).astype(jnp.bfloat16)


def update_kernel(groups, *refs):
    key_refs, value_refs, refs = refs[:groups], refs[groups : 2 * groups], refs[2 * groups :]
    keys, values, lengths_in, keys_updated, values_updated, done, lengths, semaphore = refs
    number = pltpu.make_async_copy(lengths_in, lengths, semaphore)
    number.start()
    keys_updated[...] = keys[...]
    values_updated[...] = values[...]
    done[...] = jnp.zeros(done.shape, done.dtype)
    number.wait()
    request, position_in = place_of(lengths.shape[0])
    rows = key_refs[0].shape[0]
    for turn in range(groups):
        source = source_of(position_in, turn, groups)
        first = lengths[request] + source * rows - position_in * keys.shape[0]
        write_rows(keys_updated, key_refs[turn][...], first)
        write_rows(values_updated, value_refs[turn][...], first)


def update(lengths, new_keys, new_values, keys, values, earlier):
    groups = len(new_keys)
    slab = jax.ShapeDtypeStruct(keys.shape, keys.dtype)
    return call(
        functools.partial(update_kernel, groups),
        [slab, slab, jax.ShapeDtypeStruct((STAT_ROWS, LANES), jnp.float32)],
        [*new_keys, *new_values, keys, values, lengths],
        20,
        4 * new_keys[0].size * new_keys[0].shape[0] * groups,
        0,
        "update_caches",
        earlier,
        [pltpu.SMEM(lengths.shape, lengths.dtype), pltpu.SemaphoreType.DMA],
    )


def combine_kernel(own_partial, own_stats, *refs):
    heads = lax.axis_size("head")
    chips = heads // CORES
    outputs = 2 * chips - 1
    received = refs[: -1 - outputs]
    w_out, merged_rows = refs[-1 - outputs], refs[-outputs]
    far = refs[1 - outputs :]
    rows, width = own_partial.shape
    logs = [stat_columns(own_stats[...])[:rows]]
    places, lanes = stat_places(rows, width)
    for ref in received:
        stats = sum(
            ref[rows + row : rows + row + ROW_TILE, lane : lane + lanes].astype(jnp.float32)
            for row, lane in places
        )
        logs.append(stat_columns(stats[:STAT_ROWS])[:rows])
    largest = functools.reduce(jnp.maximum, logs)
    shares = [jnp.exp2(log - largest) for log in logs]
    total = functools.reduce(jnp.add, shares)
    shares = [share / total for share in shares]
    attended = []
    for head in range(width // HD):
        own = slice(head * HD, (head + 1) * HD)
        column = slice(head, head + 1)
        merged = own_partial[:, own] * shares[0][:, column]
        for ref, share in zip(received, shares[1:]):
            merged = merged + ref[:rows, own].astype(jnp.float32) * share[:, column]
        attended.append(merged.astype(jnp.bfloat16))
    attended = jnp.concatenate(attended, 1)
    merged_rows[...] = attended
    for ahead in range(1, chips):
        result = block_product(attended, w_out, ahead, 1)
        middle = result.shape[1] // 2
        far[2 * ahead - 2][...] = result[:, :middle]
        far[2 * ahead - 1][...] = result[:, middle:]


def block_product(attended, w_out, ahead, flip):
    heads = lax.axis_size("head")
    block_width = w_out.shape[1] // heads
    block = lax.rem(lax.axis_index("head") + CORES * ahead, heads) ^ flip
    along = pl.ds(pl.multiple_of(block * block_width, LANES), block_width)
    return dot(attended, w_out[:, along]).astype(jnp.bfloat16)


def project_kernel(merged_rows, w_out, far, *near):
    attended = merged_rows[...]
    far[...] = block_product(attended, w_out, 0, 1)
    for ahead, target in enumerate(near):
        target[...] = block_product(attended, w_out, ahead, 0)


def combine(own, received, w_out, heads, earlier):
    chips = heads // CORES
    rows = own[0].shape[0]
    width = w_out.shape[1] // heads
    merged = jax.ShapeDtypeStruct((rows, own[0].shape[1]), jnp.bfloat16)
    half = jax.ShapeDtypeStruct((rows, width // 2), jnp.bfloat16)
    merged, *far = call(
        combine_kernel,
        [merged] + [half] * (2 * chips - 2),
        [*own, *received, w_out],
        20,
        rows * w_out.size,
        0,
        "combine",
        earlier,
    )
    return merged, [far[2 * k : 2 * k + 2] for k in range(chips - 1)]


def project(merged, w_out, heads):
    block = jax.ShapeDtypeStruct((merged.shape[0], w_out.shape[1] // heads), jnp.bfloat16)
    far, *near = call(
        project_kernel,
        [block] * (1 + heads // CORES),
        [merged, w_out],
        20,
        2 * merged.shape[0] * w_out.size,
        0,
        "project",
    )
    return far, near


def store_pieces(block, targets):
    width = targets[0].shape[1]
    for index, target in enumerate(targets):
        target[...] = block[:, index * width : (index + 1) * width]


def sum_kernel(count, near, *refs):
    far, pieces = refs[:count], refs[count:]
    total = jnp.concatenate([ref[...] for ref in far], 1).astype(jnp.float32)
    store_pieces((near[...].astype(jnp.float32) + total).astype(jnp.bfloat16), pieces)


def sum_cores(near, far, pieces, earlier):
    rows, width = near.shape
    shape = jax.ShapeDtypeStruct((rows, width // pieces), near.dtype)
    kernel = functools.partial(sum_kernel, len(far))
    return call(kernel, [shape] * pieces, [near, *far], 8, near.size, 0, "sum_cores", earlier)


def finish_kernel(counts, *refs):
    flat = [count for chunk in counts for count in chunk]
    blocks, (result,) = split_refs(flat, refs)
    at = 0
    for chunk in counts:
        total = 0.0
        for pieces in blocks[: len(chunk)]:
            whole = jnp.concatenate([ref[...] for ref in pieces], 1)
            total = total + whole.astype(jnp.float32)
        blocks = blocks[len(chunk) :]
        result[at : at + total.shape[0]] = total.astype(result.dtype)
        at += total.shape[0]


def finish(chunks, earlier):
    flat = [piece for chunk in chunks for pieces in chunk for piece in pieces]
    rows = sum(chunk[0][0].shape[0] for chunk in chunks)
    width = sum(piece.shape[1] for piece in chunks[0][0])
    shape = jax.ShapeDtypeStruct((rows, width), jnp.bfloat16)
    kernel = functools.partial(finish_kernel, [[len(pieces) for pieces in c] for c in chunks])
    return call(kernel, [shape], flat, 8, 0, 0, "finish", earlier)[0]


def shards(
    tokens,
    norm_gain,
    w_query,
    w_key,
    w_value,
    w_out,
    keys_cache,
    values_cache,
    cached_lengths,
    rope_offsets,
):
    rows, width = tokens.shape
    requests = cached_lengths.shape[0]
    groups = lax.axis_size("seq") // requests
    heads = lax.axis_size("head")
    chips = heads // CORES
    sizes = [rows * units // sum(CHUNK_UNITS) for units in CHUNK_UNITS]
    starts = [0, sizes[0]]
    gain = norm_gain.reshape(heads, 1, width)

    mark = marks(keys_cache.shape[0])
    tables = rope_tables(cached_lengths, rope_offsets, groups, rows, [mark])
    wide_keys, wide_values = widen(keys_cache, values_cache, mark, cached_lengths, tables[:1])

    def attend_rows(pieces, turn, chunk, earlier):
        at = starts[chunk]
        return attend(
            pieces, gain, w_query, tables, [wide_keys, wide_values], mark, new_rows[0],
            (groups, requests), turn, 0 if turn else at, sizes[chunk], turn * rows + at, earlier,
        )

    def in_halves(size):
        low = -(-size // (2 * ROW_TILE)) * ROW_TILE
        return [low, size - low]

    from_chips = other_chips(tokens)
    crossed = other_core(tokens)
    own, early, late = relay([tokens], [rows, *sizes], [])
    first = [shifted(early, "seq", turn * requests) for turn in range(1, groups)]
    (late,) = relay([late], sizes[1:], from_chips + [wide_keys])
    second = [shifted(late, "seq", turn * requests) for turn in range(1, groups)]
    own_cuts = [
        relay([piece], [rows, *in_halves(sizes[0]), sizes[1]], [late]) for piece in from_chips
    ]
    own_pieces = [[own]] + [[cut[0]] for cut in own_cuts] + [[crossed]]
    own_pieces += [[other_core(block) for block in cut[1:]] for cut in own_cuts]
    own_early = [
        blocks if len(blocks) == 1 else blocks[: len(blocks) - 1] for blocks in own_pieces
    ]
    earlier = [cut[0] for cut in own_cuts]
    first = [relay([piece], sizes[:1], earlier)[0] for piece in first]
    first_from_chips = [other_chips(piece) for piece in first]
    new_rows = [fresh(own_pieces, gain, w_key, w_value, tables, 0, first)]
    own_part = attend_rows(own_early, 0, 0, [new_rows[0][0]])
    earlier = own_part[:1]
    second = [relay([piece], sizes[1:], earlier)[0] for piece in second]
    second_from_chips = [other_chips(piece) for piece in second]
    earlier = second

    def gather_cores(piece, from_chips, earlier):
        size = piece.shape[0]
        passed = [relay([one], [size, *in_halves(size)], earlier) for one in from_chips]
        blocks = [[piece]] + [[one[0]] for one in passed] + [[other_core(piece)]]
        blocks += [[other_core(part) for part in one[1:]] for one in passed]
        return blocks, [one[0] for one in passed]

    gathered = []
    for piece, from_chips in zip(first, first_from_chips):
        blocks, passed = gather_cores(piece, from_chips, earlier)
        gathered.append([blocks])
        earlier = earlier + passed
    received = [[] for _ in range(len(sizes))]
    for turn in range(1, groups):
        (packed,) = attend_rows(gathered[turn - 1][0], turn, 0, earlier)
        received[0].append(shifted(packed, "seq", -turn * requests))
        earlier = [packed]
    own_part = [own_part, attend_rows(own_pieces, 0, 1, earlier)]
    earlier = [own_part[1][0]]
    for blocks, piece, from_chips in zip(gathered, second, second_from_chips):
        along, passed = gather_cores(piece, from_chips, earlier)
        blocks.append(along)
        earlier = earlier + passed
    for turn in range(1, groups):
        (packed,) = attend_rows(gathered[turn - 1][1], turn, 1, earlier)
        received[1].append(shifted(packed, "seq", -turn * requests))
        earlier = [packed]
    parts = []
    before_sums = []
    for chunk in range(len(sizes)):
        merged, fars = combine(own_part[chunk], received[chunk], w_out, heads, earlier)
        fars = [[other_core(part) for part in far] for far in fars]
        far, near = project(merged, w_out, heads)
        earlier = [far] + before_sums
        pieces = 1
        sums = [sum_cores(one, parts_far, pieces, earlier) for one, parts_far in zip(near[1:], fars)]
        from_chips = [
            [shifted(piece, "head", CORES * k) for piece in pieces]
            for k, pieces in enumerate(sums, 1)
        ]
        parts.append([[near[0]], [other_core(far)], *from_chips])
        earlier = [pieces[0] for pieces in sums]
        before_sums = [piece for pieces in from_chips for piece in pieces]
    for turn in range(1, groups):
        pieces = [sum(blocks, []) for blocks in zip(*gathered[turn - 1])]
        new_rows.append(fresh(pieces, gain, w_key, w_value, tables, turn * rows, earlier))
        earlier = [new_rows[-1][0]]
    new_keys, new_values = zip(*new_rows)
    keys_updated, values_updated, done = update(
        cached_lengths, new_keys, new_values, keys_cache, values_cache, earlier
    )
    return (finish(parts, [done]), keys_updated, values_updated)


def solution(mesh):
    return jax.shard_map(
        shards,
        mesh=mesh,
        in_specs=(
            P("seq", "head"),
            P(),
            P(None, "head"),
            P(None, "head"),
            P(None, "head"),
            P("head", None),
            P("seq", "head"),
            P("seq", "head"),
            P(),
            P(),
        ),
        out_specs=(P("seq", "head"), P("seq", "head"), P("seq", "head")),
        check_vma=False,
    )
```

```python
import functools
import math

import jax
import jax.numpy as jnp
from jax import lax
from jax.experimental import pallas as pl
from jax.experimental.pallas import tpu as pltpu
from jax.sharding import PartitionSpec as P

HD = 128
LANES = 128
STAT_ROWS = 8
ROW_TILE = 16
CORES = 2
CHUNKS = 2
COST_WEIGHT = 0.0005
FIRST_MICROS = 2
FLOPS_PER_MICRO = 1_000_000_000
MIB = 1 << 20

rope_base = 500000.0
neg_large = -1e30
log2_scale = math.log2(math.e) / math.sqrt(HD)

VMEM = pl.BlockSpec(memory_space=pltpu.VMEM)
ANY = pl.BlockSpec(memory_space=pl.ANY)


def shifted(shard, axis, by):
    devices = lax.axis_size(axis)
    return lax.ppermute(shard, axis, [(i, (i + by) % devices) for i in range(devices)])


def other_core(shard):
    devices = lax.axis_size("head")
    return lax.ppermute(shard, "head", [(i, i ^ 1) for i in range(devices)])


def other_chips(own):
    chips = lax.axis_size("head") // CORES
    return [shifted(own, "head", CORES * k) for k in range(1, chips)]


def place_of(requests):
    member = lax.axis_index("seq")
    return lax.rem(member, requests), lax.div(member, requests)


def source_of(position_in, turn, groups):
    return lax.rem(position_in + (groups - turn), groups)


def dot(left, right):
    return jnp.dot(left, right, preferred_element_type=jnp.float32)


def dot_transposed(left, right):
    return lax.dot_general(
        left, right, (((1,), (1,)), ((), ())), preferred_element_type=jnp.float32
    )


def call(
    kernel, out_shape, arrays, limit, flops, transcendentals, name, earlier=(),
    scratch=(), micros=0,
):
    moved = sum(a.size * a.dtype.itemsize for a in arrays)
    moved += sum(math.prod(s.shape) * s.dtype.itemsize for s in out_shape)
    read = len(arrays)
    skipped = len(earlier)

    def body(*refs):
        kernel(*refs[:read], *refs[read + skipped :])

    return pl.pallas_call(
        body,
        out_shape=out_shape,
        in_specs=[VMEM] * len(arrays) + [ANY] * skipped,
        out_specs=[VMEM] * len(out_shape),
        scratch_shapes=scratch,
        compiler_params=pltpu.CompilerParams(vmem_limit_bytes=limit * MIB),
        cost_estimate=pl.CostEstimate(
            flops=max(int(COST_WEIGHT * flops), micros * FLOPS_PER_MICRO),
            bytes_accessed=int(COST_WEIGHT * moved),
            transcendentals=int(COST_WEIGHT * transcendentals),
        ),
        name=name,
    )(*arrays, *earlier)


def whole_of(blocks):
    parts = [block[...] for block in blocks]
    return jnp.concatenate(parts, 0) if len(parts) > 1 else parts[0]


def relay_kernel(count, *refs):
    whole = whole_of(refs[:count])
    at = 0
    for ref in refs[count:]:
        ref[...] = whole[at : at + ref.shape[0]]
        at = (at + ref.shape[0]) % whole.shape[0]


def relay(blocks, sizes, earlier):
    shapes = [jax.ShapeDtypeStruct((size, *blocks[0].shape[1:]), blocks[0].dtype) for size in sizes]
    kernel = functools.partial(relay_kernel, len(blocks))
    return call(kernel, shapes, [*blocks], 4, 0, 0, "relay", earlier)


def mark_kernel(mark):
    lane = lax.broadcasted_iota(jnp.int32, mark.shape, 1)
    mark[...] = jnp.where(lane == 0, 1.0, 0.0).astype(mark.dtype)


def marks(rows):
    shape = jax.ShapeDtypeStruct((rows, LANES), jnp.bfloat16)
    return call(mark_kernel, [shape], [], 4, 0, 0, "marks", micros=FIRST_MICROS)[0]


def tables_kernel(groups, lengths_in, offsets_in, cosine, sine, *scratch):
    lengths, offsets, semaphores = scratch
    numbers = [
        pltpu.make_async_copy(lengths_in, lengths, semaphores.at[0]),
        pltpu.make_async_copy(offsets_in, offsets, semaphores.at[1]),
    ]
    for copy in numbers:
        copy.start()
    rows = cosine.shape[0] // groups
    for copy in numbers:
        copy.wait()
    request, position_in = place_of(lengths.shape[0])
    lane = lax.broadcasted_iota(jnp.int32, (rows, LANES), 1)
    row = lax.broadcasted_iota(jnp.int32, (rows, LANES), 0)
    half = lax.rem(lane, HD // 2).astype(jnp.float32)
    frequency = jnp.exp2(half * (-2.0 / HD * math.log2(rope_base)))
    sign = jnp.where(lane < HD // 2, -1.0, 1.0)
    for turn in range(groups):
        first = source_of(position_in, turn, groups) * rows
        first = first + offsets[request] + lengths[request]
        angles = (row + first).astype(jnp.float32) * frequency
        part = slice(turn * rows, (turn + 1) * rows)
        cosine[part] = jnp.cos(angles)
        sine[part] = jnp.sin(angles) * sign


def rope_tables(lengths, offsets, groups, rows, earlier):
    table = jax.ShapeDtypeStruct((groups * rows, LANES), jnp.float32)
    return call(
        functools.partial(tables_kernel, groups),
        [table, table],
        [lengths, offsets],
        12,
        0,
        0,
        "rope_tables",
        earlier,
        [
            pltpu.SMEM(lengths.shape, lengths.dtype),
            pltpu.SMEM(offsets.shape, offsets.dtype),
            pltpu.SemaphoreType.DMA((2,)),
        ],
    )


def widen_kernel(keys, values, mark, lengths_in, wide_keys, wide_values, lengths, semaphore):
    number = pltpu.make_async_copy(lengths_in, lengths, semaphore)
    number.start()
    slots = keys.shape[0]
    heads = keys.shape[1] // HD
    for head in range(heads):
        own = slice(head * HD, (head + 1) * HD)
        wide_keys[head, :, :HD] = keys[:, own]
        wide_values[head, :, :HD] = values[:, own]
        wide_values[head, :, HD:] = mark[:slots]
    number.wait()
    request, position_in = place_of(lengths.shape[0])
    slot = lax.broadcasted_iota(jnp.int32, (slots, LANES), 0) + position_in * slots
    lane = lax.broadcasted_iota(jnp.int32, (slots, LANES), 1)
    bias = jnp.where((lane == 0) & (slot >= lengths[request]), neg_large, 0.0).astype(jnp.bfloat16)
    for head in range(heads):
        wide_keys[head, :, HD:] = bias


def widen(keys, values, mark, lengths, earlier):
    slots, width = keys.shape
    wide = jax.ShapeDtypeStruct((width // HD, slots, HD + LANES), jnp.bfloat16)
    return call(
        widen_kernel,
        [wide, wide],
        [keys, values, mark, lengths],
        12,
        0,
        0,
        "widen_caches",
        earlier,
        [pltpu.SMEM(lengths.shape, lengths.dtype), pltpu.SemaphoreType.DMA],
    )


def rotate(vectors, cosine, sine):
    return vectors * cosine + pltpu.roll(vectors, HD // 2, 1) * sine


def project_normed(pieces, gain, weights):
    heads = gain.shape[0]
    width = gain.shape[2]
    me = lax.axis_index("head")
    squares = 0.0
    sums = [0.0] * len(weights)
    for index, piece in enumerate(pieces):
        owner = lax.rem(me + (heads - CORES * (index % (heads // CORES))), heads)
        if index >= heads // CORES:
            owner = owner ^ 1
        wide = piece.astype(jnp.float32)
        scaled = (wide * gain[owner]).astype(jnp.bfloat16)
        along = pl.ds(pl.multiple_of(owner * width, LANES), width)
        for place, weight in enumerate(weights):
            sums[place] = sums[place] + dot(scaled, weight[along, :])
        squares = squares + jnp.sum(wide * wide, -1, keepdims=True)
    factor = lax.rsqrt(squares / (heads * width) + 1e-05)
    return [total * factor for total in sums]


def stat_rows(columns, rows):
    lane = lax.broadcasted_iota(jnp.int32, (rows, LANES), 1)
    table = jnp.zeros((rows, LANES), jnp.float32)
    for index, column in enumerate(columns):
        table = jnp.where(lane == index, column, table)
    return table.T[:STAT_ROWS]


def split_refs(counts, refs):
    parts = []
    for count in counts:
        parts.append(refs[:count])
        refs = refs[count:]
    return parts, refs


def rows_of(blocks, row_at, rows):
    parts = []
    at = 0
    for block in blocks:
        size = block.shape[0]
        low, high = max(row_at - at, 0), min(row_at + rows - at, size)
        if low < high:
            parts.append(block[low:high])
        at += size
    return jnp.concatenate(parts, 0) if len(parts) > 1 else parts[0]


def attend_kernel(counts, own, row_at, rows, table_at, *refs):
    blocks, refs = split_refs(counts, refs)
    gain, w_query, cosine, sine, wide_keys, wide_values, mark, *outputs = refs
    pieces = [rows_of(one, row_at, rows) for one in blocks]
    (product,) = project_normed(pieces, gain, [w_query])
    cosine = cosine[table_at : table_at + rows]
    sine = sine[table_at : table_at + rows]
    kv_heads = wide_keys.shape[0]
    repeat = product.shape[1] // HD // kv_heads
    queries = [
        (rotate(product[:, head * HD : (head + 1) * HD], cosine, sine) * log2_scale).astype(
            jnp.bfloat16
        )
        for head in range(kv_heads * repeat)
    ]
    step = min(rows, LANES)
    mark = mark[: repeat * step]
    tiles = [(head, at) for head in range(kv_heads) for at in range(0, rows, step)]

    def scores_of(head, at):
        stacked = jnp.concatenate(
            [query[at : at + step] for query in queries[head * repeat : (head + 1) * repeat]], 0
        )
        return dot_transposed(jnp.concatenate([stacked, mark], 1), wide_keys[head])

    columns = {}
    following = scores_of(*tiles[0])
    for index, (head, at) in enumerate(tiles):
        scores = following
        if index + 1 < len(tiles):
            following = scores_of(*tiles[index + 1])
        largest = jnp.max(scores, -1, keepdims=True)
        weights = jnp.exp2(scores - largest).astype(jnp.bfloat16)
        summed = dot(weights, wide_values[head])
        denominator = summed[:, HD : HD + 1]
        result = summed[:, :HD] / denominator
        logs = largest + jnp.log2(denominator)
        for turn in range(repeat):
            part = slice(turn * step, (turn + 1) * step)
            to = slice((head * repeat + turn) * HD, (head * repeat + turn + 1) * HD)
            outputs[0][at : at + step, to] = result[part].astype(outputs[0].dtype)
            columns.setdefault(head * repeat + turn, []).append(logs[part])
    stats = stat_rows([jnp.concatenate(parts, 0) for parts in columns.values()], rows)
    if own:
        outputs[1][...] = stats
        outputs[2][...] = jnp.concatenate(queries, 1)
        return
    outputs[0][rows:] = jnp.zeros((ROW_TILE, outputs[0].shape[1]), jnp.bfloat16)
    rest = jnp.concatenate([stats, jnp.zeros((ROW_TILE - STAT_ROWS, rows), jnp.float32)], 0)
    for part in range(3):
        rounded = rest.astype(jnp.bfloat16)
        outputs[0][rows:, part * rows : (part + 1) * rows] = rounded
        rest = rest - rounded.astype(jnp.float32)


def attend(
    pieces, gain, w_query, tables, wide_keys, wide_values, mark, own, row_at, rows, table_at,
    earlier,
):
    counts = [len(blocks) for blocks in pieces]
    flat = [block for blocks in pieces for block in blocks]
    out_width = w_query.shape[1]
    slots = wide_keys.shape[1]
    if own:
        out_shape = [
            jax.ShapeDtypeStruct((rows, out_width), jnp.float32),
            jax.ShapeDtypeStruct((STAT_ROWS, rows), jnp.float32),
            jax.ShapeDtypeStruct((rows, out_width), jnp.bfloat16),
        ]
    else:
        out_shape = [jax.ShapeDtypeStruct((rows + ROW_TILE, out_width), jnp.bfloat16)]
    return call(
        functools.partial(attend_kernel, counts, own, row_at, rows, table_at),
        out_shape,
        [*flat, gain, w_query, *tables, wide_keys, wide_values, mark],
        28,
        2 * rows * out_width * (w_query.shape[0] + 4 * slots),
        rows * out_width // HD * slots,
        "attend_own" if own else "attend_partner",
        earlier,
    )


def fresh_kernel(counts, table_at, *refs):
    blocks, refs = split_refs(counts, refs)
    gain, w_key, w_value, cosine, sine, new_keys, new_values = refs
    rows = new_keys.shape[0]
    pieces = [whole_of(one) for one in blocks]
    keys, values = project_normed(pieces, gain, [w_key, w_value])
    cosine = cosine[table_at : table_at + rows]
    sine = sine[table_at : table_at + rows]
    for head in range(keys.shape[1] // HD):
        own = slice(head * HD, (head + 1) * HD)
        new_keys[:, own] = rotate(keys[:, own], cosine, sine).astype(jnp.bfloat16)
    new_values[...] = values.astype(jnp.bfloat16)


def fresh(pieces, gain, w_key, w_value, tables, table_at, earlier):
    flat = [block for blocks in pieces for block in blocks]
    rows = sum(block.shape[0] for block in pieces[0])
    shape = jax.ShapeDtypeStruct((rows, w_key.shape[1]), jnp.bfloat16)
    return call(
        functools.partial(fresh_kernel, [len(blocks) for blocks in pieces], table_at),
        [shape, shape],
        [*flat, gain, w_key, w_value, *tables],
        20,
        4 * rows * w_key.size,
        0,
        "fresh_kv",
        earlier,
    )


def write_rows(target, fresh_rows, first):
    rows = fresh_rows.shape[0]
    slab_rows = target.shape[0]
    span = rows + ROW_TILE
    start = jnp.clip(first, 0, slab_rows - span)
    start = start - lax.rem(start, ROW_TILE)
    window = pl.ds(pl.multiple_of(start, ROW_TILE), span)
    shift = start - first
    place = lax.broadcasted_iota(jnp.int32, (span, rows), 0) + shift
    chosen = place == lax.broadcasted_iota(jnp.int32, (span, rows), 1)
    moved = dot(chosen.astype(jnp.bfloat16), fresh_rows)
    row = lax.broadcasted_iota(jnp.int32, (span, target.shape[1]), 0) + shift
    inside = (row >= 0) & (row < rows)
    old = target[window, :].astype(jnp.float32)
    target[window, :] = jnp.where(inside, moved, old).astype(jnp.bfloat16)


def attend_fresh_kernel(groups, requests, *refs):
    query_refs, refs = refs[:CHUNKS], refs[CHUNKS:]
    key_refs, value_refs, refs = refs[:groups], refs[groups : 2 * groups], refs[2 * groups :]
    partial, stats = refs
    position_in = place_of(requests)[1]
    rows, width = partial.shape
    kv_heads = key_refs[0].shape[1] // HD
    repeat = width // HD // kv_heads
    queries = whole_of(query_refs)
    token = lax.broadcasted_iota(jnp.int32, (rows, rows), 0)
    within = lax.broadcasted_iota(jnp.int32, (rows, rows), 1)
    causal = jnp.where(within <= token, 0.0, neg_large)
    causal = jnp.concatenate([causal] * repeat, 0)
    lane = lax.broadcasted_iota(jnp.int32, (rows, LANES), 1)
    ones = jnp.where(lane == 0, 1.0, 0.0).astype(jnp.bfloat16)
    hidden = [jnp.zeros((rows, LANES), jnp.bfloat16)]
    for turn in range(1, groups):
        later = source_of(position_in, turn, groups) > position_in
        hidden.append(jnp.where((lane == 0) & later, neg_large, 0.0).astype(jnp.bfloat16))
    columns = []
    for head in range(kv_heads):
        own = [
            slice((head * repeat + turn) * HD, (head * repeat + turn + 1) * HD)
            for turn in range(repeat)
        ]
        shared = slice(head * HD, (head + 1) * HD)
        stacked = jnp.concatenate([queries[:, one] for one in own], 0)
        stacked = jnp.concatenate([stacked, jnp.concatenate([ones] * repeat, 0)], 1)
        scores = [
            dot_transposed(stacked, jnp.concatenate([ref[:, shared], bias], 1))
            for ref, bias in zip(key_refs, hidden)
        ]
        scores = jnp.concatenate([scores[0] + causal] + scores[1:], 1)
        largest = jnp.max(scores, -1, keepdims=True)
        weights = jnp.exp2(scores - largest).astype(jnp.bfloat16)
        wide_values = [jnp.concatenate([ref[:, shared], ones], 1) for ref in value_refs]
        summed = dot(weights, jnp.concatenate(wide_values, 0))
        denominator = summed[:, HD : HD + 1]
        result = summed[:, :HD] / denominator
        logs = largest + jnp.log2(denominator)
        for turn, one in enumerate(own):
            part = slice(turn * rows, (turn + 1) * rows)
            partial[:, one] = result[part]
            columns.append(logs[part])
    stats[...] = stat_rows(columns, rows)


def attend_fresh(requests, queries, new_keys, new_values):
    groups = len(new_keys)
    rows = new_keys[0].shape[0]
    width = queries[0].shape[1]
    return call(
        functools.partial(attend_fresh_kernel, groups, requests),
        [
            jax.ShapeDtypeStruct((rows, width), jnp.float32),
            jax.ShapeDtypeStruct((STAT_ROWS, rows), jnp.float32),
        ],
        [*queries, *new_keys, *new_values],
        24,
        4 * rows * width * rows * groups,
        rows * width // HD * rows * groups,
        "attend_fresh",
    )


def update_kernel(groups, *refs):
    key_refs, value_refs, refs = refs[:groups], refs[groups : 2 * groups], refs[2 * groups :]
    keys, values, lengths_in, keys_updated, values_updated, done, lengths, semaphore = refs
    number = pltpu.make_async_copy(lengths_in, lengths, semaphore)
    number.start()
    keys_updated[...] = keys[...]
    values_updated[...] = values[...]
    done[...] = jnp.zeros(done.shape, done.dtype)
    number.wait()
    request, position_in = place_of(lengths.shape[0])
    rows = key_refs[0].shape[0]
    for turn in range(groups):
        source = source_of(position_in, turn, groups)
        first = lengths[request] + source * rows - position_in * keys.shape[0]
        write_rows(keys_updated, key_refs[turn][...], first)
        write_rows(values_updated, value_refs[turn][...], first)


def update(lengths, new_keys, new_values, keys, values, earlier):
    groups = len(new_keys)
    slab = jax.ShapeDtypeStruct(keys.shape, keys.dtype)
    return call(
        functools.partial(update_kernel, groups),
        [slab, slab, jax.ShapeDtypeStruct((STAT_ROWS, LANES), jnp.float32)],
        [*new_keys, *new_values, keys, values, lengths],
        20,
        4 * new_keys[0].size * new_keys[0].shape[0] * groups,
        0,
        "update_caches",
        earlier,
        [pltpu.SMEM(lengths.shape, lengths.dtype), pltpu.SemaphoreType.DMA],
    )


def combine_kernel(row_at, own_partial, own_stats, fresh_partial, fresh_stats, *refs):
    heads = lax.axis_size("head")
    chips = heads // CORES
    outputs = 2 * chips - 1
    received = refs[: -1 - outputs]
    w_out, merged_rows = refs[-1 - outputs], refs[-outputs]
    far = refs[1 - outputs :]
    width = own_partial.shape[1]
    rows = merged_rows.shape[0]
    part = slice(row_at, row_at + rows)
    padding = jnp.zeros((LANES - STAT_ROWS, rows), jnp.float32)
    stats = [own_stats[...], fresh_stats[:, part]]
    for ref in received:
        stats.append(
            sum(
                ref[rows:, turn * rows : (turn + 1) * rows].astype(jnp.float32)
                for turn in range(3)
            )[:STAT_ROWS]
        )
    logs = [jnp.concatenate([stat, padding], 0).T for stat in stats]
    largest = functools.reduce(jnp.maximum, logs)
    shares = [jnp.exp2(log - largest) for log in logs]
    total = functools.reduce(jnp.add, shares)
    shares = [share / total for share in shares]
    attended = []
    for head in range(width // HD):
        own = slice(head * HD, (head + 1) * HD)
        column = slice(head, head + 1)
        merged = own_partial[:, own] * shares[0][:, column]
        merged = merged + fresh_partial[part, own] * shares[1][:, column]
        for ref, share in zip(received, shares[2:]):
            merged = merged + ref[:rows, own].astype(jnp.float32) * share[:, column]
        attended.append(merged.astype(jnp.bfloat16))
    attended = jnp.concatenate(attended, 1)
    merged_rows[...] = attended
    for ahead in range(1, chips):
        result = block_product(attended, w_out, ahead, 1)
        middle = result.shape[1] // 2
        far[2 * ahead - 2][...] = result[:, :middle]
        far[2 * ahead - 1][...] = result[:, middle:]


def block_product(attended, w_out, ahead, flip):
    heads = lax.axis_size("head")
    block_width = w_out.shape[1] // heads
    block = lax.rem(lax.axis_index("head") + CORES * ahead, heads) ^ flip
    along = pl.ds(pl.multiple_of(block * block_width, LANES), block_width)
    return dot(attended, w_out[:, along]).astype(jnp.bfloat16)


def project_kernel(merged_rows, w_out, far, *near):
    attended = merged_rows[...]
    far[...] = block_product(attended, w_out, 0, 1)
    for ahead, target in enumerate(near):
        target[...] = block_product(attended, w_out, ahead, 0)


def combine(row_at, rows, own, fresh_part, received, w_out, heads, earlier):
    chips = heads // CORES
    width = w_out.shape[1] // heads
    merged = jax.ShapeDtypeStruct((rows, own[0].shape[1]), jnp.bfloat16)
    half = jax.ShapeDtypeStruct((rows, width // 2), jnp.bfloat16)
    merged, *far = call(
        functools.partial(combine_kernel, row_at),
        [merged] + [half] * (2 * chips - 2),
        [*own, *fresh_part, *received, w_out],
        20,
        rows * w_out.size,
        0,
        "combine",
        earlier,
    )
    return merged, [far[2 * k : 2 * k + 2] for k in range(chips - 1)]


def project(merged, w_out, heads):
    block = jax.ShapeDtypeStruct((merged.shape[0], w_out.shape[1] // heads), jnp.bfloat16)
    far, *near = call(
        project_kernel,
        [block] * (1 + heads // CORES),
        [merged, w_out],
        20,
        2 * merged.shape[0] * w_out.size,
        0,
        "project",
    )
    return far, near


def sum_kernel(count, *refs):
    total = refs[0][...].astype(jnp.float32)
    total = total + jnp.concatenate([ref[...] for ref in refs[1:count]], 1).astype(jnp.float32)
    refs[count][...] = total.astype(jnp.bfloat16)


def sum_cores(near, far, earlier):
    return call(
        functools.partial(sum_kernel, 1 + len(far)),
        [jax.ShapeDtypeStruct(near.shape, near.dtype)],
        [near, *far],
        8,
        near.size,
        0,
        "sum_cores",
        earlier,
    )[0]


def collect_kernel(count, *refs):
    *parts, ready, base = refs
    ready[...] = sum(ref[...].astype(jnp.float32) for ref in parts[:count]).astype(ready.dtype)
    base[...] = sum(ref[...].astype(jnp.float32) for ref in parts[count:])


def finish_kernel(ready, base, *refs):
    *landed, result = refs
    rows = ready.shape[0]
    result[:rows] = ready[...]
    total = base[...]
    for ref in landed:
        total = total + ref[...].astype(jnp.float32)
    result[rows:] = total.astype(result.dtype)


def finish(parts, earlier):
    count = len(parts) // CHUNKS
    rows, width = parts[0].shape
    shape = jax.ShapeDtypeStruct((rows, width), jnp.bfloat16)
    base = jax.ShapeDtypeStruct((rows, width), jnp.float32)
    kernel = functools.partial(collect_kernel, count)
    found = call(kernel, [shape, base], parts[: count + CORES], 8, 0, 0, "collect", earlier)
    result = jax.ShapeDtypeStruct((CHUNKS * rows, width), jnp.bfloat16)
    return call(finish_kernel, [result], [*found, *parts[count + CORES :]], 8, 0, 0, "finish")[0]


def shards(
    tokens,
    norm_gain,
    w_query,
    w_key,
    w_value,
    w_out,
    keys_cache,
    values_cache,
    cached_lengths,
    rope_offsets,
):
    rows, width = tokens.shape
    requests = cached_lengths.shape[0]
    groups = lax.axis_size("seq") // requests
    heads = lax.axis_size("head")
    chips = heads // CORES
    chunk_rows = rows // CHUNKS
    gain = norm_gain.reshape(heads, 1, width)

    mark = marks(keys_cache.shape[0])
    tables = rope_tables(cached_lengths, rope_offsets, groups, rows, [mark])
    wide_keys, wide_values = widen(keys_cache, values_cache, mark, cached_lengths, tables[:1])

    def attend_rows(pieces, own, chunk, turn, earlier):
        at = chunk * chunk_rows
        return attend(
            pieces, gain, w_query, tables, wide_keys, wide_values, mark, own, at if own else 0,
            chunk_rows, turn * rows + at, earlier,
        )

    half = chunk_rows // 2
    from_chips = other_chips(tokens)
    crossed = other_core(tokens)
    own, early, late = relay([tokens], [rows, chunk_rows, rows - chunk_rows], [])
    first = [shifted(early, "seq", turn * requests) for turn in range(1, groups)]
    (late,) = relay([late], [rows - chunk_rows], from_chips + [wide_keys])
    second = [shifted(late, "seq", turn * requests) for turn in range(1, groups)]
    own_cuts = [relay([piece], [rows, half, half, rows - chunk_rows], [late]) for piece in from_chips]
    own_pieces = [[own]] + [[cut[0]] for cut in own_cuts] + [[crossed]]
    own_pieces += [[other_core(block) for block in cut[1:]] for cut in own_cuts]
    own_early = [
        blocks if len(blocks) == 1 else blocks[: len(blocks) - 1] for blocks in own_pieces
    ]
    earlier = [cut[0] for cut in own_cuts]
    first = [relay([piece], [chunk_rows], earlier)[0] for piece in first]
    first_from_chips = [other_chips(piece) for piece in first]
    *own_part, queries = attend_rows(own_early, True, 0, 0, first)
    own_queries = [queries]
    new_rows = [fresh(own_pieces, gain, w_key, w_value, tables, 0, [queries])]
    earlier = [new_rows[0][0]]
    second = [relay([piece], [rows - chunk_rows], earlier)[0] for piece in second]
    second_from_chips = [other_chips(piece) for piece in second]
    earlier = second

    def gather_cores(piece, from_chips, earlier):
        size = piece.shape[0]
        passed = [relay([one], [size, size // 2, size // 2], earlier) for one in from_chips]
        blocks = [[piece]] + [[one[0]] for one in passed] + [[other_core(piece)]]
        blocks += [[other_core(part) for part in one[1:]] for one in passed]
        return blocks, [one[0] for one in passed]

    gathered = []
    for piece, from_chips in zip(first, first_from_chips):
        blocks, passed = gather_cores(piece, from_chips, earlier)
        gathered.append([blocks])
        earlier = earlier + passed
    received = [[] for _ in range(CHUNKS)]
    for turn in range(1, groups):
        (packed,) = attend_rows(gathered[turn - 1][0], False, 0, turn, earlier)
        received[0].append(shifted(packed, "seq", -turn * requests))
        earlier = [packed]
    *late_part, queries = attend_rows(own_pieces, True, 1, 0, earlier)
    own_part += late_part
    own_queries.append(queries)
    earlier = [queries]
    for blocks, piece, from_chips in zip(gathered, second, second_from_chips):
        along, passed = gather_cores(piece, from_chips, earlier)
        blocks.append(along)
        earlier = earlier + passed
    for turn in range(1, groups):
        (packed,) = attend_rows(gathered[turn - 1][1], False, 1, turn, earlier)
        received[1].append(shifted(packed, "seq", -turn * requests))
        earlier = [packed]
    for turn in range(1, groups):
        pieces = [sum(blocks, []) for blocks in zip(*gathered[turn - 1])]
        new_rows.append(fresh(pieces, gain, w_key, w_value, tables, turn * rows, earlier))
    new_keys, new_values = zip(*new_rows)
    fresh_part = attend_fresh(requests, own_queries, new_keys, new_values)

    parts = []
    earlier = before_sums = []
    for chunk in range(CHUNKS):
        merged, fars = combine(
            chunk * chunk_rows, chunk_rows, own_part[2 * chunk : 2 * chunk + 2], fresh_part,
            received[chunk], w_out, heads, earlier,
        )
        fars = [[other_core(part) for part in far] for far in fars]
        far, near = project(merged, w_out, heads)
        earlier = [far] + before_sums
        sums = [sum_cores(one, parts_far, earlier) for one, parts_far in zip(near[1:], fars)]
        from_chips = [shifted(one, "head", CORES * k) for k, one in enumerate(sums, 1)]
        parts += [near[0], other_core(far), *from_chips]
        earlier, before_sums = sums, from_chips
    keys_updated, values_updated, done = update(
        cached_lengths, new_keys, new_values, keys_cache, values_cache, earlier
    )
    return (finish(parts, [done]), keys_updated, values_updated)


def solution(mesh):
    return jax.shard_map(
        shards,
        mesh=mesh,
        in_specs=(
            P("seq", "head"),
            P(),
            P(None, "head"),
            P(None, "head"),
            P(None, "head"),
            P("head", None),
            P("seq", "head"),
            P("seq", "head"),
            P(),
            P(),
        ),
        out_specs=(P("seq", "head"), P("seq", "head"), P("seq", "head")),
        check_vma=False,
    )
```
